32 devices in a mesh: batch: 4 (over x, core), item: 8 (over z, y).
Axes of the slice: x: 2, y: 2, z: 4, core: 2. Of those that a mesh axis runs over, the one named last changes fastest.
Arguments:
- user_vectors: bfloat16 [8192, 512], P(('batch', 'item')), may hold values from -6 to 6
- item_table: bfloat16 [131072, 512], P(('batch', 'item')), may hold values from -0.25 to 0.25
- tower_weight: bfloat16 [512, 512], replicated, may hold values from -3 to 3
- item_owner: int32 [8192, 1], P(('batch', 'item')), may hold values from 0 to 31; in each aligned block of 256 rows (0 to 255, 256 to 511, ...) at most 16 rows name the same one
- item_row: int32 [8192], P(('batch', 'item')), may hold values from 0 to 4095
Outputs:
- table_grad: bfloat16 [131072, 512], P(('batch', 'item'))
- weight_grad: float32 [512, 512], P(('batch', 'item'))
The draws below stay inside these ranges and needn't reach their ends.
Inputs may be any that keep to these rules, and one draw needn't show every extreme that they name: `item_owner`: within the rows of one device (aligned blocks of 256 rows) no owner is named by more than 16 rows, a bound that some block reaches.
All inputs are finite; a program needn't handle non-finite values.
Results may differ from the reference program's by a relative error of at most 0.0075.
Values may be sent and summed in bfloat16 or wider, within the bound.
No kernel may reach another device: no remote copies, remote signals or barrier semaphores. Data moves between devices by JAX's collectives and lax.ppermute only.
A program may use at most 64 MiB of HBM per device.

```python
import math
import jax
import jax.numpy as jnp
import numpy as np
from jax import lax

D = 512
B_DEV = 256
ROWS_DEV = 4096
TOTAL = 8192
ITEMS = 131072
OWNERS = 32
CAP = 16
GROUP = 1024
N_BATCH = 4
N_ITEM = 8


def place_ends(entries, rng, low, top_value):
    shape = entries.shape
    spot = [jax.random.randint(jax.random.fold_in(rng, axis), (), 0, shape[axis]) for axis in range(len(shape))]
    entries = entries.at[tuple(spot)].set(low)
    longest = shape.index(max(shape))
    spot[longest] = (spot[longest] + 1) % shape[longest]
    return entries.at[tuple(spot)].set(top_value)


def block_scale(key, dims, shards, least, largest):
    level, own = 1.0, jax.random.fold_in(key, 6)
    for dim, blocks in shards:
        heights = jnp.exp(jax.random.uniform(jax.random.fold_in(own, dim), (blocks,), jnp.float32, least / len(shards), largest / len(shards)))
        level = level * jnp.repeat(heights, dims[dim] // blocks).reshape([-1 if axis == dim else 1 for axis in range(len(dims))])
    return level


def deal_out(key, own, number, rows, number_of, top, limit, slope):
    ranking = jax.random.permutation(key, number_of)
    crowded, ordinary = shares(number_of, rows * top, limit, slope, True), shares(number_of, rows * top, limit, slope, False)
    places = jnp.arange(number_of)

    def named(tallies, turn):
        used = int((tallies > 0).sum())
        fixed = max(1, used // 4)
        shifted = fixed + (places - fixed + turn * (used - fixed)) % max(1, number_of - fixed)
        return jnp.zeros((number_of,), jnp.int32).at[ranking[jnp.where(places < fixed, places, shifted)]].set(jnp.asarray(tallies, jnp.int32))

    tallies = jnp.where(number % 4 == 0, named(crowded, number // 4), named(ordinary, number - number // 4 - 1))
    mixed = jax.random.permutation(jax.random.fold_in(own, 3), number_of)
    giver, taker = mixed[0:number_of // 2 * 2:2], mixed[1:number_of // 2 * 2:2]
    margin = jnp.minimum(tallies[giver] - 1, limit - tallies[taker]) // 2
    margin = jnp.where((giver == ranking[0]) | (taker == ranking[0]) | (tallies[taker] == 0), 0, jnp.maximum(margin, 0))
    shifted = jax.random.randint(jax.random.fold_in(own, 4), (number_of // 2,), 0, 1 << 20) % (margin + 1)
    tallies = tallies.at[giver].add(-shifted).at[taker].add(shifted)
    labels = jnp.searchsorted(jnp.cumsum(tallies), jnp.arange(rows * top), side="right").astype(jnp.int32)
    listing = labels.reshape(top, rows).T
    listing = listing[jax.random.permutation(jax.random.fold_in(own, 1), rows)]
    turn = jax.random.randint(jax.random.fold_in(own, 2), (rows, 1), 0, top)
    return jnp.take_along_axis(listing, (jnp.arange(top)[None, :] + turn) % top, axis=1)


def shares(number_of, total, bound, lean, full):
    portions = [(1 << 20) // math.isqrt(grade ** lean) + 1 for grade in range(1, number_of + 1)]
    largest = bound if full else min(bound, max(-(-total // number_of), total * portions[0] // sum(portions)))
    least = 1 if total - largest >= number_of - 1 else 0
    holding, spare = [largest] + [least] * (number_of - 1), total - largest - least * (number_of - 1)
    while spare > 0:
        free = [i for i in range(1, number_of) if holding[i] < largest] or [i for i in range(1, number_of) if holding[i] < bound]
        whole, left = sum([portions[i] for i in free]), spare
        for i in free:
            addition = min(bound - holding[i], max(1, left * portions[i] // whole), spare)
            holding[i] = holding[i] + addition
            spare = spare - addition
    return np.array(holding)


def bell_draw(own_key, shape, width, bound, cuts=(), kind=jnp.bfloat16):
    drawn = jax.random.normal(own_key, shape, jnp.float32) * width
    if len(cuts) > 0:
        drawn = block_scale(own_key, shape, cuts, -0.22, 0.18) * drawn
    return jnp.clip(drawn, min=-bound, max=bound).astype(kind)


def setup_inputs(seed: int = 0) -> dict:
    keys = jax.random.split(jax.random.key(seed), 6)
    user_vectors = bell_draw(keys[0], (TOTAL, D), 1.0, 6.0, ((0, 32),))
    item_table = bell_draw(keys[1], (ITEMS, D), D ** -0.5, 0.25, ((0, 32),))
    tower_weight = bell_draw(keys[2], (D, D), (D // 128) ** -0.5, 3.0)
    item_owner_keys = jax.random.split(jax.random.fold_in(keys[3], 1), TOTAL // B_DEV)
    item_owner_turns = jax.random.permutation(jax.random.fold_in(keys[3], 3), TOTAL // B_DEV)
    item_owner = jax.vmap(lambda own, number: deal_out(jax.random.fold_in(keys[3], 2), own, number, B_DEV, OWNERS, 1, CAP, 2))(item_owner_keys, item_owner_turns).reshape((TOTAL, 1))
    item_row = place_ends(jax.random.randint(keys[4], (TOTAL,), 0, ROWS_DEV), jax.random.fold_in(keys[4], 1), 0, ROWS_DEV - 1).astype(jnp.int32)
    return {"user_vectors": user_vectors, "item_table": item_table, "tower_weight": tower_weight, "item_owner": item_owner, "item_row": item_row}


epsilon = 1e-06
score_scale = 60.0
cauchy_scale = 4.0

def group_grad(pair):
    item_vec, user_unit = pair
    score = jnp.dot(item_vec, user_unit.T, preferred_element_type=jnp.float32) * score_scale
    expo = jnp.exp(score)
    total = lax.optimization_barrier(jnp.sum(expo, axis=1))
    mixed = jnp.dot(expo.astype(jnp.bfloat16), user_unit, preferred_element_type=jnp.float32)
    user_f = user_unit.astype(jnp.float32)
    positive = lax.optimization_barrier(jnp.sum(item_vec.astype(jnp.float32) * user_f, axis=1)) * score_scale
    xent = jnp.log(total) - positive
    cweight = 1.0 / (1.0 + xent / cauchy_scale)
    return cweight[:, None] * score_scale * (mixed / total[:, None] - user_f)

def regroup(values):
    return values.reshape(N_BATCH, N_ITEM, B_DEV, D).transpose(1, 0, 2, 3).reshape(N_ITEM, GROUP, D)

def reference(user_vectors, item_table, tower_weight, item_owner, item_row):
    item_id = (item_owner[:, 0] * ROWS_DEV + item_row).astype(jnp.int32)
    embed = item_table[item_id]
    hidden = jnp.dot(embed, tower_weight, preferred_element_type=jnp.float32)
    rscale = lax.rsqrt(lax.optimization_barrier(jnp.mean(hidden * hidden, axis=1, keepdims=True)) + epsilon)
    item_vec = (hidden * rscale / jnp.sqrt(jnp.float32(D))).astype(jnp.bfloat16)
    user_f = user_vectors.astype(jnp.float32)
    user_unit = (user_f * lax.rsqrt(lax.optimization_barrier(jnp.mean(user_f * user_f, axis=1, keepdims=True)) + epsilon) / jnp.sqrt(jnp.float32(D))).astype(jnp.bfloat16)
    dvec = lax.map(group_grad, (regroup(item_vec), regroup(user_unit)))
    dvec = dvec.reshape(N_ITEM, N_BATCH, B_DEV, D).transpose(1, 0, 2, 3).reshape(TOTAL, D)
    inner = lax.optimization_barrier(jnp.sum(hidden * dvec, axis=1, keepdims=True))
    dhidden = (rscale / jnp.sqrt(jnp.float32(D)) * (dvec - hidden * rscale * rscale * inner / D)).astype(jnp.bfloat16)
    weight_grad = jnp.dot(embed.T, dhidden, preferred_element_type=jnp.float32)
    drow = jnp.dot(dhidden, tower_weight.T, preferred_element_type=jnp.float32)
    table_grad = jnp.zeros((ITEMS, D), jnp.float32).at[item_id].add(drow).astype(jnp.bfloat16)
    return (table_grad, weight_grad)
```

```python
import functools

import jax
import jax.numpy as jnp
from jax import lax
from jax.experimental import pallas as pl
from jax.experimental.pallas import tpu as pltpu
from jax.sharding import PartitionSpec as P

epsilon = 1e-06
score_scale = 60.0
cauchy_scale = 4.0
f32 = jnp.float32
bf16 = jnp.bfloat16
i32 = jnp.int32
VMEM_LIMIT = 32 * 1024 * 1024


def iota(shape, dim):
    return lax.broadcasted_iota(i32, shape, dim)


def hot(mask):
    return jnp.where(mask, 1.0, 0.0).astype(bf16)


def dot(a, b, a_dim=1, b_dim=0):
    return lax.dot_general(a, b, (((a_dim,), (b_dim,)), ((), ())), preferred_element_type=f32)


def halves(value):
    return (value >> 8).astype(f32), (value & 255).astype(f32)


def request_kernel(owner_ref, row_ref, request_ref, place_ref):
    devices, slots = request_ref.shape
    n = owner_ref.shape[1]
    owner = owner_ref[...]
    named = owner == iota((devices, n), 0)
    count = dot(hot(named), hot(iota((n, n), 0) <= iota((n, n), 1)))
    rank = jnp.sum(jnp.where(named, count, 0.0), axis=0, keepdims=True).astype(i32) - 1
    in_slot = hot(rank == iota((slots, n), 0))
    high, low = halves(row_ref[...] + 1)
    high = dot(jnp.where(named, high, 0.0).astype(bf16), in_slot, 1, 1)
    low = dot(jnp.where(named, low, 0.0).astype(bf16), in_slot, 1, 1)
    request_ref[...] = (high * 256.0 + low).astype(i32) - 1
    place_ref[...] = owner * slots + rank


def asked_column(asked):
    devices, slots = asked.shape
    total = devices * slots
    first = iota((total, devices), 1) * slots
    spot = iota((total, devices), 0)
    pick = hot((spot >= first) & (spot < first + slots))
    high, low = halves(asked)
    value = dot(pick, high.astype(bf16)) * 256.0 + dot(pick, low.astype(bf16))
    mine = lax.rem(iota((total, slots), 0), slots) == iota((total, slots), 1)
    return jnp.sum(jnp.where(mine, value, 0.0), axis=1, keepdims=True)


def asked_line(asked):
    devices, slots = asked.shape
    total = devices * slots
    pick = hot(lax.rem(iota((slots, total), 1), slots) == iota((slots, total), 0))
    high, low = halves(asked)
    value = dot(high.astype(bf16), pick) * 256.0 + dot(low.astype(bf16), pick)
    first = iota((devices, total), 0) * slots
    spot = iota((devices, total), 1)
    mine = (spot >= first) & (spot < first + slots)
    return jnp.sum(jnp.where(mine, value, 0.0), axis=0, keepdims=True)


def fetch_kernel(asked_ref, table_ref, found_ref, column, total):
    step = pl.program_id(0)
    chunk = table_ref.shape[0]

    @pl.when(step == 0)
    def _():
        column[...] = asked_column(asked_ref[...]).astype(i32)

    pick = hot(column[...] - step * chunk == iota((column.shape[0], chunk), 1))
    part = dot(pick, table_ref[...])

    @pl.when(step == 0)
    def _():
        total[...] = part

    @pl.when(step > 0)
    def _():
        total[...] += part

    @pl.when(step == pl.num_programs(0) - 1)
    def _():
        found_ref[...] = total[...].astype(bf16)


def unit_of(users):
    width = users.shape[1]
    users = users.astype(f32)
    mean = jnp.mean(users * users, axis=1, keepdims=True)
    return (users * lax.rsqrt(mean + epsilon) * (1.0 / width**0.5)).astype(bf16)


def prepare_kernel(place_ref, asked_ref, own_ref, users_ref, unit_ref, own_unit_ref, take_ref, give_ref, line_ref):
    n, total = take_ref.shape
    unit_ref[...] = unit_of(users_ref[...])
    own_unit_ref[...] = unit_of(own_ref[...])
    place = place_ref[...]
    column = jnp.sum(jnp.where(iota((n, n), 0) == iota((n, n), 1), place, 0), axis=1, keepdims=True)
    take_ref[...] = hot(column == iota((n, total), 1))
    give_ref[...] = hot(place == iota((total, n), 0))
    line_ref[...] = asked_line(asked_ref[...]).astype(i32)


def main_kernel(fetched_ref, weight_ref, unit_ref, own_unit_ref, take_ref, give_ref, outgoing_ref, embed_ref, dhidden_ref):
    width = weight_ref.shape[0]
    root = 1.0 / width**0.5
    embed = dot(take_ref[...], fetched_ref[...]).astype(bf16)
    hidden = dot(embed, weight_ref[...])
    rscale = lax.rsqrt(jnp.mean(hidden * hidden, axis=1, keepdims=True) + epsilon)
    item_vec = (hidden * (rscale * root)).astype(bf16)
    unit = unit_ref[...]
    expo = jnp.exp(dot(item_vec, unit, 1, 1) * score_scale)
    total = jnp.sum(expo, axis=1, keepdims=True)
    mixed = dot(expo.astype(bf16), unit)
    own = own_unit_ref[...].astype(f32)
    positive = jnp.sum(item_vec.astype(f32) * own, axis=1, keepdims=True) * score_scale
    xent = jnp.log(total) - positive
    cweight = 1.0 / (1.0 + xent * (1.0 / cauchy_scale))
    dvec = (cweight * score_scale) * (mixed * (1.0 / total) - own)
    inner = jnp.sum(hidden * dvec, axis=1, keepdims=True)
    dhidden = (rscale * root * (dvec - hidden * (rscale * rscale * inner * (1.0 / width)))).astype(bf16)
    outgoing_ref[...] = dot(give_ref[...], dhidden).astype(bf16)
    embed_ref[...] = embed
    dhidden_ref[...] = dhidden


def share_kernel(embed_ref, dhidden_ref, share_ref):
    share_ref[...] = dot(embed_ref[...], dhidden_ref[...], 0, 0).astype(bf16)


def table_kernel(line_ref, incoming_ref, weight_ref, table_grad_ref, drow):
    step = pl.program_id(0)
    chunk = table_grad_ref.shape[0]

    @pl.when(step == 0)
    def _():
        drow[...] = dot(incoming_ref[...], weight_ref[...], 1, 1).astype(bf16)

    pick = hot(line_ref[...] - step * chunk == iota((chunk, line_ref.shape[1]), 0))
    table_grad_ref[...] = dot(pick, drow[...]).astype(bf16)


def params():
    return pltpu.CompilerParams(vmem_limit_bytes=VMEM_LIMIT)


def call(kernel, outs, *args, flops=0):
    return pl.pallas_call(
        kernel,
        out_shape=[jax.ShapeDtypeStruct(shape, dtype) for shape, dtype in outs],
        compiler_params=params(),
        cost_estimate=pl.CostEstimate(flops=flops, bytes_accessed=1 << 20, transcendentals=0),
    )(*args)


def local(user_vectors, item_table, tower_weight, item_owner, item_row):
    n, width = user_vectors.shape
    rows = item_table.shape[0]
    axes = ("batch", "item")
    devices = lax.axis_size("batch") * lax.axis_size("item")
    slots = 2 * n // devices
    total = devices * slots
    chunk = min(512, rows)

    exchange = functools.partial(lax.all_to_all, axis_name=axes, split_axis=0, concat_axis=0, tiled=True)

    users = lax.all_gather(user_vectors, "batch", axis=0, tiled=True)
    request, place = call(
        request_kernel,
        [((devices, slots), i32), ((1, n), i32)],
        item_owner.reshape(1, n),
        item_row.reshape(1, n),
    )
    asked = exchange(request)
    found = pl.pallas_call(
        fetch_kernel,
        grid=(rows // chunk,),
        in_specs=[
            pl.BlockSpec((devices, slots), lambda k: (0, 0)),
            pl.BlockSpec((chunk, width), lambda k: (k, 0)),
        ],
        out_specs=pl.BlockSpec((total, width), lambda k: (0, 0)),
        out_shape=jax.ShapeDtypeStruct((total, width), bf16),
        scratch_shapes=[pltpu.VMEM((total, 1), i32), pltpu.VMEM((total, width), f32)],
        compiler_params=params(),
        cost_estimate=pl.CostEstimate(flops=2 * total * rows * width, bytes_accessed=2 * rows * width, transcendentals=0),
    )(asked, item_table)
    fetched = exchange(found.reshape(devices, slots, width)).reshape(total, width)
    unit, own_unit, take, give, line = call(
        prepare_kernel,
        [
            (users.shape, bf16),
            ((n, width), bf16),
            ((n, total), bf16),
            ((total, n), bf16),
            ((1, total), i32),
        ],
        place,
        asked,
        user_vectors,
        users,
        flops=1 << 28,
    )
    outgoing, embed, dhidden = call(
        main_kernel,
        [((total, width), bf16), ((n, width), bf16), ((n, width), bf16)],
        fetched,
        tower_weight,
        unit,
        own_unit,
        take,
        give,
        flops=1 << 30,
    )
    incoming = exchange(outgoing.reshape(devices, slots, width)).reshape(total, width)
    (share,) = call(share_kernel, [((width, width), bf16)], embed, dhidden, flops=1 << 27)
    shares = exchange(share.reshape(devices, width // devices, width))
    weight_grad = jnp.sum(shares.astype(f32), axis=0)
    table_grad = pl.pallas_call(
        table_kernel,
        grid=(rows // chunk,),
        in_specs=[
            pl.BlockSpec((1, total), lambda k: (0, 0)),
            pl.BlockSpec((total, width), lambda k: (0, 0)),
            pl.BlockSpec((width, width), lambda k: (0, 0)),
        ],
        out_specs=pl.BlockSpec((chunk, width), lambda k: (k, 0)),
        out_shape=jax.ShapeDtypeStruct((rows, width), bf16),
        scratch_shapes=[pltpu.VMEM((total, width), bf16)],
        compiler_params=params(),
        cost_estimate=pl.CostEstimate(flops=2 * total * rows * width, bytes_accessed=2 * rows * width, transcendentals=0),
    )(line, incoming, tower_weight)
    return (table_grad, weight_grad)


def solution(mesh):
    return jax.shard_map(
        local,
        mesh=mesh,
        in_specs=(
            P(("batch", "item"), None),
            P(("batch", "item"), None),
            P(),
            P(("batch", "item"), None),
            P(("batch", "item")),
        ),
        out_specs=(P(("batch", "item"), None), P(("batch", "item"), None)),
        check_vma=False,
    )
```

```python
import functools

import jax
import jax.numpy as jnp
from jax import lax
from jax.experimental import pallas as pl
from jax.experimental.pallas import tpu as pltpu
from jax.sharding import PartitionSpec as P

epsilon = 1e-06
score_scale = 60.0
cauchy_scale = 4.0
f32 = jnp.float32
bf16 = jnp.bfloat16
i32 = jnp.int32
BLOCK = 256


def iota(shape, dim):
    return lax.broadcasted_iota(i32, shape, dim)


def hot(mask):
    return jnp.where(mask, 1.0, 0.0).astype(bf16)


def dot(a, b, a_dim=1, b_dim=0):
    return lax.dot_general(a, b, (((a_dim,), (b_dim,)), ((), ())), preferred_element_type=f32)


def halves(value):
    return (value >> 8).astype(f32), (value & 255).astype(f32)


def request_kernel(owner_ref, row_ref, request_ref, place_ref):
    devices, slots = request_ref.shape
    n = owner_ref.shape[1]
    owner = owner_ref[...]
    named = owner == iota((devices, n), 0)
    count = dot(hot(named), hot(iota((n, n), 0) <= iota((n, n), 1)))
    rank = jnp.sum(jnp.where(named, count, 0.0), axis=0, keepdims=True).astype(i32) - 1
    in_slot = hot(rank == iota((slots, n), 0))
    high, low = halves(row_ref[...] + 1)
    high = dot(jnp.where(named, high, 0.0).astype(bf16), in_slot, 1, 1)
    low = dot(jnp.where(named, low, 0.0).astype(bf16), in_slot, 1, 1)
    request_ref[...] = (high * 256.0 + low).astype(i32) - 1
    place_ref[...] = owner * slots + rank


def asked_column(asked):
    devices, slots = asked.shape
    total = devices * slots
    first = iota((total, devices), 1) * slots
    spot = iota((total, devices), 0)
    pick = hot((spot >= first) & (spot < first + slots))
    high, low = halves(asked)
    value = dot(pick, high.astype(bf16)) * 256.0 + dot(pick, low.astype(bf16))
    mine = lax.rem(iota((total, slots), 0), slots) == iota((total, slots), 1)
    return jnp.sum(jnp.where(mine, value, 0.0), axis=1, keepdims=True)


def asked_line(asked):
    devices, slots = asked.shape
    total = devices * slots
    pick = hot(lax.rem(iota((slots, total), 1), slots) == iota((slots, total), 0))
    high, low = halves(asked)
    value = dot(high.astype(bf16), pick) * 256.0 + dot(low.astype(bf16), pick)
    first = iota((devices, total), 0) * slots
    spot = iota((devices, total), 1)
    mine = (spot >= first) & (spot < first + slots)
    return jnp.sum(jnp.where(mine, value, 0.0), axis=0, keepdims=True)


def parts_of(value):
    return value >> 8, value & 255


def fetch_kernel(asked_ref, table_hbm, found_ref, table, sems):
    groups = sems.shape[0]
    size = table.shape[0] // groups
    copies = [
        pltpu.make_async_copy(table_hbm.at[pl.ds(g * size, size)], table.at[pl.ds(g * size, size)], sems.at[g])
        for g in range(groups)
    ]
    for copy in copies:
        copy.start()
    block, low = parts_of(asked_column(asked_ref[...]).astype(i32))
    total = block.shape[0]
    low_hot = hot(low == iota((total, BLOCK), 1))
    block = jnp.broadcast_to(block.astype(f32), (total, BLOCK)).astype(bf16)
    found = None
    for g, copy in enumerate(copies):
        picks = [
            jnp.where(block == jnp.bfloat16(k), low_hot, jnp.bfloat16(0))
            for k in range(g * size // BLOCK, (g + 1) * size // BLOCK)
        ]
        copy.wait()
        part = dot(jnp.concatenate(picks, axis=1), table[pl.ds(g * size, size)])
        found = part if found is None else found + part
    found_ref[...] = found.astype(bf16)


def unit_of(users):
    width = users.shape[1]
    users = users.astype(f32)
    mean = jnp.mean(users * users, axis=1, keepdims=True)
    return (users * lax.rsqrt(mean + epsilon) * (1.0 / width**0.5)).astype(bf16)


def prepare_kernel(place_ref, asked_ref, *refs):
    *users, unit_ref, column_ref, line_ref = refs
    n = place_ref.shape[1]
    for k, users_ref in enumerate(users):
        unit_ref[pl.ds(k * n, n)] = unit_of(users_ref[...])
    eye = iota((n, n), 0) == iota((n, n), 1)
    column_ref[...] = jnp.sum(jnp.where(eye, place_ref[...], 0), axis=1, keepdims=True)
    line_ref[...] = asked_line(asked_ref[...]).astype(i32)


def main_kernel(fetched_ref, weight_ref, unit_ref, place_ref, column_ref, outgoing_ref, embed_ref, dhidden_ref):
    n = place_ref.shape[1]
    total, width = fetched_ref.shape
    root = 1.0 / width**0.5
    embed = dot(hot(column_ref[...] == iota((n, total), 1)), fetched_ref[...]).astype(bf16)
    hidden = dot(embed, weight_ref[...])
    rscale = lax.rsqrt(jnp.mean(hidden * hidden, axis=1, keepdims=True) + epsilon)
    item_vec = (hidden * (rscale * root)).astype(bf16)
    unit = unit_ref[...]
    expo = jnp.exp(dot(item_vec, unit, 1, 1) * score_scale)
    sums = jnp.sum(expo, axis=1, keepdims=True)
    mixed = dot(expo.astype(bf16), unit)
    own = unit_ref[pl.ds(0, n)].astype(f32)
    positive = jnp.sum(item_vec.astype(f32) * own, axis=1, keepdims=True) * score_scale
    xent = jnp.log(sums) - positive
    cweight = 1.0 / (1.0 + xent * (1.0 / cauchy_scale))
    dvec = (cweight * score_scale) * (mixed * (1.0 / sums) - own)
    inner = jnp.sum(hidden * dvec, axis=1, keepdims=True)
    dhidden = (rscale * root * (dvec - hidden * (rscale * rscale * inner * (1.0 / width)))).astype(bf16)
    outgoing_ref[...] = dot(hot(place_ref[...] == iota((total, n), 0)), dhidden).astype(bf16)
    embed_ref[...] = embed
    dhidden_ref[...] = dhidden


def share_kernel(embed_ref, dhidden_ref, keep_ref, *refs):
    *sends, share = refs
    share[...] = dot(embed_ref[...], dhidden_ref[...], 0, 0)
    count, size = len(sends) + 1, keep_ref.shape[0]
    me = lax.axis_index("batch")
    for step, ref in enumerate([keep_ref, *sends]):
        start = pl.multiple_of(lax.rem(me + step, count) * size, size)
        ref[...] = share[pl.ds(start, size)].astype(ref.dtype)


def combine_kernel(count, *refs):
    (kept, *came), (keep_ref, *sends), total = refs[:count], refs[count:-1], refs[-1]
    total[...] = kept[...] + sum(ref[...].astype(f32) for ref in came)
    me = lax.axis_index("item")
    for step, ref in enumerate([keep_ref, *sends]):
        ref[...] = total[lax.rem(me + step, total.shape[0])]


def table_kernel(line_ref, incoming_ref, weight_ref, table_grad_ref, drow, low_hot, block, pick):
    step = pl.program_id(0)
    chunk, total = pick.shape

    @pl.when(step == 0)
    def _():
        drow[...] = dot(incoming_ref[...], weight_ref[...], 1, 1).astype(bf16)
        high, low = parts_of(line_ref[...])
        low_hot[...] = hot(low == iota((BLOCK, total), 0))
        block[...] = jnp.broadcast_to(high.astype(f32), (BLOCK, total)).astype(bf16)

    for k in range(chunk // BLOCK):
        mine = (step * (chunk // BLOCK) + k).astype(f32).astype(bf16)
        pick[pl.ds(k * BLOCK, BLOCK)] = jnp.where(block[...] == mine, low_hot[...], jnp.bfloat16(0))
    table_grad_ref[...] = dot(pick[...], drow[...]).astype(bf16)


def params(mib=16):
    return pltpu.CompilerParams(vmem_limit_bytes=mib * 1024 * 1024)


def cost(flops, bytes_accessed=1 << 20):
    return pl.CostEstimate(flops=flops, bytes_accessed=bytes_accessed, transcendentals=0)


def call(kernel, outs, *args, flops=0, scratch=()):
    return pl.pallas_call(
        kernel,
        out_shape=[jax.ShapeDtypeStruct(shape, dtype) for shape, dtype in outs],
        scratch_shapes=scratch,
        compiler_params=params(),
        cost_estimate=cost(flops),
    )(*args)


def shift(value, axis, step):
    size = lax.axis_size(axis)
    return lax.ppermute(value, axis, [(k, (k + step) % size) for k in range(size)])


def local(user_vectors, item_table, tower_weight, item_owner, item_row):
    n, width = user_vectors.shape
    rows = item_table.shape[0]
    axes = ("batch", "item")
    n_batch, n_item = lax.axis_size("batch"), lax.axis_size("item")
    devices = n_batch * n_item
    slots = 2 * n // devices
    total = devices * slots
    chunk = min(1024, rows)
    groups = rows // chunk

    exchange = functools.partial(lax.all_to_all, axis_name=axes, split_axis=0, concat_axis=0, tiled=True)

    users = [user_vectors] + [shift(user_vectors, "batch", step) for step in range(1, n_batch)]
    request, place = call(
        request_kernel,
        [((devices, slots), i32), ((1, n), i32)],
        item_owner.reshape(1, n),
        item_row.reshape(1, n),
    )
    asked = exchange(request)
    found = pl.pallas_call(
        fetch_kernel,
        in_specs=[pl.BlockSpec(memory_space=pltpu.VMEM), pl.BlockSpec(memory_space=pltpu.HBM)],
        out_shape=jax.ShapeDtypeStruct((total, width), bf16),
        scratch_shapes=[pltpu.VMEM((rows, width), bf16), pltpu.SemaphoreType.DMA((groups,))],
        compiler_params=params(32),
        cost_estimate=cost(2 * total * rows * width, 2 * rows * width),
    )(asked, item_table)
    fetched = exchange(found.reshape(devices, slots, width)).reshape(total, width)
    unit, column, line = call(
        prepare_kernel,
        [((n_batch * n, width), bf16), ((n, 1), i32), ((1, total), i32)],
        place,
        asked,
        *users,
        flops=1 << 28,
    )
    outgoing, embed, dhidden = call(
        main_kernel,
        [((total, width), bf16), ((n, width), bf16), ((n, width), bf16)],
        fetched,
        tower_weight,
        unit,
        place,
        column,
        flops=1 << 30,
    )
    incoming = exchange(outgoing.reshape(devices, slots, width)).reshape(total, width)

    half = width // n_batch
    kept, *sends = call(
        share_kernel,
        [((half, width), f32)] + [((half, width), bf16)] * (n_batch - 1),
        embed,
        dhidden,
        flops=1 << 27,
        scratch=[pltpu.VMEM((width, width), f32)],
    )
    came = [shift(value, "batch", step + 1) for step, value in enumerate(sends)]
    part = half // n_item
    kept, *sends = call(
        functools.partial(combine_kernel, n_batch),
        [((part, width), f32)] * n_item,
        *[value.reshape(n_item, part, width) for value in [kept, *came]],
        flops=1 << 20,
        scratch=[pltpu.VMEM((n_item, part, width), f32)],
    )
    weight_grad = kept
    for step, value in enumerate(sends):
        weight_grad += shift(value, "item", step + 1)

    table_grad = pl.pallas_call(
        table_kernel,
        grid=(groups,),
        in_specs=[
            pl.BlockSpec((1, total), lambda k: (0, 0)),
            pl.BlockSpec((total, width), lambda k: (0, 0)),
            pl.BlockSpec((width, width), lambda k: (0, 0)),
        ],
        out_specs=pl.BlockSpec((chunk, width), lambda k: (k, 0)),
        out_shape=jax.ShapeDtypeStruct((rows, width), bf16),
        scratch_shapes=[
            pltpu.VMEM((total, width), bf16),
            pltpu.VMEM((BLOCK, total), bf16),
            pltpu.VMEM((BLOCK, total), bf16),
            pltpu.VMEM((chunk, total), bf16),
        ],
        compiler_params=params(32),
        cost_estimate=cost(2 * total * rows * width, 2 * rows * width),
    )(line, incoming, tower_weight)
    return (table_grad, weight_grad)


def solution(mesh):
    return jax.shard_map(
        local,
        mesh=mesh,
        in_specs=(
            P(("batch", "item"), None),
            P(("batch", "item"), None),
            P(),
            P(("batch", "item"), None),
            P(("batch", "item")),
        ),
        out_specs=(P(("batch", "item"), None), P(("batch", "item"), None)),
        check_vma=False,
    )
```

```python
import functools

import jax
import jax.numpy as jnp
from jax import lax
from jax.experimental import pallas as pl
from jax.experimental.pallas import tpu as pltpu
from jax.sharding import PartitionSpec as P

epsilon = 1e-06
score_scale = 60.0
cauchy_scale = 4.0
f32 = jnp.float32
bf16 = jnp.bfloat16
i32 = jnp.int32
BLOCK = 256


def iota(shape, dim):
    return lax.broadcasted_iota(i32, shape, dim)


def hot(mask):
    return jnp.where(mask, 1.0, 0.0).astype(bf16)


def dot(a, b, a_dim=1, b_dim=0):
    return lax.dot_general(a, b, (((a_dim,), (b_dim,)), ((), ())), preferred_element_type=f32)


def halves(value):
    return (value >> 8).astype(f32), (value & 255).astype(f32)


def request_kernel(named_ref, request_ref, place_ref):
    devices, slots = request_ref.shape
    n = named_ref.shape[1]
    owner, row = named_ref[0:1], named_ref[1:2]
    named = owner == iota((devices, n), 0)
    count = dot(hot(named), hot(iota((n, n), 0) <= iota((n, n), 1)))
    rank = jnp.sum(jnp.where(named, count, 0.0), axis=0, keepdims=True).astype(i32) - 1
    in_slot = hot(rank == iota((slots, n), 0))
    high, low = halves(row + 1)
    high = dot(jnp.where(named, high, 0.0).astype(bf16), in_slot, 1, 1)
    low = dot(jnp.where(named, low, 0.0).astype(bf16), in_slot, 1, 1)
    request_ref[...] = (high * 256.0 + low).astype(i32) - 1
    place_ref[...] = owner * slots + rank


def asked_column(asked):
    devices, slots = asked.shape
    total = devices * slots
    first = iota((total, devices), 1) * slots
    spot = iota((total, devices), 0)
    pick = hot((spot >= first) & (spot < first + slots))
    high, low = halves(asked)
    value = dot(pick, high.astype(bf16)) * 256.0 + dot(pick, low.astype(bf16))
    mine = lax.rem(iota((total, slots), 0), slots) == iota((total, slots), 1)
    return jnp.sum(jnp.where(mine, value, 0.0), axis=1, keepdims=True)


def asked_line(asked):
    devices, slots = asked.shape
    total = devices * slots
    pick = hot(lax.rem(iota((slots, total), 1), slots) == iota((slots, total), 0))
    high, low = halves(asked)
    value = dot(high.astype(bf16), pick) * 256.0 + dot(low.astype(bf16), pick)
    first = iota((devices, total), 0) * slots
    spot = iota((devices, total), 1)
    mine = (spot >= first) & (spot < first + slots)
    return jnp.sum(jnp.where(mine, value, 0.0), axis=0, keepdims=True)


def parts_of(value):
    return value >> 8, value & 255


def fetch_kernel(asked_ref, table_hbm, found_ref, table, sems):
    groups = sems.shape[0]
    size = table.shape[0] // groups
    copies = [
        pltpu.make_async_copy(table_hbm.at[pl.ds(g * size, size)], table.at[pl.ds(g * size, size)], sems.at[g])
        for g in range(groups)
    ]
    for copy in copies:
        copy.start()
    block, low = parts_of(asked_column(asked_ref[...]).astype(i32))
    total = block.shape[0]
    low_hot = hot(low == iota((total, BLOCK), 1))
    block = jnp.broadcast_to(block.astype(f32), (total, BLOCK)).astype(bf16)
    found = None
    for g, copy in enumerate(copies):
        picks = [
            jnp.where(block == jnp.bfloat16(k), low_hot, jnp.bfloat16(0))
            for k in range(g * size // BLOCK, (g + 1) * size // BLOCK)
        ]
        copy.wait()
        part = dot(jnp.concatenate(picks, axis=1), table[pl.ds(g * size, size)])
        found = part if found is None else found + part
    found_ref[...] = found.astype(bf16)


def unit_of(users):
    width = users.shape[1]
    users = users.astype(f32)
    mean = jnp.mean(users * users, axis=1, keepdims=True)
    return (users * lax.rsqrt(mean + epsilon) * (1.0 / width**0.5)).astype(bf16)


def prepare_kernel(place_ref, asked_ref, *refs):
    *users, unit_ref, column_ref, line_ref = refs
    n = place_ref.shape[1]
    for k, users_ref in enumerate(users):
        unit_ref[pl.ds(k * n, n)] = unit_of(users_ref[...])
    eye = iota((n, n), 0) == iota((n, n), 1)
    column_ref[...] = jnp.sum(jnp.where(eye, place_ref[...], 0), axis=1, keepdims=True)
    line_ref[...] = asked_line(asked_ref[...]).astype(i32)


def main_kernel(fetched_ref, weight_ref, unit_ref, place_ref, column_ref, outgoing_ref, embed_ref, dhidden_ref):
    n = place_ref.shape[1]
    total, width = fetched_ref.shape
    root = 1.0 / width**0.5
    embed = dot(hot(column_ref[...] == iota((n, total), 1)), fetched_ref[...]).astype(bf16)
    hidden = dot(embed, weight_ref[...])
    rscale = lax.rsqrt(jnp.mean(hidden * hidden, axis=1, keepdims=True) + epsilon)
    item_vec = (hidden * (rscale * root)).astype(bf16)
    unit = unit_ref[...]
    expo = jnp.exp(dot(item_vec, unit, 1, 1) * score_scale)
    sums = jnp.sum(expo, axis=1, keepdims=True)
    mixed = dot(expo.astype(bf16), unit)
    own = unit_ref[pl.ds(0, n)].astype(f32)
    positive = jnp.sum(item_vec.astype(f32) * own, axis=1, keepdims=True) * score_scale
    xent = jnp.log(sums) - positive
    cweight = 1.0 / (1.0 + xent * (1.0 / cauchy_scale))
    dvec = (cweight * score_scale) * (mixed * (1.0 / sums) - own)
    inner = jnp.sum(hidden * dvec, axis=1, keepdims=True)
    dhidden = (rscale * root * (dvec - hidden * (rscale * rscale * inner * (1.0 / width)))).astype(bf16)
    outgoing_ref[...] = dot(hot(place_ref[...] == iota((total, n), 0)), dhidden).astype(bf16)
    embed_ref[...] = embed
    dhidden_ref[...] = dhidden


def halve(blocks, bit, keep_ref, send_ref):
    half = keep_ref.shape[0]
    axis, level = bit
    mine = (lax.axis_index(axis) >> level) & 1
    keep_ref[...] = blocks[pl.ds(mine * half, half)]
    send_ref[...] = blocks[pl.ds((1 - mine) * half, half)].astype(send_ref.dtype)


def share_kernel(order, bit, embed_ref, dhidden_ref, keep_ref, send_ref, blocks):
    share = dot(embed_ref[...], dhidden_ref[...], 0, 0)
    size = blocks.shape[1]
    for spot, block in enumerate(order):
        blocks[spot] = share[block * size : (block + 1) * size]
    halve(blocks, bit, keep_ref, send_ref)


def halve_kernel(bit, kept_ref, came_ref, keep_ref, send_ref, blocks):
    blocks[...] = kept_ref[...] + came_ref[...].astype(f32)
    halve(blocks, bit, keep_ref, send_ref)


def table_kernel(line_ref, incoming_ref, weight_ref, table_grad_ref, drow, low_hot, block, pick):
    step = pl.program_id(0)
    chunk, total = pick.shape

    @pl.when(step == 0)
    def _():
        drow[...] = dot(incoming_ref[...], weight_ref[...], 1, 1).astype(bf16)
        high, low = parts_of(line_ref[...])
        low_hot[...] = hot(low == iota((BLOCK, total), 0))
        block[...] = jnp.broadcast_to(high.astype(f32), (BLOCK, total)).astype(bf16)

    for k in range(chunk // BLOCK):
        mine = (step * (chunk // BLOCK) + k).astype(f32).astype(bf16)
        pick[pl.ds(k * BLOCK, BLOCK)] = jnp.where(block[...] == mine, low_hot[...], jnp.bfloat16(0))
    table_grad_ref[...] = dot(pick[...], drow[...]).astype(bf16)


def params(mib=16):
    return pltpu.CompilerParams(vmem_limit_bytes=mib * 1024 * 1024)


def cost(flops, bytes_accessed=1 << 20):
    return pl.CostEstimate(flops=flops, bytes_accessed=bytes_accessed, transcendentals=0)


def call(kernel, outs, *args, flops=0, scratch=()):
    return pl.pallas_call(
        kernel,
        out_shape=[jax.ShapeDtypeStruct(shape, dtype) for shape, dtype in outs],
        scratch_shapes=scratch,
        compiler_params=params(),
        cost_estimate=cost(flops),
    )(*args)


def swap(value, bit):
    axis, level = bit
    return lax.ppermute(value, axis, [(k, k ^ (1 << level)) for k in range(lax.axis_size(axis))])


def bits_of(axis):
    return [(axis, level) for level in range(lax.axis_size(axis).bit_length() - 1)]


def local(user_vectors, item_table, tower_weight, item_owner, item_row):
    n, width = user_vectors.shape
    rows = item_table.shape[0]
    axes = ("batch", "item")
    n_batch, n_item = lax.axis_size("batch"), lax.axis_size("item")
    devices = n_batch * n_item
    slots = 2 * n // devices
    total = devices * slots
    chunk = min(1024, rows)
    groups = rows // chunk

    exchange = functools.partial(lax.all_to_all, axis_name=axes, split_axis=0, concat_axis=0, tiled=True)

    users = [user_vectors]
    for bit in reversed(bits_of("batch")):
        users += [swap(value, bit) for value in users]
    request, place = call(
        request_kernel,
        [((devices, slots), i32), ((1, n), i32)],
        jnp.stack([item_owner.reshape(n), item_row]),
    )
    early = n_batch // 2 + 1
    asked, *users[1:early] = lax.optimization_barrier((exchange(request), *users[1:early]))
    found = pl.pallas_call(
        fetch_kernel,
        in_specs=[pl.BlockSpec(memory_space=pltpu.VMEM), pl.BlockSpec(memory_space=pltpu.HBM)],
        out_shape=jax.ShapeDtypeStruct((total, width), bf16),
        scratch_shapes=[pltpu.VMEM((rows, width), bf16), pltpu.SemaphoreType.DMA((groups,))],
        compiler_params=params(61),
        cost_estimate=cost(2 * total * rows * width, 2 * rows * width),
    )(asked, item_table)
    fetched = exchange(found.reshape(devices, slots, width)).reshape(total, width)
    unit, column, line = call(
        prepare_kernel,
        [((n_batch * n, width), bf16), ((n, 1), i32), ((1, total), i32)],
        place,
        asked,
        *users,
        flops=1 << 28,
    )
    outgoing, embed, dhidden = call(
        main_kernel,
        [((total, width), bf16), ((n, width), bf16), ((n, width), bf16)],
        fetched,
        tower_weight,
        unit,
        place,
        column,
        flops=1 << 30,
    )
    incoming = exchange(outgoing.reshape(devices, slots, width)).reshape(total, width)

    part = width // devices
    bits = bits_of("batch") + bits_of("item")
    order = []
    for spot in range(devices):
        at = {"batch": 0, "item": 0}
        for k, (axis, level) in enumerate(bits):
            at[axis] |= (spot >> (len(bits) - 1 - k) & 1) << level
        order.append(at["batch"] * n_item + at["item"])
    kept, came = None, None
    for k, bit in enumerate(bits):
        half = devices >> (k + 1)
        outs = [((half, part, width), f32), ((half, part, width), bf16 if half >= 4 else f32)]
        scratch = [pltpu.VMEM((2 * half, part, width), f32)]
        if k == 0:
            kernel = functools.partial(share_kernel, order, bit)
            kept, sent = call(kernel, outs, embed, dhidden, flops=1 << 27, scratch=scratch)
        else:
            kept, sent = call(functools.partial(halve_kernel, bit), outs, kept, came, scratch=scratch)
        came = swap(sent, bit)
    weight_grad = (kept + came.astype(f32)).reshape(part, width)

    table_grad = pl.pallas_call(
        table_kernel,
        grid=(groups,),
        in_specs=[
            pl.BlockSpec((1, total), lambda k: (0, 0)),
            pl.BlockSpec((total, width), lambda k: (0, 0)),
            pl.BlockSpec((width, width), lambda k: (0, 0)),
        ],
        out_specs=pl.BlockSpec((chunk, width), lambda k: (k, 0)),
        out_shape=jax.ShapeDtypeStruct((rows, width), bf16),
        scratch_shapes=[
            pltpu.VMEM((total, width), bf16),
            pltpu.VMEM((BLOCK, total), bf16),
            pltpu.VMEM((BLOCK, total), bf16),
            pltpu.VMEM((chunk, total), bf16),
        ],
        compiler_params=params(32),
        cost_estimate=cost(2 * total * rows * width, 2 * rows * width),
    )(line, incoming, tower_weight)
    return (table_grad, weight_grad)


def solution(mesh):
    return jax.shard_map(
        local,
        mesh=mesh,
        in_specs=(
            P(("batch", "item"), None),
            P(("batch", "item"), None),
            P(),
            P(("batch", "item"), None),
            P(("batch", "item")),
        ),
        out_specs=(P(("batch", "item"), None), P(("batch", "item"), None)),
        check_vma=False,
    )
```

```python
import functools

import jax
import jax.numpy as jnp
from jax import lax
from jax.experimental import pallas as pl
from jax.experimental.pallas import tpu as pltpu
from jax.sharding import PartitionSpec as P

epsilon = 1e-06
score_scale = 60.0
cauchy_scale = 4.0
f32 = jnp.float32
bf16 = jnp.bfloat16
i32 = jnp.int32
BLOCK = 256


def iota(shape, dim):
    return lax.broadcasted_iota(i32, shape, dim)


def hot(mask):
    return jnp.where(mask, 1.0, 0.0).astype(bf16)


def dot(a, b, a_dim=1, b_dim=0):
    return lax.dot_general(a, b, (((a_dim,), (b_dim,)), ((), ())), preferred_element_type=f32)


def halves(value):
    return (value >> 8).astype(f32), (value & 255).astype(f32)


def request_kernel(named_ref, request_ref, place_ref):
    devices, slots = request_ref.shape
    n = named_ref.shape[1]
    owner, row = named_ref[0:1], named_ref[1:2]
    named = owner == iota((devices, n), 0)
    count = dot(hot(named), hot(iota((n, n), 0) <= iota((n, n), 1)))
    rank = jnp.sum(jnp.where(named, count, 0.0), axis=0, keepdims=True).astype(i32) - 1
    in_slot = hot(rank == iota((slots, n), 0))
    high, low = halves(row + 1)
    high = dot(jnp.where(named, high, 0.0).astype(bf16), in_slot, 1, 1)
    low = dot(jnp.where(named, low, 0.0).astype(bf16), in_slot, 1, 1)
    request_ref[...] = (high * 256.0 + low).astype(i32) - 1
    place_ref[...] = owner * slots + rank


def asked_column(asked):
    devices, slots = asked.shape
    total = devices * slots
    first = iota((total, devices), 1) * slots
    spot = iota((total, devices), 0)
    pick = hot((spot >= first) & (spot < first + slots))
    high, low = halves(asked)
    value = dot(pick, high.astype(bf16)) * 256.0 + dot(pick, low.astype(bf16))
    mine = lax.rem(iota((total, slots), 0), slots) == iota((total, slots), 1)
    return jnp.sum(jnp.where(mine, value, 0.0), axis=1, keepdims=True)


def asked_line(asked):
    devices, slots = asked.shape
    total = devices * slots
    pick = hot(lax.rem(iota((slots, total), 1), slots) == iota((slots, total), 0))
    high, low = halves(asked)
    value = dot(high.astype(bf16), pick) * 256.0 + dot(low.astype(bf16), pick)
    first = iota((devices, total), 0) * slots
    spot = iota((devices, total), 1)
    mine = (spot >= first) & (spot < first + slots)
    return jnp.sum(jnp.where(mine, value, 0.0), axis=0, keepdims=True)


def parts_of(value):
    return value >> 8, value & 255


def fetch_kernel(asked_ref, table_ref, found_ref):
    block, low = parts_of(asked_column(asked_ref[...]).astype(i32))
    total = block.shape[0]
    low_hot = hot(low == iota((total, BLOCK), 1))
    block = jnp.broadcast_to(block.astype(f32), (total, BLOCK)).astype(bf16)
    picks = [
        jnp.where(block == jnp.bfloat16(k), low_hot, jnp.bfloat16(0)) for k in range(table_ref.shape[0] // BLOCK)
    ]
    found_ref[...] = dot(jnp.concatenate(picks, axis=1), table_ref[...]).astype(bf16)


def unit_of(users):
    width = users.shape[1]
    users = users.astype(f32)
    mean = jnp.mean(users * users, axis=1, keepdims=True)
    return (users * lax.rsqrt(mean + epsilon) * (1.0 / width**0.5)).astype(bf16)


def prepare_kernel(place_ref, asked_ref, *refs):
    *users, unit_ref, column_ref, pick_ref = refs
    n = place_ref.shape[1]
    for k, users_ref in enumerate(users):
        unit_ref[pl.ds(k * n, n)] = unit_of(users_ref[...])
    eye = iota((n, n), 0) == iota((n, n), 1)
    column_ref[...] = jnp.sum(jnp.where(eye, place_ref[...], 0), axis=1, keepdims=True)
    block, low = parts_of(asked_line(asked_ref[...]).astype(i32))
    total = block.shape[1]
    low_hot = hot(low == iota((BLOCK, total), 0))
    block = jnp.broadcast_to(block.astype(f32), (BLOCK, total)).astype(bf16)
    for k in range(pick_ref.shape[0] // BLOCK):
        pick_ref[pl.ds(k * BLOCK, BLOCK)] = jnp.where(block == jnp.bfloat16(k), low_hot, jnp.bfloat16(0))


def main_kernel(fetched_ref, weight_ref, unit_ref, place_ref, column_ref, outgoing_ref, embed_ref, dhidden_ref):
    n = place_ref.shape[1]
    total, width = fetched_ref.shape
    root = 1.0 / width**0.5
    embed = dot(hot(column_ref[...] == iota((n, total), 1)), fetched_ref[...]).astype(bf16)
    hidden = dot(embed, weight_ref[...])
    rscale = lax.rsqrt(jnp.mean(hidden * hidden, axis=1, keepdims=True) + epsilon)
    item_vec = (hidden * (rscale * root)).astype(bf16)
    unit = unit_ref[...]
    expo = jnp.exp(dot(item_vec, unit, 1, 1) * score_scale)
    sums = jnp.sum(expo, axis=1, keepdims=True)
    mixed = dot(expo.astype(bf16), unit)
    own = unit_ref[pl.ds(0, n)].astype(f32)
    positive = jnp.sum(item_vec.astype(f32) * own, axis=1, keepdims=True) * score_scale
    xent = jnp.log(sums) - positive
    cweight = 1.0 / (1.0 + xent * (1.0 / cauchy_scale))
    dvec = (cweight * score_scale) * (mixed * (1.0 / sums) - own)
    inner = jnp.sum(hidden * dvec, axis=1, keepdims=True)
    dhidden = (rscale * root * (dvec - hidden * (rscale * rscale * inner * (1.0 / width)))).astype(bf16)
    outgoing_ref[...] = dot(hot(place_ref[...] == iota((total, n), 0)), dhidden).astype(bf16)
    embed_ref[...] = embed
    dhidden_ref[...] = dhidden


def halve(blocks, bit, keep_ref, send_ref):
    half = keep_ref.shape[0]
    axis, level = bit
    mine = (lax.axis_index(axis) >> level) & 1
    keep_ref[...] = blocks[pl.ds(mine * half, half)]
    send_ref[...] = blocks[pl.ds((1 - mine) * half, half)].astype(send_ref.dtype)


def share_kernel(order, bit, embed_ref, dhidden_ref, keep_ref, send_ref, blocks):
    share = dot(embed_ref[...], dhidden_ref[...], 0, 0)
    size = blocks.shape[1]
    for spot, block in enumerate(order):
        blocks[spot] = share[block * size : (block + 1) * size]
    halve(blocks, bit, keep_ref, send_ref)


def halve_kernel(bit, kept_ref, came_ref, keep_ref, send_ref, blocks):
    blocks[...] = kept_ref[...] + came_ref[...].astype(f32)
    halve(blocks, bit, keep_ref, send_ref)


def add_kernel(kept_ref, came_ref, total_ref):
    total_ref[...] = kept_ref[...] + came_ref[...].astype(f32)


def table_kernel(pick_ref, incoming_ref, weight_ref, table_grad_hbm, ready, sems):
    drow = dot(incoming_ref[...], weight_ref[...], 1, 1).astype(bf16)
    groups = sems.shape[0]
    size = ready.shape[0] // groups
    copies = []
    for g in range(groups):
        here = pl.ds(g * size, size)
        ready[here] = dot(pick_ref[here], drow).astype(bf16)
        copy = pltpu.make_async_copy(ready.at[here], table_grad_hbm.at[here], sems.at[g])
        copy.start()
        copies.append(copy)
    for copy in copies:
        copy.wait()


def params(mib=16):
    return pltpu.CompilerParams(vmem_limit_bytes=mib * 1024 * 1024)


def cost(flops, bytes_accessed=1 << 20):
    return pl.CostEstimate(flops=flops, bytes_accessed=bytes_accessed, transcendentals=0)


def call(kernel, outs, *args, flops=0, scratch=()):
    return pl.pallas_call(
        kernel,
        out_shape=[jax.ShapeDtypeStruct(shape, dtype) for shape, dtype in outs],
        scratch_shapes=scratch,
        compiler_params=params(),
        cost_estimate=cost(flops),
    )(*args)


def swap(value, bit):
    axis, level = bit
    return lax.ppermute(value, axis, [(k, k ^ (1 << level)) for k in range(lax.axis_size(axis))])


def bits_of(axis):
    return [(axis, level) for level in range(lax.axis_size(axis).bit_length() - 1)]


def local(user_vectors, item_table, tower_weight, item_owner, item_row):
    n, width = user_vectors.shape
    rows = item_table.shape[0]
    axes = ("batch", "item")
    n_batch, n_item = lax.axis_size("batch"), lax.axis_size("item")
    devices = n_batch * n_item
    slots = 2 * n // devices
    total = devices * slots
    groups = rows // min(512, rows)

    exchange = functools.partial(lax.all_to_all, axis_name=axes, split_axis=0, concat_axis=0, tiled=True)

    far, *near = reversed(bits_of("batch"))
    users = [user_vectors, swap(user_vectors, far)]
    request, place = call(
        request_kernel,
        [((devices, slots), i32), ((1, n), i32)],
        jnp.stack([item_owner.reshape(n), item_row]),
        flops=1 << 34,
    )
    asked, *users = lax.optimization_barrier((exchange(request), *users))
    (found,) = call(fetch_kernel, [((total, width), bf16)], asked, item_table, flops=2 * total * rows * width)
    fetched = exchange(found.reshape(devices, slots, width)).reshape(total, width)
    for bit in near:
        users += [swap(value, bit) for value in users]
    unit, column, pick = call(
        prepare_kernel,
        [((n_batch * n, width), bf16), ((n, 1), i32), ((rows, total), bf16)],
        place,
        asked,
        *users,
        flops=1 << 28,
    )
    outgoing, embed, dhidden = call(
        main_kernel,
        [((total, width), bf16), ((n, width), bf16), ((n, width), bf16)],
        fetched,
        tower_weight,
        unit,
        place,
        column,
        flops=1 << 30,
    )
    incoming = exchange(outgoing.reshape(devices, slots, width)).reshape(total, width)

    part = width // devices
    bits = bits_of("batch")
    order = []
    for spot in range(n_batch):
        at = sum((spot >> (len(bits) - 1 - k) & 1) << level for k, (_, level) in enumerate(bits))
        order += [at * n_item + item for item in range(n_item)]
    kept, came = None, None
    for k, bit in enumerate(bits):
        half = devices >> (k + 1)
        outs = [((half, part, width), f32), ((half, part, width), bf16)]
        scratch = [pltpu.VMEM((2 * half, part, width), f32)]
        if k == 0:
            kernel = functools.partial(share_kernel, order, bit)
            kept, sent = call(kernel, outs, embed, dhidden, flops=1 << 27, scratch=scratch)
        else:
            kept, sent = call(functools.partial(halve_kernel, bit), outs, kept, came, scratch=scratch)
        came = swap(sent, bit)
    (share,) = call(add_kernel, [((n_item, part, width), f32)], kept, came)
    shares = lax.all_to_all(share, "item", split_axis=0, concat_axis=0, tiled=True)
    weight_grad = jnp.sum(shares, axis=0)

    table_grad = pl.pallas_call(
        table_kernel,
        out_specs=pl.BlockSpec(memory_space=pl.ANY),
        out_shape=jax.ShapeDtypeStruct((rows, width), bf16),
        scratch_shapes=[pltpu.VMEM((rows, width), bf16), pltpu.SemaphoreType.DMA((groups,))],
        compiler_params=params(),
        cost_estimate=cost(2 * total * rows * width, 2 * rows * width),
    )(pick, incoming, tower_weight)
    return (table_grad, weight_grad)


def solution(mesh):
    return jax.shard_map(
        local,
        mesh=mesh,
        in_specs=(
            P(("batch", "item"), None),
            P(("batch", "item"), None),
            P(),
            P(("batch", "item"), None),
            P(("batch", "item")),
        ),
        out_specs=(P(("batch", "item"), None), P(("batch", "item"), None)),
        check_vma=False,
    )
```

```python
import functools

import jax
import jax.numpy as jnp
from jax import lax
from jax.experimental import pallas as pl
from jax.experimental.pallas import tpu as pltpu
from jax.sharding import PartitionSpec as P

epsilon = 1e-06
score_scale = 60.0
cauchy_scale = 4.0
f32 = jnp.float32
bf16 = jnp.bfloat16
i32 = jnp.int32
BLOCK = 256


def iota(shape, dim):
    return lax.broadcasted_iota(i32, shape, dim)


def hot(mask):
    return jnp.where(mask, 1.0, 0.0).astype(bf16)


def dot(a, b, a_dim=1, b_dim=0):
    return lax.dot_general(a, b, (((a_dim,), (b_dim,)), ((), ())), preferred_element_type=f32)


def halves(value):
    return (value >> 8).astype(f32), (value & 255).astype(f32)


def request_kernel(named_ref, request_ref, place_ref):
    devices, slots = request_ref.shape
    n = named_ref.shape[1]
    owner, row = named_ref[0:1], named_ref[1:2]
    named = owner == iota((devices, n), 0)
    count = dot(hot(named), hot(iota((n, n), 0) <= iota((n, n), 1)))
    rank = jnp.sum(jnp.where(named, count, 0.0), axis=0, keepdims=True).astype(i32) - 1
    in_slot = hot(rank == iota((slots, n), 0))
    high, low = halves(row + 1)
    high = dot(jnp.where(named, high, 0.0).astype(bf16), in_slot, 1, 1)
    low = dot(jnp.where(named, low, 0.0).astype(bf16), in_slot, 1, 1)
    request_ref[...] = (high * 256.0 + low).astype(i32) - 1
    place_ref[...] = owner * slots + rank


def asked_column(asked):
    devices, slots = asked.shape
    total = devices * slots
    first = iota((total, devices), 1) * slots
    spot = iota((total, devices), 0)
    pick = hot((spot >= first) & (spot < first + slots))
    high, low = halves(asked)
    value = dot(pick, high.astype(bf16)) * 256.0 + dot(pick, low.astype(bf16))
    mine = lax.rem(iota((total, slots), 0), slots) == iota((total, slots), 1)
    return jnp.sum(jnp.where(mine, value, 0.0), axis=1, keepdims=True)


def asked_line(asked):
    devices, slots = asked.shape
    total = devices * slots
    pick = hot(lax.rem(iota((slots, total), 1), slots) == iota((slots, total), 0))
    high, low = halves(asked)
    value = dot(high.astype(bf16), pick) * 256.0 + dot(low.astype(bf16), pick)
    first = iota((devices, total), 0) * slots
    spot = iota((devices, total), 1)
    mine = (spot >= first) & (spot < first + slots)
    return jnp.sum(jnp.where(mine, value, 0.0), axis=0, keepdims=True)


def parts_of(value):
    return value >> 8, value & 255


def fetch_kernel(asked_ref, table_ref, found_ref):
    block, low = parts_of(asked_column(asked_ref[...]).astype(i32))
    total = block.shape[0]
    low_hot = hot(low == iota((total, BLOCK), 1))
    block = jnp.broadcast_to(block.astype(f32), (total, BLOCK)).astype(bf16)
    picks = [
        jnp.where(block == jnp.bfloat16(k), low_hot, jnp.bfloat16(0)) for k in range(table_ref.shape[0] // BLOCK)
    ]
    found_ref[...] = dot(jnp.concatenate(picks, axis=1), table_ref[...]).astype(bf16)


def unit_of(users):
    width = users.shape[1]
    users = users.astype(f32)
    mean = jnp.mean(users * users, axis=1, keepdims=True)
    return (users * lax.rsqrt(mean + epsilon) * (1.0 / width**0.5)).astype(bf16)


def prepare_kernel(place_ref, asked_ref, *refs):
    *users, unit_ref, column_ref, low_hot_ref, block_ref = refs
    n = place_ref.shape[1]
    for k, users_ref in enumerate(users):
        unit_ref[pl.ds(k * n, n)] = unit_of(users_ref[...])
    eye = iota((n, n), 0) == iota((n, n), 1)
    column_ref[...] = jnp.sum(jnp.where(eye, place_ref[...], 0), axis=1, keepdims=True)
    block, low = parts_of(asked_line(asked_ref[...]).astype(i32))
    low_hot_ref[...] = hot(low == iota(low_hot_ref.shape, 0))
    block_ref[...] = jnp.broadcast_to(block.astype(f32), block_ref.shape).astype(bf16)


def main_kernel(fetched_ref, weight_ref, unit_ref, place_ref, column_ref, outgoing_ref, embed_ref, dhidden_ref):
    n = place_ref.shape[1]
    total, width = fetched_ref.shape
    root = 1.0 / width**0.5
    embed = dot(hot(column_ref[...] == iota((n, total), 1)), fetched_ref[...]).astype(bf16)
    hidden = dot(embed, weight_ref[...])
    rscale = lax.rsqrt(jnp.mean(hidden * hidden, axis=1, keepdims=True) + epsilon)
    item_vec = (hidden * (rscale * root)).astype(bf16)
    unit = unit_ref[...]
    expo = jnp.exp(dot(item_vec, unit, 1, 1) * score_scale)
    sums = jnp.sum(expo, axis=1, keepdims=True)
    mixed = dot(expo.astype(bf16), unit)
    own = unit_ref[pl.ds(0, n)].astype(f32)
    positive = jnp.sum(item_vec.astype(f32) * own, axis=1, keepdims=True) * score_scale
    xent = jnp.log(sums) - positive
    cweight = 1.0 / (1.0 + xent * (1.0 / cauchy_scale))
    dvec = (cweight * score_scale) * (mixed * (1.0 / sums) - own)
    inner = jnp.sum(hidden * dvec, axis=1, keepdims=True)
    dhidden = (rscale * root * (dvec - hidden * (rscale * rscale * inner * (1.0 / width)))).astype(bf16)
    outgoing_ref[...] = dot(hot(place_ref[...] == iota((total, n), 0)), dhidden).astype(bf16)
    embed_ref[...] = embed
    dhidden_ref[...] = dhidden


def cut(blocks, bits, refs):
    size = refs[0].shape[0]
    mine = sum(((lax.axis_index(axis) >> level) & 1) << k for k, (axis, level) in enumerate(reversed(bits)))
    for step, ref in enumerate(refs):
        ref[...] = blocks[pl.ds((mine ^ step) * size, size)].astype(ref.dtype)


def share_kernel(order, bits, embed_ref, dhidden_ref, *refs):
    *refs, blocks = refs
    share = dot(embed_ref[...], dhidden_ref[...], 0, 0)
    size = blocks.shape[1]
    for spot, block in enumerate(order):
        blocks[spot] = share[block * size : (block + 1) * size]
    cut(blocks, bits, refs)


def sum_of(refs):
    return sum(ref[...].astype(f32) for ref in refs)


def stage_kernel(bits, count, *refs):
    came, (*refs, blocks) = refs[:count], refs[count:]
    blocks[...] = sum_of(came)
    cut(blocks, bits, refs)


def last_kernel(*refs):
    *came, total_ref = refs
    total_ref[...] = sum_of(came)[0]


def table_kernel(low_hot_ref, block_ref, incoming_ref, weight_ref, table_grad_hbm, ready, sems):
    drow = dot(incoming_ref[...], weight_ref[...], 1, 1).astype(bf16)
    groups = sems.shape[0]
    size = ready.shape[0] // groups
    copies = []
    for g in range(groups):
        here = pl.ds(g * size, size)
        picks = [
            jnp.where(block_ref[...] == jnp.bfloat16(k), low_hot_ref[...], jnp.bfloat16(0))
            for k in range(g * size // BLOCK, (g + 1) * size // BLOCK)
        ]
        ready[here] = dot(jnp.concatenate(picks, axis=0), drow).astype(bf16)
        copy = pltpu.make_async_copy(ready.at[here], table_grad_hbm.at[here], sems.at[g])
        copy.start()
        copies.append(copy)
    for copy in copies:
        copy.wait()


def params(mib=16):
    return pltpu.CompilerParams(vmem_limit_bytes=mib * 1024 * 1024)


def cost(flops, bytes_accessed=1 << 20):
    return pl.CostEstimate(flops=flops, bytes_accessed=bytes_accessed, transcendentals=0)


def call(kernel, outs, *args, flops=0, scratch=()):
    return pl.pallas_call(
        kernel,
        out_shape=[jax.ShapeDtypeStruct(shape, dtype) for shape, dtype in outs],
        scratch_shapes=scratch,
        compiler_params=params(),
        cost_estimate=cost(flops),
    )(*args)


def swap(value, *bits):
    n_item, devices = lax.axis_size("item"), lax.axis_size("batch") * lax.axis_size("item")
    mask = sum((n_item if axis == "batch" else 1) << level for axis, level in bits)
    return lax.ppermute(value, ("batch", "item"), [(k, k ^ mask) for k in range(devices)])


def bits_of(axis):
    return [(axis, level) for level in range(lax.axis_size(axis).bit_length() - 1)]


def reduce_scatter(embed, dhidden):
    width = embed.shape[1]
    n_item, devices = lax.axis_size("item"), lax.axis_size("batch") * lax.axis_size("item")
    part = width // devices
    bits = bits_of("batch") + bits_of("item")
    order = []
    for spot in range(devices):
        at = {"batch": 0, "item": 0}
        for k, (axis, level) in enumerate(bits):
            at[axis] |= (spot >> (len(bits) - 1 - k) & 1) << level
        order.append(at["batch"] * n_item + at["item"])
    odd = len(bits) % 2
    stages = [bits[:1]] * odd + [bits[k : k + 2] for k in range(odd, len(bits), 2)]
    left, values = devices, [embed, dhidden]
    for k, stage in enumerate(stages):
        whole, left = left, left >> len(stage)
        sent = f32 if k == len(stages) - 1 else bf16
        kernel = functools.partial(*((stage_kernel, stage, len(values)) if k else (share_kernel, order, stage)))
        kept, *sends = call(
            kernel,
            [((left, part, width), f32)] + [((left, part, width), sent)] * ((1 << len(stage)) - 1),
            *values,
            scratch=[pltpu.VMEM((whole, part, width), f32)],
        )
        values = [kept]
        for step, value in enumerate(sends, 1):
            values.append(swap(value, *[bit for j, bit in enumerate(reversed(stage)) if step >> j & 1]))
    return call(last_kernel, [((part, width), f32)], *values)[0]


def local(user_vectors, item_table, tower_weight, item_owner, item_row):
    n, width = user_vectors.shape
    rows = item_table.shape[0]
    axes = ("batch", "item")
    n_batch, n_item = lax.axis_size("batch"), lax.axis_size("item")
    devices = n_batch * n_item
    slots = 2 * n // devices
    total = devices * slots
    groups = rows // min(512, rows)

    exchange = functools.partial(lax.all_to_all, axis_name=axes, split_axis=0, concat_axis=0, tiled=True)

    far, *near = reversed(bits_of("batch"))
    users = [user_vectors, swap(user_vectors, far)]
    request, place = call(
        request_kernel,
        [((devices, slots), i32), ((1, n), i32)],
        jnp.stack([item_owner.reshape(n), item_row]),
        flops=1 << 34,
    )
    asked, *users = lax.optimization_barrier((exchange(request), *users))
    (found,) = call(fetch_kernel, [((total, width), bf16)], asked, item_table, flops=2 * total * rows * width)
    fetched = exchange(found.reshape(devices, slots, width)).reshape(total, width)
    for bit in near:
        users += [swap(value, bit) for value in users]
    unit, column, low_hot, block = call(
        prepare_kernel,
        [((n_batch * n, width), bf16), ((n, 1), i32), ((BLOCK, total), bf16), ((BLOCK, total), bf16)],
        place,
        asked,
        *users,
        flops=1 << 28,
    )
    outgoing, embed, dhidden = call(
        main_kernel,
        [((total, width), bf16), ((n, width), bf16), ((n, width), bf16)],
        fetched,
        tower_weight,
        unit,
        place,
        column,
        flops=1 << 30,
    )
    incoming = exchange(outgoing.reshape(devices, slots, width)).reshape(total, width)

    weight_grad = reduce_scatter(embed, dhidden)

    table_grad = pl.pallas_call(
        table_kernel,
        out_specs=pl.BlockSpec(memory_space=pl.ANY),
        out_shape=jax.ShapeDtypeStruct((rows, width), bf16),
        scratch_shapes=[pltpu.VMEM((rows, width), bf16), pltpu.SemaphoreType.DMA((groups,))],
        compiler_params=params(),
        cost_estimate=cost(2 * total * rows * width, 2 * rows * width),
    )(low_hot, block, incoming, tower_weight)
    return (table_grad, weight_grad)


def solution(mesh):
    return jax.shard_map(
        local,
        mesh=mesh,
        in_specs=(
            P(("batch", "item"), None),
            P(("batch", "item"), None),
            P(),
            P(("batch", "item"), None),
            P(("batch", "item")),
        ),
        out_specs=(P(("batch", "item"), None), P(("batch", "item"), None)),
        check_vma=False,
    )
```

```python
import functools

import jax
import jax.numpy as jnp
from jax import lax
from jax.experimental import pallas as pl
from jax.experimental.pallas import tpu as pltpu
from jax.sharding import PartitionSpec as P

epsilon = 1e-06
score_scale = 60.0
cauchy_scale = 4.0
f32 = jnp.float32
bf16 = jnp.bfloat16
i32 = jnp.int32
BLOCK = 256


def iota(shape, dim):
    return lax.broadcasted_iota(i32, shape, dim)


def hot(mask):
    return jnp.where(mask, 1.0, 0.0).astype(bf16)


def dot(a, b, a_dim=1, b_dim=0):
    return lax.dot_general(a, b, (((a_dim,), (b_dim,)), ((), ())), preferred_element_type=f32)


def halves(value):
    return (value >> 8).astype(f32), (value & 255).astype(f32)


def request_kernel(named_ref, request_ref, place_ref):
    devices, slots = request_ref.shape
    n = named_ref.shape[1]
    owner, row = named_ref[0:1], named_ref[1:2]
    named = owner == iota((devices, n), 0)
    count = dot(hot(named), hot(iota((n, n), 0) <= iota((n, n), 1)))
    rank = jnp.sum(jnp.where(named, count, 0.0), axis=0, keepdims=True).astype(i32) - 1
    in_slot = hot(rank == iota((slots, n), 0))
    high, low = halves(row + 1)
    high = dot(jnp.where(named, high, 0.0).astype(bf16), in_slot, 1, 1)
    low = dot(jnp.where(named, low, 0.0).astype(bf16), in_slot, 1, 1)
    request_ref[...] = (high * 256.0 + low).astype(i32) - 1
    place_ref[...] = owner * slots + rank


def asked_column(asked):
    devices, slots = asked.shape
    total = devices * slots
    first = iota((total, devices), 1) * slots
    spot = iota((total, devices), 0)
    pick = hot((spot >= first) & (spot < first + slots))
    high, low = halves(asked)
    value = dot(pick, high.astype(bf16)) * 256.0 + dot(pick, low.astype(bf16))
    mine = lax.rem(iota((total, slots), 0), slots) == iota((total, slots), 1)
    return jnp.sum(jnp.where(mine, value, 0.0), axis=1, keepdims=True)


def asked_line(asked):
    devices, slots = asked.shape
    total = devices * slots
    pick = hot(lax.rem(iota((slots, total), 1), slots) == iota((slots, total), 0))
    high, low = halves(asked)
    value = dot(high.astype(bf16), pick) * 256.0 + dot(low.astype(bf16), pick)
    first = iota((devices, total), 0) * slots
    spot = iota((devices, total), 1)
    mine = (spot >= first) & (spot < first + slots)
    return jnp.sum(jnp.where(mine, value, 0.0), axis=0, keepdims=True)


def parts_of(value):
    return value >> 8, value & 255


def fetch_kernel(asked_ref, table_ref, found_ref):
    block, low = parts_of(asked_column(asked_ref[...]).astype(i32))
    total = block.shape[0]
    low_hot = hot(low == iota((total, BLOCK), 1))
    block = jnp.broadcast_to(block.astype(f32), (total, BLOCK)).astype(bf16)
    picks = [
        jnp.where(block == jnp.bfloat16(k), low_hot, jnp.bfloat16(0)) for k in range(table_ref.shape[0] // BLOCK)
    ]
    found_ref[...] = dot(jnp.concatenate(picks, axis=1), table_ref[...]).astype(bf16)


def unit_of(users):
    width = users.shape[1]
    users = users.astype(f32)
    mean = jnp.mean(users * users, axis=1, keepdims=True)
    return (users * lax.rsqrt(mean + epsilon) * (1.0 / width**0.5)).astype(bf16)


def prepare_kernel(place_ref, asked_ref, *refs):
    *users, unit_ref, column_ref, low_hot_ref, block_ref = refs
    n = place_ref.shape[1]
    for k, users_ref in enumerate(users):
        unit_ref[pl.ds(k * n, n)] = unit_of(users_ref[...])
    eye = iota((n, n), 0) == iota((n, n), 1)
    column_ref[...] = jnp.sum(jnp.where(eye, place_ref[...], 0), axis=1, keepdims=True)
    block, low = parts_of(asked_line(asked_ref[...]).astype(i32))
    low_hot_ref[...] = hot(low == iota(low_hot_ref.shape, 0))
    block_ref[...] = jnp.broadcast_to(block.astype(f32), block_ref.shape).astype(bf16)


def main_kernel(fetched_ref, weight_ref, unit_ref, place_ref, column_ref, outgoing_ref, embed_ref, dhidden_ref):
    n = place_ref.shape[1]
    total, width = fetched_ref.shape
    root = 1.0 / width**0.5
    embed = dot(hot(column_ref[...] == iota((n, total), 1)), fetched_ref[...]).astype(bf16)
    hidden = dot(embed, weight_ref[...])
    rscale = lax.rsqrt(jnp.mean(hidden * hidden, axis=1, keepdims=True) + epsilon)
    item_vec = (hidden * (rscale * root)).astype(bf16)
    unit = unit_ref[...]
    expo = jnp.exp(dot(item_vec, unit, 1, 1) * score_scale)
    sums = jnp.sum(expo, axis=1, keepdims=True)
    mixed = dot(expo.astype(bf16), unit)
    own = unit_ref[pl.ds(0, n)].astype(f32)
    positive = jnp.sum(item_vec.astype(f32) * own, axis=1, keepdims=True) * score_scale
    xent = jnp.log(sums) - positive
    cweight = 1.0 / (1.0 + xent * (1.0 / cauchy_scale))
    dvec = (cweight * score_scale) * (mixed * (1.0 / sums) - own)
    inner = jnp.sum(hidden * dvec, axis=1, keepdims=True)
    dhidden = (rscale * root * (dvec - hidden * (rscale * rscale * inner * (1.0 / width)))).astype(bf16)
    outgoing_ref[...] = dot(hot(place_ref[...] == iota((total, n), 0)), dhidden).astype(bf16)
    embed_ref[...] = embed
    dhidden_ref[...] = dhidden


def cut(blocks, bits, refs):
    size = refs[0].shape[0]
    mine = sum(((lax.axis_index(axis) >> level) & 1) << k for k, (axis, level) in enumerate(reversed(bits)))
    for step, ref in enumerate(refs):
        ref[...] = blocks[pl.ds((mine ^ step) * size, size)].astype(ref.dtype)


def share_kernel(order, bits, embed_ref, dhidden_ref, *refs):
    *refs, blocks = refs
    share = dot(embed_ref[...], dhidden_ref[...], 0, 0)
    size = blocks.shape[1]
    for spot, block in enumerate(order):
        blocks[spot] = share[block * size : (block + 1) * size]
    cut(blocks, bits, refs)


def sum_of(refs):
    return sum(ref[...].astype(f32) for ref in refs)


def stage_kernel(bits, count, *refs):
    came, (*refs, blocks) = refs[:count], refs[count:]
    blocks[...] = sum_of(came)
    cut(blocks, bits, refs)


def last_kernel(*refs):
    *came, total_ref = refs
    total_ref[...] = sum_of(came)[0]


def table_kernel(low_hot_ref, block_ref, incoming_ref, weight_ref, table_grad_hbm, ready, sems):
    drow = dot(incoming_ref[...], weight_ref[...], 1, 1).astype(bf16)
    groups = sems.shape[0]
    size = ready.shape[0] // groups
    copies = []
    for g in range(groups):
        here = pl.ds(g * size, size)
        picks = [
            jnp.where(block_ref[...] == jnp.bfloat16(k), low_hot_ref[...], jnp.bfloat16(0))
            for k in range(g * size // BLOCK, (g + 1) * size // BLOCK)
        ]
        ready[here] = dot(jnp.concatenate(picks, axis=0), drow).astype(bf16)
        copy = pltpu.make_async_copy(ready.at[here], table_grad_hbm.at[here], sems.at[g])
        copy.start()
        copies.append(copy)
    for copy in copies:
        copy.wait()


def params(mib=16):
    return pltpu.CompilerParams(vmem_limit_bytes=mib * 1024 * 1024)


def cost(flops, bytes_accessed=1 << 20):
    return pl.CostEstimate(flops=flops, bytes_accessed=bytes_accessed, transcendentals=0)


def call(kernel, outs, *args, flops=0, scratch=()):
    return pl.pallas_call(
        kernel,
        out_shape=[jax.ShapeDtypeStruct(shape, dtype) for shape, dtype in outs],
        scratch_shapes=scratch,
        compiler_params=params(),
        cost_estimate=cost(flops),
    )(*args)


def swap(value, *bits):
    n_item, devices = lax.axis_size("item"), lax.axis_size("batch") * lax.axis_size("item")
    mask = sum((n_item if axis == "batch" else 1) << level for axis, level in bits)
    return lax.ppermute(value, ("batch", "item"), [(k, k ^ mask) for k in range(devices)])


def bits_of(axis):
    return [(axis, level) for level in range(lax.axis_size(axis).bit_length() - 1)]


def reduce_scatter(embed, dhidden):
    width = embed.shape[1]
    n_item, devices = lax.axis_size("item"), lax.axis_size("batch") * lax.axis_size("item")
    part = width // devices
    bits = bits_of("batch") + bits_of("item")
    order = []
    for spot in range(devices):
        at = {"batch": 0, "item": 0}
        for k, (axis, level) in enumerate(bits):
            at[axis] |= (spot >> (len(bits) - 1 - k) & 1) << level
        order.append(at["batch"] * n_item + at["item"])
    odd = len(bits) % 2
    stages = [bits[:1]] * odd + [bits[k : k + 2] for k in range(odd, len(bits), 2)]
    left, values = devices, [embed, dhidden]
    for k, stage in enumerate(stages):
        whole, left = left, left >> len(stage)
        sent = f32 if k == len(stages) - 1 else bf16
        kernel = functools.partial(*((stage_kernel, stage, len(values)) if k else (share_kernel, order, stage)))
        kept, *sends = call(
            kernel,
            [((left, part, width), f32)] + [((left, part, width), sent)] * ((1 << len(stage)) - 1),
            *values,
            scratch=[pltpu.VMEM((whole, part, width), f32)],
        )
        values = [kept]
        for step, value in enumerate(sends, 1):
            values.append(swap(value, *[bit for j, bit in enumerate(reversed(stage)) if step >> j & 1]))
    return values


def local(user_vectors, item_table, tower_weight, item_owner, item_row):
    n, width = user_vectors.shape
    rows = item_table.shape[0]
    axes = ("batch", "item")
    n_batch, n_item = lax.axis_size("batch"), lax.axis_size("item")
    devices = n_batch * n_item
    slots = 2 * n // devices
    total = devices * slots
    groups = rows // min(512, rows)

    exchange = functools.partial(lax.all_to_all, axis_name=axes, split_axis=0, concat_axis=0, tiled=True)

    far, *near = reversed(bits_of("batch"))
    users = [user_vectors, swap(user_vectors, far)]
    request, place = call(
        request_kernel,
        [((devices, slots), i32), ((1, n), i32)],
        jnp.stack([item_owner.reshape(n), item_row]),
        flops=1 << 34,
    )
    asked, *users = lax.optimization_barrier((exchange(request), *users))
    (found,) = call(fetch_kernel, [((total, width), bf16)], asked, item_table, flops=2 * total * rows * width)
    fetched = exchange(found.reshape(devices, slots, width)).reshape(total, width)
    for bit in near:
        users += [swap(value, bit) for value in users]
    unit, column, low_hot, block = call(
        prepare_kernel,
        [((n_batch * n, width), bf16), ((n, 1), i32), ((BLOCK, total), bf16), ((BLOCK, total), bf16)],
        place,
        asked,
        *users,
        flops=1 << 28,
    )
    outgoing, embed, dhidden = call(
        main_kernel,
        [((total, width), bf16), ((n, width), bf16), ((n, width), bf16)],
        fetched,
        tower_weight,
        unit,
        place,
        column,
        flops=1 << 30,
    )
    incoming = exchange(outgoing.reshape(devices, slots, width)).reshape(total, width)

    terms = reduce_scatter(embed, dhidden)

    table_grad = pl.pallas_call(
        table_kernel,
        out_specs=pl.BlockSpec(memory_space=pl.ANY),
        out_shape=jax.ShapeDtypeStruct((rows, width), bf16),
        scratch_shapes=[pltpu.VMEM((rows, width), bf16), pltpu.SemaphoreType.DMA((groups,))],
        compiler_params=params(),
        cost_estimate=cost(2 * total * rows * width, 2 * rows * width),
    )(low_hot, block, incoming, tower_weight)
    table_grad, *terms = lax.optimization_barrier((table_grad, *terms))
    (weight_grad,) = call(last_kernel, [((width // devices, width), f32)], *terms)
    return (table_grad, weight_grad)


def solution(mesh):
    return jax.shard_map(
        local,
        mesh=mesh,
        in_specs=(
            P(("batch", "item"), None),
            P(("batch", "item"), None),
            P(),
            P(("batch", "item"), None),
            P(("batch", "item")),
        ),
        out_specs=(P(("batch", "item"), None), P(("batch", "item"), None)),
        check_vma=False,
    )
```

```python
import functools

import jax
import jax.numpy as jnp
from jax import lax
from jax.experimental import pallas as pl
from jax.experimental.pallas import tpu as pltpu
from jax.sharding import PartitionSpec as P

epsilon = 1e-06
score_scale = 60.0
cauchy_scale = 4.0
f32 = jnp.float32
bf16 = jnp.bfloat16
i32 = jnp.int32
BLOCK = 256


def iota(shape, dim):
    return lax.broadcasted_iota(i32, shape, dim)


def hot(mask):
    return jnp.where(mask, 1.0, 0.0).astype(bf16)


def dot(a, b, a_dim=1, b_dim=0):
    return lax.dot_general(a, b, (((a_dim,), (b_dim,)), ((), ())), preferred_element_type=f32)


def halves(value):
    return (value >> 8).astype(f32), (value & 255).astype(f32)


def position():
    return lax.axis_index("batch") * lax.axis_size("item") + lax.axis_index("item")


def log2(value):
    return value.bit_length() - 1


def unit_kernel(users_ref, unit_ref):
    width = users_ref.shape[1]
    users = users_ref[...].astype(f32)
    mean = jnp.mean(users * users, axis=1, keepdims=True)
    unit_ref[...] = (users * lax.rsqrt(mean + epsilon) * (1.0 / width**0.5)).astype(bf16)


def request_kernel(named_ref, request_ref):
    devices, lanes = request_ref.shape
    slots = lanes // 3
    n = named_ref.shape[1]
    owner, row = named_ref[0:1], named_ref[1:2]
    named = owner == iota((devices, n), 0)
    count = dot(hot(named), hot(iota((n, n), 0) <= iota((n, n), 1)))
    rank = jnp.sum(jnp.where(named, count, 0.0), axis=0, keepdims=True).astype(i32) - 1
    in_slot = hot(rank == iota((slots, n), 0))
    partner = (owner ^ 1) == iota((devices, n), 0)
    which = iota((1, n), 1)
    for k, (mask, value) in enumerate([(named, row), (named, which), (partner, which)]):
        high, low = halves(value + 1)
        high = dot(jnp.where(mask, high, 0.0).astype(bf16), in_slot, 1, 1)
        low = dot(jnp.where(mask, low, 0.0).astype(bf16), in_slot, 1, 1)
        request_ref[:, k * slots : (k + 1) * slots] = (high * 256.0 + low).astype(i32) - 1


def asker_of(spot, part, n_batch, slots):
    n_item = lax.axis_size("item")
    batch = (spot >> log2(slots)) & (n_batch - 1)
    level = spot >> log2(slots * n_batch)
    return position() ^ (batch * n_item + level * 2 + part)


def slot_column(asked, n_batch, part):
    devices, slots = asked.shape
    total = devices * slots // 2
    pick = hot(asker_of(iota((total, devices), 0), part, n_batch, slots) == iota((total, devices), 1))
    high, low = halves(asked)
    value = dot(pick, high.astype(bf16)) * 256.0 + dot(pick, low.astype(bf16))
    mine = (iota((total, slots), 0) & (slots - 1)) == iota((total, slots), 1)
    return jnp.sum(jnp.where(mine, value, 0.0), axis=1, keepdims=True)


def slot_line(asked, n_batch):
    devices, slots = asked.shape
    total = devices * slots
    pick = hot((iota((slots, total), 1) & (slots - 1)) == iota((slots, total), 0))
    high, low = halves(asked)
    value = dot(high.astype(bf16), pick) * 256.0 + dot(low.astype(bf16), pick)
    spot = iota((devices, total), 1)
    part = spot >> log2(total // 2)
    mine = asker_of(spot & (total // 2 - 1), part, n_batch, slots) == iota((devices, total), 0)
    return jnp.sum(jnp.where(mine, value, 0.0), axis=0, keepdims=True)


def parts_of(value):
    return value >> 8, value & 255


def fetch_kernel(n_batch, part, asked_ref, table_ref, found_ref):
    slots = asked_ref.shape[1] // 3
    block, low = parts_of(slot_column(asked_ref[:, :slots], n_batch, part).astype(i32))
    total = block.shape[0]
    low_hot = hot(low == iota((total, BLOCK), 1))
    block = jnp.broadcast_to(block.astype(f32), (total, BLOCK)).astype(bf16)
    picks = [
        jnp.where(block == jnp.bfloat16(k), low_hot, jnp.bfloat16(0)) for k in range(table_ref.shape[0] // BLOCK)
    ]
    found_ref[...] = dot(jnp.concatenate(picks, axis=1), table_ref[...]).astype(bf16)


def prepare_kernel(n_batch, n, asked_ref, own_ref, partner_ref, low_hot_ref, block_ref):
    slots = asked_ref.shape[1] // 3
    total = own_ref.shape[0]
    batch = (iota((total, 1), 0) >> log2(slots)) & (n_batch - 1)
    for k, ref in enumerate([own_ref, partner_ref], 1):
        which = slot_column(asked_ref[:, k * slots : (k + 1) * slots], n_batch, 0).astype(i32)
        ref[...] = jnp.where(which < 0, -1, batch * n + which)
    block, low = parts_of(slot_line(asked_ref[:, :slots], n_batch).astype(i32))
    low_hot_ref[...] = hot(low == iota(low_hot_ref.shape, 0))
    block_ref[...] = jnp.broadcast_to(block.astype(f32), block_ref.shape).astype(bf16)


def main_kernel(first, n_batch, weight_ref, *refs):
    fetched, places, (*units, out_a, out_b) = refs[:2], refs[2:4], refs[4:]
    width = weight_ref.shape[0]
    groups = len(units) // n_batch
    size = out_a.shape[0] // groups
    n = units[0].shape[0]
    root = 1.0 / width**0.5
    for group in range(groups):
        here = pl.ds((first + group) * size, size)
        embed = jnp.concatenate([ref[here] for ref in fetched], axis=0)
        place = jnp.concatenate([ref[here] for ref in places], axis=0)
        hidden = dot(embed, weight_ref[...])
        rscale = lax.rsqrt(jnp.mean(hidden * hidden, axis=1, keepdims=True) + epsilon)
        item_vec = (hidden * (rscale * root)).astype(bf16)
        sums, both = 0.0, 0.0
        for k in range(n_batch):
            unit = units[group * n_batch + k][...]
            expo = jnp.exp(dot(item_vec, unit, 1, 1) * score_scale)
            sums += jnp.sum(expo, axis=1, keepdims=True)
            mine = hot(place - k * n == iota((2 * size, n), 1))
            both += dot(jnp.concatenate([expo.astype(bf16), mine], axis=0), unit)
        mixed, own = both[: 2 * size], both[2 * size :]
        positive = jnp.sum(item_vec.astype(f32) * own, axis=1, keepdims=True) * score_scale
        xent = jnp.log(sums) - positive
        cweight = 1.0 / (1.0 + xent * (1.0 / cauchy_scale))
        dvec = (cweight * score_scale) * (mixed * (1.0 / sums) - own)
        inner = jnp.sum(hidden * dvec, axis=1, keepdims=True)
        dhidden = (rscale * root * (dvec - hidden * (rscale * rscale * inner * (1.0 / width)))).astype(bf16)
        out_a[pl.ds(group * size, size)] = dhidden[:size]
        out_b[pl.ds(group * size, size)] = dhidden[size:]


def cut(blocks, bits, refs):
    size = refs[0].shape[0]
    mine = sum(((lax.axis_index(axis) >> level) & 1) << k for k, (axis, level) in enumerate(reversed(bits)))
    for step, ref in enumerate(refs):
        ref[...] = blocks[pl.ds((mine ^ step) * size, size)].astype(ref.dtype)


def share_kernel(order, bits, count, *refs):
    fetched, dhidden, (*refs, blocks) = refs[:2], refs[2:count], refs[count:]
    half = len(dhidden) // 2
    share = 0.0
    for k, ref in enumerate(fetched):
        share += dot(ref[...], jnp.concatenate([d[...] for d in dhidden[k * half : (k + 1) * half]], axis=0), 0, 0)
    size = blocks.shape[1]
    for spot, block in enumerate(order):
        blocks[spot] = share[block * size : (block + 1) * size]
    cut(blocks, bits, refs)


def sum_of(refs):
    return sum(ref[...].astype(f32) for ref in refs)


def stage_kernel(bits, count, *refs):
    came, (*refs, blocks) = refs[:count], refs[count:]
    blocks[...] = sum_of(came)
    cut(blocks, bits, refs)


def last_kernel(*refs):
    *came, total_ref = refs
    total_ref[...] = sum_of(came)[0]


def table_kernel(low_hot_ref, block_ref, weight_ref, *refs):
    *incoming, table_grad_hbm, ready, sems = refs
    drow = jnp.concatenate([dot(ref[...], weight_ref[...], 1, 1).astype(bf16) for ref in incoming], axis=0)
    groups = sems.shape[0]
    size = ready.shape[0] // groups
    copies = []
    for g in range(groups):
        here = pl.ds(g * size, size)
        picks = [
            jnp.where(block_ref[...] == jnp.bfloat16(k), low_hot_ref[...], jnp.bfloat16(0))
            for k in range(g * size // BLOCK, (g + 1) * size // BLOCK)
        ]
        ready[here] = dot(jnp.concatenate(picks, axis=0), drow).astype(bf16)
        copy = pltpu.make_async_copy(ready.at[here], table_grad_hbm.at[here], sems.at[g])
        copy.start()
        copies.append(copy)
    for copy in copies:
        copy.wait()


def params(mib):
    return pltpu.CompilerParams(vmem_limit_bytes=mib * 1024 * 1024)


def cost(flops, bytes_accessed=1 << 20):
    return pl.CostEstimate(flops=flops, bytes_accessed=bytes_accessed, transcendentals=0)


def call(kernel, outs, *args, flops=0, scratch=(), mib=16):
    return pl.pallas_call(
        kernel,
        out_shape=[jax.ShapeDtypeStruct(shape, dtype) for shape, dtype in outs],
        scratch_shapes=scratch,
        compiler_params=params(mib),
        cost_estimate=cost(flops),
    )(*args)


def swap(value, mask):
    devices = lax.axis_size("batch") * lax.axis_size("item")
    return lax.ppermute(value, ("batch", "item"), [(k, k ^ mask) for k in range(devices)])


def bits_of(axis):
    return [(axis, level) for level in range(log2(lax.axis_size(axis)))]


def mask_of(bits):
    return sum((lax.axis_size("item") if axis == "batch" else 1) << level for axis, level in bits)


def reduce_scatter(values, width):
    n_item, devices = lax.axis_size("item"), lax.axis_size("batch") * lax.axis_size("item")
    part = width // devices
    bits = bits_of("batch") + bits_of("item")
    order = []
    for spot in range(devices):
        at = {"batch": 0, "item": 0}
        for k, (axis, level) in enumerate(bits):
            at[axis] |= (spot >> (len(bits) - 1 - k) & 1) << level
        order.append(at["batch"] * n_item + at["item"])
    odd = len(bits) % 2
    stages = [bits[:1]] * odd + [bits[k : k + 2] for k in range(odd, len(bits), 2)]
    left = devices
    for k, stage in enumerate(stages):
        whole, left = left, left >> len(stage)
        sent = f32 if k == len(stages) - 1 else bf16
        kernel = functools.partial(*((stage_kernel, stage) if k else (share_kernel, order, stage)), len(values))
        kept, *sends = call(
            kernel,
            [((left, part, width), f32)] + [((left, part, width), sent)] * ((1 << len(stage)) - 1),
            *values,
            scratch=[pltpu.VMEM((whole, part, width), f32)],
        )
        values = [kept]
        for step, value in enumerate(sends, 1):
            values.append(swap(value, mask_of([bit for j, bit in enumerate(reversed(stage)) if step >> j & 1])))
    return values


def local(user_vectors, item_table, tower_weight, item_owner, item_row):
    n, width = user_vectors.shape
    rows = item_table.shape[0]
    n_batch, n_item = lax.axis_size("batch"), lax.axis_size("item")
    devices = n_batch * n_item
    levels = n_item // 2
    slots = 2 * n // devices
    total = devices * slots
    half = total // 2
    groups = rows // min(512, rows)

    (unit,) = call(unit_kernel, [((n, width), bf16)], user_vectors)
    far = [batch * n_item for batch in range(2, n_batch, 2)]
    units = {0: unit}
    for mask in far + [2 << k for k in range(log2(levels))]:
        units[mask] = swap(unit, mask)

    (request,) = call(
        request_kernel,
        [((devices, 3 * slots), i32)],
        jnp.stack([item_owner.reshape(n), item_row]),
        flops=1 << 34,
    )
    asked = lax.all_to_all(request, ("batch", "item"), split_axis=0, concat_axis=0, tiled=True)
    early = list(units)
    asked, *values = lax.optimization_barrier((asked, *units.values()))
    units = dict(zip(early, values))

    def fetch(part):
        kernel = functools.partial(fetch_kernel, n_batch, part)
        return call(kernel, [((half, width), bf16)], asked, item_table, flops=2 * half * rows * width)[0]

    fetched = [None, swap(fetch(1), 1)]
    fetched[0] = fetch(0)

    for level in range(1, levels):
        if 2 * level not in units:
            top = 1 << log2(level)
            units[2 * level] = swap(units[2 * (level - top)], 2 * top)
        for mask in far:
            units[mask + 2 * level] = swap(units[2 * level], mask)
    for mask in list(units):
        units[mask + n_item] = swap(units[mask], n_item)

    *places, low_hot, block = call(
        functools.partial(prepare_kernel, n_batch, n),
        [((half, 1), i32)] * 2 + [((BLOCK, total), bf16)] * 2,
        asked,
    )
    dhidden = [[], []]
    size = half // levels
    for first, count in [(0, levels - 1), (levels - 1, 1)]:
        outs = call(
            functools.partial(main_kernel, first, n_batch),
            [((count * size, width), bf16)] * 2,
            tower_weight,
            *fetched,
            *places,
            *[units[2 * level + batch * n_item] for level in range(first, first + count) for batch in range(n_batch)],
            flops=count << 29,
            mib=40,
        )
        for part, value in zip(dhidden, outs):
            part.append(value)
    incoming = dhidden[0] + [swap(value, 1) for value in dhidden[1]]
    terms = reduce_scatter([*fetched, *dhidden[0], *dhidden[1]], width)
    table_grad = pl.pallas_call(
        table_kernel,
        out_specs=pl.BlockSpec(memory_space=pl.ANY),
        out_shape=jax.ShapeDtypeStruct((rows, width), bf16),
        scratch_shapes=[pltpu.VMEM((rows, width), bf16), pltpu.SemaphoreType.DMA((groups,))],
        compiler_params=params(16),
        cost_estimate=cost(2 * total * rows * width, 2 * rows * width),
    )(low_hot, block, tower_weight, *incoming)
    table_grad, *terms = lax.optimization_barrier((table_grad, *terms))
    (weight_grad,) = call(last_kernel, [((width // devices, width), f32)], *terms)
    return (table_grad, weight_grad)


def solution(mesh):
    return jax.shard_map(
        local,
        mesh=mesh,
        in_specs=(
            P(("batch", "item"), None),
            P(("batch", "item"), None),
            P(),
            P(("batch", "item"), None),
            P(("batch", "item")),
        ),
        out_specs=(P(("batch", "item"), None), P(("batch", "item"), None)),
        check_vma=False,
    )
```

```python
import functools

import jax
import jax.numpy as jnp
from jax import lax
from jax.experimental import pallas as pl
from jax.experimental.pallas import tpu as pltpu
from jax.sharding import PartitionSpec as P

epsilon = 1e-06
score_scale = 60.0
cauchy_scale = 4.0
f32 = jnp.float32
bf16 = jnp.bfloat16
i32 = jnp.int32
BLOCK = 256


def iota(shape, dim):
    return lax.broadcasted_iota(i32, shape, dim)


def hot(mask):
    return jnp.where(mask, 1.0, 0.0).astype(bf16)


def dot(a, b, a_dim=1, b_dim=0):
    return lax.dot_general(a, b, (((a_dim,), (b_dim,)), ((), ())), preferred_element_type=f32)


def halves(value):
    return (value >> 8).astype(f32), (value & 255).astype(f32)


def position():
    return lax.axis_index("batch") * lax.axis_size("item") + lax.axis_index("item")


def log2(value):
    return value.bit_length() - 1


def request_kernel(near, named_ref, request_ref):
    devices, lanes = request_ref.shape
    slots = lanes // (1 + near)
    n = named_ref.shape[1]
    owner, row = named_ref[0:1], named_ref[1:2]
    device = iota((devices, n), 0)
    named = owner == device
    count = dot(hot(named), hot(iota((n, n), 0) <= iota((n, n), 1)))
    rank = jnp.sum(jnp.where(named, count, 0.0), axis=0, keepdims=True).astype(i32) - 1
    in_slot = hot(rank == iota((slots, n), 0))
    which = iota((1, n), 1)
    for k, (value, mask) in enumerate([(row, 0)] + [(which, mask) for mask in range(near)]):
        high, low = halves(value + 1)
        here = (owner ^ mask) == device
        high = dot(jnp.where(here, high, 0.0).astype(bf16), in_slot, 1, 1)
        low = dot(jnp.where(here, low, 0.0).astype(bf16), in_slot, 1, 1)
        request_ref[:, k * slots : (k + 1) * slots] = (high * 256.0 + low).astype(i32) - 1


def asker_of(spot, part, near, n_batch, slots):
    batch = (spot >> log2(slots)) & (n_batch - 1)
    level = spot >> log2(slots * n_batch)
    return position() ^ (batch * lax.axis_size("item") + level * near + part)


def slot_column(asked, part, near, n_batch):
    devices, slots = asked.shape
    total = devices * slots // near
    asker = asker_of(iota((total, devices), 0), part, near, n_batch, slots)
    pick = hot(asker == iota((total, devices), 1))
    high, low = halves(asked)
    value = dot(pick, high.astype(bf16)) * 256.0 + dot(pick, low.astype(bf16))
    mine = (iota((total, slots), 0) & (slots - 1)) == iota((total, slots), 1)
    return jnp.sum(jnp.where(mine, value, 0.0), axis=1, keepdims=True)


def slot_line(asked, near, n_batch):
    devices, slots = asked.shape
    total = devices * slots
    pick = hot((iota((slots, total), 1) & (slots - 1)) == iota((slots, total), 0))
    high, low = halves(asked)
    value = dot(high.astype(bf16), pick) * 256.0 + dot(low.astype(bf16), pick)
    spot = iota((devices, total), 1)
    asker = asker_of(spot & (total // near - 1), spot >> log2(total // near), near, n_batch, slots)
    return jnp.sum(jnp.where(asker == iota((devices, total), 0), value, 0.0), axis=0, keepdims=True)


def parts_of(value):
    return value >> 8, value & 255


def fetch_kernel(parts, near, n_batch, asked_ref, table_ref, *found):
    slots = asked_ref.shape[1] // (1 + near)
    asked = asked_ref[:, :slots]
    column = jnp.concatenate([slot_column(asked, part, near, n_batch) for part in parts], axis=0)
    block, low = parts_of(column.astype(i32))
    total = block.shape[0]
    low_hot = hot(low == iota((total, BLOCK), 1))
    block = jnp.broadcast_to(block.astype(f32), (total, BLOCK)).astype(bf16)
    picks = [
        jnp.where(block == jnp.bfloat16(k), low_hot, jnp.bfloat16(0)) for k in range(table_ref.shape[0] // BLOCK)
    ]
    rows = dot(jnp.concatenate(picks, axis=1), table_ref[...]).astype(bf16)
    size = total // len(found)
    for k, ref in enumerate(found):
        ref[...] = rows[k * size : (k + 1) * size]


def prepare_kernel(near, n_batch, n, asked_ref, place_ref, low_hot_ref, block_ref):
    slots = asked_ref.shape[1] // (1 + near)
    size = place_ref.shape[0] // near
    batch = (iota((size, 1), 0) >> log2(slots)) & (n_batch - 1)
    for part in range(near):
        asked = asked_ref[:, (1 + part) * slots : (2 + part) * slots]
        which = slot_column(asked, 0, near, n_batch).astype(i32)
        place_ref[pl.ds(part * size, size)] = jnp.where(which < 0, -1, batch * n + which)
    block, low = parts_of(slot_line(asked_ref[:, :slots], near, n_batch).astype(i32))
    low_hot_ref[...] = hot(low == iota(low_hot_ref.shape, 0))
    block_ref[...] = jnp.broadcast_to(block.astype(f32), block_ref.shape).astype(bf16)


def users_kernel(level, near, place_ref, *refs):
    *users, unit_ref, own_ref = refs
    n, width = users[0].shape
    for k, ref in enumerate(users):
        value = ref[...].astype(f32)
        mean = jnp.mean(value * value, axis=1, keepdims=True)
        unit_ref[pl.ds(k * n, n)] = (value * lax.rsqrt(mean + epsilon) * (1.0 / width**0.5)).astype(bf16)
    step = place_ref.shape[0] // near
    size = own_ref.shape[0] // near
    place = jnp.concatenate([place_ref[pl.ds(k * step + level * size, size)] for k in range(near)], axis=0)
    own_ref[...] = dot(hot(place == iota((place.shape[0], unit_ref.shape[0]), 1)), unit_ref[...]).astype(bf16)


def main_kernel(levels, weight_ref, *refs):
    parts = (len(refs) - 2 * levels) // 2
    fetched, units, owns, outs = refs[:parts], refs[parts : parts + levels], refs[parts + levels : parts + 2 * levels], refs[-parts:]
    width = weight_ref.shape[0]
    size = outs[0].shape[0] // levels
    root = 1.0 / width**0.5
    for level in range(levels):
        here = pl.ds(level * size, size)
        embed = jnp.concatenate([ref[here] for ref in fetched], axis=0)
        hidden = dot(embed, weight_ref[...])
        rscale = lax.rsqrt(jnp.mean(hidden * hidden, axis=1, keepdims=True) + epsilon)
        item_vec = (hidden * (rscale * root)).astype(bf16)
        unit = units[level][...]
        expo = jnp.exp(dot(item_vec, unit, 1, 1) * score_scale)
        sums = jnp.sum(expo, axis=1, keepdims=True)
        mixed = dot(expo.astype(bf16), unit)
        own = owns[level][...].astype(f32)
        positive = jnp.sum(item_vec.astype(f32) * own, axis=1, keepdims=True) * score_scale
        xent = jnp.log(sums) - positive
        cweight = 1.0 / (1.0 + xent * (1.0 / cauchy_scale))
        dvec = (cweight * score_scale) * (mixed * (1.0 / sums) - own)
        inner = jnp.sum(hidden * dvec, axis=1, keepdims=True)
        dhidden = (rscale * root * (dvec - hidden * (rscale * rscale * inner * (1.0 / width)))).astype(bf16)
        for part, ref in enumerate(outs):
            ref[here] = dhidden[part * size : (part + 1) * size]


def cut(blocks, bits, refs):
    size = refs[0].shape[0]
    mine = sum(((lax.axis_index(axis) >> level) & 1) << k for k, (axis, level) in enumerate(reversed(bits)))
    for step, ref in enumerate(refs):
        ref[...] = blocks[pl.ds((mine ^ step) * size, size)].astype(ref.dtype)


def share_kernel(order, bits, count, *refs):
    values, (*refs, blocks) = refs[:count], refs[count:]
    embed, dhidden = (jnp.concatenate([ref[...] for ref in half], axis=0) for half in (values[: count // 2], values[count // 2 :]))
    share = dot(embed, dhidden, 0, 0)
    size = blocks.shape[1]
    for spot, block in enumerate(order):
        blocks[spot] = share[block * size : (block + 1) * size]
    cut(blocks, bits, refs)


def sum_of(refs):
    return sum(ref[...].astype(f32) for ref in refs)


def stage_kernel(bits, count, *refs):
    came, (*refs, blocks) = refs[:count], refs[count:]
    blocks[...] = sum_of(came)
    cut(blocks, bits, refs)


def last_kernel(*refs):
    *came, total_ref = refs
    total_ref[...] = sum_of(came)[0]


def table_kernel(low_hot_ref, block_ref, weight_ref, *refs):
    *incoming, table_grad_hbm, ready, sems = refs
    drow = jnp.concatenate([dot(ref[...], weight_ref[...], 1, 1).astype(bf16) for ref in incoming], axis=0)
    groups = sems.shape[0]
    size = ready.shape[0] // groups
    copies = []
    for g in range(groups):
        here = pl.ds(g * size, size)
        picks = [
            jnp.where(block_ref[...] == jnp.bfloat16(k), low_hot_ref[...], jnp.bfloat16(0))
            for k in range(g * size // BLOCK, (g + 1) * size // BLOCK)
        ]
        ready[here] = dot(jnp.concatenate(picks, axis=0), drow).astype(bf16)
        copy = pltpu.make_async_copy(ready.at[here], table_grad_hbm.at[here], sems.at[g])
        copy.start()
        copies.append(copy)
    for copy in copies:
        copy.wait()


def params(mib):
    return pltpu.CompilerParams(vmem_limit_bytes=mib * 1024 * 1024)


def cost(flops, bytes_accessed=1 << 20):
    return pl.CostEstimate(flops=flops, bytes_accessed=bytes_accessed, transcendentals=0)


def call(kernel, outs, *args, flops=0, scratch=(), mib=16):
    return pl.pallas_call(
        kernel,
        out_shape=[jax.ShapeDtypeStruct(shape, dtype) for shape, dtype in outs],
        scratch_shapes=scratch,
        compiler_params=params(mib),
        cost_estimate=cost(flops),
    )(*args)


def swap(value, mask):
    devices = lax.axis_size("batch") * lax.axis_size("item")
    return lax.ppermute(value, ("batch", "item"), [(k, k ^ mask) for k in range(devices)])


def bits_of(axis):
    return [(axis, level) for level in range(log2(lax.axis_size(axis)))]


def mask_of(bits):
    return sum((lax.axis_size("item") if axis == "batch" else 1) << level for axis, level in bits)


def reduce_scatter(values, width):
    n_item, devices = lax.axis_size("item"), lax.axis_size("batch") * lax.axis_size("item")
    part = width // devices
    bits = bits_of("batch") + bits_of("item")
    order = []
    for spot in range(devices):
        at = {"batch": 0, "item": 0}
        for k, (axis, level) in enumerate(bits):
            at[axis] |= (spot >> (len(bits) - 1 - k) & 1) << level
        order.append(at["batch"] * n_item + at["item"])
    odd = len(bits) % 2
    stages = [bits[:1]] * odd + [bits[k : k + 2] for k in range(odd, len(bits), 2)]
    left = devices
    for k, stage in enumerate(stages):
        whole, left = left, left >> len(stage)
        sent = f32 if k == len(stages) - 1 else bf16
        kernel = functools.partial(*((stage_kernel, stage) if k else (share_kernel, order, stage)), len(values))
        kept, *sends = call(
            kernel,
            [((left, part, width), f32)] + [((left, part, width), sent)] * ((1 << len(stage)) - 1),
            *values,
            scratch=[pltpu.VMEM((whole, part, width), f32)],
        )
        values = [kept]
        for step, value in enumerate(sends, 1):
            values.append(swap(value, mask_of([bit for j, bit in enumerate(reversed(stage)) if step >> j & 1])))
    return values


def local(user_vectors, item_table, tower_weight, item_owner, item_row):
    n, width = user_vectors.shape
    rows = item_table.shape[0]
    n_batch, n_item = lax.axis_size("batch"), lax.axis_size("item")
    devices = n_batch * n_item
    near = min(4, n_item)
    levels = n_item // near
    slots = 2 * n // devices
    total = devices * slots
    size = total // near
    groups = rows // min(512, rows)

    far = [batch * n_item for batch in range(2, n_batch, 2)]
    users = {0: user_vectors}
    for mask in [near << k for k in range(log2(levels))] + far:
        users[mask] = swap(user_vectors, mask)

    (request,) = call(
        functools.partial(request_kernel, near),
        [((devices, (1 + near) * slots), i32)],
        jnp.stack([item_owner.reshape(n), item_row]),
        flops=1 << 34,
    )
    asked = lax.all_to_all(request, ("batch", "item"), split_axis=0, concat_axis=0, tiled=True)
    early = list(users)
    asked, *values = lax.optimization_barrier((asked, *users.values()))
    users = dict(zip(early, values))

    for level in range(1, levels):
        if near * level not in users:
            top = 1 << log2(level)
            users[near * level] = swap(users[near * (level - top)], near * top)
        for mask in far:
            users[mask + near * level] = swap(users[near * level], mask)

    def fetch(parts):
        return call(
            functools.partial(fetch_kernel, parts, near, n_batch),
            [((size, width), bf16)] * len(parts),
            asked,
            item_table,
            flops=2 * size * len(parts) * rows * width,
        )

    others = list(range(1, near))
    fetched = [swap(value, part) for part, value in zip(others, fetch(others))]
    fetched = [*fetch([0]), *fetched]

    for mask in list(users):
        users[mask + n_item] = swap(users[mask], n_item)

    place, low_hot, block = call(
        functools.partial(prepare_kernel, near, n_batch, n),
        [((total, 1), i32)] + [((BLOCK, total), bf16)] * 2,
        asked,
    )
    units, owns = zip(
        *[
            call(
                functools.partial(users_kernel, level, near),
                [((n_batch * n, width), bf16), ((total // levels, width), bf16)],
                place,
                *[users[near * level + batch * n_item] for batch in range(n_batch)],
                flops=1 << 29,
            )
            for level in range(levels)
        ]
    )
    dhidden = call(
        functools.partial(main_kernel, levels),
        [((size, width), bf16)] * near,
        tower_weight,
        *fetched,
        *units,
        *owns,
        flops=1 << 31,
        mib=40,
    )
    incoming = [dhidden[0]] + [swap(dhidden[part], part) for part in others]
    terms = reduce_scatter([*fetched, *dhidden], width)
    table_grad = pl.pallas_call(
        table_kernel,
        out_specs=pl.BlockSpec(memory_space=pl.ANY),
        out_shape=jax.ShapeDtypeStruct((rows, width), bf16),
        scratch_shapes=[pltpu.VMEM((rows, width), bf16), pltpu.SemaphoreType.DMA((groups,))],
        compiler_params=params(16),
        cost_estimate=cost(2 * total * rows * width, 2 * rows * width),
    )(low_hot, block, tower_weight, *incoming)
    table_grad, *terms = lax.optimization_barrier((table_grad, *terms))
    (weight_grad,) = call(last_kernel, [((width // devices, width), f32)], *terms)
    return (table_grad, weight_grad)


def solution(mesh):
    return jax.shard_map(
        local,
        mesh=mesh,
        in_specs=(
            P(("batch", "item"), None),
            P(("batch", "item"), None),
            P(),
            P(("batch", "item"), None),
            P(("batch", "item")),
        ),
        out_specs=(P(("batch", "item"), None), P(("batch", "item"), None)),
        check_vma=False,
    )
```

```python
import functools

import jax
import jax.numpy as jnp
from jax import lax
from jax.experimental import pallas as pl
from jax.experimental.pallas import tpu as pltpu
from jax.sharding import PartitionSpec as P

epsilon = 1e-06
score_scale = 60.0
cauchy_scale = 4.0
f32 = jnp.float32
bf16 = jnp.bfloat16
i32 = jnp.int32
BLOCK = 256


def iota(shape, dim):
    return lax.broadcasted_iota(i32, shape, dim)


def hot(mask):
    return jnp.where(mask, 1.0, 0.0).astype(bf16)


def dot(a, b, a_dim=1, b_dim=0):
    return lax.dot_general(a, b, (((a_dim,), (b_dim,)), ((), ())), preferred_element_type=f32)


def halves(value):
    return (value >> 8).astype(f32), (value & 255).astype(f32)


def position():
    return lax.axis_index("batch") * lax.axis_size("item") + lax.axis_index("item")


def log2(value):
    return value.bit_length() - 1


def request_kernel(near, named_ref, request_ref):
    devices, lanes = request_ref.shape
    slots = lanes // (1 + near)
    n = named_ref.shape[1]
    owner, row = named_ref[0:1], named_ref[1:2]
    device = iota((devices, n), 0)
    named = owner == device
    count = dot(hot(named), hot(iota((n, n), 0) <= iota((n, n), 1)))
    rank = jnp.sum(jnp.where(named, count, 0.0), axis=0, keepdims=True).astype(i32) - 1
    in_slot = hot(rank == iota((slots, n), 0))
    which = iota((1, n), 1)
    for k, (value, mask) in enumerate([(row, 0)] + [(which, mask) for mask in range(near)]):
        high, low = halves(value + 1)
        here = (owner ^ mask) == device
        high = dot(jnp.where(here, high, 0.0).astype(bf16), in_slot, 1, 1)
        low = dot(jnp.where(here, low, 0.0).astype(bf16), in_slot, 1, 1)
        request_ref[:, k * slots : (k + 1) * slots] = (high * 256.0 + low).astype(i32) - 1


def asker_of(spot, part, near, n_batch, slots):
    batch = (spot >> log2(slots)) & (n_batch - 1)
    level = spot >> log2(slots * n_batch)
    return position() ^ (batch * lax.axis_size("item") + level * near + part)


def slot_column(asked, part, near, n_batch):
    devices, slots = asked.shape
    total = devices * slots // near
    asker = asker_of(iota((total, devices), 0), part, near, n_batch, slots)
    pick = hot(asker == iota((total, devices), 1))
    high, low = halves(asked)
    value = dot(pick, high.astype(bf16)) * 256.0 + dot(pick, low.astype(bf16))
    mine = (iota((total, slots), 0) & (slots - 1)) == iota((total, slots), 1)
    return jnp.sum(jnp.where(mine, value, 0.0), axis=1, keepdims=True)


def slot_line(asked, near, n_batch):
    devices, slots = asked.shape
    total = devices * slots
    pick = hot((iota((slots, total), 1) & (slots - 1)) == iota((slots, total), 0))
    high, low = halves(asked)
    value = dot(high.astype(bf16), pick) * 256.0 + dot(low.astype(bf16), pick)
    spot = iota((devices, total), 1)
    asker = asker_of(spot & (total // near - 1), spot >> log2(total // near), near, n_batch, slots)
    return jnp.sum(jnp.where(asker == iota((devices, total), 0), value, 0.0), axis=0, keepdims=True)


def parts_of(value):
    return value >> 8, value & 255


def fetch_kernel(parts, near, n_batch, asked_ref, table_ref, *found):
    slots = asked_ref.shape[1] // (1 + near)
    asked = asked_ref[:, :slots]
    column = jnp.concatenate([slot_column(asked, part, near, n_batch) for part in parts], axis=0)
    block, low = parts_of(column.astype(i32))
    total = block.shape[0]
    low_hot = hot(low == iota((total, BLOCK), 1))
    block = jnp.broadcast_to(block.astype(f32), (total, BLOCK)).astype(bf16)
    picks = [
        jnp.where(block == jnp.bfloat16(k), low_hot, jnp.bfloat16(0)) for k in range(table_ref.shape[0] // BLOCK)
    ]
    rows = dot(jnp.concatenate(picks, axis=1), table_ref[...]).astype(bf16)
    size = total // len(found)
    for k, ref in enumerate(found):
        ref[...] = rows[k * size : (k + 1) * size]


def prepare_kernel(near, n_batch, n, asked_ref, place_ref, low_hot_ref, block_ref):
    slots = asked_ref.shape[1] // (1 + near)
    size = place_ref.shape[0] // near
    batch = (iota((size, 1), 0) >> log2(slots)) & (n_batch - 1)
    for part in range(near):
        asked = asked_ref[:, (1 + part) * slots : (2 + part) * slots]
        which = slot_column(asked, 0, near, n_batch).astype(i32)
        place_ref[pl.ds(part * size, size)] = jnp.where(which < 0, -1, batch * n + which)
    block, low = parts_of(slot_line(asked_ref[:, :slots], near, n_batch).astype(i32))
    low_hot_ref[...] = hot(low == iota(low_hot_ref.shape, 0))
    block_ref[...] = jnp.broadcast_to(block.astype(f32), block_ref.shape).astype(bf16)


def users_kernel(level, near, place_ref, *refs):
    *users, unit_ref, own_ref = refs
    n, width = users[0].shape
    for k, ref in enumerate(users):
        value = ref[...].astype(f32)
        mean = jnp.mean(value * value, axis=1, keepdims=True)
        unit_ref[pl.ds(k * n, n)] = (value * lax.rsqrt(mean + epsilon) * (1.0 / width**0.5)).astype(bf16)
    step = place_ref.shape[0] // near
    size = own_ref.shape[0] // near
    place = jnp.concatenate([place_ref[pl.ds(k * step + level * size, size)] for k in range(near)], axis=0)
    own_ref[...] = dot(hot(place == iota((place.shape[0], unit_ref.shape[0]), 1)), unit_ref[...]).astype(bf16)


def main_kernel(levels, weight_ref, *refs):
    parts = (len(refs) - 2 * levels) // 2
    fetched, units, owns, outs = refs[:parts], refs[parts : parts + levels], refs[parts + levels : parts + 2 * levels], refs[-parts:]
    width = weight_ref.shape[0]
    size = outs[0].shape[0] // levels
    root = 1.0 / width**0.5
    for level in range(levels):
        here = pl.ds(level * size, size)
        embed = jnp.concatenate([ref[here] for ref in fetched], axis=0)
        hidden = dot(embed, weight_ref[...])
        rscale = lax.rsqrt(jnp.mean(hidden * hidden, axis=1, keepdims=True) + epsilon)
        item_vec = (hidden * (rscale * root)).astype(bf16)
        unit = units[level][...]
        expo = jnp.exp(dot(item_vec, unit, 1, 1) * score_scale)
        sums = jnp.sum(expo, axis=1, keepdims=True)
        mixed = dot(expo.astype(bf16), unit)
        own = owns[level][...].astype(f32)
        positive = jnp.sum(item_vec.astype(f32) * own, axis=1, keepdims=True) * score_scale
        xent = jnp.log(sums) - positive
        cweight = 1.0 / (1.0 + xent * (1.0 / cauchy_scale))
        dvec = (cweight * score_scale) * (mixed * (1.0 / sums) - own)
        inner = jnp.sum(hidden * dvec, axis=1, keepdims=True)
        dhidden = (rscale * root * (dvec - hidden * (rscale * rscale * inner * (1.0 / width)))).astype(bf16)
        for part, ref in enumerate(outs):
            ref[here] = dhidden[part * size : (part + 1) * size]


def cut(blocks, bits, refs):
    size = refs[0].shape[0]
    mine = sum(((lax.axis_index(axis) >> level) & 1) << k for k, (axis, level) in enumerate(reversed(bits)))
    for step, ref in enumerate(refs):
        ref[...] = blocks[pl.ds((mine ^ step) * size, size)].astype(ref.dtype)


def share_kernel(order, bits, count, *refs):
    values, (*refs, blocks) = refs[:count], refs[count:]
    embed, dhidden = (jnp.concatenate([ref[...] for ref in half], axis=0) for half in (values[: count // 2], values[count // 2 :]))
    share = dot(embed, dhidden, 0, 0)
    size = blocks.shape[1]
    for spot, block in enumerate(order):
        blocks[spot] = share[block * size : (block + 1) * size]
    cut(blocks, bits, refs)


def sum_of(refs):
    return sum(ref[...].astype(f32) for ref in refs)


def stage_kernel(bits, count, *refs):
    came, (*refs, blocks) = refs[:count], refs[count:]
    blocks[...] = sum_of(came)
    cut(blocks, bits, refs)


def last_kernel(*refs):
    *came, total_ref = refs
    total_ref[...] = sum_of(came)[0]


def table_kernel(low_hot_ref, block_ref, weight_ref, *refs):
    *incoming, table_grad_hbm, ready, sems = refs
    drow = jnp.concatenate([dot(ref[...], weight_ref[...], 1, 1).astype(bf16) for ref in incoming], axis=0)
    groups = sems.shape[0]
    size = ready.shape[0] // groups
    copies = []
    for g in range(groups):
        here = pl.ds(g * size, size)
        picks = [
            jnp.where(block_ref[...] == jnp.bfloat16(k), low_hot_ref[...], jnp.bfloat16(0))
            for k in range(g * size // BLOCK, (g + 1) * size // BLOCK)
        ]
        ready[here] = dot(jnp.concatenate(picks, axis=0), drow).astype(bf16)
        copy = pltpu.make_async_copy(ready.at[here], table_grad_hbm.at[here], sems.at[g])
        copy.start()
        copies.append(copy)
    for copy in copies:
        copy.wait()


def params(mib):
    return pltpu.CompilerParams(vmem_limit_bytes=mib * 1024 * 1024)


def cost(flops, bytes_accessed=1 << 20):
    return pl.CostEstimate(flops=flops, bytes_accessed=bytes_accessed, transcendentals=0)


def call(kernel, outs, *args, flops=0, scratch=(), mib=16):
    return pl.pallas_call(
        kernel,
        out_shape=[jax.ShapeDtypeStruct(shape, dtype) for shape, dtype in outs],
        scratch_shapes=scratch,
        compiler_params=params(mib),
        cost_estimate=cost(flops),
    )(*args)


def swap(value, mask):
    devices = lax.axis_size("batch") * lax.axis_size("item")
    return lax.ppermute(value, ("batch", "item"), [(k, k ^ mask) for k in range(devices)])


def bits_of(axis):
    return [(axis, level) for level in range(log2(lax.axis_size(axis)))]


def mask_of(bits):
    return sum((lax.axis_size("item") if axis == "batch" else 1) << level for axis, level in bits)


def reduce_scatter(values, width, between):
    n_item, devices = lax.axis_size("item"), lax.axis_size("batch") * lax.axis_size("item")
    part = width // devices
    bits = bits_of("batch") + bits_of("item")
    order = []
    for spot in range(devices):
        at = {"batch": 0, "item": 0}
        for k, (axis, level) in enumerate(bits):
            at[axis] |= (spot >> (len(bits) - 1 - k) & 1) << level
        order.append(at["batch"] * n_item + at["item"])
    odd = len(bits) % 2
    stages = [bits[:1]] * odd + [bits[k : k + 2] for k in range(odd, len(bits), 2)]
    left = devices
    for k, stage in enumerate(stages):
        whole, left = left, left >> len(stage)
        sent = f32 if k == len(stages) - 1 else bf16
        kernel = functools.partial(*((stage_kernel, stage) if k else (share_kernel, order, stage)), len(values))
        kept, *sends = call(
            kernel,
            [((left, part, width), f32)] + [((left, part, width), sent)] * ((1 << len(stage)) - 1),
            *values,
            scratch=[pltpu.VMEM((whole, part, width), f32)],
        )
        values = [kept]
        for step, value in enumerate(sends, 1):
            values.append(swap(value, mask_of([bit for j, bit in enumerate(reversed(stage)) if step >> j & 1])))
        if k == 1:
            values[1] = between(values[1])
    return values


def local(user_vectors, item_table, tower_weight, item_owner, item_row):
    n, width = user_vectors.shape
    rows = item_table.shape[0]
    n_batch, n_item = lax.axis_size("batch"), lax.axis_size("item")
    devices = n_batch * n_item
    near = min(4, n_item)
    levels = n_item // near
    slots = 2 * n // devices
    total = devices * slots
    size = total // near
    groups = rows // min(512, rows)

    far = [batch * n_item for batch in range(2, n_batch, 2)]
    users = {0: user_vectors}
    for mask in [near << k for k in range(log2(levels))] + far:
        users[mask] = swap(user_vectors, mask)

    (request,) = call(
        functools.partial(request_kernel, near),
        [((devices, (1 + near) * slots), i32)],
        jnp.stack([item_owner.reshape(n), item_row]),
        flops=1 << 34,
    )
    asked = lax.all_to_all(request, ("batch", "item"), split_axis=0, concat_axis=0, tiled=True)
    early = list(users)
    asked, *values = lax.optimization_barrier((asked, *users.values()))
    users = dict(zip(early, values))

    for level in range(1, levels):
        if near * level not in users:
            top = 1 << log2(level)
            users[near * level] = swap(users[near * (level - top)], near * top)
        for mask in far:
            users[mask + near * level] = swap(users[near * level], mask)

    def fetch(parts):
        return call(
            functools.partial(fetch_kernel, parts, near, n_batch),
            [((size, width), bf16)] * len(parts),
            asked,
            item_table,
            flops=2 * size * len(parts) * rows * width,
        )

    fetched = {}
    for parts in [[near - 1], list(range(1, near - 1)), [0]]:
        asked, *values = lax.optimization_barrier((asked, *fetch(parts)))
        for part, value in zip(parts, values):
            fetched[part] = swap(value, part) if part else value
    late = [mask for mask in users if mask not in early]
    fetched[0], *values = lax.optimization_barrier((fetched[0], *[users[mask] for mask in late]))
    users.update(zip(late, values))
    fetched = [fetched[part] for part in range(near)]

    for mask in list(users):
        users[mask + n_item] = swap(users[mask], n_item)

    place, low_hot, block = call(
        functools.partial(prepare_kernel, near, n_batch, n),
        [((total, 1), i32)] + [((BLOCK, total), bf16)] * 2,
        asked,
    )
    units, owns = zip(
        *[
            call(
                functools.partial(users_kernel, level, near),
                [((n_batch * n, width), bf16), ((total // levels, width), bf16)],
                place,
                *[users[near * level + batch * n_item] for batch in range(n_batch)],
                flops=1 << 29,
            )
            for level in range(levels)
        ]
    )
    dhidden = call(
        functools.partial(main_kernel, levels),
        [((size, width), bf16)] * near,
        tower_weight,
        *fetched,
        *units,
        *owns,
        flops=1 << 31,
        mib=40,
    )
    incoming = [dhidden[0]]

    def give_back(value):
        value, *given = lax.optimization_barrier((value, *dhidden[1:]))
        incoming.extend(swap(rows, part) for part, rows in enumerate(given, 1))
        return value

    terms = reduce_scatter([*fetched, *dhidden], width, give_back)
    table_grad = pl.pallas_call(
        table_kernel,
        out_specs=pl.BlockSpec(memory_space=pl.ANY),
        out_shape=jax.ShapeDtypeStruct((rows, width), bf16),
        scratch_shapes=[pltpu.VMEM((rows, width), bf16), pltpu.SemaphoreType.DMA((groups,))],
        compiler_params=params(16),
        cost_estimate=cost(2 * total * rows * width, 2 * rows * width),
    )(low_hot, block, tower_weight, *incoming)
    table_grad, *terms = lax.optimization_barrier((table_grad, *terms))
    (weight_grad,) = call(last_kernel, [((width // devices, width), f32)], *terms)
    return (table_grad, weight_grad)


def solution(mesh):
    return jax.shard_map(
        local,
        mesh=mesh,
        in_specs=(
            P(("batch", "item"), None),
            P(("batch", "item"), None),
            P(),
            P(("batch", "item"), None),
            P(("batch", "item")),
        ),
        out_specs=(P(("batch", "item"), None), P(("batch", "item"), None)),
        check_vma=False,
    )
```

```python
import functools

import jax
import jax.numpy as jnp
from jax import lax
from jax.experimental import pallas as pl
from jax.experimental.pallas import tpu as pltpu
from jax.sharding import PartitionSpec as P

epsilon = 1e-06
score_scale = 60.0
cauchy_scale = 4.0
f32 = jnp.float32
bf16 = jnp.bfloat16
i32 = jnp.int32
BLOCK = 256


def iota(shape, dim):
    return lax.broadcasted_iota(i32, shape, dim)


def hot(mask):
    return jnp.where(mask, 1.0, 0.0).astype(bf16)


def dot(a, b, a_dim=1, b_dim=0):
    return lax.dot_general(a, b, (((a_dim,), (b_dim,)), ((), ())), preferred_element_type=f32)


def halves(value):
    return (value >> 8).astype(f32), (value & 255).astype(f32)


def position():
    return lax.axis_index("batch") * lax.axis_size("item") + lax.axis_index("item")


def log2(value):
    return value.bit_length() - 1


def request_kernel(near, named_ref, request_ref):
    devices, lanes = request_ref.shape
    slots = lanes // (1 + near)
    n = named_ref.shape[1]
    owner, row = named_ref[0:1], named_ref[1:2]
    device = iota((devices, n), 0)
    named = owner == device
    count = dot(hot(named), hot(iota((n, n), 0) <= iota((n, n), 1)))
    rank = jnp.sum(jnp.where(named, count, 0.0), axis=0, keepdims=True).astype(i32) - 1
    in_slot = hot(rank == iota((slots, n), 0))
    which = iota((1, n), 1)
    for k, (value, mask) in enumerate([(row, 0)] + [(which, mask) for mask in range(near)]):
        high, low = halves(value + 1)
        here = (owner ^ mask) == device
        high = dot(jnp.where(here, high, 0.0).astype(bf16), in_slot, 1, 1)
        low = dot(jnp.where(here, low, 0.0).astype(bf16), in_slot, 1, 1)
        request_ref[:, k * slots : (k + 1) * slots] = (high * 256.0 + low).astype(i32) - 1


def asker_of(spot, part, near, n_batch, slots):
    batch = (spot >> log2(slots)) & (n_batch - 1)
    level = spot >> log2(slots * n_batch)
    return position() ^ (batch * lax.axis_size("item") + level * near + part)


def slot_column(asked, part, near, n_batch):
    devices, slots = asked.shape
    total = devices * slots // near
    asker = asker_of(iota((total, devices), 0), part, near, n_batch, slots)
    pick = hot(asker == iota((total, devices), 1))
    high, low = halves(asked)
    value = dot(pick, high.astype(bf16)) * 256.0 + dot(pick, low.astype(bf16))
    mine = (iota((total, slots), 0) & (slots - 1)) == iota((total, slots), 1)
    return jnp.sum(jnp.where(mine, value, 0.0), axis=1, keepdims=True)


def slot_line(asked, near, n_batch):
    devices, slots = asked.shape
    total = devices * slots
    pick = hot((iota((slots, total), 1) & (slots - 1)) == iota((slots, total), 0))
    high, low = halves(asked)
    value = dot(high.astype(bf16), pick) * 256.0 + dot(low.astype(bf16), pick)
    spot = iota((devices, total), 1)
    asker = asker_of(spot & (total // near - 1), spot >> log2(total // near), near, n_batch, slots)
    return jnp.sum(jnp.where(asker == iota((devices, total), 0), value, 0.0), axis=0, keepdims=True)


def parts_of(value):
    return value >> 8, value & 255


def fetch_kernel(parts, near, n_batch, asked_ref, table_ref, *found):
    slots = asked_ref.shape[1] // (1 + near)
    asked = asked_ref[:, :slots]
    column = jnp.concatenate([slot_column(asked, part, near, n_batch) for part in parts], axis=0)
    block, low = parts_of(column.astype(i32))
    total = block.shape[0]
    low_hot = hot(low == iota((total, BLOCK), 1))
    block = jnp.broadcast_to(block.astype(f32), (total, BLOCK)).astype(bf16)
    picks = [
        jnp.where(block == jnp.bfloat16(k), low_hot, jnp.bfloat16(0)) for k in range(table_ref.shape[0] // BLOCK)
    ]
    rows = dot(jnp.concatenate(picks, axis=1), table_ref[...]).astype(bf16)
    size = total // len(found)
    for k, ref in enumerate(found):
        ref[...] = rows[k * size : (k + 1) * size]


def prepare_kernel(near, n_batch, n, asked_ref, place_ref, low_hot_ref, block_ref):
    slots = asked_ref.shape[1] // (1 + near)
    size = place_ref.shape[0] // near
    batch = (iota((size, 1), 0) >> log2(slots)) & (n_batch - 1)
    for part in range(near):
        asked = asked_ref[:, (1 + part) * slots : (2 + part) * slots]
        which = slot_column(asked, 0, near, n_batch).astype(i32)
        place_ref[pl.ds(part * size, size)] = jnp.where(which < 0, -1, batch * n + which)
    block, low = parts_of(slot_line(asked_ref[:, :slots], near, n_batch).astype(i32))
    low_hot_ref[...] = hot(low == iota(low_hot_ref.shape, 0))
    block_ref[...] = jnp.broadcast_to(block.astype(f32), block_ref.shape).astype(bf16)


def users_kernel(level, near, place_ref, *refs):
    *users, unit_ref, own_ref = refs
    n, width = users[0].shape
    for k, ref in enumerate(users):
        value = ref[...].astype(f32)
        mean = jnp.mean(value * value, axis=1, keepdims=True)
        unit_ref[pl.ds(k * n, n)] = (value * lax.rsqrt(mean + epsilon) * (1.0 / width**0.5)).astype(bf16)
    step = place_ref.shape[0] // near
    size = own_ref.shape[0] // near
    place = jnp.concatenate([place_ref[pl.ds(k * step + level * size, size)] for k in range(near)], axis=0)
    own_ref[...] = dot(hot(place == iota((place.shape[0], unit_ref.shape[0]), 1)), unit_ref[...]).astype(bf16)


def main_kernel(levels, weight_ref, *refs):
    parts = (len(refs) - 2 * levels) // 2
    fetched, units, owns, outs = refs[:parts], refs[parts : parts + levels], refs[parts + levels : parts + 2 * levels], refs[-parts:]
    width = weight_ref.shape[0]
    size = outs[0].shape[0] // levels
    root = 1.0 / width**0.5
    for level in range(levels):
        here = pl.ds(level * size, size)
        embed = jnp.concatenate([ref[here] for ref in fetched], axis=0)
        hidden = dot(embed, weight_ref[...])
        rscale = lax.rsqrt(jnp.mean(hidden * hidden, axis=1, keepdims=True) + epsilon)
        item_vec = (hidden * (rscale * root)).astype(bf16)
        unit = units[level][...]
        expo = jnp.exp(dot(item_vec, unit, 1, 1) * score_scale)
        sums = jnp.sum(expo, axis=1, keepdims=True)
        mixed = dot(expo.astype(bf16), unit)
        own = owns[level][...].astype(f32)
        positive = jnp.sum(item_vec.astype(f32) * own, axis=1, keepdims=True) * score_scale
        xent = jnp.log(sums) - positive
        cweight = 1.0 / (1.0 + xent * (1.0 / cauchy_scale))
        dvec = (cweight * score_scale) * (mixed * (1.0 / sums) - own)
        inner = jnp.sum(hidden * dvec, axis=1, keepdims=True)
        dhidden = (rscale * root * (dvec - hidden * (rscale * rscale * inner * (1.0 / width)))).astype(bf16)
        for part, ref in enumerate(outs):
            ref[here] = dhidden[part * size : (part + 1) * size]


def coordinate(bits):
    return sum(((lax.axis_index(axis) >> level) & 1) << k for k, (axis, level) in enumerate(reversed(bits)))


def cut(blocks, bits, refs):
    size = refs[0].shape[0]
    for step, ref in enumerate(refs):
        ref[...] = blocks[pl.ds((coordinate(bits) ^ step) * size, size)].astype(ref.dtype)


def share_kernel(order, bits, count, *refs):
    values, (*refs, blocks) = refs[:count], refs[count:]
    embed, dhidden = (jnp.concatenate([ref[...] for ref in half], axis=0) for half in (values[: count // 2], values[count // 2 :]))
    share = dot(embed, dhidden, 0, 0)
    size = blocks.shape[1]
    for spot, block in enumerate(order):
        blocks[spot] = share[block * size : (block + 1) * size]
    cut(blocks, bits, refs)


def stage_kernel(bits, count, extra, *refs):
    came, extras, (keep_ref, *sends, blocks) = refs[:count], refs[count : count + extra], refs[count + extra :]
    shape = blocks.shape
    total = came[0][...]
    for ref in came[1:]:
        total += ref[...][: shape[0] * shape[1]].reshape(shape).astype(f32)
    blocks[...] = total
    if not extra:
        cut(blocks, bits, [keep_ref, *sends])
        return
    size = keep_ref.shape[0]
    cut(blocks, bits, [keep_ref])
    for step, (ref, rows) in enumerate(zip(sends, extras), 1):
        part = blocks[pl.ds((coordinate(bits) ^ step) * size, size)]
        ref[pl.ds(0, size * shape[1])] = part.reshape(size * shape[1], shape[2]).astype(ref.dtype)
        ref[pl.ds(size * shape[1], rows.shape[0])] = rows[...]


def last_kernel(*refs):
    *came, total_ref = refs
    total_ref[...] = sum(ref[...].astype(f32) for ref in came)[0]


def table_kernel(low_hot_ref, block_ref, weight_ref, *refs):
    *incoming, table_grad_hbm, ready, sems = refs
    size = incoming[0].shape[0]
    dhidden = jnp.concatenate([ref[pl.ds(ref.shape[0] - size, size)] for ref in incoming], axis=0)
    drow = dot(dhidden, weight_ref[...], 1, 1).astype(bf16)
    groups = sems.shape[0]
    size = ready.shape[0] // groups
    copies = []
    for g in range(groups):
        here = pl.ds(g * size, size)
        picks = [
            jnp.where(block_ref[...] == jnp.bfloat16(k), low_hot_ref[...], jnp.bfloat16(0))
            for k in range(g * size // BLOCK, (g + 1) * size // BLOCK)
        ]
        ready[here] = dot(jnp.concatenate(picks, axis=0), drow).astype(bf16)
        copy = pltpu.make_async_copy(ready.at[here], table_grad_hbm.at[here], sems.at[g])
        copy.start()
        copies.append(copy)
    for copy in copies:
        copy.wait()


def params(mib):
    return pltpu.CompilerParams(vmem_limit_bytes=mib * 1024 * 1024)


def cost(flops, bytes_accessed=1 << 20):
    return pl.CostEstimate(flops=flops, bytes_accessed=bytes_accessed, transcendentals=0)


def call(kernel, outs, *args, flops=0, scratch=(), mib=16, free=False):
    return pl.pallas_call(
        kernel,
        out_shape=[jax.ShapeDtypeStruct(shape, dtype) for shape, dtype in outs],
        scratch_shapes=scratch,
        compiler_params=params(mib),
        cost_estimate=cost(flops, 0 if free else 1 << 20),
    )(*args)


def swap(value, mask):
    devices = lax.axis_size("batch") * lax.axis_size("item")
    return lax.ppermute(value, ("batch", "item"), [(k, k ^ mask) for k in range(devices)])


def bits_of(axis):
    return [(axis, level) for level in range(log2(lax.axis_size(axis)))]


def mask_of(bits):
    return sum((lax.axis_size("item") if axis == "batch" else 1) << level for axis, level in bits)


def reduce_scatter(fetched, dhidden):
    width = dhidden[0].shape[1]
    n_item, devices = lax.axis_size("item"), lax.axis_size("batch") * lax.axis_size("item")
    part = width // devices
    close = log2(len(dhidden))
    batch_bits, item_bits = bits_of("batch"), bits_of("item")
    stages = [batch_bits[:1], item_bits[:close]]
    rest = batch_bits[1:] + item_bits[close:]
    stages += [rest[k : k + 2] for k in range(0, len(rest), 2)]
    bits = sum(stages, [])
    order = []
    for spot in range(devices):
        at = {"batch": 0, "item": 0}
        for k, (axis, level) in enumerate(bits):
            at[axis] |= (spot >> (len(bits) - 1 - k) & 1) << level
        order.append(at["batch"] * n_item + at["item"])
    left, values, back = devices, [*fetched, *dhidden], {}
    for k, stage in enumerate(stages):
        whole, left = left, left >> len(stage)
        masks = [
            mask_of([bit for j, bit in enumerate(reversed(stage)) if step >> j & 1]) for step in range(1, 1 << len(stage))
        ]
        extras = [dhidden[mask] for mask in masks] if k == 1 else []
        if k == 1:
            sent = ((left * part + dhidden[0].shape[0], width), bf16)
        else:
            sent = ((left, part, width), f32 if k == len(stages) - 1 else bf16)
        count = len(values)
        kernel = functools.partial(stage_kernel, stage, count, len(extras)) if k else functools.partial(share_kernel, order, stage, count)
        kept, *sends = call(
            kernel,
            [((left, part, width), f32)] + [sent] * len(masks),
            *values,
            *extras,
            scratch=[pltpu.VMEM((whole, part, width), f32)],
        )
        values = [kept] + [swap(value, mask) for mask, value in zip(masks, sends)]
        if k == 1:
            back = dict(zip(masks, values[1:]))
    return values, [back[mask] for mask in range(1, len(dhidden))]


def local(user_vectors, item_table, tower_weight, item_owner, item_row):
    n, width = user_vectors.shape
    rows = item_table.shape[0]
    n_batch, n_item = lax.axis_size("batch"), lax.axis_size("item")
    devices = n_batch * n_item
    near = min(4, n_item)
    levels = n_item // near
    slots = 2 * n // devices
    total = devices * slots
    size = total // near
    groups = rows // min(512, rows)

    far = [batch * n_item for batch in range(2, n_batch, 2)]
    users = {0: user_vectors}
    for mask in [near << k for k in range(log2(levels))] + far:
        users[mask] = swap(user_vectors, mask)

    (request,) = call(
        functools.partial(request_kernel, near),
        [((devices, (1 + near) * slots), i32)],
        jnp.stack([item_owner.reshape(n), item_row]),
        flops=1 << 34,
    )
    asked = lax.all_to_all(request, ("batch", "item"), split_axis=0, concat_axis=0, tiled=True)
    early = list(users)
    asked, *values = lax.optimization_barrier((asked, *users.values()))
    users = dict(zip(early, values))

    for level in range(1, levels):
        if near * level not in users:
            top = 1 << log2(level)
            users[near * level] = swap(users[near * (level - top)], near * top)
        for mask in far:
            users[mask + near * level] = swap(users[near * level], mask)

    def fetch(parts):
        return call(
            functools.partial(fetch_kernel, parts, near, n_batch),
            [((size, width), bf16)] * len(parts),
            asked,
            item_table,
            flops=2 * size * len(parts) * rows * width,
        )

    fetched = {}
    for parts in [[near - 1], list(range(1, near - 1)), [0]]:
        asked, *values = lax.optimization_barrier((asked, *fetch(parts)))
        for part, value in zip(parts, values):
            fetched[part] = swap(value, part) if part else value
    late = [mask for mask in users if mask not in early]
    fetched[0], fetched[near - 1], *values = lax.optimization_barrier(
        (fetched[0], fetched[near - 1], *[users[mask] for mask in late])
    )
    users.update(zip(late, values))
    fetched = [fetched[part] for part in range(near)]

    for mask in list(users):
        users[mask + n_item] = swap(users[mask], n_item)

    place, low_hot, block = call(
        functools.partial(prepare_kernel, near, n_batch, n),
        [((total, 1), i32)] + [((BLOCK, total), bf16)] * 2,
        asked,
        free=True,
    )
    units, owns = zip(
        *[
            call(
                functools.partial(users_kernel, level, near),
                [((n_batch * n, width), bf16), ((total // levels, width), bf16)],
                place,
                *[users[near * level + batch * n_item] for batch in range(n_batch)],
                free=True,
            )
            for level in range(levels)
        ]
    )
    dhidden = call(
        functools.partial(main_kernel, levels),
        [((size, width), bf16)] * near,
        tower_weight,
        *fetched,
        *units,
        *owns,
        flops=1 << 31,
        mib=40,
    )
    terms, incoming = reduce_scatter(fetched, dhidden)
    table_grad = pl.pallas_call(
        table_kernel,
        out_specs=pl.BlockSpec(memory_space=pl.ANY),
        out_shape=jax.ShapeDtypeStruct((rows, width), bf16),
        scratch_shapes=[pltpu.VMEM((rows, width), bf16), pltpu.SemaphoreType.DMA((groups,))],
        compiler_params=params(16),
        cost_estimate=cost(2 * total * rows * width, 2 * rows * width),
    )(low_hot, block, tower_weight, dhidden[0], *incoming)
    table_grad, *terms = lax.optimization_barrier((table_grad, *terms))
    (weight_grad,) = call(last_kernel, [((width // devices, width), f32)], *terms)
    return (table_grad, weight_grad)


def solution(mesh):
    return jax.shard_map(
        local,
        mesh=mesh,
        in_specs=(
            P(("batch", "item"), None),
            P(("batch", "item"), None),
            P(),
            P(("batch", "item"), None),
            P(("batch", "item")),
        ),
        out_specs=(P(("batch", "item"), None), P(("batch", "item"), None)),
        check_vma=False,
    )
```

```python
import functools

import jax
import jax.numpy as jnp
from jax import lax
from jax.experimental import pallas as pl
from jax.experimental.pallas import tpu as pltpu
from jax.sharding import PartitionSpec as P

epsilon = 1e-06
score_scale = 60.0
cauchy_scale = 4.0
f32 = jnp.float32
bf16 = jnp.bfloat16
i32 = jnp.int32
BLOCK = 256


def iota(shape, dim):
    return lax.broadcasted_iota(i32, shape, dim)


def hot(mask):
    return jnp.where(mask, 1.0, 0.0).astype(bf16)


def dot(a, b, a_dim=1, b_dim=0):
    return lax.dot_general(a, b, (((a_dim,), (b_dim,)), ((), ())), preferred_element_type=f32)


def halves(value):
    return (value >> 8).astype(f32), (value & 255).astype(f32)


def position():
    return lax.axis_index("batch") * lax.axis_size("item") + lax.axis_index("item")


def log2(value):
    return value.bit_length() - 1


def request_kernel(near, named_ref, request_ref):
    devices, lanes = request_ref.shape
    slots = lanes // (1 + near)
    n = named_ref.shape[1]
    owner, row = named_ref[0:1], named_ref[1:2]
    device = iota((devices, n), 0)
    named = owner == device
    count = dot(hot(named), hot(iota((n, n), 0) <= iota((n, n), 1)))
    rank = jnp.sum(jnp.where(named, count, 0.0), axis=0, keepdims=True).astype(i32) - 1
    in_slot = hot(rank == iota((slots, n), 0))
    which = iota((1, n), 1)
    for k, (value, mask) in enumerate([(row, 0)] + [(which, mask) for mask in range(near)]):
        high, low = halves(value + 1)
        here = (owner ^ mask) == device
        high = dot(jnp.where(here, high, 0.0).astype(bf16), in_slot, 1, 1)
        low = dot(jnp.where(here, low, 0.0).astype(bf16), in_slot, 1, 1)
        request_ref[:, k * slots : (k + 1) * slots] = (high * 256.0 + low).astype(i32) - 1


def asker_of(spot, part, near, n_batch, slots):
    batch = (spot >> log2(slots)) & (n_batch - 1)
    level = spot >> log2(slots * n_batch)
    return position() ^ (batch * lax.axis_size("item") + level * near + part)


def slot_column(asked, part, near, n_batch):
    devices, slots = asked.shape
    total = devices * slots // near
    asker = asker_of(iota((total, devices), 0), part, near, n_batch, slots)
    pick = hot(asker == iota((total, devices), 1))
    high, low = halves(asked)
    value = dot(pick, high.astype(bf16)) * 256.0 + dot(pick, low.astype(bf16))
    mine = (iota((total, slots), 0) & (slots - 1)) == iota((total, slots), 1)
    return jnp.sum(jnp.where(mine, value, 0.0), axis=1, keepdims=True)


def slot_line(asked, near, n_batch):
    devices, slots = asked.shape
    total = devices * slots
    pick = hot((iota((slots, total), 1) & (slots - 1)) == iota((slots, total), 0))
    high, low = halves(asked)
    value = dot(high.astype(bf16), pick) * 256.0 + dot(low.astype(bf16), pick)
    spot = iota((devices, total), 1)
    asker = asker_of(spot & (total // near - 1), spot >> log2(total // near), near, n_batch, slots)
    return jnp.sum(jnp.where(asker == iota((devices, total), 0), value, 0.0), axis=0, keepdims=True)


def parts_of(value):
    return value >> 8, value & 255


def fetch_kernel(parts, near, n_batch, asked_ref, table_ref, *found):
    slots = asked_ref.shape[1] // (1 + near)
    asked = asked_ref[:, :slots]
    column = jnp.concatenate([slot_column(asked, part, near, n_batch) for part in parts], axis=0)
    block, low = parts_of(column.astype(i32))
    total = block.shape[0]
    low_hot = hot(low == iota((total, BLOCK), 1))
    block = jnp.broadcast_to(block.astype(f32), (total, BLOCK)).astype(bf16)
    picks = [
        jnp.where(block == jnp.bfloat16(k), low_hot, jnp.bfloat16(0)) for k in range(table_ref.shape[0] // BLOCK)
    ]
    rows = dot(jnp.concatenate(picks, axis=1), table_ref[...]).astype(bf16)
    size = total // len(found)
    for k, ref in enumerate(found):
        ref[...] = rows[k * size : (k + 1) * size]


def prepare_kernel(near, n_batch, n, asked_ref, place_ref, low_hot_ref, block_ref):
    slots = asked_ref.shape[1] // (1 + near)
    size = place_ref.shape[0] // near
    batch = (iota((size, 1), 0) >> log2(slots)) & (n_batch - 1)
    for part in range(near):
        asked = asked_ref[:, (1 + part) * slots : (2 + part) * slots]
        which = slot_column(asked, 0, near, n_batch).astype(i32)
        place_ref[pl.ds(part * size, size)] = jnp.where(which < 0, -1, batch * n + which)
    block, low = parts_of(slot_line(asked_ref[:, :slots], near, n_batch).astype(i32))
    low_hot_ref[...] = hot(low == iota(low_hot_ref.shape, 0))
    block_ref[...] = jnp.broadcast_to(block.astype(f32), block_ref.shape).astype(bf16)


def users_kernel(level, near, place_ref, *refs):
    *users, unit_ref, own_ref = refs
    n, width = users[0].shape
    for k, ref in enumerate(users):
        value = ref[...].astype(f32)
        mean = jnp.mean(value * value, axis=1, keepdims=True)
        unit_ref[pl.ds(k * n, n)] = (value * lax.rsqrt(mean + epsilon) * (1.0 / width**0.5)).astype(bf16)
    step = place_ref.shape[0] // near
    size = own_ref.shape[0] // near
    place = jnp.concatenate([place_ref[pl.ds(k * step + level * size, size)] for k in range(near)], axis=0)
    own_ref[...] = dot(hot(place == iota((place.shape[0], unit_ref.shape[0]), 1)), unit_ref[...]).astype(bf16)


def main_kernel(levels, weight_ref, *refs):
    parts = (len(refs) - 2 * levels) // 2
    fetched, units, owns, outs = refs[:parts], refs[parts : parts + levels], refs[parts + levels : parts + 2 * levels], refs[-parts:]
    width = weight_ref.shape[0]
    size = outs[0].shape[0] // levels
    root = 1.0 / width**0.5
    for level in range(levels):
        here = pl.ds(level * size, size)
        embed = jnp.concatenate([ref[here] for ref in fetched], axis=0)
        hidden = dot(embed, weight_ref[...])
        rscale = lax.rsqrt(jnp.mean(hidden * hidden, axis=1, keepdims=True) + epsilon)
        item_vec = (hidden * (rscale * root)).astype(bf16)
        unit = units[level][...]
        expo = jnp.exp(dot(item_vec, unit, 1, 1) * score_scale)
        sums = jnp.sum(expo, axis=1, keepdims=True)
        mixed = dot(expo.astype(bf16), unit)
        own = owns[level][...].astype(f32)
        positive = jnp.sum(item_vec.astype(f32) * own, axis=1, keepdims=True) * score_scale
        xent = jnp.log(sums) - positive
        cweight = 1.0 / (1.0 + xent * (1.0 / cauchy_scale))
        dvec = (cweight * score_scale) * (mixed * (1.0 / sums) - own)
        inner = jnp.sum(hidden * dvec, axis=1, keepdims=True)
        dhidden = (rscale * root * (dvec - hidden * (rscale * rscale * inner * (1.0 / width)))).astype(bf16)
        for part, ref in enumerate(outs):
            ref[here] = dhidden[part * size : (part + 1) * size]


def coordinate(bits):
    return sum(((lax.axis_index(axis) >> level) & 1) << k for k, (axis, level) in enumerate(reversed(bits)))


def cut(blocks, bits, refs):
    size = refs[0].shape[0]
    for step, ref in enumerate(refs):
        ref[...] = blocks[pl.ds((coordinate(bits) ^ step) * size, size)].astype(ref.dtype)


def share_kernel(order, bits, count, *refs):
    values, (*refs, blocks) = refs[:count], refs[count:]
    embed, dhidden = (jnp.concatenate([ref[...] for ref in half], axis=0) for half in (values[: count // 2], values[count // 2 :]))
    share = dot(embed, dhidden, 0, 0)
    size = blocks.shape[1]
    for spot, block in enumerate(order):
        blocks[spot] = share[block * size : (block + 1) * size]
    cut(blocks, bits, refs)


def stage_kernel(bits, count, *refs):
    came, (*refs, blocks) = refs[:count], refs[count:]
    blocks[...] = sum(ref[...].astype(f32) for ref in came)
    cut(blocks, bits, refs)


def last_kernel(*refs):
    *came, total_ref = refs
    total_ref[...] = sum(ref[...].astype(f32) for ref in came)[0]


def table_kernel(low_hot_ref, block_ref, weight_ref, *refs):
    *incoming, table_grad_hbm, ready, sems = refs
    dhidden = jnp.concatenate([ref[...] for ref in incoming], axis=0)
    drow = dot(dhidden, weight_ref[...], 1, 1).astype(bf16)
    groups = sems.shape[0]
    size = ready.shape[0] // groups
    copies = []
    for g in range(groups):
        here = pl.ds(g * size, size)
        picks = [
            jnp.where(block_ref[...] == jnp.bfloat16(k), low_hot_ref[...], jnp.bfloat16(0))
            for k in range(g * size // BLOCK, (g + 1) * size // BLOCK)
        ]
        ready[here] = dot(jnp.concatenate(picks, axis=0), drow).astype(bf16)
        copy = pltpu.make_async_copy(ready.at[here], table_grad_hbm.at[here], sems.at[g])
        copy.start()
        copies.append(copy)
    for copy in copies:
        copy.wait()


def params(mib):
    return pltpu.CompilerParams(vmem_limit_bytes=mib * 1024 * 1024)


def cost(flops, bytes_accessed=1 << 20):
    return pl.CostEstimate(flops=flops, bytes_accessed=bytes_accessed, transcendentals=0)


def call(kernel, outs, *args, flops=0, scratch=(), mib=16, free=False):
    return pl.pallas_call(
        kernel,
        out_shape=[jax.ShapeDtypeStruct(shape, dtype) for shape, dtype in outs],
        scratch_shapes=scratch,
        compiler_params=params(mib),
        cost_estimate=cost(flops, 0 if free else 1 << 20),
    )(*args)


def swap(value, mask):
    devices = lax.axis_size("batch") * lax.axis_size("item")
    return lax.ppermute(value, ("batch", "item"), [(k, k ^ mask) for k in range(devices)])


def bits_of(axis):
    return [(axis, level) for level in range(log2(lax.axis_size(axis)))]


def mask_of(bits):
    return sum((lax.axis_size("item") if axis == "batch" else 1) << level for axis, level in bits)


def reduce_scatter(fetched, dhidden, incoming):
    width = dhidden[0].shape[1]
    n_item, devices = lax.axis_size("item"), lax.axis_size("batch") * lax.axis_size("item")
    part = width // devices
    close = log2(len(dhidden))
    batch_bits, item_bits = bits_of("batch"), bits_of("item")
    rest = batch_bits[1:] + item_bits[close:]
    stages = [batch_bits[:1]] + [rest[k : k + 2] for k in range(0, len(rest), 2)] + [item_bits[:close]]
    bits = sum(stages, [])
    order = []
    for spot in range(devices):
        at = {"batch": 0, "item": 0}
        for k, (axis, level) in enumerate(bits):
            at[axis] |= (spot >> (len(bits) - 1 - k) & 1) << level
        order.append(at["batch"] * n_item + at["item"])
    left, values = devices, [*fetched, *dhidden]
    for k, stage in enumerate(stages):
        whole, left = left, left >> len(stage)
        masks = [
            mask_of([bit for j, bit in enumerate(reversed(stage)) if step >> j & 1]) for step in range(1, 1 << len(stage))
        ]
        sent = f32 if k == len(stages) - 1 else bf16
        count = len(values)
        kernel = functools.partial(stage_kernel, stage, count) if k else functools.partial(share_kernel, order, stage, count)
        kept, *sends = call(
            kernel,
            [((left, part, width), f32)] + [((left, part, width), sent)] * len(masks),
            *values,
            scratch=[pltpu.VMEM((whole, part, width), f32)],
            free=True,
        )
        values = [kept] + [swap(value, mask) for mask, value in zip(masks, sends)]
        if k == 1:
            values, incoming = lax.optimization_barrier((values, incoming))
    return values, incoming


def local(user_vectors, item_table, tower_weight, item_owner, item_row):
    n, width = user_vectors.shape
    rows = item_table.shape[0]
    n_batch, n_item = lax.axis_size("batch"), lax.axis_size("item")
    devices = n_batch * n_item
    near = min(4, n_item)
    levels = n_item // near
    slots = 2 * n // devices
    total = devices * slots
    size = total // near
    groups = rows // min(512, rows)

    far = [batch * n_item for batch in range(2, n_batch, 2)]
    users = {0: user_vectors}
    for mask in [near << k for k in range(log2(levels))] + far:
        users[mask] = swap(user_vectors, mask)

    (request,) = call(
        functools.partial(request_kernel, near),
        [((devices, (1 + near) * slots), i32)],
        jnp.stack([item_owner.reshape(n), item_row]),
        flops=1 << 34,
    )
    asked = lax.all_to_all(request, ("batch", "item"), split_axis=0, concat_axis=0, tiled=True)
    early = list(users)
    asked, *values = lax.optimization_barrier((asked, *users.values()))
    users = dict(zip(early, values))

    for level in range(1, levels):
        if near * level not in users:
            top = 1 << log2(level)
            users[near * level] = swap(users[near * (level - top)], near * top)
        for mask in far:
            users[mask + near * level] = swap(users[near * level], mask)

    def fetch(parts):
        return call(
            functools.partial(fetch_kernel, parts, near, n_batch),
            [((size, width), bf16)] * len(parts),
            asked,
            item_table,
            flops=2 * size * len(parts) * rows * width,
        )

    fetched = {}
    for parts in [[near - 1], list(range(1, near - 1)), [0]]:
        asked, *values = lax.optimization_barrier((asked, *fetch(parts)))
        for part, value in zip(parts, values):
            fetched[part] = swap(value, part) if part else value
    late = [mask for mask in users if mask not in early]
    values = [fetched[part] for part in range(near)] + [users[mask] for mask in late]
    values = lax.optimization_barrier(tuple(values))
    fetched, users = list(values[:near]), users | dict(zip(late, values[near:]))

    for mask in list(users):
        users[mask + n_item] = swap(users[mask], n_item)

    place, low_hot, block = call(
        functools.partial(prepare_kernel, near, n_batch, n),
        [((total, 1), i32)] + [((BLOCK, total), bf16)] * 2,
        asked,
        free=True,
    )
    units, owns = zip(
        *[
            call(
                functools.partial(users_kernel, level, near),
                [((n_batch * n, width), bf16), ((total // levels, width), bf16)],
                place,
                *[users[near * level + batch * n_item] for batch in range(n_batch)],
                free=True,
            )
            for level in range(levels)
        ]
    )
    dhidden = call(
        functools.partial(main_kernel, levels),
        [((size, width), bf16)] * near,
        tower_weight,
        *fetched,
        *units,
        *owns,
        flops=1 << 31,
        mib=40,
    )
    incoming = [swap(dhidden[part], part) for part in range(1, near)]
    terms, incoming = reduce_scatter(fetched, dhidden, incoming)
    table_grad = pl.pallas_call(
        table_kernel,
        out_specs=pl.BlockSpec(memory_space=pl.ANY),
        out_shape=jax.ShapeDtypeStruct((rows, width), bf16),
        scratch_shapes=[pltpu.VMEM((rows, width), bf16), pltpu.SemaphoreType.DMA((groups,))],
        compiler_params=params(16),
        cost_estimate=cost(2 * total * rows * width, 2 * rows * width),
    )(low_hot, block, tower_weight, dhidden[0], *incoming)
    table_grad, *terms = lax.optimization_barrier((table_grad, *terms))
    (weight_grad,) = call(last_kernel, [((width // devices, width), f32)], *terms)
    return (table_grad, weight_grad)


def solution(mesh):
    return jax.shard_map(
        local,
        mesh=mesh,
        in_specs=(
            P(("batch", "item"), None),
            P(("batch", "item"), None),
            P(),
            P(("batch", "item"), None),
            P(("batch", "item")),
        ),
        out_specs=(P(("batch", "item"), None), P(("batch", "item"), None)),
        check_vma=False,
    )
```

```python
import functools

import jax
import jax.numpy as jnp
from jax import lax
from jax.experimental import pallas as pl
from jax.experimental.pallas import tpu as pltpu
from jax.sharding import PartitionSpec as P

epsilon = 1e-06
score_scale = 60.0
cauchy_scale = 4.0
f32 = jnp.float32
bf16 = jnp.bfloat16
i32 = jnp.int32
BLOCK = 256


def iota(shape, dim):
    return lax.broadcasted_iota(i32, shape, dim)


def hot(mask):
    return jnp.where(mask, 1.0, 0.0).astype(bf16)


def dot(a, b, a_dim=1, b_dim=0):
    return lax.dot_general(a, b, (((a_dim,), (b_dim,)), ((), ())), preferred_element_type=f32)


def halves(value):
    return (value >> 8).astype(f32), (value & 255).astype(f32)


def position():
    return lax.axis_index("batch") * lax.axis_size("item") + lax.axis_index("item")


def log2(value):
    return value.bit_length() - 1


def request_kernel(near, named_ref, request_ref):
    devices, lanes = request_ref.shape
    slots = lanes // (1 + near)
    n = named_ref.shape[1]
    owner, row = named_ref[0:1], named_ref[1:2]
    device = iota((devices, n), 0)
    named = owner == device
    count = dot(hot(named), hot(iota((n, n), 0) <= iota((n, n), 1)))
    rank = jnp.sum(jnp.where(named, count, 0.0), axis=0, keepdims=True).astype(i32) - 1
    in_slot = hot(rank == iota((slots, n), 0))
    which = iota((1, n), 1)
    for k, (value, mask) in enumerate([(row, 0)] + [(which, mask) for mask in range(near)]):
        high, low = halves(value + 1)
        here = (owner ^ mask) == device
        high = dot(jnp.where(here, high, 0.0).astype(bf16), in_slot, 1, 1)
        low = dot(jnp.where(here, low, 0.0).astype(bf16), in_slot, 1, 1)
        request_ref[:, k * slots : (k + 1) * slots] = (high * 256.0 + low).astype(i32) - 1


def asker_of(spot, part, near, n_batch, slots):
    batch = (spot >> log2(slots)) & (n_batch - 1)
    level = spot >> log2(slots * n_batch)
    return position() ^ (batch * lax.axis_size("item") + level * near + part)


def slot_column(asked, part, near, n_batch):
    devices, slots = asked.shape
    total = devices * slots // near
    asker = asker_of(iota((total, devices), 0), part, near, n_batch, slots)
    pick = hot(asker == iota((total, devices), 1))
    high, low = halves(asked)
    value = dot(pick, high.astype(bf16)) * 256.0 + dot(pick, low.astype(bf16))
    mine = (iota((total, slots), 0) & (slots - 1)) == iota((total, slots), 1)
    return jnp.sum(jnp.where(mine, value, 0.0), axis=1, keepdims=True)


def slot_line(asked, near, n_batch):
    devices, slots = asked.shape
    total = devices * slots
    pick = hot((iota((slots, total), 1) & (slots - 1)) == iota((slots, total), 0))
    high, low = halves(asked)
    value = dot(high.astype(bf16), pick) * 256.0 + dot(low.astype(bf16), pick)
    spot = iota((devices, total), 1)
    asker = asker_of(spot & (total // near - 1), spot >> log2(total // near), near, n_batch, slots)
    return jnp.sum(jnp.where(asker == iota((devices, total), 0), value, 0.0), axis=0, keepdims=True)


def parts_of(value):
    return value >> 8, value & 255


def fetch_kernel(parts, near, n_batch, asked_ref, table_ref, *found):
    slots = asked_ref.shape[1] // (1 + near)
    asked = asked_ref[:, :slots]
    column = jnp.concatenate([slot_column(asked, part, near, n_batch) for part in parts], axis=0)
    block, low = parts_of(column.astype(i32))
    total = block.shape[0]
    low_hot = hot(low == iota((total, BLOCK), 1))
    block = jnp.broadcast_to(block.astype(f32), (total, BLOCK)).astype(bf16)
    picks = [
        jnp.where(block == jnp.bfloat16(k), low_hot, jnp.bfloat16(0)) for k in range(table_ref.shape[0] // BLOCK)
    ]
    rows = dot(jnp.concatenate(picks, axis=1), table_ref[...]).astype(bf16)
    size = total // len(found)
    for k, ref in enumerate(found):
        ref[...] = rows[k * size : (k + 1) * size]


def prepare_kernel(near, n_batch, n, asked_ref, place_ref, low_hot_ref, block_ref):
    slots = asked_ref.shape[1] // (1 + near)
    size = place_ref.shape[0] // near
    batch = (iota((size, 1), 0) >> log2(slots)) & (n_batch - 1)
    for part in range(near):
        asked = asked_ref[:, (1 + part) * slots : (2 + part) * slots]
        which = slot_column(asked, 0, near, n_batch).astype(i32)
        place_ref[pl.ds(part * size, size)] = jnp.where(which < 0, -1, batch * n + which)
    block, low = parts_of(slot_line(asked_ref[:, :slots], near, n_batch).astype(i32))
    low_hot_ref[...] = hot(low == iota(low_hot_ref.shape, 0))
    block_ref[...] = jnp.broadcast_to(block.astype(f32), block_ref.shape).astype(bf16)


def users_kernel(level, near, place_ref, *refs):
    *users, unit_ref, own_ref = refs
    n, width = users[0].shape
    for k, ref in enumerate(users):
        value = ref[...].astype(f32)
        mean = jnp.mean(value * value, axis=1, keepdims=True)
        unit_ref[pl.ds(k * n, n)] = (value * lax.rsqrt(mean + epsilon) * (1.0 / width**0.5)).astype(bf16)
    step = place_ref.shape[0] // near
    size = own_ref.shape[0] // near
    place = jnp.concatenate([place_ref[pl.ds(k * step + level * size, size)] for k in range(near)], axis=0)
    own_ref[...] = dot(hot(place == iota((place.shape[0], unit_ref.shape[0]), 1)), unit_ref[...]).astype(bf16)


def hidden_kernel(levels, weight_ref, *refs):
    *fetched, hidden_ref, rscale_ref, item_ref = refs
    width = weight_ref.shape[0]
    size = fetched[0].shape[0] // levels
    for level in range(levels):
        embed = jnp.concatenate([ref[pl.ds(level * size, size)] for ref in fetched], axis=0)
        here = pl.ds(level * embed.shape[0], embed.shape[0])
        hidden = dot(embed, weight_ref[...])
        rscale = lax.rsqrt(jnp.mean(hidden * hidden, axis=1, keepdims=True) + epsilon)
        hidden_ref[here] = hidden
        rscale_ref[here] = rscale
        item_ref[here] = (hidden * (rscale * (1.0 / width**0.5))).astype(bf16)


def main_kernel(levels, hidden_ref, rscale_ref, item_ref, *refs):
    units, owns, outs = refs[:levels], refs[levels : 2 * levels], refs[2 * levels :]
    total, width = hidden_ref.shape
    size = outs[0].shape[0] // levels
    root = 1.0 / width**0.5
    for level in range(levels):
        here = pl.ds(level * (total // levels), total // levels)
        hidden, rscale, item_vec = hidden_ref[here], rscale_ref[here], item_ref[here]
        unit = units[level][...]
        expo = jnp.exp(dot(item_vec, unit, 1, 1) * score_scale)
        sums = jnp.sum(expo, axis=1, keepdims=True)
        mixed = dot(expo.astype(bf16), unit)
        own = owns[level][...].astype(f32)
        positive = jnp.sum(item_vec.astype(f32) * own, axis=1, keepdims=True) * score_scale
        xent = jnp.log(sums) - positive
        cweight = 1.0 / (1.0 + xent * (1.0 / cauchy_scale))
        dvec = (cweight * score_scale) * (mixed * (1.0 / sums) - own)
        inner = jnp.sum(hidden * dvec, axis=1, keepdims=True)
        dhidden = (rscale * root * (dvec - hidden * (rscale * rscale * inner * (1.0 / width)))).astype(bf16)
        for part, ref in enumerate(outs):
            ref[pl.ds(level * size, size)] = dhidden[part * size : (part + 1) * size]


def coordinate(bits):
    return sum(((lax.axis_index(axis) >> level) & 1) << k for k, (axis, level) in enumerate(reversed(bits)))


def cut(blocks, bits, refs):
    size = refs[0].shape[0]
    for step, ref in enumerate(refs):
        ref[...] = blocks[pl.ds((coordinate(bits) ^ step) * size, size)].astype(ref.dtype)


def share_kernel(order, bits, count, *refs):
    values, (*refs, blocks) = refs[:count], refs[count:]
    embed, dhidden = (jnp.concatenate([ref[...] for ref in half], axis=0) for half in (values[: count // 2], values[count // 2 :]))
    share = dot(embed, dhidden, 0, 0)
    size = blocks.shape[1]
    for spot, block in enumerate(order):
        blocks[spot] = share[block * size : (block + 1) * size]
    cut(blocks, bits, refs)


def stage_kernel(bits, count, *refs):
    came, (*refs, blocks) = refs[:count], refs[count:]
    blocks[...] = sum(ref[...].astype(f32) for ref in came)
    cut(blocks, bits, refs)


def last_kernel(*refs):
    *came, total_ref = refs
    total_ref[...] = sum(ref[...].astype(f32) for ref in came)[0]


def table_kernel(low_hot_ref, block_ref, weight_ref, *refs):
    *incoming, table_grad_hbm, ready, sems = refs
    dhidden = jnp.concatenate([ref[...] for ref in incoming], axis=0)
    drow = dot(dhidden, weight_ref[...], 1, 1).astype(bf16)
    groups = sems.shape[0]
    size = ready.shape[0] // groups
    copies = []
    for g in range(groups):
        here = pl.ds(g * size, size)
        picks = [
            jnp.where(block_ref[...] == jnp.bfloat16(k), low_hot_ref[...], jnp.bfloat16(0))
            for k in range(g * size // BLOCK, (g + 1) * size // BLOCK)
        ]
        ready[here] = dot(jnp.concatenate(picks, axis=0), drow).astype(bf16)
        copy = pltpu.make_async_copy(ready.at[here], table_grad_hbm.at[here], sems.at[g])
        copy.start()
        copies.append(copy)
    for copy in copies:
        copy.wait()


def params(mib):
    return pltpu.CompilerParams(vmem_limit_bytes=mib * 1024 * 1024)


def cost(flops, bytes_accessed=1 << 20):
    return pl.CostEstimate(flops=flops, bytes_accessed=bytes_accessed, transcendentals=0)


def call(kernel, outs, *args, flops=0, scratch=(), mib=16, free=False):
    return pl.pallas_call(
        kernel,
        out_shape=[jax.ShapeDtypeStruct(shape, dtype) for shape, dtype in outs],
        scratch_shapes=scratch,
        compiler_params=params(mib),
        cost_estimate=cost(flops, 0 if free else 1 << 20),
    )(*args)


def swap(value, mask):
    devices = lax.axis_size("batch") * lax.axis_size("item")
    return lax.ppermute(value, ("batch", "item"), [(k, k ^ mask) for k in range(devices)])


def bits_of(axis):
    return [(axis, level) for level in range(log2(lax.axis_size(axis)))]


def mask_of(bits):
    return sum((lax.axis_size("item") if axis == "batch" else 1) << level for axis, level in bits)


def reduce_scatter(fetched, dhidden, incoming):
    width = dhidden[0].shape[1]
    n_item, devices = lax.axis_size("item"), lax.axis_size("batch") * lax.axis_size("item")
    part = width // devices
    bits = bits_of("batch") + bits_of("item")
    odd = len(bits) % 2
    stages = [bits[:1]] * odd + [bits[k : k + 2] for k in range(odd, len(bits), 2)]
    order = []
    for spot in range(devices):
        at = {"batch": 0, "item": 0}
        for k, (axis, level) in enumerate(bits):
            at[axis] |= (spot >> (len(bits) - 1 - k) & 1) << level
        order.append(at["batch"] * n_item + at["item"])
    left, values = devices, [*fetched, *dhidden]
    for k, stage in enumerate(stages):
        whole, left = left, left >> len(stage)
        masks = [
            mask_of([bit for j, bit in enumerate(reversed(stage)) if step >> j & 1]) for step in range(1, 1 << len(stage))
        ]
        sent = f32 if k == len(stages) - 1 else bf16
        count = len(values)
        kernel = functools.partial(stage_kernel, stage, count) if k else functools.partial(share_kernel, order, stage, count)
        kept, *sends = call(
            kernel,
            [((left, part, width), f32)] + [((left, part, width), sent)] * len(masks),
            *values,
            scratch=[pltpu.VMEM((whole, part, width), f32)],
            free=True,
        )
        values = [kept] + [swap(value, mask) for mask, value in zip(masks, sends)]
        if k == 1:
            values, incoming = lax.optimization_barrier((values, incoming))
    return values, incoming


def local(user_vectors, item_table, tower_weight, item_owner, item_row):
    n, width = user_vectors.shape
    rows = item_table.shape[0]
    n_batch, n_item = lax.axis_size("batch"), lax.axis_size("item")
    devices = n_batch * n_item
    near = min(4, n_item)
    levels = n_item // near
    slots = 2 * n // devices
    total = devices * slots
    size = total // near
    groups = rows // min(512, rows)

    far = [batch * n_item for batch in range(2, n_batch, 2)]
    users = {0: user_vectors}
    for mask in [near << k for k in range(log2(levels))] + far:
        users[mask] = swap(user_vectors, mask)

    (request,) = call(
        functools.partial(request_kernel, near),
        [((devices, (1 + near) * slots), i32)],
        jnp.stack([item_owner.reshape(n), item_row]),
        flops=1 << 34,
    )
    asked = lax.all_to_all(request, ("batch", "item"), split_axis=0, concat_axis=0, tiled=True)
    early = list(users)
    asked, *values = lax.optimization_barrier((asked, *users.values()))
    users = dict(zip(early, values))

    for level in range(1, levels):
        if near * level not in users:
            top = 1 << log2(level)
            users[near * level] = swap(users[near * (level - top)], near * top)
        for mask in far:
            users[mask + near * level] = swap(users[near * level], mask)

    def fetch(parts):
        return call(
            functools.partial(fetch_kernel, parts, near, n_batch),
            [((size, width), bf16)] * len(parts),
            asked,
            item_table,
            flops=2 * size * len(parts) * rows * width,
        )

    fetched = {}
    for parts in [[near - 1], list(range(1, near - 1)), [0]]:
        asked, *values = lax.optimization_barrier((asked, *fetch(parts)))
        for part, value in zip(parts, values):
            fetched[part] = swap(value, part) if part else value
    late = [mask for mask in users if mask not in early]
    fetched[0], *values = lax.optimization_barrier((fetched[0], *[users[mask] for mask in late]))
    users.update(zip(late, values))
    fetched = [fetched[part] for part in range(near)]

    for mask in list(users):
        users[mask + n_item] = swap(users[mask], n_item)

    place, low_hot, block = call(
        functools.partial(prepare_kernel, near, n_batch, n),
        [((total, 1), i32)] + [((BLOCK, total), bf16)] * 2,
        asked,
        free=True,
    )
    units, owns = zip(
        *[
            call(
                functools.partial(users_kernel, level, near),
                [((n_batch * n, width), bf16), ((total // levels, width), bf16)],
                place,
                *[users[near * level + batch * n_item] for batch in range(n_batch)],
                free=True,
            )
            for level in range(levels)
        ]
    )
    hidden = call(
        functools.partial(hidden_kernel, levels),
        [((total, width), f32), ((total, 1), f32), ((total, width), bf16)],
        tower_weight,
        *fetched,
        flops=1 << 32,
    )
    dhidden = call(
        functools.partial(main_kernel, levels),
        [((size, width), bf16)] * near,
        *hidden,
        *units,
        *owns,
        flops=1 << 31,
        mib=40,
    )
    incoming = [swap(dhidden[part], part) for part in range(1, near)]
    terms, incoming = reduce_scatter(fetched, dhidden, incoming)
    table_grad = pl.pallas_call(
        table_kernel,
        out_specs=pl.BlockSpec(memory_space=pl.ANY),
        out_shape=jax.ShapeDtypeStruct((rows, width), bf16),
        scratch_shapes=[pltpu.VMEM((rows, width), bf16), pltpu.SemaphoreType.DMA((groups,))],
        compiler_params=params(16),
        cost_estimate=cost(2 * total * rows * width, 2 * rows * width),
    )(low_hot, block, tower_weight, dhidden[0], *incoming)
    table_grad, *terms = lax.optimization_barrier((table_grad, *terms))
    (weight_grad,) = call(last_kernel, [((width // devices, width), f32)], *terms)
    return (table_grad, weight_grad)


def solution(mesh):
    return jax.shard_map(
        local,
        mesh=mesh,
        in_specs=(
            P(("batch", "item"), None),
            P(("batch", "item"), None),
            P(),
            P(("batch", "item"), None),
            P(("batch", "item")),
        ),
        out_specs=(P(("batch", "item"), None), P(("batch", "item"), None)),
        check_vma=False,
    )
```

```python
import functools

import jax
import jax.numpy as jnp
from jax import lax
from jax.experimental import pallas as pl
from jax.experimental.pallas import tpu as pltpu
from jax.sharding import PartitionSpec as P

epsilon = 1e-06
score_scale = 60.0
cauchy_scale = 4.0
f32 = jnp.float32
bf16 = jnp.bfloat16
i32 = jnp.int32
BLOCK = 256


def iota(shape, dim):
    return lax.broadcasted_iota(i32, shape, dim)


def hot(mask):
    return jnp.where(mask, 1.0, 0.0).astype(bf16)


def dot(a, b, a_dim=1, b_dim=0):
    return lax.dot_general(a, b, (((a_dim,), (b_dim,)), ((), ())), preferred_element_type=f32)


def halves(value):
    return (value >> 8).astype(f32), (value & 255).astype(f32)


def position():
    return lax.axis_index("batch") * lax.axis_size("item") + lax.axis_index("item")


def log2(value):
    return value.bit_length() - 1


def request_kernel(near, named_ref, request_ref):
    devices, lanes = request_ref.shape
    slots = lanes // (1 + near)
    n = named_ref.shape[1]
    owner, row = named_ref[0:1], named_ref[1:2]
    device = iota((devices, n), 0)
    named = owner == device
    count = dot(hot(named), hot(iota((n, n), 0) <= iota((n, n), 1)))
    rank = jnp.sum(jnp.where(named, count, 0.0), axis=0, keepdims=True).astype(i32) - 1
    in_slot = hot(rank == iota((slots, n), 0))
    which = iota((1, n), 1)
    for k, (value, mask) in enumerate([(row, 0)] + [(which, mask) for mask in range(near)]):
        high, low = halves(value + 1)
        here = (owner ^ mask) == device
        high = dot(jnp.where(here, high, 0.0).astype(bf16), in_slot, 1, 1)
        low = dot(jnp.where(here, low, 0.0).astype(bf16), in_slot, 1, 1)
        request_ref[:, k * slots : (k + 1) * slots] = (high * 256.0 + low).astype(i32) - 1


def asker_of(spot, part, near, n_batch, slots):
    batch = (spot >> log2(slots)) & (n_batch - 1)
    level = spot >> log2(slots * n_batch)
    return position() ^ (batch * lax.axis_size("item") + level * near + part)


def slot_column(asked, part, near, n_batch):
    devices, slots = asked.shape
    total = devices * slots // near
    asker = asker_of(iota((total, devices), 0), part, near, n_batch, slots)
    pick = hot(asker == iota((total, devices), 1))
    high, low = halves(asked)
    value = dot(pick, high.astype(bf16)) * 256.0 + dot(pick, low.astype(bf16))
    mine = (iota((total, slots), 0) & (slots - 1)) == iota((total, slots), 1)
    return jnp.sum(jnp.where(mine, value, 0.0), axis=1, keepdims=True)


def slot_line(asked, near, n_batch):
    devices, slots = asked.shape
    total = devices * slots
    pick = hot((iota((slots, total), 1) & (slots - 1)) == iota((slots, total), 0))
    high, low = halves(asked)
    value = dot(high.astype(bf16), pick) * 256.0 + dot(low.astype(bf16), pick)
    spot = iota((devices, total), 1)
    asker = asker_of(spot & (total // near - 1), spot >> log2(total // near), near, n_batch, slots)
    return jnp.sum(jnp.where(asker == iota((devices, total), 0), value, 0.0), axis=0, keepdims=True)


def parts_of(value):
    return value >> 8, value & 255


def fetch_kernel(parts, near, n_batch, asked_ref, table_ref, *found):
    slots = asked_ref.shape[1] // (1 + near)
    asked = asked_ref[:, :slots]
    column = jnp.concatenate([slot_column(asked, part, near, n_batch) for part in parts], axis=0)
    block, low = parts_of(column.astype(i32))
    total = block.shape[0]
    low_hot = hot(low == iota((total, BLOCK), 1))
    block = jnp.broadcast_to(block.astype(f32), (total, BLOCK)).astype(bf16)
    picks = [
        jnp.where(block == jnp.bfloat16(k), low_hot, jnp.bfloat16(0)) for k in range(table_ref.shape[0] // BLOCK)
    ]
    rows = dot(jnp.concatenate(picks, axis=1), table_ref[...]).astype(bf16)
    size = total // len(found)
    for k, ref in enumerate(found):
        ref[...] = rows[k * size : (k + 1) * size]


def prepare_kernel(near, n_batch, n, asked_ref, place_ref, low_hot_ref, block_ref):
    slots = asked_ref.shape[1] // (1 + near)
    size = place_ref.shape[0] // near
    batch = (iota((size, 1), 0) >> log2(slots)) & (n_batch - 1)
    for part in range(near):
        asked = asked_ref[:, (1 + part) * slots : (2 + part) * slots]
        which = slot_column(asked, 0, near, n_batch).astype(i32)
        place_ref[pl.ds(part * size, size)] = jnp.where(which < 0, -1, batch * n + which)
    block, low = parts_of(slot_line(asked_ref[:, :slots], near, n_batch).astype(i32))
    low_hot_ref[...] = hot(low == iota(low_hot_ref.shape, 0))
    block_ref[...] = jnp.broadcast_to(block.astype(f32), block_ref.shape).astype(bf16)


def users_kernel(level, near, place_ref, *refs):
    *users, unit_ref, own_ref = refs
    n, width = users[0].shape
    for k, ref in enumerate(users):
        value = ref[...].astype(f32)
        mean = jnp.mean(value * value, axis=1, keepdims=True)
        unit_ref[pl.ds(k * n, n)] = (value * lax.rsqrt(mean + epsilon) * (1.0 / width**0.5)).astype(bf16)
    step = place_ref.shape[0] // near
    size = own_ref.shape[0] // near
    place = jnp.concatenate([place_ref[pl.ds(k * step + level * size, size)] for k in range(near)], axis=0)
    own_ref[...] = dot(hot(place == iota((place.shape[0], unit_ref.shape[0]), 1)), unit_ref[...]).astype(bf16)


def hidden_kernel(levels, weight_ref, *refs):
    *fetched, hidden_ref, rscale_ref, item_ref = refs
    width = weight_ref.shape[0]
    size = fetched[0].shape[0] // levels
    for level in range(levels):
        embed = jnp.concatenate([ref[pl.ds(level * size, size)] for ref in fetched], axis=0)
        here = pl.ds(level * embed.shape[0], embed.shape[0])
        hidden = dot(embed, weight_ref[...])
        rscale = lax.rsqrt(jnp.mean(hidden * hidden, axis=1, keepdims=True) + epsilon)
        hidden_ref[here] = hidden
        rscale_ref[here] = rscale
        item_ref[here] = (hidden * (rscale * (1.0 / width**0.5))).astype(bf16)


def main_kernel(levels, hidden_ref, rscale_ref, item_ref, *refs):
    units, owns, outs = refs[:levels], refs[levels : 2 * levels], refs[2 * levels :]
    total, width = hidden_ref.shape
    size = outs[0].shape[0] // levels
    root = 1.0 / width**0.5
    for level in range(levels):
        here = pl.ds(level * (total // levels), total // levels)
        hidden, rscale, item_vec = hidden_ref[here], rscale_ref[here], item_ref[here]
        unit = units[level][...]
        expo = jnp.exp(dot(item_vec, unit, 1, 1) * score_scale)
        sums = jnp.sum(expo, axis=1, keepdims=True)
        mixed = dot(expo.astype(bf16), unit)
        own = owns[level][...].astype(f32)
        positive = jnp.sum(item_vec.astype(f32) * own, axis=1, keepdims=True) * score_scale
        xent = jnp.log(sums) - positive
        cweight = 1.0 / (1.0 + xent * (1.0 / cauchy_scale))
        dvec = (cweight * score_scale) * (mixed * (1.0 / sums) - own)
        inner = jnp.sum(hidden * dvec, axis=1, keepdims=True)
        dhidden = (rscale * root * (dvec - hidden * (rscale * rscale * inner * (1.0 / width)))).astype(bf16)
        for part, ref in enumerate(outs):
            ref[pl.ds(level * size, size)] = dhidden[part * size : (part + 1) * size]


def coordinate(bits):
    return sum(((lax.axis_index(axis) >> level) & 1) << k for k, (axis, level) in enumerate(reversed(bits)))


def cut(blocks, bits, refs):
    size = refs[0].shape[0]
    for step, ref in enumerate(refs):
        ref[...] = blocks[pl.ds((coordinate(bits) ^ step) * size, size)].astype(ref.dtype)


def share_kernel(order, bits, count, *refs):
    values, (*refs, blocks) = refs[:count], refs[count:]
    embed, dhidden = (jnp.concatenate([ref[...] for ref in half], axis=0) for half in (values[: count // 2], values[count // 2 :]))
    share = dot(embed, dhidden, 0, 0)
    size = blocks.shape[1]
    for spot, block in enumerate(order):
        blocks[spot] = share[block * size : (block + 1) * size]
    cut(blocks, bits, refs)


def stage_kernel(bits, count, *refs):
    came, (*refs, blocks) = refs[:count], refs[count:]
    blocks[...] = sum(ref[...].astype(f32) for ref in came)
    cut(blocks, bits, refs)


def last_kernel(*refs):
    *came, total_ref = refs
    total_ref[...] = sum(ref[...].astype(f32) for ref in came)[0]


def table_kernel(low_hot_ref, block_ref, weight_ref, *refs):
    *incoming, table_grad_hbm, ready, sems = refs
    dhidden = jnp.concatenate([ref[...] for ref in incoming], axis=0)
    drow = dot(dhidden, weight_ref[...], 1, 1).astype(bf16)
    groups = sems.shape[0]
    size = ready.shape[0] // groups
    copies = []
    for g in range(groups):
        here = pl.ds(g * size, size)
        picks = [
            jnp.where(block_ref[...] == jnp.bfloat16(k), low_hot_ref[...], jnp.bfloat16(0))
            for k in range(g * size // BLOCK, (g + 1) * size // BLOCK)
        ]
        ready[here] = dot(jnp.concatenate(picks, axis=0), drow).astype(bf16)
        copy = pltpu.make_async_copy(ready.at[here], table_grad_hbm.at[here], sems.at[g])
        copy.start()
        copies.append(copy)
    for copy in copies:
        copy.wait()


def params(mib):
    return pltpu.CompilerParams(vmem_limit_bytes=mib * 1024 * 1024)


def cost(flops, bytes_accessed=1 << 20):
    return pl.CostEstimate(flops=flops, bytes_accessed=bytes_accessed, transcendentals=0)


def call(kernel, outs, *args, flops=0, scratch=(), mib=16, free=False):
    return pl.pallas_call(
        kernel,
        out_shape=[jax.ShapeDtypeStruct(shape, dtype) for shape, dtype in outs],
        scratch_shapes=scratch,
        compiler_params=params(mib),
        cost_estimate=cost(flops, 0 if free else 1 << 20),
    )(*args)


def swap(value, mask):
    devices = lax.axis_size("batch") * lax.axis_size("item")
    return lax.ppermute(value, ("batch", "item"), [(k, k ^ mask) for k in range(devices)])


def bits_of(axis):
    return [(axis, level) for level in range(log2(lax.axis_size(axis)))]


def mask_of(bits):
    return sum((lax.axis_size("item") if axis == "batch" else 1) << level for axis, level in bits)


def reduce_scatter(fetched, dhidden, incoming):
    width = dhidden[0].shape[1]
    n_item, devices = lax.axis_size("item"), lax.axis_size("batch") * lax.axis_size("item")
    part = width // devices
    close = log2(len(dhidden))
    batch_bits, item_bits = bits_of("batch"), bits_of("item")
    stages = [batch_bits[:1], batch_bits[1:], item_bits[:close], item_bits[close:]]
    bits = sum(stages, [])
    order = []
    for spot in range(devices):
        at = {"batch": 0, "item": 0}
        for k, (axis, level) in enumerate(bits):
            at[axis] |= (spot >> (len(bits) - 1 - k) & 1) << level
        order.append(at["batch"] * n_item + at["item"])
    left, values = devices, [*fetched, *dhidden]
    for k, stage in enumerate(stages):
        whole, left = left, left >> len(stage)
        masks = [
            mask_of([bit for j, bit in enumerate(reversed(stage)) if step >> j & 1]) for step in range(1, 1 << len(stage))
        ]
        sent = f32 if k == len(stages) - 1 else bf16
        count = len(values)
        kernel = functools.partial(stage_kernel, stage, count) if k else functools.partial(share_kernel, order, stage, count)
        kept, *sends = call(
            kernel,
            [((left, part, width), f32)] + [((left, part, width), sent)] * len(masks),
            *values,
            scratch=[pltpu.VMEM((whole, part, width), f32)],
            free=True,
        )
        values = [kept] + [swap(value, mask) for mask, value in zip(masks, sends)]
        if k == 2:
            values, incoming = lax.optimization_barrier((values, incoming))
    return values, incoming


def local(user_vectors, item_table, tower_weight, item_owner, item_row):
    n, width = user_vectors.shape
    rows = item_table.shape[0]
    n_batch, n_item = lax.axis_size("batch"), lax.axis_size("item")
    devices = n_batch * n_item
    near = min(4, n_item)
    levels = n_item // near
    slots = 2 * n // devices
    total = devices * slots
    size = total // near
    groups = rows // min(512, rows)

    far = [batch * n_item for batch in range(2, n_batch, 2)]
    users = {0: user_vectors}
    for mask in [near << k for k in range(log2(levels))] + far:
        users[mask] = swap(user_vectors, mask)

    (request,) = call(
        functools.partial(request_kernel, near),
        [((devices, (1 + near) * slots), i32)],
        jnp.stack([item_owner.reshape(n), item_row]),
        flops=1 << 34,
    )
    asked = lax.all_to_all(request, ("batch", "item"), split_axis=0, concat_axis=0, tiled=True)
    early = list(users)
    asked, *values = lax.optimization_barrier((asked, *users.values()))
    users = dict(zip(early, values))

    for level in range(1, levels):
        if near * level not in users:
            top = 1 << log2(level)
            users[near * level] = swap(users[near * (level - top)], near * top)
        for mask in far:
            users[mask + near * level] = swap(users[near * level], mask)

    def fetch(parts):
        return call(
            functools.partial(fetch_kernel, parts, near, n_batch),
            [((size, width), bf16)] * len(parts),
            asked,
            item_table,
            flops=2 * size * len(parts) * rows * width,
        )

    fetched = {}
    for parts in [[near - 1], list(range(1, near - 1)), [0]]:
        asked, *values = lax.optimization_barrier((asked, *fetch(parts)))
        for part, value in zip(parts, values):
            fetched[part] = swap(value, part) if part else value
    late = [mask for mask in users if mask not in early]
    fetched[0], *values = lax.optimization_barrier((fetched[0], *[users[mask] for mask in late]))
    users.update(zip(late, values))
    fetched = [fetched[part] for part in range(near)]

    for mask in list(users):
        users[mask + n_item] = swap(users[mask], n_item)

    place, low_hot, block = call(
        functools.partial(prepare_kernel, near, n_batch, n),
        [((total, 1), i32)] + [((BLOCK, total), bf16)] * 2,
        asked,
        free=True,
    )
    units, owns = zip(
        *[
            call(
                functools.partial(users_kernel, level, near),
                [((n_batch * n, width), bf16), ((total // levels, width), bf16)],
                place,
                *[users[near * level + batch * n_item] for batch in range(n_batch)],
                free=True,
            )
            for level in range(levels)
        ]
    )
    fetched[0], first = lax.optimization_barrier((fetched[0], (units[0], owns[0])))
    units, owns = (first[0], *units[1:]), (first[1], *owns[1:])
    hidden = call(
        functools.partial(hidden_kernel, levels),
        [((total, width), f32), ((total, 1), f32), ((total, width), bf16)],
        tower_weight,
        *fetched,
        flops=1 << 34,
    )
    dhidden = call(
        functools.partial(main_kernel, levels),
        [((size, width), bf16)] * near,
        *hidden,
        *units,
        *owns,
        flops=1 << 31,
        mib=40,
    )
    incoming = [swap(dhidden[part], part) for part in range(1, near)]
    terms, incoming = reduce_scatter(fetched, dhidden, incoming)
    table_grad = pl.pallas_call(
        table_kernel,
        out_specs=pl.BlockSpec(memory_space=pl.ANY),
        out_shape=jax.ShapeDtypeStruct((rows, width), bf16),
        scratch_shapes=[pltpu.VMEM((rows, width), bf16), pltpu.SemaphoreType.DMA((groups,))],
        compiler_params=params(16),
        cost_estimate=cost(2 * total * rows * width, 2 * rows * width),
    )(low_hot, block, tower_weight, dhidden[0], *incoming)
    table_grad, *terms = lax.optimization_barrier((table_grad, *terms))
    (weight_grad,) = call(last_kernel, [((width // devices, width), f32)], *terms)
    return (table_grad, weight_grad)


def solution(mesh):
    return jax.shard_map(
        local,
        mesh=mesh,
        in_specs=(
            P(("batch", "item"), None),
            P(("batch", "item"), None),
            P(),
            P(("batch", "item"), None),
            P(("batch", "item")),
        ),
        out_specs=(P(("batch", "item"), None), P(("batch", "item"), None)),
        check_vma=False,
    )
```

```python
import functools

import jax
import jax.numpy as jnp
from jax import lax
from jax.experimental import pallas as pl
from jax.experimental.pallas import tpu as pltpu
from jax.sharding import PartitionSpec as P

epsilon = 1e-06
score_scale = 60.0
cauchy_scale = 4.0
f32 = jnp.float32
bf16 = jnp.bfloat16
i32 = jnp.int32
BLOCK = 256


def iota(shape, dim):
    return lax.broadcasted_iota(i32, shape, dim)


def hot(mask):
    return jnp.where(mask, 1.0, 0.0).astype(bf16)


def dot(a, b, a_dim=1, b_dim=0):
    return lax.dot_general(a, b, (((a_dim,), (b_dim,)), ((), ())), preferred_element_type=f32)


def halves(value):
    return (value >> 8).astype(f32), (value & 255).astype(f32)


def position():
    return lax.axis_index("batch") * lax.axis_size("item") + lax.axis_index("item")


def log2(value):
    return value.bit_length() - 1


def request_kernel(near, named_ref, request_ref):
    devices, lanes = request_ref.shape
    slots = lanes // (1 + near)
    n = named_ref.shape[1]
    owner, row = named_ref[0:1], named_ref[1:2]
    device = iota((devices, n), 0)
    named = owner == device
    count = dot(hot(named), hot(iota((n, n), 0) <= iota((n, n), 1)))
    rank = jnp.sum(jnp.where(named, count, 0.0), axis=0, keepdims=True).astype(i32) - 1
    in_slot = hot(rank == iota((slots, n), 0))
    which = iota((1, n), 1)
    for k, (value, mask) in enumerate([(row, 0)] + [(which, mask) for mask in range(near)]):
        high, low = halves(value + 1)
        here = (owner ^ mask) == device
        high = dot(jnp.where(here, high, 0.0).astype(bf16), in_slot, 1, 1)
        low = dot(jnp.where(here, low, 0.0).astype(bf16), in_slot, 1, 1)
        request_ref[:, k * slots : (k + 1) * slots] = (high * 256.0 + low).astype(i32) - 1


def asker_of(spot, part, near, n_batch, slots):
    batch = (spot >> log2(slots)) & (n_batch - 1)
    level = spot >> log2(slots * n_batch)
    return position() ^ (batch * lax.axis_size("item") + level * near + part)


def slot_column(asked, part, near, n_batch):
    devices, slots = asked.shape
    total = devices * slots // near
    asker = asker_of(iota((total, devices), 0), part, near, n_batch, slots)
    pick = hot(asker == iota((total, devices), 1))
    high, low = halves(asked)
    value = dot(pick, high.astype(bf16)) * 256.0 + dot(pick, low.astype(bf16))
    mine = (iota((total, slots), 0) & (slots - 1)) == iota((total, slots), 1)
    return jnp.sum(jnp.where(mine, value, 0.0), axis=1, keepdims=True)


def slot_line(asked, near, n_batch):
    devices, slots = asked.shape
    total = devices * slots
    pick = hot((iota((slots, total), 1) & (slots - 1)) == iota((slots, total), 0))
    high, low = halves(asked)
    value = dot(high.astype(bf16), pick) * 256.0 + dot(low.astype(bf16), pick)
    spot = iota((devices, total), 1)
    asker = asker_of(spot & (total // near - 1), spot >> log2(total // near), near, n_batch, slots)
    return jnp.sum(jnp.where(asker == iota((devices, total), 0), value, 0.0), axis=0, keepdims=True)


def parts_of(value):
    return value >> 8, value & 255


def fetch_kernel(parts, near, n_batch, asked_ref, table_ref, *found):
    slots = asked_ref.shape[1] // (1 + near)
    asked = asked_ref[:, :slots]
    column = jnp.concatenate([slot_column(asked, part, near, n_batch) for part in parts], axis=0)
    block, low = parts_of(column.astype(i32))
    total = block.shape[0]
    low_hot = hot(low == iota((total, BLOCK), 1))
    block = jnp.broadcast_to(block.astype(f32), (total, BLOCK)).astype(bf16)
    picks = [
        jnp.where(block == jnp.bfloat16(k), low_hot, jnp.bfloat16(0)) for k in range(table_ref.shape[0] // BLOCK)
    ]
    rows = dot(jnp.concatenate(picks, axis=1), table_ref[...]).astype(bf16)
    size = total // len(found)
    for k, ref in enumerate(found):
        ref[...] = rows[k * size : (k + 1) * size]


def prepare_kernel(near, n_batch, asked_ref, *refs):
    *users, place_ref, low_hot_ref, block_ref, unit_ref, own_ref = refs
    n = users[0].shape[0]
    slots = asked_ref.shape[1] // (1 + near)
    size = place_ref.shape[0] // near
    batch = (iota((size, 1), 0) >> log2(slots)) & (n_batch - 1)
    for part in range(near):
        asked = asked_ref[:, (1 + part) * slots : (2 + part) * slots]
        which = slot_column(asked, 0, near, n_batch).astype(i32)
        place_ref[pl.ds(part * size, size)] = jnp.where(which < 0, -1, batch * n + which)
    block, low = parts_of(slot_line(asked_ref[:, :slots], near, n_batch).astype(i32))
    low_hot_ref[...] = hot(low == iota(low_hot_ref.shape, 0))
    block_ref[...] = jnp.broadcast_to(block.astype(f32), block_ref.shape).astype(bf16)
    users_kernel(0, near, place_ref, *users, unit_ref, own_ref)


def users_kernel(level, near, place_ref, *refs):
    *users, unit_ref, own_ref = refs
    n, width = users[0].shape
    for k, ref in enumerate(users):
        value = ref[...].astype(f32)
        mean = jnp.mean(value * value, axis=1, keepdims=True)
        unit_ref[pl.ds(k * n, n)] = (value * lax.rsqrt(mean + epsilon) * (1.0 / width**0.5)).astype(bf16)
    step = place_ref.shape[0] // near
    size = own_ref.shape[0] // near
    place = jnp.concatenate([place_ref[pl.ds(k * step + level * size, size)] for k in range(near)], axis=0)
    own_ref[...] = dot(hot(place == iota((place.shape[0], unit_ref.shape[0]), 1)), unit_ref[...]).astype(bf16)


def hidden_kernel(levels, weight_ref, *refs):
    *fetched, hidden_ref, rscale_ref, item_ref = refs
    width = weight_ref.shape[0]
    size = fetched[0].shape[0] // levels
    for level in range(levels):
        embed = jnp.concatenate([ref[pl.ds(level * size, size)] for ref in fetched], axis=0)
        here = pl.ds(level * embed.shape[0], embed.shape[0])
        hidden = dot(embed, weight_ref[...])
        rscale = lax.rsqrt(jnp.mean(hidden * hidden, axis=1, keepdims=True) + epsilon)
        hidden_ref[here] = hidden
        rscale_ref[here] = rscale
        item_ref[here] = (hidden * (rscale * (1.0 / width**0.5))).astype(bf16)


def main_kernel(levels, hidden_ref, rscale_ref, item_ref, *refs):
    units, owns, outs = refs[:levels], refs[levels : 2 * levels], refs[2 * levels :]
    total, width = hidden_ref.shape
    size = outs[0].shape[0] // levels
    root = 1.0 / width**0.5
    for level in range(levels):
        here = pl.ds(level * (total // levels), total // levels)
        hidden, rscale, item_vec = hidden_ref[here], rscale_ref[here], item_ref[here]
        unit = units[level][...]
        expo = jnp.exp(dot(item_vec, unit, 1, 1) * score_scale)
        sums = jnp.sum(expo, axis=1, keepdims=True)
        mixed = dot(expo.astype(bf16), unit)
        own = owns[level][...].astype(f32)
        positive = jnp.sum(item_vec.astype(f32) * own, axis=1, keepdims=True) * score_scale
        xent = jnp.log(sums) - positive
        cweight = 1.0 / (1.0 + xent * (1.0 / cauchy_scale))
        dvec = (cweight * score_scale) * (mixed * (1.0 / sums) - own)
        inner = jnp.sum(hidden * dvec, axis=1, keepdims=True)
        dhidden = (rscale * root * (dvec - hidden * (rscale * rscale * inner * (1.0 / width)))).astype(bf16)
        for part, ref in enumerate(outs):
            ref[pl.ds(level * size, size)] = dhidden[part * size : (part + 1) * size]


def coordinate(bits):
    return sum(((lax.axis_index(axis) >> level) & 1) << k for k, (axis, level) in enumerate(reversed(bits)))


def cut(blocks, bits, refs):
    size = refs[0].shape[0]
    for step, ref in enumerate(refs):
        ref[...] = blocks[pl.ds((coordinate(bits) ^ step) * size, size)].astype(ref.dtype)


def share_kernel(order, bits, count, *refs):
    values, (*refs, blocks) = refs[:count], refs[count:]
    embed, dhidden = (jnp.concatenate([ref[...] for ref in half], axis=0) for half in (values[: count // 2], values[count // 2 :]))
    share = dot(embed, dhidden, 0, 0)
    size = blocks.shape[1]
    for spot, block in enumerate(order):
        blocks[spot] = share[block * size : (block + 1) * size]
    cut(blocks, bits, refs)


def stage_kernel(bits, count, *refs):
    came, (*refs, blocks) = refs[:count], refs[count:]
    blocks[...] = sum(ref[...].astype(f32) for ref in came)
    cut(blocks, bits, refs)


def last_kernel(*refs):
    *came, total_ref = refs
    total_ref[...] = sum(ref[...].astype(f32) for ref in came)[0]


def table_kernel(low_hot_ref, block_ref, weight_ref, *refs):
    *incoming, table_grad_hbm, ready, sems = refs
    dhidden = jnp.concatenate([ref[...] for ref in incoming], axis=0)
    drow = dot(dhidden, weight_ref[...], 1, 1).astype(bf16)
    groups = sems.shape[0]
    size = ready.shape[0] // groups
    copies = []
    for g in range(groups):
        here = pl.ds(g * size, size)
        picks = [
            jnp.where(block_ref[...] == jnp.bfloat16(k), low_hot_ref[...], jnp.bfloat16(0))
            for k in range(g * size // BLOCK, (g + 1) * size // BLOCK)
        ]
        ready[here] = dot(jnp.concatenate(picks, axis=0), drow).astype(bf16)
        copy = pltpu.make_async_copy(ready.at[here], table_grad_hbm.at[here], sems.at[g])
        copy.start()
        copies.append(copy)
    for copy in copies:
        copy.wait()


def params(mib):
    return pltpu.CompilerParams(vmem_limit_bytes=mib * 1024 * 1024)


def cost(flops, bytes_accessed=1 << 20):
    return pl.CostEstimate(flops=flops, bytes_accessed=bytes_accessed, transcendentals=0)


def call(kernel, outs, *args, flops=0, scratch=(), mib=16, free=False):
    return pl.pallas_call(
        kernel,
        out_shape=[jax.ShapeDtypeStruct(shape, dtype) for shape, dtype in outs],
        scratch_shapes=scratch,
        compiler_params=params(mib),
        cost_estimate=cost(flops, 0 if free else 1 << 20),
    )(*args)


def swap(value, mask):
    devices = lax.axis_size("batch") * lax.axis_size("item")
    return lax.ppermute(value, ("batch", "item"), [(k, k ^ mask) for k in range(devices)])


def bits_of(axis):
    return [(axis, level) for level in range(log2(lax.axis_size(axis)))]


def mask_of(bits):
    return sum((lax.axis_size("item") if axis == "batch" else 1) << level for axis, level in bits)


def reduce_scatter(fetched, dhidden, incoming):
    width = dhidden[0].shape[1]
    n_item, devices = lax.axis_size("item"), lax.axis_size("batch") * lax.axis_size("item")
    part = width // devices
    close = log2(len(dhidden))
    batch_bits, item_bits = bits_of("batch"), bits_of("item")
    stages = [batch_bits[:1], batch_bits[1:], item_bits[:close], item_bits[close:]]
    bits = sum(stages, [])
    order = []
    for spot in range(devices):
        at = {"batch": 0, "item": 0}
        for k, (axis, level) in enumerate(bits):
            at[axis] |= (spot >> (len(bits) - 1 - k) & 1) << level
        order.append(at["batch"] * n_item + at["item"])
    left, values = devices, [*fetched, *dhidden]
    for k, stage in enumerate(stages):
        whole, left = left, left >> len(stage)
        masks = [
            mask_of([bit for j, bit in enumerate(reversed(stage)) if step >> j & 1]) for step in range(1, 1 << len(stage))
        ]
        sent = f32 if k == len(stages) - 1 else bf16
        count = len(values)
        kernel = functools.partial(stage_kernel, stage, count) if k else functools.partial(share_kernel, order, stage, count)
        kept, *sends = call(
            kernel,
            [((left, part, width), f32)] + [((left, part, width), sent)] * len(masks),
            *values,
            scratch=[pltpu.VMEM((whole, part, width), f32)],
            free=True,
        )
        values = [kept] + [swap(value, mask) for mask, value in zip(masks, sends)]
        if k == 2:
            values, incoming = lax.optimization_barrier((values, incoming))
    return values, incoming


def local(user_vectors, item_table, tower_weight, item_owner, item_row):
    n, width = user_vectors.shape
    rows = item_table.shape[0]
    n_batch, n_item = lax.axis_size("batch"), lax.axis_size("item")
    devices = n_batch * n_item
    near = min(4, n_item)
    levels = n_item // near
    slots = 2 * n // devices
    total = devices * slots
    size = total // near
    groups = rows // min(512, rows)

    far = [batch * n_item for batch in range(2, n_batch, 2)]
    users = {0: user_vectors}
    for mask in [near << k for k in range(log2(levels))] + far:
        users[mask] = swap(user_vectors, mask)

    (request,) = call(
        functools.partial(request_kernel, near),
        [((devices, (1 + near) * slots), i32)],
        jnp.stack([item_owner.reshape(n), item_row]),
        flops=1 << 34,
    )
    asked = lax.all_to_all(request, ("batch", "item"), split_axis=0, concat_axis=0, tiled=True)
    early = list(users)
    asked, *values = lax.optimization_barrier((asked, *users.values()))
    users = dict(zip(early, values))

    for level in range(1, levels):
        if near * level not in users:
            top = 1 << log2(level)
            users[near * level] = swap(users[near * (level - top)], near * top)
        for mask in far:
            users[mask + near * level] = swap(users[near * level], mask)

    def fetch(parts):
        return call(
            functools.partial(fetch_kernel, parts, near, n_batch),
            [((size, width), bf16)] * len(parts),
            asked,
            item_table,
            flops=2 * size * len(parts) * rows * width,
        )

    fetched = {}
    for parts in [[near - 1], list(range(1, near - 1)), [0]]:
        asked, *values = lax.optimization_barrier((asked, *fetch(parts)))
        for part, value in zip(parts, values):
            fetched[part] = swap(value, part) if part else value
    late = [mask for mask in users if mask not in early]
    fetched[0], *values = lax.optimization_barrier((fetched[0], *[users[mask] for mask in late]))
    users.update(zip(late, values))
    fetched = [fetched[part] for part in range(near)]

    for mask in list(users):
        users[mask + n_item] = swap(users[mask], n_item)

    def group(level):
        return [users[near * level + batch * n_item] for batch in range(n_batch)]

    group_outs = [((n_batch * n, width), bf16), ((total // levels, width), bf16)]
    place, low_hot, block, *first = call(
        functools.partial(prepare_kernel, near, n_batch),
        [((total, 1), i32)] + [((BLOCK, total), bf16)] * 2 + group_outs,
        asked,
        *group(0),
        free=True,
    )
    units, owns = zip(
        first,
        *[
            call(functools.partial(users_kernel, level, near), group_outs, place, *group(level), free=True)
            for level in range(1, levels)
        ],
    )
    hidden = call(
        functools.partial(hidden_kernel, levels),
        [((total, width), f32), ((total, 1), f32), ((total, width), bf16)],
        tower_weight,
        *fetched,
        flops=1 << 34,
    )
    dhidden = call(
        functools.partial(main_kernel, levels),
        [((size, width), bf16)] * near,
        *hidden,
        *units,
        *owns,
        flops=1 << 31,
        mib=40,
    )
    incoming = [swap(dhidden[part], part) for part in range(1, near)]
    terms, incoming = reduce_scatter(fetched, dhidden, incoming)
    table_grad = pl.pallas_call(
        table_kernel,
        out_specs=pl.BlockSpec(memory_space=pl.ANY),
        out_shape=jax.ShapeDtypeStruct((rows, width), bf16),
        scratch_shapes=[pltpu.VMEM((rows, width), bf16), pltpu.SemaphoreType.DMA((groups,))],
        compiler_params=params(16),
        cost_estimate=cost(2 * total * rows * width, 2 * rows * width),
    )(low_hot, block, tower_weight, dhidden[0], *incoming)
    table_grad, *terms = lax.optimization_barrier((table_grad, *terms))
    (weight_grad,) = call(last_kernel, [((width // devices, width), f32)], *terms)
    return (table_grad, weight_grad)


def solution(mesh):
    return jax.shard_map(
        local,
        mesh=mesh,
        in_specs=(
            P(("batch", "item"), None),
            P(("batch", "item"), None),
            P(),
            P(("batch", "item"), None),
            P(("batch", "item")),
        ),
        out_specs=(P(("batch", "item"), None), P(("batch", "item"), None)),
        check_vma=False,
    )
```

```python
import functools

import jax
import jax.numpy as jnp
from jax import lax
from jax.experimental import pallas as pl
from jax.experimental.pallas import tpu as pltpu
from jax.sharding import PartitionSpec as P

epsilon = 1e-06
score_scale = 60.0
cauchy_scale = 4.0
f32 = jnp.float32
bf16 = jnp.bfloat16
i32 = jnp.int32
BLOCK = 256


def iota(shape, dim):
    return lax.broadcasted_iota(i32, shape, dim)


def hot(mask):
    return jnp.where(mask, 1.0, 0.0).astype(bf16)


def dot(a, b, a_dim=1, b_dim=0):
    return lax.dot_general(a, b, (((a_dim,), (b_dim,)), ((), ())), preferred_element_type=f32)


def halves(value):
    return (value >> 8).astype(f32), (value & 255).astype(f32)


def position():
    return lax.axis_index("batch") * lax.axis_size("item") + lax.axis_index("item")


def log2(value):
    return value.bit_length() - 1


def request_kernel(near, named_ref, request_ref):
    devices, lanes = request_ref.shape
    slots = lanes // (1 + near)
    n = named_ref.shape[1]
    owner, row = named_ref[0:1], named_ref[1:2]
    device = iota((devices, n), 0)
    named = owner == device
    count = dot(hot(named), hot(iota((n, n), 0) <= iota((n, n), 1)))
    rank = jnp.sum(jnp.where(named, count, 0.0), axis=0, keepdims=True).astype(i32) - 1
    in_slot = hot(rank == iota((slots, n), 0))
    which = iota((1, n), 1)
    for k, (value, mask) in enumerate([(row, 0)] + [(which, mask) for mask in range(near)]):
        high, low = halves(value + 1)
        here = (owner ^ mask) == device
        high = dot(jnp.where(here, high, 0.0).astype(bf16), in_slot, 1, 1)
        low = dot(jnp.where(here, low, 0.0).astype(bf16), in_slot, 1, 1)
        request_ref[:, k * slots : (k + 1) * slots] = (high * 256.0 + low).astype(i32) - 1


def asker_of(spot, part, near, n_batch, slots):
    batch = (spot >> log2(slots)) & (n_batch - 1)
    level = spot >> log2(slots * n_batch)
    return position() ^ (batch * lax.axis_size("item") + level * near + part)


def slot_column(asked, part, near, n_batch):
    devices, slots = asked.shape
    total = devices * slots // near
    asker = asker_of(iota((total, devices), 0), part, near, n_batch, slots)
    pick = hot(asker == iota((total, devices), 1))
    high, low = halves(asked)
    value = dot(pick, high.astype(bf16)) * 256.0 + dot(pick, low.astype(bf16))
    mine = (iota((total, slots), 0) & (slots - 1)) == iota((total, slots), 1)
    return jnp.sum(jnp.where(mine, value, 0.0), axis=1, keepdims=True)


def slot_line(asked, near, n_batch):
    devices, slots = asked.shape
    total = devices * slots
    pick = hot((iota((slots, total), 1) & (slots - 1)) == iota((slots, total), 0))
    high, low = halves(asked)
    value = dot(high.astype(bf16), pick) * 256.0 + dot(low.astype(bf16), pick)
    spot = iota((devices, total), 1)
    asker = asker_of(spot & (total // near - 1), spot >> log2(total // near), near, n_batch, slots)
    return jnp.sum(jnp.where(asker == iota((devices, total), 0), value, 0.0), axis=0, keepdims=True)


def parts_of(value):
    return value >> 8, value & 255


def fetch_kernel(parts, near, n_batch, asked_ref, table_ref, *found):
    slots = asked_ref.shape[1] // (1 + near)
    asked = asked_ref[:, :slots]
    column = jnp.concatenate([slot_column(asked, part, near, n_batch) for part in parts], axis=0)
    block, low = parts_of(column.astype(i32))
    total = block.shape[0]
    low_hot = hot(low == iota((total, BLOCK), 1))
    block = jnp.broadcast_to(block.astype(f32), (total, BLOCK)).astype(bf16)
    picks = [
        jnp.where(block == jnp.bfloat16(k), low_hot, jnp.bfloat16(0)) for k in range(table_ref.shape[0] // BLOCK)
    ]
    rows = dot(jnp.concatenate(picks, axis=1), table_ref[...]).astype(bf16)
    size = total // len(found)
    for k, ref in enumerate(found):
        ref[...] = rows[k * size : (k + 1) * size]


def prepare_kernel(near, n_batch, asked_ref, *refs):
    *users, place_ref, low_hot_ref, block_ref, unit_ref, own_ref = refs
    n = users[0].shape[0]
    slots = asked_ref.shape[1] // (1 + near)
    size = place_ref.shape[0] // near
    batch = (iota((size, 1), 0) >> log2(slots)) & (n_batch - 1)
    for part in range(near):
        asked = asked_ref[:, (1 + part) * slots : (2 + part) * slots]
        which = slot_column(asked, 0, near, n_batch).astype(i32)
        place_ref[pl.ds(part * size, size)] = jnp.where(which < 0, -1, batch * n + which)
    block, low = parts_of(slot_line(asked_ref[:, :slots], near, n_batch).astype(i32))
    low_hot_ref[...] = hot(low == iota(low_hot_ref.shape, 0))
    block_ref[...] = jnp.broadcast_to(block.astype(f32), block_ref.shape).astype(bf16)
    users_kernel(0, near, place_ref, *users, unit_ref, own_ref)


def users_kernel(level, near, place_ref, *refs):
    *users, unit_ref, own_ref = refs
    n, width = users[0].shape
    for k, ref in enumerate(users):
        value = ref[...].astype(f32)
        mean = jnp.mean(value * value, axis=1, keepdims=True)
        unit_ref[pl.ds(k * n, n)] = (value * lax.rsqrt(mean + epsilon) * (1.0 / width**0.5)).astype(bf16)
    step = place_ref.shape[0] // near
    size = own_ref.shape[0] // near
    place = jnp.concatenate([place_ref[pl.ds(k * step + level * size, size)] for k in range(near)], axis=0)
    own_ref[...] = dot(hot(place == iota((place.shape[0], unit_ref.shape[0]), 1)), unit_ref[...]).astype(bf16)


def hidden_kernel(levels, weight_ref, *refs):
    *fetched, hidden_ref, rscale_ref, item_ref = refs
    width = weight_ref.shape[0]
    size = fetched[0].shape[0] // levels
    for level in range(levels):
        embed = jnp.concatenate([ref[pl.ds(level * size, size)] for ref in fetched], axis=0)
        here = pl.ds(level * embed.shape[0], embed.shape[0])
        hidden = dot(embed, weight_ref[...])
        rscale = lax.rsqrt(jnp.mean(hidden * hidden, axis=1, keepdims=True) + epsilon)
        hidden_ref[here] = hidden
        rscale_ref[here] = rscale
        item_ref[here] = (hidden * (rscale * (1.0 / width**0.5))).astype(bf16)


def main_kernel(levels, hidden_ref, rscale_ref, item_ref, *refs):
    units, owns, outs = refs[:levels], refs[levels : 2 * levels], refs[2 * levels :]
    total, width = hidden_ref.shape
    size = outs[0].shape[0] // levels
    root = 1.0 / width**0.5
    for level in range(levels):
        here = pl.ds(level * (total // levels), total // levels)
        hidden, rscale, item_vec = hidden_ref[here], rscale_ref[here], item_ref[here]
        unit = units[level][...]
        expo = jnp.exp(dot(item_vec, unit, 1, 1) * score_scale)
        sums = jnp.sum(expo, axis=1, keepdims=True)
        mixed = dot(expo.astype(bf16), unit)
        own = owns[level][...].astype(f32)
        positive = jnp.sum(item_vec.astype(f32) * own, axis=1, keepdims=True) * score_scale
        xent = jnp.log(sums) - positive
        cweight = 1.0 / (1.0 + xent * (1.0 / cauchy_scale))
        dvec = (cweight * score_scale) * (mixed * (1.0 / sums) - own)
        inner = jnp.sum(hidden * dvec, axis=1, keepdims=True)
        dhidden = (rscale * root * (dvec - hidden * (rscale * rscale * inner * (1.0 / width)))).astype(bf16)
        for part, ref in enumerate(outs):
            ref[pl.ds(level * size, size)] = dhidden[part * size : (part + 1) * size]


def coordinate(bits):
    return sum(((lax.axis_index(axis) >> level) & 1) << k for k, (axis, level) in enumerate(reversed(bits)))


def cut(blocks, bits, refs):
    size = refs[0].shape[0]
    for step, ref in enumerate(refs):
        ref[...] = blocks[pl.ds((coordinate(bits) ^ step) * size, size)].astype(ref.dtype)


def share_kernel(order, bits, count, *refs):
    values, (*refs, blocks) = refs[:count], refs[count:]
    embed, dhidden = (jnp.concatenate([ref[...] for ref in half], axis=0) for half in (values[: count // 2], values[count // 2 :]))
    share = dot(embed, dhidden, 0, 0)
    size = blocks.shape[1]
    for spot, block in enumerate(order):
        blocks[spot] = share[block * size : (block + 1) * size]
    cut(blocks, bits, refs)


def stage_kernel(bits, count, *refs):
    came, (*refs, blocks) = refs[:count], refs[count:]
    blocks[...] = sum(ref[...].astype(f32) for ref in came)
    cut(blocks, bits, refs)


def last_kernel(*refs):
    *came, total_ref = refs
    total_ref[...] = sum(ref[...].astype(f32) for ref in came)[0]


def table_kernel(low_hot_ref, block_ref, weight_ref, *refs):
    *incoming, table_grad_hbm, ready, sems = refs
    dhidden = jnp.concatenate([ref[...] for ref in incoming], axis=0)
    drow = dot(dhidden, weight_ref[...], 1, 1).astype(bf16)
    groups = sems.shape[0]
    size = ready.shape[0] // groups
    copies = []
    for g in range(groups):
        here = pl.ds(g * size, size)
        picks = [
            jnp.where(block_ref[...] == jnp.bfloat16(k), low_hot_ref[...], jnp.bfloat16(0))
            for k in range(g * size // BLOCK, (g + 1) * size // BLOCK)
        ]
        ready[here] = dot(jnp.concatenate(picks, axis=0), drow).astype(bf16)
        copy = pltpu.make_async_copy(ready.at[here], table_grad_hbm.at[here], sems.at[g])
        copy.start()
        copies.append(copy)
    for copy in copies:
        copy.wait()


def params(mib):
    return pltpu.CompilerParams(vmem_limit_bytes=mib * 1024 * 1024)


def cost(flops, bytes_accessed=1 << 20):
    return pl.CostEstimate(flops=flops, bytes_accessed=bytes_accessed, transcendentals=0)


def call(kernel, outs, *args, flops=0, scratch=(), mib=16, free=False):
    return pl.pallas_call(
        kernel,
        out_shape=[jax.ShapeDtypeStruct(shape, dtype) for shape, dtype in outs],
        scratch_shapes=scratch,
        compiler_params=params(mib),
        cost_estimate=cost(flops, 0 if free else 1 << 20),
    )(*args)


def swap(value, mask):
    devices = lax.axis_size("batch") * lax.axis_size("item")
    return lax.ppermute(value, ("batch", "item"), [(k, k ^ mask) for k in range(devices)])


def bits_of(axis):
    return [(axis, level) for level in range(log2(lax.axis_size(axis)))]


def mask_of(bits):
    return sum((lax.axis_size("item") if axis == "batch" else 1) << level for axis, level in bits)


def reduce_scatter(fetched, dhidden, incoming):
    width = dhidden[0].shape[1]
    n_item, devices = lax.axis_size("item"), lax.axis_size("batch") * lax.axis_size("item")
    part = width // devices
    close = log2(len(dhidden))
    batch_bits, item_bits = bits_of("batch"), bits_of("item")
    stages = [batch_bits[:1], batch_bits[1:], item_bits[:close], item_bits[close:]]
    bits = sum(stages, [])
    order = []
    for spot in range(devices):
        at = {"batch": 0, "item": 0}
        for k, (axis, level) in enumerate(bits):
            at[axis] |= (spot >> (len(bits) - 1 - k) & 1) << level
        order.append(at["batch"] * n_item + at["item"])
    left, values = devices, [*fetched, *dhidden]
    for k, stage in enumerate(stages):
        whole, left = left, left >> len(stage)
        masks = [
            mask_of([bit for j, bit in enumerate(reversed(stage)) if step >> j & 1]) for step in range(1, 1 << len(stage))
        ]
        sent = f32 if k == len(stages) - 1 else bf16
        count = len(values)
        kernel = functools.partial(stage_kernel, stage, count) if k else functools.partial(share_kernel, order, stage, count)
        kept, *sends = call(
            kernel,
            [((left, part, width), f32)] + [((left, part, width), sent)] * len(masks),
            *values,
            scratch=[pltpu.VMEM((whole, part, width), f32)],
            free=True,
        )
        values = [kept] + [swap(value, mask) for mask, value in zip(masks, sends)]
        if k == 2:
            values, incoming = lax.optimization_barrier((values, incoming))
    return values, incoming


def local(user_vectors, item_table, tower_weight, item_owner, item_row):
    n, width = user_vectors.shape
    rows = item_table.shape[0]
    n_batch, n_item = lax.axis_size("batch"), lax.axis_size("item")
    devices = n_batch * n_item
    near = min(4, n_item)
    levels = n_item // near
    slots = 2 * n // devices
    total = devices * slots
    size = total // near
    groups = rows // min(512, rows)

    far = [batch * n_item for batch in range(2, n_batch, 2)]
    users = {0: user_vectors}
    for mask in [near << k for k in range(log2(levels))] + far:
        users[mask] = swap(user_vectors, mask)

    (request,) = call(
        functools.partial(request_kernel, near),
        [((devices, (1 + near) * slots), i32)],
        jnp.stack([item_owner.reshape(n), item_row]),
        flops=1 << 34,
    )
    asked = lax.all_to_all(request, ("batch", "item"), split_axis=0, concat_axis=0, tiled=True)
    early = list(users)
    asked, *values = lax.optimization_barrier((asked, *users.values()))
    users = dict(zip(early, values))

    for level in range(1, levels):
        if near * level not in users:
            top = 1 << log2(level)
            users[near * level] = swap(users[near * (level - top)], near * top)
        for mask in far:
            users[mask + near * level] = swap(users[near * level], mask)

    def fetch(parts):
        return call(
            functools.partial(fetch_kernel, parts, near, n_batch),
            [((size, width), bf16)] * len(parts),
            asked,
            item_table,
            flops=2 * size * len(parts) * rows * width,
        )

    fetched = {}
    for parts in [[near - 1], list(range(1, near - 1)), [0]]:
        asked, *values = lax.optimization_barrier((asked, *fetch(parts)))
        for part, value in zip(parts, values):
            fetched[part] = swap(value, part) if part else value
    fetched = [fetched[part] for part in range(near)]

    for mask in [0, *far]:
        users[mask + n_item] = swap(users[mask], n_item)

    def group(level):
        return [users[near * level + batch * n_item] for batch in range(n_batch)]

    group_outs = [((n_batch * n, width), bf16), ((total // levels, width), bf16)]
    place, low_hot, block, *first = call(
        functools.partial(prepare_kernel, near, n_batch),
        [((total, 1), i32)] + [((BLOCK, total), bf16)] * 2 + group_outs,
        asked,
        *group(0),
        free=True,
    )
    late = {mask: users[mask] for mask in users if mask & (n_item - near)}
    place, late = lax.optimization_barrier((place, late))
    users |= late | {mask + n_item: swap(late[mask], n_item) for mask in late}
    units, owns = zip(
        first,
        *[
            call(functools.partial(users_kernel, level, near), group_outs, place, *group(level), free=True)
            for level in range(1, levels)
        ],
    )
    hidden = call(
        functools.partial(hidden_kernel, levels),
        [((total, width), f32), ((total, 1), f32), ((total, width), bf16)],
        tower_weight,
        *fetched,
        flops=1 << 34,
    )
    dhidden = call(
        functools.partial(main_kernel, levels),
        [((size, width), bf16)] * near,
        *hidden,
        *units,
        *owns,
        flops=1 << 31,
        mib=40,
    )
    incoming = [swap(dhidden[part], part) for part in range(1, near)]
    terms, incoming = reduce_scatter(fetched, dhidden, incoming)
    table_grad = pl.pallas_call(
        table_kernel,
        out_specs=pl.BlockSpec(memory_space=pl.ANY),
        out_shape=jax.ShapeDtypeStruct((rows, width), bf16),
        scratch_shapes=[pltpu.VMEM((rows, width), bf16), pltpu.SemaphoreType.DMA((groups,))],
        compiler_params=params(16),
        cost_estimate=cost(2 * total * rows * width, 2 * rows * width),
    )(low_hot, block, tower_weight, dhidden[0], *incoming)
    table_grad, *terms = lax.optimization_barrier((table_grad, *terms))
    (weight_grad,) = call(last_kernel, [((width // devices, width), f32)], *terms)
    return (table_grad, weight_grad)


def solution(mesh):
    return jax.shard_map(
        local,
        mesh=mesh,
        in_specs=(
            P(("batch", "item"), None),
            P(("batch", "item"), None),
            P(),
            P(("batch", "item"), None),
            P(("batch", "item")),
        ),
        out_specs=(P(("batch", "item"), None), P(("batch", "item"), None)),
        check_vma=False,
    )
```

```python
import functools

import jax
import jax.numpy as jnp
from jax import lax
from jax.experimental import pallas as pl
from jax.experimental.pallas import tpu as pltpu
from jax.sharding import PartitionSpec as P

epsilon = 1e-06
score_scale = 60.0
cauchy_scale = 4.0
f32 = jnp.float32
bf16 = jnp.bfloat16
i32 = jnp.int32
BLOCK = 256


def iota(shape, dim):
    return lax.broadcasted_iota(i32, shape, dim)


def hot(mask):
    return jnp.where(mask, 1.0, 0.0).astype(bf16)


def dot(a, b, a_dim=1, b_dim=0):
    return lax.dot_general(a, b, (((a_dim,), (b_dim,)), ((), ())), preferred_element_type=f32)


def halves(value):
    return (value >> 8).astype(f32), (value & 255).astype(f32)


def position():
    return lax.axis_index("batch") * lax.axis_size("item") + lax.axis_index("item")


def log2(value):
    return value.bit_length() - 1


def request_kernel(near, named_ref, request_ref):
    devices, lanes = request_ref.shape
    slots = lanes // (1 + near)
    n = named_ref.shape[1]
    owner, row = named_ref[0:1], named_ref[1:2]
    device = iota((devices, n), 0)
    named = owner == device
    count = dot(hot(named), hot(iota((n, n), 0) <= iota((n, n), 1)))
    rank = jnp.sum(jnp.where(named, count, 0.0), axis=0, keepdims=True).astype(i32) - 1
    in_slot = hot(rank == iota((slots, n), 0))
    which = iota((1, n), 1)
    for k, (value, mask) in enumerate([(row, 0)] + [(which, mask) for mask in range(near)]):
        high, low = halves(value + 1)
        here = (owner ^ mask) == device
        high = dot(jnp.where(here, high, 0.0).astype(bf16), in_slot, 1, 1)
        low = dot(jnp.where(here, low, 0.0).astype(bf16), in_slot, 1, 1)
        request_ref[:, k * slots : (k + 1) * slots] = (high * 256.0 + low).astype(i32) - 1


def asker_of(spot, part, near, n_batch, slots):
    batch = (spot >> log2(slots)) & (n_batch - 1)
    level = spot >> log2(slots * n_batch)
    return position() ^ (batch * lax.axis_size("item") + level * near + part)


def slot_column(asked, part, near, n_batch):
    devices, slots = asked.shape
    total = devices * slots // near
    asker = asker_of(iota((total, devices), 0), part, near, n_batch, slots)
    pick = hot(asker == iota((total, devices), 1))
    high, low = halves(asked)
    value = dot(pick, high.astype(bf16)) * 256.0 + dot(pick, low.astype(bf16))
    mine = (iota((total, slots), 0) & (slots - 1)) == iota((total, slots), 1)
    return jnp.sum(jnp.where(mine, value, 0.0), axis=1, keepdims=True)


def slot_line(asked, near, n_batch):
    devices, slots = asked.shape
    total = devices * slots
    pick = hot((iota((slots, total), 1) & (slots - 1)) == iota((slots, total), 0))
    high, low = halves(asked)
    value = dot(high.astype(bf16), pick) * 256.0 + dot(low.astype(bf16), pick)
    spot = iota((devices, total), 1)
    asker = asker_of(spot & (total // near - 1), spot >> log2(total // near), near, n_batch, slots)
    return jnp.sum(jnp.where(asker == iota((devices, total), 0), value, 0.0), axis=0, keepdims=True)


def parts_of(value):
    return value >> 8, value & 255


def fetch_kernel(parts, near, n_batch, asked_ref, table_ref, *found):
    slots = asked_ref.shape[1] // (1 + near)
    asked = asked_ref[:, :slots]
    column = jnp.concatenate([slot_column(asked, part, near, n_batch) for part in parts], axis=0)
    block, low = parts_of(column.astype(i32))
    total = block.shape[0]
    low_hot = hot(low == iota((total, BLOCK), 1))
    block = jnp.broadcast_to(block.astype(f32), (total, BLOCK)).astype(bf16)
    picks = [
        jnp.where(block == jnp.bfloat16(k), low_hot, jnp.bfloat16(0)) for k in range(table_ref.shape[0] // BLOCK)
    ]
    rows = dot(jnp.concatenate(picks, axis=1), table_ref[...]).astype(bf16)
    size = total // len(found)
    for k, ref in enumerate(found):
        ref[...] = rows[k * size : (k + 1) * size]


def prepare_kernel(near, n_batch, asked_ref, *refs):
    *users, place_ref, low_hot_ref, block_ref, unit_ref, own_ref = refs
    n = users[0].shape[0]
    slots = asked_ref.shape[1] // (1 + near)
    size = place_ref.shape[0] // near
    batch = (iota((size, 1), 0) >> log2(slots)) & (n_batch - 1)
    for part in range(near):
        asked = asked_ref[:, (1 + part) * slots : (2 + part) * slots]
        which = slot_column(asked, 0, near, n_batch).astype(i32)
        place_ref[pl.ds(part * size, size)] = jnp.where(which < 0, -1, batch * n + which)
    block, low = parts_of(slot_line(asked_ref[:, :slots], near, n_batch).astype(i32))
    low_hot_ref[...] = hot(low == iota(low_hot_ref.shape, 0))
    block_ref[...] = jnp.broadcast_to(block.astype(f32), block_ref.shape).astype(bf16)
    users_kernel(0, near, place_ref, *users, unit_ref, own_ref)


def users_kernel(level, near, place_ref, *refs):
    *users, unit_ref, own_ref = refs
    n, width = users[0].shape
    for k, ref in enumerate(users):
        value = ref[...].astype(f32)
        mean = jnp.mean(value * value, axis=1, keepdims=True)
        unit_ref[pl.ds(k * n, n)] = (value * lax.rsqrt(mean + epsilon) * (1.0 / width**0.5)).astype(bf16)
    step = place_ref.shape[0] // near
    size = own_ref.shape[0] // near
    place = jnp.concatenate([place_ref[pl.ds(k * step + level * size, size)] for k in range(near)], axis=0)
    own_ref[...] = dot(hot(place == iota((place.shape[0], unit_ref.shape[0]), 1)), unit_ref[...]).astype(bf16)


def hidden_kernel(levels, weight_ref, *refs):
    *fetched, hidden_ref, rscale_ref, item_ref = refs
    width = weight_ref.shape[0]
    size = fetched[0].shape[0] // levels
    for level in range(levels):
        embed = jnp.concatenate([ref[pl.ds(level * size, size)] for ref in fetched], axis=0)
        here = pl.ds(level * embed.shape[0], embed.shape[0])
        hidden = dot(embed, weight_ref[...])
        rscale = lax.rsqrt(jnp.mean(hidden * hidden, axis=1, keepdims=True) + epsilon)
        hidden_ref[here] = hidden
        rscale_ref[here] = rscale
        item_ref[here] = (hidden * (rscale * (1.0 / width**0.5))).astype(bf16)


def main_kernel(levels, hidden_ref, rscale_ref, item_ref, *refs):
    units, owns, outs = refs[:levels], refs[levels : 2 * levels], refs[2 * levels :]
    total, width = hidden_ref.shape
    size = outs[0].shape[0] // levels
    root = 1.0 / width**0.5
    for level in range(levels):
        here = pl.ds(level * (total // levels), total // levels)
        hidden, rscale, item_vec = hidden_ref[here], rscale_ref[here], item_ref[here]
        unit = units[level][...]
        expo = jnp.exp(dot(item_vec, unit, 1, 1) * score_scale)
        sums = jnp.sum(expo, axis=1, keepdims=True)
        mixed = dot(expo.astype(bf16), unit)
        own = owns[level][...].astype(f32)
        positive = jnp.sum(item_vec.astype(f32) * own, axis=1, keepdims=True) * score_scale
        xent = jnp.log(sums) - positive
        cweight = 1.0 / (1.0 + xent * (1.0 / cauchy_scale))
        dvec = (cweight * score_scale) * (mixed * (1.0 / sums) - own)
        inner = jnp.sum(hidden * dvec, axis=1, keepdims=True)
        dhidden = (rscale * root * (dvec - hidden * (rscale * rscale * inner * (1.0 / width)))).astype(bf16)
        for part, ref in enumerate(outs):
            ref[pl.ds(level * size, size)] = dhidden[part * size : (part + 1) * size]


def coordinate(bits):
    return sum(((lax.axis_index(axis) >> level) & 1) << k for k, (axis, level) in enumerate(reversed(bits)))


def cut(blocks, bits, refs):
    size = refs[0].shape[0]
    for step, ref in enumerate(refs):
        ref[...] = blocks[pl.ds((coordinate(bits) ^ step) * size, size)].astype(ref.dtype)


def share_kernel(order, bits, count, *refs):
    values, (*refs, blocks) = refs[:count], refs[count:]
    embed, dhidden = (jnp.concatenate([ref[...] for ref in half], axis=0) for half in (values[: count // 2], values[count // 2 :]))
    share = dot(embed, dhidden, 0, 0)
    size = blocks.shape[1]
    for spot, block in enumerate(order):
        blocks[spot] = share[block * size : (block + 1) * size]
    cut(blocks, bits, refs)


def stage_kernel(bits, count, *refs):
    came, (*refs, blocks) = refs[:count], refs[count:]
    blocks[...] = sum(ref[...].astype(f32) for ref in came)
    cut(blocks, bits, refs)


def last_kernel(*refs):
    *came, total_ref = refs
    total_ref[...] = sum(ref[...].astype(f32) for ref in came)[0]


def table_kernel(low_hot_ref, block_ref, weight_ref, *refs):
    *incoming, table_grad_hbm, ready, sems = refs
    dhidden = jnp.concatenate([ref[...] for ref in incoming], axis=0)
    drow = dot(dhidden, weight_ref[...], 1, 1).astype(bf16)
    groups = sems.shape[0]
    size = ready.shape[0] // groups
    copies = []
    for g in range(groups):
        here = pl.ds(g * size, size)
        picks = [
            jnp.where(block_ref[...] == jnp.bfloat16(k), low_hot_ref[...], jnp.bfloat16(0))
            for k in range(g * size // BLOCK, (g + 1) * size // BLOCK)
        ]
        ready[here] = dot(jnp.concatenate(picks, axis=0), drow).astype(bf16)
        copy = pltpu.make_async_copy(ready.at[here], table_grad_hbm.at[here], sems.at[g])
        copy.start()
        copies.append(copy)
    for copy in copies:
        copy.wait()


def params(mib):
    return pltpu.CompilerParams(vmem_limit_bytes=mib * 1024 * 1024)


def cost(flops, bytes_accessed=1 << 20):
    return pl.CostEstimate(flops=flops, bytes_accessed=bytes_accessed, transcendentals=0)


def call(kernel, outs, *args, flops=0, scratch=(), mib=16, free=False):
    return pl.pallas_call(
        kernel,
        out_shape=[jax.ShapeDtypeStruct(shape, dtype) for shape, dtype in outs],
        scratch_shapes=scratch,
        compiler_params=params(mib),
        cost_estimate=cost(flops, 0 if free else 1 << 20),
    )(*args)


def swap(value, mask):
    devices = lax.axis_size("batch") * lax.axis_size("item")
    return lax.ppermute(value, ("batch", "item"), [(k, k ^ mask) for k in range(devices)])


def bits_of(axis):
    return [(axis, level) for level in range(log2(lax.axis_size(axis)))]


def mask_of(bits):
    return sum((lax.axis_size("item") if axis == "batch" else 1) << level for axis, level in bits)


def reduce_scatter(fetched, dhidden, incoming):
    width = dhidden[0].shape[1]
    n_item, devices = lax.axis_size("item"), lax.axis_size("batch") * lax.axis_size("item")
    part = width // devices
    bits = bits_of("batch") + bits_of("item")
    stages = [[bit] for bit in bits]
    order = []
    for spot in range(devices):
        at = {"batch": 0, "item": 0}
        for k, (axis, level) in enumerate(bits):
            at[axis] |= (spot >> (len(bits) - 1 - k) & 1) << level
        order.append(at["batch"] * n_item + at["item"])
    left, values = devices, [*fetched, *dhidden]
    for k, stage in enumerate(stages):
        whole, left = left, left >> len(stage)
        masks = [
            mask_of([bit for j, bit in enumerate(reversed(stage)) if step >> j & 1]) for step in range(1, 1 << len(stage))
        ]
        sent = bf16 if left > 2 else f32
        count = len(values)
        kernel = functools.partial(stage_kernel, stage, count) if k else functools.partial(share_kernel, order, stage, count)
        kept, *sends = call(
            kernel,
            [((left, part, width), f32)] + [((left, part, width), sent)] * len(masks),
            *values,
            scratch=[pltpu.VMEM((whole, part, width), f32)],
            free=True,
        )
        values = [kept] + [swap(value, mask) for mask, value in zip(masks, sends)]
        if k == 2:
            values, incoming = lax.optimization_barrier((values, incoming))
    return values, incoming


def local(user_vectors, item_table, tower_weight, item_owner, item_row):
    n, width = user_vectors.shape
    rows = item_table.shape[0]
    n_batch, n_item = lax.axis_size("batch"), lax.axis_size("item")
    devices = n_batch * n_item
    near = min(4, n_item)
    levels = n_item // near
    slots = 2 * n // devices
    total = devices * slots
    size = total // near
    groups = rows // min(512, rows)

    far = [batch * n_item for batch in range(2, n_batch, 2)]
    users = {0: user_vectors}
    for mask in [near << k for k in range(log2(levels))] + far:
        users[mask] = swap(user_vectors, mask)

    (request,) = call(
        functools.partial(request_kernel, near),
        [((devices, (1 + near) * slots), i32)],
        jnp.stack([item_owner.reshape(n), item_row]),
        flops=1 << 34,
    )
    asked = lax.all_to_all(request, ("batch", "item"), split_axis=0, concat_axis=0, tiled=True)
    early = list(users)
    asked, *values = lax.optimization_barrier((asked, *users.values()))
    users = dict(zip(early, values))

    for level in range(1, levels):
        if near * level not in users:
            top = 1 << log2(level)
            users[near * level] = swap(users[near * (level - top)], near * top)
        for mask in far:
            users[mask + near * level] = swap(users[near * level], mask)

    def fetch(parts):
        return call(
            functools.partial(fetch_kernel, parts, near, n_batch),
            [((size, width), bf16)] * len(parts),
            asked,
            item_table,
            flops=2 * size * len(parts) * rows * width,
        )

    fetched = {}
    for parts in [[near - 1], list(range(1, near - 1)), [0]]:
        asked, *values = lax.optimization_barrier((asked, *fetch(parts)))
        for part, value in zip(parts, values):
            fetched[part] = swap(value, part) if part else value
    fetched = [fetched[part] for part in range(near)]

    for mask in [0, *far]:
        users[mask + n_item] = swap(users[mask], n_item)

    def group(level):
        return [users[near * level + batch * n_item] for batch in range(n_batch)]

    group_outs = [((n_batch * n, width), bf16), ((total // levels, width), bf16)]
    place, low_hot, block, *first = call(
        functools.partial(prepare_kernel, near, n_batch),
        [((total, 1), i32)] + [((BLOCK, total), bf16)] * 2 + group_outs,
        asked,
        *group(0),
        free=True,
    )
    late = {mask: users[mask] for mask in users if mask & (n_item - near)}
    place, late = lax.optimization_barrier((place, late))
    users |= late | {mask + n_item: swap(late[mask], n_item) for mask in late}
    units, owns = zip(
        first,
        *[
            call(functools.partial(users_kernel, level, near), group_outs, place, *group(level), free=True)
            for level in range(1, levels)
        ],
    )
    hidden = call(
        functools.partial(hidden_kernel, levels),
        [((total, width), f32), ((total, 1), f32), ((total, width), bf16)],
        tower_weight,
        *fetched,
        flops=1 << 34,
    )
    dhidden = call(
        functools.partial(main_kernel, levels),
        [((size, width), bf16)] * near,
        *hidden,
        *units,
        *owns,
        flops=1 << 31,
        mib=40,
    )
    incoming = [swap(dhidden[part], part) for part in reversed(range(1, near))][::-1]
    terms, incoming = reduce_scatter(fetched, dhidden, incoming)
    table_grad = pl.pallas_call(
        table_kernel,
        out_specs=pl.BlockSpec(memory_space=pl.ANY),
        out_shape=jax.ShapeDtypeStruct((rows, width), bf16),
        scratch_shapes=[pltpu.VMEM((rows, width), bf16), pltpu.SemaphoreType.DMA((groups,))],
        compiler_params=params(16),
        cost_estimate=cost(2 * total * rows * width, 2 * rows * width),
    )(low_hot, block, tower_weight, dhidden[0], *incoming)
    table_grad, *terms = lax.optimization_barrier((table_grad, *terms))
    (weight_grad,) = call(last_kernel, [((width // devices, width), f32)], *terms)
    return (table_grad, weight_grad)


def solution(mesh):
    return jax.shard_map(
        local,
        mesh=mesh,
        in_specs=(
            P(("batch", "item"), None),
            P(("batch", "item"), None),
            P(),
            P(("batch", "item"), None),
            P(("batch", "item")),
        ),
        out_specs=(P(("batch", "item"), None), P(("batch", "item"), None)),
        check_vma=False,
    )
```

```python
import functools

import jax
import jax.numpy as jnp
from jax import lax
from jax.experimental import pallas as pl
from jax.experimental.pallas import tpu as pltpu
from jax.sharding import PartitionSpec as P

epsilon = 1e-06
score_scale = 60.0
cauchy_scale = 4.0
f32 = jnp.float32
bf16 = jnp.bfloat16
i32 = jnp.int32
BLOCK = 256


def iota(shape, dim):
    return lax.broadcasted_iota(i32, shape, dim)


def hot(mask):
    return jnp.where(mask, 1.0, 0.0).astype(bf16)


def dot(a, b, a_dim=1, b_dim=0):
    return lax.dot_general(a, b, (((a_dim,), (b_dim,)), ((), ())), preferred_element_type=f32)


def halves(value):
    return (value >> 8).astype(f32), (value & 255).astype(f32)


def position():
    return lax.axis_index("batch") * lax.axis_size("item") + lax.axis_index("item")


def log2(value):
    return value.bit_length() - 1


def request_kernel(near, named_ref, request_ref):
    devices, lanes = request_ref.shape
    slots = lanes // (1 + near)
    n = named_ref.shape[1]
    owner, row = named_ref[0:1], named_ref[1:2]
    device = iota((devices, n), 0)
    named = owner == device
    count = dot(hot(named), hot(iota((n, n), 0) <= iota((n, n), 1)))
    rank = jnp.sum(jnp.where(named, count, 0.0), axis=0, keepdims=True).astype(i32) - 1
    in_slot = hot(rank == iota((slots, n), 0))
    which = iota((1, n), 1)
    for k, (value, mask) in enumerate([(row, 0)] + [(which, mask) for mask in range(near)]):
        high, low = halves(value + 1)
        here = (owner ^ mask) == device
        high = dot(jnp.where(here, high, 0.0).astype(bf16), in_slot, 1, 1)
        low = dot(jnp.where(here, low, 0.0).astype(bf16), in_slot, 1, 1)
        request_ref[:, k * slots : (k + 1) * slots] = (high * 256.0 + low).astype(i32) - 1


def asker_of(spot, part, near, n_batch, slots):
    batch = (spot >> log2(slots)) & (n_batch - 1)
    level = spot >> log2(slots * n_batch)
    return position() ^ (batch * lax.axis_size("item") + level * near + part)


def slot_column(asked, part, near, n_batch):
    devices, slots = asked.shape
    total = devices * slots // near
    asker = asker_of(iota((total, devices), 0), part, near, n_batch, slots)
    pick = hot(asker == iota((total, devices), 1))
    high, low = halves(asked)
    value = dot(pick, high.astype(bf16)) * 256.0 + dot(pick, low.astype(bf16))
    mine = (iota((total, slots), 0) & (slots - 1)) == iota((total, slots), 1)
    return jnp.sum(jnp.where(mine, value, 0.0), axis=1, keepdims=True)


def slot_line(asked, near, n_batch):
    devices, slots = asked.shape
    total = devices * slots
    pick = hot((iota((slots, total), 1) & (slots - 1)) == iota((slots, total), 0))
    high, low = halves(asked)
    value = dot(high.astype(bf16), pick) * 256.0 + dot(low.astype(bf16), pick)
    spot = iota((devices, total), 1)
    asker = asker_of(spot & (total // near - 1), spot >> log2(total // near), near, n_batch, slots)
    return jnp.sum(jnp.where(asker == iota((devices, total), 0), value, 0.0), axis=0, keepdims=True)


def parts_of(value):
    return value >> 8, value & 255


def fetch_kernel(parts, near, n_batch, asked_ref, table_ref, *found):
    slots = asked_ref.shape[1] // (1 + near)
    asked = asked_ref[:, :slots]
    column = jnp.concatenate([slot_column(asked, part, near, n_batch) for part in parts], axis=0)
    block, low = parts_of(column.astype(i32))
    total = block.shape[0]
    low_hot = hot(low == iota((total, BLOCK), 1))
    block = jnp.broadcast_to(block.astype(f32), (total, BLOCK)).astype(bf16)
    picks = [
        jnp.where(block == jnp.bfloat16(k), low_hot, jnp.bfloat16(0)) for k in range(table_ref.shape[0] // BLOCK)
    ]
    rows = dot(jnp.concatenate(picks, axis=1), table_ref[...]).astype(bf16)
    size = total // len(found)
    for k, ref in enumerate(found):
        ref[...] = rows[k * size : (k + 1) * size]


def prepare_kernel(near, n_batch, asked_ref, *refs):
    *users, place_ref, low_hot_ref, block_ref, unit_ref, own_ref = refs
    n = users[0].shape[0]
    slots = asked_ref.shape[1] // (1 + near)
    size = place_ref.shape[0] // near
    batch = (iota((size, 1), 0) >> log2(slots)) & (n_batch - 1)
    for part in range(near):
        asked = asked_ref[:, (1 + part) * slots : (2 + part) * slots]
        which = slot_column(asked, 0, near, n_batch).astype(i32)
        place_ref[pl.ds(part * size, size)] = jnp.where(which < 0, -1, batch * n + which)
    block, low = parts_of(slot_line(asked_ref[:, :slots], near, n_batch).astype(i32))
    low_hot_ref[...] = hot(low == iota(low_hot_ref.shape, 0))
    block_ref[...] = jnp.broadcast_to(block.astype(f32), block_ref.shape).astype(bf16)
    users_kernel(0, near, place_ref, *users, unit_ref, own_ref)


def users_kernel(level, near, place_ref, *refs):
    *users, unit_ref, own_ref = refs
    n, width = users[0].shape
    for k, ref in enumerate(users):
        value = ref[...].astype(f32)
        mean = jnp.mean(value * value, axis=1, keepdims=True)
        unit_ref[pl.ds(k * n, n)] = (value * lax.rsqrt(mean + epsilon) * (1.0 / width**0.5)).astype(bf16)
    step = place_ref.shape[0] // near
    size = own_ref.shape[0] // near
    place = jnp.concatenate([place_ref[pl.ds(k * step + level * size, size)] for k in range(near)], axis=0)
    own_ref[...] = dot(hot(place == iota((place.shape[0], unit_ref.shape[0]), 1)), unit_ref[...]).astype(bf16)


def hidden_kernel(levels, weight_ref, *refs):
    *fetched, hidden_ref, rscale_ref, item_ref = refs
    width = weight_ref.shape[0]
    size = fetched[0].shape[0] // levels
    for level in range(levels):
        embed = jnp.concatenate([ref[pl.ds(level * size, size)] for ref in fetched], axis=0)
        here = pl.ds(level * embed.shape[0], embed.shape[0])
        hidden = dot(embed, weight_ref[...])
        rscale = lax.rsqrt(jnp.mean(hidden * hidden, axis=1, keepdims=True) + epsilon)
        hidden_ref[here] = hidden
        rscale_ref[here] = rscale
        item_ref[here] = (hidden * (rscale * (1.0 / width**0.5))).astype(bf16)


def main_kernel(levels, hidden_ref, rscale_ref, item_ref, *refs):
    units, owns, outs = refs[:levels], refs[levels : 2 * levels], refs[2 * levels :]
    total, width = hidden_ref.shape
    size = outs[0].shape[0] // levels
    root = 1.0 / width**0.5
    for level in range(levels):
        here = pl.ds(level * (total // levels), total // levels)
        hidden, rscale, item_vec = hidden_ref[here], rscale_ref[here], item_ref[here]
        unit = units[level][...]
        expo = jnp.exp(dot(item_vec, unit, 1, 1) * score_scale)
        sums = jnp.sum(expo, axis=1, keepdims=True)
        mixed = dot(expo.astype(bf16), unit)
        own = owns[level][...].astype(f32)
        positive = jnp.sum(item_vec.astype(f32) * own, axis=1, keepdims=True) * score_scale
        xent = jnp.log(sums) - positive
        cweight = 1.0 / (1.0 + xent * (1.0 / cauchy_scale))
        dvec = (cweight * score_scale) * (mixed * (1.0 / sums) - own)
        inner = jnp.sum(hidden * dvec, axis=1, keepdims=True)
        dhidden = (rscale * root * (dvec - hidden * (rscale * rscale * inner * (1.0 / width)))).astype(bf16)
        for part, ref in enumerate(outs):
            ref[pl.ds(level * size, size)] = dhidden[part * size : (part + 1) * size]


def coordinate(bits):
    return sum(((lax.axis_index(axis) >> level) & 1) << k for k, (axis, level) in enumerate(reversed(bits)))


def cut(blocks, bits, refs):
    size = refs[0].shape[0]
    for step, ref in enumerate(refs):
        ref[...] = blocks[pl.ds((coordinate(bits) ^ step) * size, size)].astype(ref.dtype)


def share_kernel(order, bits, count, *refs):
    values, (*refs, blocks) = refs[:count], refs[count:]
    embed, dhidden = (jnp.concatenate([ref[...] for ref in half], axis=0) for half in (values[: count // 2], values[count // 2 :]))
    share = dot(embed, dhidden, 0, 0)
    size = blocks.shape[1]
    for spot, block in enumerate(order):
        blocks[spot] = share[block * size : (block + 1) * size]
    cut(blocks, bits, refs)


def stage_kernel(bits, count, *refs):
    came, (*refs, blocks) = refs[:count], refs[count:]
    blocks[...] = sum(ref[...].astype(f32) for ref in came)
    cut(blocks, bits, refs)


def last_kernel(*refs):
    *came, total_ref = refs
    total_ref[...] = sum(ref[...].astype(f32) for ref in came)[0]


def table_kernel(low_hot_ref, block_ref, weight_ref, *refs):
    *incoming, table_grad_hbm, ready, sems = refs
    dhidden = jnp.concatenate([ref[...] for ref in incoming], axis=0)
    drow = dot(dhidden, weight_ref[...], 1, 1).astype(bf16)
    groups = sems.shape[0]
    size = ready.shape[0] // groups
    copies = []
    for g in range(groups):
        here = pl.ds(g * size, size)
        picks = [
            jnp.where(block_ref[...] == jnp.bfloat16(k), low_hot_ref[...], jnp.bfloat16(0))
            for k in range(g * size // BLOCK, (g + 1) * size // BLOCK)
        ]
        ready[here] = dot(jnp.concatenate(picks, axis=0), drow).astype(bf16)
        copy = pltpu.make_async_copy(ready.at[here], table_grad_hbm.at[here], sems.at[g])
        copy.start()
        copies.append(copy)
    for copy in copies:
        copy.wait()


def params(mib):
    return pltpu.CompilerParams(vmem_limit_bytes=mib * 1024 * 1024)


def cost(flops, bytes_accessed=1 << 20):
    return pl.CostEstimate(flops=flops, bytes_accessed=bytes_accessed, transcendentals=0)


def call(kernel, outs, *args, flops=0, scratch=(), mib=16, free=False):
    return pl.pallas_call(
        kernel,
        out_shape=[jax.ShapeDtypeStruct(shape, dtype) for shape, dtype in outs],
        scratch_shapes=scratch,
        compiler_params=params(mib),
        cost_estimate=cost(flops, 0 if free else 1 << 20),
    )(*args)


def swap(value, mask):
    devices = lax.axis_size("batch") * lax.axis_size("item")
    return lax.ppermute(value, ("batch", "item"), [(k, k ^ mask) for k in range(devices)])


def bits_of(axis):
    return [(axis, level) for level in range(log2(lax.axis_size(axis)))]


def mask_of(bits):
    return sum((lax.axis_size("item") if axis == "batch" else 1) << level for axis, level in bits)


def reduce_scatter(fetched, dhidden):
    width = dhidden[0].shape[1]
    n_item, devices = lax.axis_size("item"), lax.axis_size("batch") * lax.axis_size("item")
    part = width // devices
    close = log2(len(dhidden))
    batch_bits, item_bits = bits_of("batch"), bits_of("item")
    stages = [batch_bits[:1], batch_bits[1:], item_bits[close:], item_bits[:close]]
    bits = sum(stages, [])
    order = []
    for spot in range(devices):
        at = {"batch": 0, "item": 0}
        for k, (axis, level) in enumerate(bits):
            at[axis] |= (spot >> (len(bits) - 1 - k) & 1) << level
        order.append(at["batch"] * n_item + at["item"])
    left, values = devices, [*fetched, *dhidden]
    for k, stage in enumerate(stages):
        whole, left = left, left >> len(stage)
        masks = [
            mask_of([bit for j, bit in enumerate(reversed(stage)) if step >> j & 1]) for step in range(1, 1 << len(stage))
        ]
        sent = f32 if k == len(stages) - 1 else bf16
        count = len(values)
        kernel = functools.partial(stage_kernel, stage, count) if k else functools.partial(share_kernel, order, stage, count)
        kept, *sends = call(
            kernel,
            [((left, part, width), f32)] + [((left, part, width), sent)] * len(masks),
            *values,
            scratch=[pltpu.VMEM((whole, part, width), f32)],
            free=True,
        )
        values = [kept] + [swap(value, mask) for mask, value in zip(masks, sends)]
    return values


def local(user_vectors, item_table, tower_weight, item_owner, item_row):
    n, width = user_vectors.shape
    rows = item_table.shape[0]
    n_batch, n_item = lax.axis_size("batch"), lax.axis_size("item")
    devices = n_batch * n_item
    near = min(4, n_item)
    levels = n_item // near
    slots = 2 * n // devices
    total = devices * slots
    size = total // near
    groups = rows // min(512, rows)

    far = [batch * n_item for batch in range(2, n_batch, 2)]
    users = {0: user_vectors}
    for mask in [near << k for k in range(log2(levels))] + far:
        users[mask] = swap(user_vectors, mask)

    (request,) = call(
        functools.partial(request_kernel, near),
        [((devices, (1 + near) * slots), i32)],
        jnp.stack([item_owner.reshape(n), item_row]),
        flops=1 << 34,
    )
    asked = lax.all_to_all(request, ("batch", "item"), split_axis=0, concat_axis=0, tiled=True)
    early = list(users)
    asked, *values = lax.optimization_barrier((asked, *users.values()))
    users = dict(zip(early, values))

    for level in range(1, levels):
        if near * level not in users:
            top = 1 << log2(level)
            users[near * level] = swap(users[near * (level - top)], near * top)
        for mask in far:
            users[mask + near * level] = swap(users[near * level], mask)

    def fetch(parts):
        return call(
            functools.partial(fetch_kernel, parts, near, n_batch),
            [((size, width), bf16)] * len(parts),
            asked,
            item_table,
            flops=2 * size * len(parts) * rows * width,
        )

    fetched = {}
    for parts in [[near - 1], list(range(1, near - 1)), [0]]:
        asked, *values = lax.optimization_barrier((asked, *fetch(parts)))
        for part, value in zip(parts, values):
            fetched[part] = swap(value, part) if part else value
    fetched = [fetched[part] for part in range(near)]

    for mask in [0, *far]:
        users[mask + n_item] = swap(users[mask], n_item)

    def group(level):
        return [users[near * level + batch * n_item] for batch in range(n_batch)]

    group_outs = [((n_batch * n, width), bf16), ((total // levels, width), bf16)]
    place, low_hot, block, *first = call(
        functools.partial(prepare_kernel, near, n_batch),
        [((total, 1), i32)] + [((BLOCK, total), bf16)] * 2 + group_outs,
        asked,
        *group(0),
        free=True,
    )
    late = {mask: users[mask] for mask in users if mask & (n_item - near)}
    place, late = lax.optimization_barrier((place, late))
    users |= late | {mask + n_item: swap(late[mask], n_item) for mask in late}
    units, owns = zip(
        first,
        *[
            call(functools.partial(users_kernel, level, near), group_outs, place, *group(level), free=True)
            for level in range(1, levels)
        ],
    )
    hidden = call(
        functools.partial(hidden_kernel, levels),
        [((total, width), f32), ((total, 1), f32), ((total, width), bf16)],
        tower_weight,
        *fetched,
        flops=1 << 34,
    )
    dhidden = call(
        functools.partial(main_kernel, levels),
        [((size, width), bf16)] * near,
        *hidden,
        *units,
        *owns,
        flops=1 << 31,
        mib=40,
    )
    incoming = [swap(dhidden[part], part) for part in range(1, near)]
    terms = reduce_scatter(fetched, dhidden)
    table_grad = pl.pallas_call(
        table_kernel,
        out_specs=pl.BlockSpec(memory_space=pl.ANY),
        out_shape=jax.ShapeDtypeStruct((rows, width), bf16),
        scratch_shapes=[pltpu.VMEM((rows, width), bf16), pltpu.SemaphoreType.DMA((groups,))],
        compiler_params=params(16),
        cost_estimate=cost(2 * total * rows * width, 2 * rows * width),
    )(low_hot, block, tower_weight, dhidden[0], *incoming)
    table_grad, *terms = lax.optimization_barrier((table_grad, *terms))
    (weight_grad,) = call(last_kernel, [((width // devices, width), f32)], *terms)
    return (table_grad, weight_grad)


def solution(mesh):
    return jax.shard_map(
        local,
        mesh=mesh,
        in_specs=(
            P(("batch", "item"), None),
            P(("batch", "item"), None),
            P(),
            P(("batch", "item"), None),
            P(("batch", "item")),
        ),
        out_specs=(P(("batch", "item"), None), P(("batch", "item"), None)),
        check_vma=False,
    )
```

```python
import functools

import jax
import jax.numpy as jnp
from jax import lax
from jax.experimental import pallas as pl
from jax.experimental.pallas import tpu as pltpu
from jax.sharding import PartitionSpec as P

epsilon = 1e-06
score_scale = 60.0
cauchy_scale = 4.0
f32 = jnp.float32
bf16 = jnp.bfloat16
i32 = jnp.int32
BLOCK = 256


def iota(shape, dim):
    return lax.broadcasted_iota(i32, shape, dim)


def hot(mask):
    return jnp.where(mask, 1.0, 0.0).astype(bf16)


def dot(a, b, a_dim=1, b_dim=0):
    return lax.dot_general(a, b, (((a_dim,), (b_dim,)), ((), ())), preferred_element_type=f32)


def halves(value):
    return (value >> 8).astype(f32), (value & 255).astype(f32)


def position():
    return lax.axis_index("batch") * lax.axis_size("item") + lax.axis_index("item")


def log2(value):
    return value.bit_length() - 1


def request_kernel(near, named_ref, request_ref):
    devices, lanes = request_ref.shape
    slots = lanes // (1 + near)
    n = named_ref.shape[1]
    owner, row = named_ref[0:1], named_ref[1:2]
    device = iota((devices, n), 0)
    named = owner == device
    count = dot(hot(named), hot(iota((n, n), 0) <= iota((n, n), 1)))
    rank = jnp.sum(jnp.where(named, count, 0.0), axis=0, keepdims=True).astype(i32) - 1
    in_slot = hot(rank == iota((slots, n), 0))
    which = iota((1, n), 1)
    for k, (value, mask) in enumerate([(row, 0)] + [(which, mask) for mask in range(near)]):
        high, low = halves(value + 1)
        here = (owner ^ mask) == device
        high = dot(jnp.where(here, high, 0.0).astype(bf16), in_slot, 1, 1)
        low = dot(jnp.where(here, low, 0.0).astype(bf16), in_slot, 1, 1)
        request_ref[:, k * slots : (k + 1) * slots] = (high * 256.0 + low).astype(i32) - 1


def asker_of(spot, part, near, n_batch, slots):
    batch = (spot >> log2(slots)) & (n_batch - 1)
    level = spot >> log2(slots * n_batch)
    return position() ^ (batch * lax.axis_size("item") + level * near + part)


def slot_column(asked, part, near, n_batch):
    devices, slots = asked.shape
    total = devices * slots // near
    asker = asker_of(iota((total, devices), 0), part, near, n_batch, slots)
    pick = hot(asker == iota((total, devices), 1))
    high, low = halves(asked)
    value = dot(pick, high.astype(bf16)) * 256.0 + dot(pick, low.astype(bf16))
    mine = (iota((total, slots), 0) & (slots - 1)) == iota((total, slots), 1)
    return jnp.sum(jnp.where(mine, value, 0.0), axis=1, keepdims=True)


def slot_line(asked, near, n_batch):
    devices, slots = asked.shape
    total = devices * slots
    pick = hot((iota((slots, total), 1) & (slots - 1)) == iota((slots, total), 0))
    high, low = halves(asked)
    value = dot(high.astype(bf16), pick) * 256.0 + dot(low.astype(bf16), pick)
    spot = iota((devices, total), 1)
    asker = asker_of(spot & (total // near - 1), spot >> log2(total // near), near, n_batch, slots)
    return jnp.sum(jnp.where(asker == iota((devices, total), 0), value, 0.0), axis=0, keepdims=True)


def parts_of(value):
    return value >> 8, value & 255


def fetch_kernel(parts, near, n_batch, asked_ref, table_ref, *found):
    slots = asked_ref.shape[1] // (1 + near)
    asked = asked_ref[:, :slots]
    column = jnp.concatenate([slot_column(asked, part, near, n_batch) for part in parts], axis=0)
    block, low = parts_of(column.astype(i32))
    total = block.shape[0]
    low_hot = hot(low == iota((total, BLOCK), 1))
    block = jnp.broadcast_to(block.astype(f32), (total, BLOCK)).astype(bf16)
    picks = [
        jnp.where(block == jnp.bfloat16(k), low_hot, jnp.bfloat16(0)) for k in range(table_ref.shape[0] // BLOCK)
    ]
    rows = dot(jnp.concatenate(picks, axis=1), table_ref[...]).astype(bf16)
    size = total // len(found)
    for k, ref in enumerate(found):
        ref[...] = rows[k * size : (k + 1) * size]


def prepare_kernel(near, n_batch, asked_ref, *refs):
    *users, place_ref, low_hot_ref, block_ref, unit_ref, own_ref = refs
    n = users[0].shape[0]
    slots = asked_ref.shape[1] // (1 + near)
    size = place_ref.shape[0] // near
    batch = (iota((size, 1), 0) >> log2(slots)) & (n_batch - 1)
    for part in range(near):
        asked = asked_ref[:, (1 + part) * slots : (2 + part) * slots]
        which = slot_column(asked, 0, near, n_batch).astype(i32)
        place_ref[pl.ds(part * size, size)] = jnp.where(which < 0, -1, batch * n + which)
    block, low = parts_of(slot_line(asked_ref[:, :slots], near, n_batch).astype(i32))
    low_hot_ref[...] = hot(low == iota(low_hot_ref.shape, 0))
    block_ref[...] = jnp.broadcast_to(block.astype(f32), block_ref.shape).astype(bf16)
    users_kernel(0, near, place_ref, *users, unit_ref, own_ref)


def users_kernel(level, near, place_ref, *refs):
    *users, unit_ref, own_ref = refs
    n, width = users[0].shape
    for k, ref in enumerate(users):
        value = ref[...].astype(f32)
        mean = jnp.mean(value * value, axis=1, keepdims=True)
        unit_ref[pl.ds(k * n, n)] = (value * lax.rsqrt(mean + epsilon) * (1.0 / width**0.5)).astype(bf16)
    step = place_ref.shape[0] // near
    size = own_ref.shape[0] // near
    place = jnp.concatenate([place_ref[pl.ds(k * step + level * size, size)] for k in range(near)], axis=0)
    own_ref[...] = dot(hot(place == iota((place.shape[0], unit_ref.shape[0]), 1)), unit_ref[...]).astype(bf16)


def hidden_kernel(levels, weight_ref, *refs):
    *fetched, hidden_ref, rscale_ref, item_ref = refs
    width = weight_ref.shape[0]
    size = fetched[0].shape[0] // levels
    for level in range(levels):
        embed = jnp.concatenate([ref[pl.ds(level * size, size)] for ref in fetched], axis=0)
        here = pl.ds(level * embed.shape[0], embed.shape[0])
        hidden = dot(embed, weight_ref[...])
        rscale = lax.rsqrt(jnp.mean(hidden * hidden, axis=1, keepdims=True) + epsilon)
        hidden_ref[here] = hidden
        rscale_ref[here] = rscale
        item_ref[here] = (hidden * (rscale * (1.0 / width**0.5))).astype(bf16)


def main_kernel(levels, hidden_ref, rscale_ref, item_ref, *refs):
    units, owns, outs = refs[:levels], refs[levels : 2 * levels], refs[2 * levels :]
    total, width = hidden_ref.shape
    size = outs[0].shape[0] // levels
    root = 1.0 / width**0.5
    for level in range(levels):
        here = pl.ds(level * (total // levels), total // levels)
        hidden, rscale, item_vec = hidden_ref[here], rscale_ref[here], item_ref[here]
        unit = units[level][...]
        expo = jnp.exp(dot(item_vec, unit, 1, 1) * score_scale)
        sums = jnp.sum(expo, axis=1, keepdims=True)
        mixed = dot(expo.astype(bf16), unit)
        own = owns[level][...].astype(f32)
        positive = jnp.sum(item_vec.astype(f32) * own, axis=1, keepdims=True) * score_scale
        xent = jnp.log(sums) - positive
        cweight = 1.0 / (1.0 + xent * (1.0 / cauchy_scale))
        dvec = (cweight * score_scale) * (mixed * (1.0 / sums) - own)
        inner = jnp.sum(hidden * dvec, axis=1, keepdims=True)
        dhidden = (rscale * root * (dvec - hidden * (rscale * rscale * inner * (1.0 / width)))).astype(bf16)
        for part, ref in enumerate(outs):
            ref[pl.ds(level * size, size)] = dhidden[part * size : (part + 1) * size]


def coordinate(bits):
    return sum(((lax.axis_index(axis) >> level) & 1) << k for k, (axis, level) in enumerate(reversed(bits)))


def cut(blocks, bits, refs):
    size = refs[0].shape[0]
    for step, ref in enumerate(refs):
        ref[...] = blocks[pl.ds((coordinate(bits) ^ step) * size, size)].astype(ref.dtype)


def share_kernel(order, bits, count, *refs):
    values, (*refs, blocks) = refs[:count], refs[count:]
    embed, dhidden = (jnp.concatenate([ref[...] for ref in half], axis=0) for half in (values[: count // 2], values[count // 2 :]))
    share = dot(embed, dhidden, 0, 0)
    size = blocks.shape[1]
    for spot, block in enumerate(order):
        blocks[spot] = share[block * size : (block + 1) * size]
    cut(blocks, bits, refs)


def stage_kernel(bits, count, *refs):
    came, (*refs, blocks) = refs[:count], refs[count:]
    blocks[...] = sum(ref[...].astype(f32) for ref in came)
    cut(blocks, bits, refs)


def last_kernel(*refs):
    *came, total_ref = refs
    total_ref[...] = sum(ref[...].astype(f32) for ref in came)[0]


def row_kernel(weight_ref, *refs):
    *incoming, drow_ref = refs
    drow_ref[...] = dot(jnp.concatenate([ref[...] for ref in incoming], axis=0), weight_ref[...], 1, 1).astype(bf16)


def table_kernel(sizes, low_hot_ref, block_ref, drow_ref, table_grad_hbm, ready, sems):
    copies, start = [], 0
    for g, size in enumerate(sizes):
        here = pl.ds(start, size)
        picks = [
            jnp.where(block_ref[...] == jnp.bfloat16(k), low_hot_ref[...], jnp.bfloat16(0))
            for k in range(start // BLOCK, (start + size) // BLOCK)
        ]
        ready[here] = dot(jnp.concatenate(picks, axis=0), drow_ref[...]).astype(bf16)
        copy = pltpu.make_async_copy(ready.at[here], table_grad_hbm.at[here], sems.at[g])
        copy.start()
        copies.append(copy)
        start += size
    for copy in copies:
        copy.wait()


def params(mib):
    return pltpu.CompilerParams(vmem_limit_bytes=mib * 1024 * 1024)


def cost(flops, bytes_accessed=1 << 20):
    return pl.CostEstimate(flops=flops, bytes_accessed=bytes_accessed, transcendentals=0)


def call(kernel, outs, *args, flops=0, scratch=(), mib=16, free=False):
    return pl.pallas_call(
        kernel,
        out_shape=[jax.ShapeDtypeStruct(shape, dtype) for shape, dtype in outs],
        scratch_shapes=scratch,
        compiler_params=params(mib),
        cost_estimate=cost(flops, 0 if free else 1 << 20),
    )(*args)


def swap(value, mask):
    devices = lax.axis_size("batch") * lax.axis_size("item")
    return lax.ppermute(value, ("batch", "item"), [(k, k ^ mask) for k in range(devices)])


def bits_of(axis):
    return [(axis, level) for level in range(log2(lax.axis_size(axis)))]


def mask_of(bits):
    return sum((lax.axis_size("item") if axis == "batch" else 1) << level for axis, level in bits)


def reduce_scatter(fetched, dhidden, drow):
    width = dhidden[0].shape[1]
    n_item, devices = lax.axis_size("item"), lax.axis_size("batch") * lax.axis_size("item")
    part = width // devices
    close = log2(len(dhidden))
    batch_bits, item_bits = bits_of("batch"), bits_of("item")
    stages = [batch_bits[:1], batch_bits[1:], item_bits[:close], item_bits[close:]]
    bits = sum(stages, [])
    order = []
    for spot in range(devices):
        at = {"batch": 0, "item": 0}
        for k, (axis, level) in enumerate(bits):
            at[axis] |= (spot >> (len(bits) - 1 - k) & 1) << level
        order.append(at["batch"] * n_item + at["item"])
    left, values = devices, [*fetched, *dhidden]
    for k, stage in enumerate(stages):
        whole, left = left, left >> len(stage)
        masks = [
            mask_of([bit for j, bit in enumerate(reversed(stage)) if step >> j & 1]) for step in range(1, 1 << len(stage))
        ]
        sent = f32 if k == len(stages) - 1 else bf16
        count = len(values)
        kernel = functools.partial(stage_kernel, stage, count) if k else functools.partial(share_kernel, order, stage, count)
        kept, *sends = call(
            kernel,
            [((left, part, width), f32)] + [((left, part, width), sent)] * len(masks),
            *values,
            scratch=[pltpu.VMEM((whole, part, width), f32)],
            free=True,
        )
        values = [kept] + [swap(value, mask) for mask, value in zip(masks, sends)]
        if k == 2:
            values, drow = lax.optimization_barrier((values, drow))
    return values, drow


def local(user_vectors, item_table, tower_weight, item_owner, item_row):
    n, width = user_vectors.shape
    rows = item_table.shape[0]
    n_batch, n_item = lax.axis_size("batch"), lax.axis_size("item")
    devices = n_batch * n_item
    near = min(4, n_item)
    levels = n_item // near
    slots = 2 * n // devices
    total = devices * slots
    size = total // near
    sizes = [rows // 2, rows // 4, rows // 8, rows // 8]

    far = [batch * n_item for batch in range(2, n_batch, 2)]
    users = {0: user_vectors}
    for mask in [near << k for k in range(log2(levels))] + far:
        users[mask] = swap(user_vectors, mask)

    (request,) = call(
        functools.partial(request_kernel, near),
        [((devices, (1 + near) * slots), i32)],
        jnp.stack([item_owner.reshape(n), item_row]),
        flops=1 << 34,
    )
    asked = lax.all_to_all(request, ("batch", "item"), split_axis=0, concat_axis=0, tiled=True)
    early = list(users)
    asked, *values = lax.optimization_barrier((asked, *users.values()))
    users = dict(zip(early, values))

    for level in range(1, levels):
        if near * level not in users:
            top = 1 << log2(level)
            users[near * level] = swap(users[near * (level - top)], near * top)
        for mask in far:
            users[mask + near * level] = swap(users[near * level], mask)

    def fetch(parts):
        return call(
            functools.partial(fetch_kernel, parts, near, n_batch),
            [((size, width), bf16)] * len(parts),
            asked,
            item_table,
            flops=2 * size * len(parts) * rows * width,
        )

    fetched = {}
    for parts in [[near - 1], list(range(1, near - 1)), [0]]:
        close = {mask: users[mask] for mask in [0, *far]}
        (asked, close), *values = lax.optimization_barrier(((asked, close), *fetch(parts)))
        users |= close if 0 not in parts else {}
        for part, value in zip(parts, values):
            fetched[part] = swap(value, part) if part else value
    fetched = [fetched[part] for part in range(near)]

    for mask in [0, *far]:
        users[mask + n_item] = swap(users[mask], n_item)

    def group(level):
        return [users[near * level + batch * n_item] for batch in range(n_batch)]

    group_outs = [((n_batch * n, width), bf16), ((total // levels, width), bf16)]
    place, low_hot, block, *first = call(
        functools.partial(prepare_kernel, near, n_batch),
        [((total, 1), i32)] + [((BLOCK, total), bf16)] * 2 + group_outs,
        asked,
        *group(0),
        free=True,
    )
    late = {mask: users[mask] for mask in users if mask & (n_item - near)}
    place, late = lax.optimization_barrier((place, late))
    users |= late | {mask + n_item: swap(late[mask], n_item) for mask in late}
    units, owns = zip(
        first,
        *[
            call(functools.partial(users_kernel, level, near), group_outs, place, *group(level), free=True)
            for level in range(1, levels)
        ],
    )
    hidden = call(
        functools.partial(hidden_kernel, levels),
        [((total, width), f32), ((total, 1), f32), ((total, width), bf16)],
        tower_weight,
        *fetched,
        flops=1 << 34,
    )
    dhidden = call(
        functools.partial(main_kernel, levels),
        [((size, width), bf16)] * near,
        *hidden,
        *units,
        *owns,
        flops=1 << 31,
        mib=40,
    )
    incoming = [swap(dhidden[part], part) for part in range(1, near)]
    (drow,) = call(row_kernel, [((total, width), bf16)], tower_weight, dhidden[0], *incoming, free=True)
    terms, drow = reduce_scatter(fetched, dhidden, drow)
    table_grad = pl.pallas_call(
        functools.partial(table_kernel, sizes),
        out_specs=pl.BlockSpec(memory_space=pl.ANY),
        out_shape=jax.ShapeDtypeStruct((rows, width), bf16),
        scratch_shapes=[pltpu.VMEM((rows, width), bf16), pltpu.SemaphoreType.DMA((len(sizes),))],
        compiler_params=params(16),
        cost_estimate=cost(2 * total * rows * width, 2 * rows * width),
    )(low_hot, block, drow)
    table_grad, *terms = lax.optimization_barrier((table_grad, *terms))
    (weight_grad,) = call(last_kernel, [((width // devices, width), f32)], *terms)
    return (table_grad, weight_grad)


def solution(mesh):
    return jax.shard_map(
        local,
        mesh=mesh,
        in_specs=(
            P(("batch", "item"), None),
            P(("batch", "item"), None),
            P(),
            P(("batch", "item"), None),
            P(("batch", "item")),
        ),
        out_specs=(P(("batch", "item"), None), P(("batch", "item"), None)),
        check_vma=False,
    )
```

```python
import functools

import jax
import jax.numpy as jnp
from jax import lax
from jax.experimental import pallas as pl
from jax.experimental.pallas import tpu as pltpu
from jax.sharding import PartitionSpec as P

epsilon = 1e-06
score_scale = 60.0
cauchy_scale = 4.0
f32 = jnp.float32
bf16 = jnp.bfloat16
i32 = jnp.int32
BLOCK = 256


def iota(shape, dim):
    return lax.broadcasted_iota(i32, shape, dim)


def hot(mask):
    return jnp.where(mask, 1.0, 0.0).astype(bf16)


def dot(a, b, a_dim=1, b_dim=0):
    return lax.dot_general(a, b, (((a_dim,), (b_dim,)), ((), ())), preferred_element_type=f32)


def halves(value):
    return (value >> 8).astype(f32), (value & 255).astype(f32)


def position():
    return lax.axis_index("batch") * lax.axis_size("item") + lax.axis_index("item")


def log2(value):
    return value.bit_length() - 1


def request_kernel(near, named_ref, request_ref):
    devices, lanes = request_ref.shape
    slots = lanes // (1 + near)
    n = named_ref.shape[1]
    owner, row = named_ref[0:1], named_ref[1:2]
    device = iota((devices, n), 0)
    named = owner == device
    count = dot(hot(named), hot(iota((n, n), 0) <= iota((n, n), 1)))
    rank = jnp.sum(jnp.where(named, count, 0.0), axis=0, keepdims=True).astype(i32) - 1
    in_slot = hot(rank == iota((slots, n), 0))
    which = iota((1, n), 1)
    for k, (value, mask) in enumerate([(row, 0)] + [(which, mask) for mask in range(near)]):
        high, low = halves(value + 1)
        here = (owner ^ mask) == device
        high = dot(jnp.where(here, high, 0.0).astype(bf16), in_slot, 1, 1)
        low = dot(jnp.where(here, low, 0.0).astype(bf16), in_slot, 1, 1)
        request_ref[:, k * slots : (k + 1) * slots] = (high * 256.0 + low).astype(i32) - 1


def asker_of(spot, part, near, n_batch, slots):
    batch = (spot >> log2(slots)) & (n_batch - 1)
    level = spot >> log2(slots * n_batch)
    return position() ^ (batch * lax.axis_size("item") + level * near + part)


def slot_column(asked, part, near, n_batch):
    devices, slots = asked.shape
    total = devices * slots // near
    asker = asker_of(iota((total, devices), 0), part, near, n_batch, slots)
    pick = hot(asker == iota((total, devices), 1))
    high, low = halves(asked)
    value = dot(pick, high.astype(bf16)) * 256.0 + dot(pick, low.astype(bf16))
    mine = (iota((total, slots), 0) & (slots - 1)) == iota((total, slots), 1)
    return jnp.sum(jnp.where(mine, value, 0.0), axis=1, keepdims=True)


def slot_line(asked, near, n_batch):
    devices, slots = asked.shape
    total = devices * slots
    pick = hot((iota((slots, total), 1) & (slots - 1)) == iota((slots, total), 0))
    high, low = halves(asked)
    value = dot(high.astype(bf16), pick) * 256.0 + dot(low.astype(bf16), pick)
    spot = iota((devices, total), 1)
    asker = asker_of(spot & (total // near - 1), spot >> log2(total // near), near, n_batch, slots)
    return jnp.sum(jnp.where(asker == iota((devices, total), 0), value, 0.0), axis=0, keepdims=True)


def parts_of(value):
    return value >> 8, value & 255


def fetch_kernel(parts, near, n_batch, asked_ref, table_ref, *found):
    slots = asked_ref.shape[1] // (1 + near)
    asked = asked_ref[:, :slots]
    column = jnp.concatenate([slot_column(asked, part, near, n_batch) for part in parts], axis=0)
    block, low = parts_of(column.astype(i32))
    total = block.shape[0]
    low_hot = hot(low == iota((total, BLOCK), 1))
    block = jnp.broadcast_to(block.astype(f32), (total, BLOCK)).astype(bf16)
    picks = [
        jnp.where(block == jnp.bfloat16(k), low_hot, jnp.bfloat16(0)) for k in range(table_ref.shape[0] // BLOCK)
    ]
    rows = dot(jnp.concatenate(picks, axis=1), table_ref[...]).astype(bf16)
    size = total // len(found)
    for k, ref in enumerate(found):
        ref[...] = rows[k * size : (k + 1) * size]


def prepare_kernel(near, n_batch, asked_ref, *refs):
    *users, place_ref, low_hot_ref, block_ref, unit_ref, own_ref = refs
    n = users[0].shape[0]
    slots = asked_ref.shape[1] // (1 + near)
    size = place_ref.shape[0] // near
    batch = (iota((size, 1), 0) >> log2(slots)) & (n_batch - 1)
    for part in range(near):
        asked = asked_ref[:, (1 + part) * slots : (2 + part) * slots]
        which = slot_column(asked, 0, near, n_batch).astype(i32)
        place_ref[pl.ds(part * size, size)] = jnp.where(which < 0, -1, batch * n + which)
    block, low = parts_of(slot_line(asked_ref[:, :slots], near, n_batch).astype(i32))
    low_hot_ref[...] = hot(low == iota(low_hot_ref.shape, 0))
    block_ref[...] = jnp.broadcast_to(block.astype(f32), block_ref.shape).astype(bf16)
    users_kernel(0, near, place_ref, *users, unit_ref, own_ref)


def users_kernel(level, near, place_ref, *refs):
    *users, unit_ref, own_ref = refs
    n, width = users[0].shape
    for k, ref in enumerate(users):
        value = ref[...].astype(f32)
        mean = jnp.mean(value * value, axis=1, keepdims=True)
        unit_ref[pl.ds(k * n, n)] = (value * lax.rsqrt(mean + epsilon) * (1.0 / width**0.5)).astype(bf16)
    step = place_ref.shape[0] // near
    size = own_ref.shape[0] // near
    place = jnp.concatenate([place_ref[pl.ds(k * step + level * size, size)] for k in range(near)], axis=0)
    own_ref[...] = dot(hot(place == iota((place.shape[0], unit_ref.shape[0]), 1)), unit_ref[...]).astype(bf16)


def hidden_kernel(levels, weight_ref, *refs):
    *fetched, hidden_ref, rscale_ref, item_ref = refs
    width = weight_ref.shape[0]
    size = fetched[0].shape[0] // levels
    for level in range(levels):
        embed = jnp.concatenate([ref[pl.ds(level * size, size)] for ref in fetched], axis=0)
        here = pl.ds(level * embed.shape[0], embed.shape[0])
        hidden = dot(embed, weight_ref[...])
        rscale = lax.rsqrt(jnp.mean(hidden * hidden, axis=1, keepdims=True) + epsilon)
        hidden_ref[here] = hidden
        rscale_ref[here] = rscale
        item_ref[here] = (hidden * (rscale * (1.0 / width**0.5))).astype(bf16)


def main_kernel(levels, hidden_ref, rscale_ref, item_ref, *refs):
    units, owns, outs = refs[:levels], refs[levels : 2 * levels], refs[2 * levels :]
    total, width = hidden_ref.shape
    size = outs[0].shape[0] // levels
    root = 1.0 / width**0.5
    for level in range(levels):
        here = pl.ds(level * (total // levels), total // levels)
        hidden, rscale, item_vec = hidden_ref[here], rscale_ref[here], item_ref[here]
        unit = units[level][...]
        expo = jnp.exp(dot(item_vec, unit, 1, 1) * score_scale)
        sums = jnp.sum(expo, axis=1, keepdims=True)
        mixed = dot(expo.astype(bf16), unit)
        own = owns[level][...].astype(f32)
        positive = jnp.sum(item_vec.astype(f32) * own, axis=1, keepdims=True) * score_scale
        xent = jnp.log(sums) - positive
        cweight = 1.0 / (1.0 + xent * (1.0 / cauchy_scale))
        dvec = (cweight * score_scale) * (mixed * (1.0 / sums) - own)
        inner = jnp.sum(hidden * dvec, axis=1, keepdims=True)
        dhidden = (rscale * root * (dvec - hidden * (rscale * rscale * inner * (1.0 / width)))).astype(bf16)
        for part, ref in enumerate(outs):
            ref[pl.ds(level * size, size)] = dhidden[part * size : (part + 1) * size]


def coordinate(bits):
    return sum(((lax.axis_index(axis) >> level) & 1) << k for k, (axis, level) in enumerate(reversed(bits)))


def cut(blocks, bits, refs):
    size = refs[0].shape[0]
    for step, ref in enumerate(refs):
        ref[...] = blocks[pl.ds((coordinate(bits) ^ step) * size, size)].astype(ref.dtype)


def share_kernel(order, bits, count, *refs):
    values, (*refs, blocks) = refs[:count], refs[count:]
    embed, dhidden = (jnp.concatenate([ref[...] for ref in half], axis=0) for half in (values[: count // 2], values[count // 2 :]))
    share = dot(embed, dhidden, 0, 0)
    size = blocks.shape[1]
    for spot, block in enumerate(order):
        blocks[spot] = share[block * size : (block + 1) * size]
    cut(blocks, bits, refs)


def stage_kernel(bits, count, *refs):
    came, (*refs, blocks) = refs[:count], refs[count:]
    blocks[...] = sum(ref[...].astype(f32) for ref in came)
    cut(blocks, bits, refs)


def last_kernel(*refs):
    *came, total_ref = refs
    total_ref[...] = sum(ref[...].astype(f32) for ref in came)[0]


def row_kernel(weight_ref, *refs):
    *incoming, drow_ref = refs
    drow_ref[...] = dot(jnp.concatenate([ref[...] for ref in incoming], axis=0), weight_ref[...], 1, 1).astype(bf16)


def table_kernel(sizes, low_hot_ref, block_ref, drow_ref, table_grad_hbm, ready, sems):
    copies, start = [], 0
    for g, size in enumerate(sizes):
        here = pl.ds(start, size)
        picks = [
            jnp.where(block_ref[...] == jnp.bfloat16(k), low_hot_ref[...], jnp.bfloat16(0))
            for k in range(start // BLOCK, (start + size) // BLOCK)
        ]
        ready[here] = dot(jnp.concatenate(picks, axis=0), drow_ref[...]).astype(bf16)
        copy = pltpu.make_async_copy(ready.at[here], table_grad_hbm.at[here], sems.at[g])
        copy.start()
        copies.append(copy)
        start += size
    for copy in copies:
        copy.wait()


def params(mib):
    return pltpu.CompilerParams(vmem_limit_bytes=mib * 1024 * 1024)


def cost(flops, bytes_accessed=1 << 20):
    return pl.CostEstimate(flops=flops, bytes_accessed=bytes_accessed, transcendentals=0)


def call(kernel, outs, *args, flops=0, scratch=(), mib=16, free=False):
    return pl.pallas_call(
        kernel,
        out_shape=[jax.ShapeDtypeStruct(shape, dtype) for shape, dtype in outs],
        scratch_shapes=scratch,
        compiler_params=params(mib),
        cost_estimate=cost(flops, 0 if free else 1 << 20),
    )(*args)


def swap(value, mask):
    devices = lax.axis_size("batch") * lax.axis_size("item")
    return lax.ppermute(value, ("batch", "item"), [(k, k ^ mask) for k in range(devices)])


def bits_of(axis):
    return [(axis, level) for level in range(log2(lax.axis_size(axis)))]


def mask_of(bits):
    return sum((lax.axis_size("item") if axis == "batch" else 1) << level for axis, level in bits)


def reduce_scatter(fetched, dhidden, drow):
    width = dhidden[0].shape[1]
    n_item, devices = lax.axis_size("item"), lax.axis_size("batch") * lax.axis_size("item")
    part = width // devices
    close = log2(len(dhidden))
    batch_bits, item_bits = bits_of("batch"), bits_of("item")
    stages = [batch_bits[:1], batch_bits[1:], item_bits[:close], item_bits[close:]]
    bits = sum(stages, [])
    order = []
    for spot in range(devices):
        at = {"batch": 0, "item": 0}
        for k, (axis, level) in enumerate(bits):
            at[axis] |= (spot >> (len(bits) - 1 - k) & 1) << level
        order.append(at["batch"] * n_item + at["item"])
    left, values = devices, [*fetched, *dhidden]
    for k, stage in enumerate(stages):
        whole, left = left, left >> len(stage)
        masks = [
            mask_of([bit for j, bit in enumerate(reversed(stage)) if step >> j & 1]) for step in range(1, 1 << len(stage))
        ]
        sent = f32 if k == len(stages) - 1 else bf16
        count = len(values)
        kernel = functools.partial(stage_kernel, stage, count) if k else functools.partial(share_kernel, order, stage, count)
        kept, *sends = call(
            kernel,
            [((left, part, width), f32)] + [((left, part, width), sent)] * len(masks),
            *values,
            scratch=[pltpu.VMEM((whole, part, width), f32)],
            free=True,
        )
        values = [kept] + [swap(value, mask) for mask, value in zip(masks, sends)]
        if k == 2:
            values, drow = lax.optimization_barrier((values, drow))
    return values, drow


def local(user_vectors, item_table, tower_weight, item_owner, item_row):
    n, width = user_vectors.shape
    rows = item_table.shape[0]
    n_batch, n_item = lax.axis_size("batch"), lax.axis_size("item")
    devices = n_batch * n_item
    near = min(4, n_item)
    levels = n_item // near
    slots = 2 * n // devices
    total = devices * slots
    size = total // near
    sizes = [rows // 8] + [rows // 4] * 3 + [rows // 8]

    far = [batch * n_item for batch in range(2, n_batch, 2)]
    users = {0: user_vectors}
    for mask in [near << k for k in range(log2(levels))] + far:
        users[mask] = swap(user_vectors, mask)

    (request,) = call(
        functools.partial(request_kernel, near),
        [((devices, (1 + near) * slots), i32)],
        jnp.stack([item_owner.reshape(n), item_row]),
        flops=1 << 34,
    )
    asked = lax.all_to_all(request, ("batch", "item"), split_axis=0, concat_axis=0, tiled=True)
    early = list(users)
    asked, *values = lax.optimization_barrier((asked, *users.values()))
    users = dict(zip(early, values))

    for level in range(1, levels):
        if near * level not in users:
            top = 1 << log2(level)
            users[near * level] = swap(users[near * (level - top)], near * top)
        for mask in far:
            users[mask + near * level] = swap(users[near * level], mask)

    def fetch(parts):
        return call(
            functools.partial(fetch_kernel, parts, near, n_batch),
            [((size, width), bf16)] * len(parts),
            asked,
            item_table,
            flops=2 * size * len(parts) * rows * width,
        )

    fetched = {}
    for parts in [[near - 1], list(range(1, near - 1)), [0]]:
        asked, *values = lax.optimization_barrier((asked, *fetch(parts)))
        for part, value in zip(parts, values):
            fetched[part] = swap(value, part) if part else value
    fetched = [fetched[part] for part in range(near)]

    for mask in [0, *far]:
        users[mask + n_item] = swap(users[mask], n_item)

    def group(level):
        return [users[near * level + batch * n_item] for batch in range(n_batch)]

    group_outs = [((n_batch * n, width), bf16), ((total // levels, width), bf16)]
    place, low_hot, block, *first = call(
        functools.partial(prepare_kernel, near, n_batch),
        [((total, 1), i32)] + [((BLOCK, total), bf16)] * 2 + group_outs,
        asked,
        *group(0),
        free=True,
    )
    late = {mask: users[mask] for mask in users if mask & (n_item - near)}
    place, late = lax.optimization_barrier((place, late))
    users |= late | {mask + n_item: swap(late[mask], n_item) for mask in late}
    units, owns = zip(
        first,
        *[
            call(functools.partial(users_kernel, level, near), group_outs, place, *group(level), free=True)
            for level in range(1, levels)
        ],
    )
    hidden = call(
        functools.partial(hidden_kernel, levels),
        [((total, width), f32), ((total, 1), f32), ((total, width), bf16)],
        tower_weight,
        *fetched,
        flops=1 << 34,
    )
    dhidden = call(
        functools.partial(main_kernel, levels),
        [((size, width), bf16)] * near,
        *hidden,
        *units,
        *owns,
        flops=1 << 31,
        mib=40,
    )
    incoming = [swap(dhidden[part], part) for part in range(1, near)]
    (drow,) = call(row_kernel, [((total, width), bf16)], tower_weight, dhidden[0], *incoming, free=True)
    terms, drow = reduce_scatter(fetched, dhidden, drow)
    table_grad = pl.pallas_call(
        functools.partial(table_kernel, sizes),
        out_specs=pl.BlockSpec(memory_space=pl.ANY),
        out_shape=jax.ShapeDtypeStruct((rows, width), bf16),
        scratch_shapes=[pltpu.VMEM((rows, width), bf16), pltpu.SemaphoreType.DMA((len(sizes),))],
        compiler_params=params(16),
        cost_estimate=cost(2 * total * rows * width, 2 * rows * width),
    )(low_hot, block, drow)
    table_grad, *terms = lax.optimization_barrier((table_grad, *terms))
    (weight_grad,) = call(last_kernel, [((width // devices, width), f32)], *terms)
    return (table_grad, weight_grad)


def solution(mesh):
    return jax.shard_map(
        local,
        mesh=mesh,
        in_specs=(
            P(("batch", "item"), None),
            P(("batch", "item"), None),
            P(),
            P(("batch", "item"), None),
            P(("batch", "item")),
        ),
        out_specs=(P(("batch", "item"), None), P(("batch", "item"), None)),
        check_vma=False,
    )
```

```python
import functools

import jax
import jax.numpy as jnp
from jax import lax
from jax.experimental import pallas as pl
from jax.experimental.pallas import tpu as pltpu
from jax.sharding import PartitionSpec as P

epsilon = 1e-06
score_scale = 60.0
cauchy_scale = 4.0
f32 = jnp.float32
bf16 = jnp.bfloat16
i32 = jnp.int32
BLOCK = 256


def iota(shape, dim):
    return lax.broadcasted_iota(i32, shape, dim)


def hot(mask):
    return jnp.where(mask, 1.0, 0.0).astype(bf16)


def dot(a, b, a_dim=1, b_dim=0):
    return lax.dot_general(a, b, (((a_dim,), (b_dim,)), ((), ())), preferred_element_type=f32)


def halves(value):
    return (value >> 8).astype(f32), (value & 255).astype(f32)


def position():
    return lax.axis_index("batch") * lax.axis_size("item") + lax.axis_index("item")


def log2(value):
    return value.bit_length() - 1


def request_kernel(near, named_ref, stay_ref, cross_ref):
    half, lanes = stay_ref.shape
    devices, n_half = 2 * half, lax.axis_size("item") // 2
    mine = lax.axis_index("item") & n_half
    slots = lanes // (1 + near)
    n = named_ref.shape[1]
    owner, row = named_ref[0:1], named_ref[1:2]
    spot = iota((devices, n), 0)
    place = spot & (half - 1)
    device = (((place >> log2(n_half)) << log2(2 * n_half)) | (place & (n_half - 1)) | mine) ^ ((spot >> log2(half)) * n_half)
    named = owner == device
    count = dot(hot(named), hot(iota((n, n), 0) <= iota((n, n), 1)))
    rank = jnp.sum(jnp.where(named, count, 0.0), axis=0, keepdims=True).astype(i32) - 1
    in_slot = hot(rank == iota((slots, n), 0))
    which = iota((1, n), 1)
    for k, (value, mask) in enumerate([(row, 0)] + [(which, mask) for mask in range(near)]):
        high, low = halves(value + 1)
        here = (owner ^ mask) == device
        high = dot(jnp.where(here, high, 0.0).astype(bf16), in_slot, 1, 1)
        low = dot(jnp.where(here, low, 0.0).astype(bf16), in_slot, 1, 1)
        value = (high * 256.0 + low).astype(i32) - 1
        stay_ref[:, k * slots : (k + 1) * slots] = value[:half]
        cross_ref[:, k * slots : (k + 1) * slots] = value[half:]


def pair_kernel(stay_ref, came_ref, pair_ref):
    for k in range(pair_ref.shape[0]):
        pair_ref[k, 0:1] = stay_ref[k : k + 1]
        pair_ref[k, 1:2] = came_ref[k : k + 1]


def asker_of(spot, part, near, n_batch, slots):
    batch = (spot >> log2(slots)) & (n_batch - 1)
    level = spot >> log2(slots * n_batch)
    n_item = lax.axis_size("item")
    asker = position() ^ (batch * n_item + level * near + part)
    low = asker & (n_item // 2 - 1)
    cross = ((asker ^ lax.axis_index("item")) >> log2(n_item // 2)) & 1
    return ((((asker >> log2(n_item)) << log2(n_item // 2)) | low) << 1) | cross


def slot_column(asked, part, near, n_batch):
    devices, slots = asked.shape
    total = devices * slots // near
    asker = asker_of(iota((total, devices), 0), part, near, n_batch, slots)
    pick = hot(asker == iota((total, devices), 1))
    high, low = halves(asked)
    value = dot(pick, high.astype(bf16)) * 256.0 + dot(pick, low.astype(bf16))
    mine = (iota((total, slots), 0) & (slots - 1)) == iota((total, slots), 1)
    return jnp.sum(jnp.where(mine, value, 0.0), axis=1, keepdims=True)


def slot_line(asked, near, n_batch):
    devices, slots = asked.shape
    total = devices * slots
    pick = hot((iota((slots, total), 1) & (slots - 1)) == iota((slots, total), 0))
    high, low = halves(asked)
    value = dot(high.astype(bf16), pick) * 256.0 + dot(low.astype(bf16), pick)
    spot = iota((devices, total), 1)
    asker = asker_of(spot & (total // near - 1), spot >> log2(total // near), near, n_batch, slots)
    return jnp.sum(jnp.where(asker == iota((devices, total), 0), value, 0.0), axis=0, keepdims=True)


def parts_of(value):
    return value >> 8, value & 255


def fetch_kernel(parts, near, n_batch, asked_ref, table_ref, *found):
    slots = asked_ref.shape[1] // (1 + near)
    asked = asked_ref[:, :slots]
    column = jnp.concatenate([slot_column(asked, part, near, n_batch) for part in parts], axis=0)
    block, low = parts_of(column.astype(i32))
    total = block.shape[0]
    low_hot = hot(low == iota((total, BLOCK), 1))
    block = jnp.broadcast_to(block.astype(f32), (total, BLOCK)).astype(bf16)
    picks = [
        jnp.where(block == jnp.bfloat16(k), low_hot, jnp.bfloat16(0)) for k in range(table_ref.shape[0] // BLOCK)
    ]
    rows = dot(jnp.concatenate(picks, axis=1), table_ref[...]).astype(bf16)
    size = total // len(found)
    for k, ref in enumerate(found):
        ref[...] = rows[k * size : (k + 1) * size]


def prepare_kernel(near, n_batch, asked_ref, *refs):
    *users, place_ref, low_hot_ref, block_ref, unit_ref, own_ref = refs
    n = users[0].shape[0]
    slots = asked_ref.shape[1] // (1 + near)
    size = place_ref.shape[0] // near
    batch = (iota((size, 1), 0) >> log2(slots)) & (n_batch - 1)
    for part in range(near):
        asked = asked_ref[:, (1 + part) * slots : (2 + part) * slots]
        which = slot_column(asked, 0, near, n_batch).astype(i32)
        place_ref[pl.ds(part * size, size)] = jnp.where(which < 0, -1, batch * n + which)
    block, low = parts_of(slot_line(asked_ref[:, :slots], near, n_batch).astype(i32))
    low_hot_ref[...] = hot(low == iota(low_hot_ref.shape, 0))
    block_ref[...] = jnp.broadcast_to(block.astype(f32), block_ref.shape).astype(bf16)
    users_kernel(0, near, place_ref, *users, unit_ref, own_ref)


def users_kernel(level, near, place_ref, *refs):
    *users, unit_ref, own_ref = refs
    n, width = users[0].shape
    for k, ref in enumerate(users):
        value = ref[...].astype(f32)
        mean = jnp.mean(value * value, axis=1, keepdims=True)
        unit_ref[pl.ds(k * n, n)] = (value * lax.rsqrt(mean + epsilon) * (1.0 / width**0.5)).astype(bf16)
    step = place_ref.shape[0] // near
    size = own_ref.shape[0] // near
    place = jnp.concatenate([place_ref[pl.ds(k * step + level * size, size)] for k in range(near)], axis=0)
    own_ref[...] = dot(hot(place == iota((place.shape[0], unit_ref.shape[0]), 1)), unit_ref[...]).astype(bf16)


def hidden_kernel(levels, weight_ref, *refs):
    *fetched, hidden_ref, rscale_ref, item_ref = refs
    width = weight_ref.shape[0]
    size = fetched[0].shape[0] // levels
    for level in range(levels):
        embed = jnp.concatenate([ref[pl.ds(level * size, size)] for ref in fetched], axis=0)
        here = pl.ds(level * embed.shape[0], embed.shape[0])
        hidden = dot(embed, weight_ref[...])
        rscale = lax.rsqrt(jnp.mean(hidden * hidden, axis=1, keepdims=True) + epsilon)
        hidden_ref[here] = hidden
        rscale_ref[here] = rscale
        item_ref[here] = (hidden * (rscale * (1.0 / width**0.5))).astype(bf16)


def main_kernel(levels, hidden_ref, rscale_ref, item_ref, *refs):
    units, owns, outs = refs[:levels], refs[levels : 2 * levels], refs[2 * levels :]
    total, width = hidden_ref.shape
    size = outs[0].shape[0] // levels
    root = 1.0 / width**0.5
    for level in range(levels):
        here = pl.ds(level * (total // levels), total // levels)
        hidden, rscale, item_vec = hidden_ref[here], rscale_ref[here], item_ref[here]
        unit = units[level][...]
        expo = jnp.exp(dot(item_vec, unit, 1, 1) * score_scale)
        sums = jnp.sum(expo, axis=1, keepdims=True)
        mixed = dot(expo.astype(bf16), unit)
        own = owns[level][...].astype(f32)
        positive = jnp.sum(item_vec.astype(f32) * own, axis=1, keepdims=True) * score_scale
        xent = jnp.log(sums) - positive
        cweight = 1.0 / (1.0 + xent * (1.0 / cauchy_scale))
        dvec = (cweight * score_scale) * (mixed * (1.0 / sums) - own)
        inner = jnp.sum(hidden * dvec, axis=1, keepdims=True)
        dhidden = (rscale * root * (dvec - hidden * (rscale * rscale * inner * (1.0 / width)))).astype(bf16)
        for part, ref in enumerate(outs):
            ref[pl.ds(level * size, size)] = dhidden[part * size : (part + 1) * size]


def coordinate(bits):
    return sum(((lax.axis_index(axis) >> level) & 1) << k for k, (axis, level) in enumerate(reversed(bits)))


def cut(blocks, bits, refs):
    size = refs[0].shape[0]
    for step, ref in enumerate(refs):
        ref[...] = blocks[pl.ds((coordinate(bits) ^ step) * size, size)].astype(ref.dtype)


def share_kernel(order, bits, count, *refs):
    values, (*refs, blocks) = refs[:count], refs[count:]
    embed, dhidden = (jnp.concatenate([ref[...] for ref in half], axis=0) for half in (values[: count // 2], values[count // 2 :]))
    share = dot(embed, dhidden, 0, 0)
    size = blocks.shape[1]
    for spot, block in enumerate(order):
        blocks[spot] = share[block * size : (block + 1) * size]
    cut(blocks, bits, refs)


def stage_kernel(bits, count, *refs):
    came, (*refs, blocks) = refs[:count], refs[count:]
    blocks[...] = sum(ref[...].astype(f32) for ref in came)
    cut(blocks, bits, refs)


def last_kernel(*refs):
    *came, total_ref = refs
    total_ref[...] = sum(ref[...].astype(f32) for ref in came)[0]


def row_kernel(weight_ref, *refs):
    *incoming, drow_ref = refs
    drow_ref[...] = dot(jnp.concatenate([ref[...] for ref in incoming], axis=0), weight_ref[...], 1, 1).astype(bf16)


def table_kernel(sizes, low_hot_ref, block_ref, drow_ref, table_grad_hbm, ready, sems):
    copies, start = [], 0
    for g, size in enumerate(sizes):
        here = pl.ds(start, size)
        picks = [
            jnp.where(block_ref[...] == jnp.bfloat16(k), low_hot_ref[...], jnp.bfloat16(0))
            for k in range(start // BLOCK, (start + size) // BLOCK)
        ]
        ready[here] = dot(jnp.concatenate(picks, axis=0), drow_ref[...]).astype(bf16)
        copy = pltpu.make_async_copy(ready.at[here], table_grad_hbm.at[here], sems.at[g])
        copy.start()
        copies.append(copy)
        start += size
    for copy in copies:
        copy.wait()


def params(mib):
    return pltpu.CompilerParams(vmem_limit_bytes=mib * 1024 * 1024)


def cost(flops, bytes_accessed=1 << 20):
    return pl.CostEstimate(flops=flops, bytes_accessed=bytes_accessed, transcendentals=0)


def call(kernel, outs, *args, flops=0, scratch=(), mib=16, free=False):
    return pl.pallas_call(
        kernel,
        out_shape=[jax.ShapeDtypeStruct(shape, dtype) for shape, dtype in outs],
        scratch_shapes=scratch,
        compiler_params=params(mib),
        cost_estimate=cost(flops, 0 if free else 1 << 20),
    )(*args)


def swap(value, mask):
    devices = lax.axis_size("batch") * lax.axis_size("item")
    return lax.ppermute(value, ("batch", "item"), [(k, k ^ mask) for k in range(devices)])


def bits_of(axis):
    return [(axis, level) for level in range(log2(lax.axis_size(axis)))]


def mask_of(bits):
    return sum((lax.axis_size("item") if axis == "batch" else 1) << level for axis, level in bits)


def reduce_scatter(fetched, dhidden, drow):
    width = dhidden[0].shape[1]
    n_item, devices = lax.axis_size("item"), lax.axis_size("batch") * lax.axis_size("item")
    part = width // devices
    close = log2(len(dhidden))
    batch_bits, item_bits = bits_of("batch"), bits_of("item")
    stages = [batch_bits[:1], batch_bits[1:], item_bits[:close], item_bits[close:]]
    bits = sum(stages, [])
    order = []
    for spot in range(devices):
        at = {"batch": 0, "item": 0}
        for k, (axis, level) in enumerate(bits):
            at[axis] |= (spot >> (len(bits) - 1 - k) & 1) << level
        order.append(at["batch"] * n_item + at["item"])
    left, values = devices, [*fetched, *dhidden]
    for k, stage in enumerate(stages):
        whole, left = left, left >> len(stage)
        masks = [
            mask_of([bit for j, bit in enumerate(reversed(stage)) if step >> j & 1]) for step in range(1, 1 << len(stage))
        ]
        sent = f32 if k == len(stages) - 1 else bf16
        count = len(values)
        kernel = functools.partial(stage_kernel, stage, count) if k else functools.partial(share_kernel, order, stage, count)
        kept, *sends = call(
            kernel,
            [((left, part, width), f32)] + [((left, part, width), sent)] * len(masks),
            *values,
            scratch=[pltpu.VMEM((whole, part, width), f32)],
            free=True,
        )
        values = [kept] + [swap(value, mask) for mask, value in zip(masks, sends)]
        if k == 2:
            values, drow = lax.optimization_barrier((values, drow))
    return values, drow


def local(user_vectors, item_table, tower_weight, item_owner, item_row):
    n, width = user_vectors.shape
    rows = item_table.shape[0]
    n_batch, n_item = lax.axis_size("batch"), lax.axis_size("item")
    devices = n_batch * n_item
    near = min(4, n_item)
    levels = n_item // near
    slots = 2 * n // devices
    total = devices * slots
    size = total // near
    sizes = [rows // 8] + [rows // 4] * 3 + [rows // 8]

    far = [batch * n_item for batch in range(2, n_batch, 2)]
    steps = [near << k for k in range(log2(levels))]
    users = {mask: swap(user_vectors, mask) for mask in far}
    stay, cross = call(
        functools.partial(request_kernel, near),
        [((devices // 2, (1 + near) * slots), i32)] * 2,
        jnp.stack([item_owner.reshape(n), item_row]),
        flops=1 << 34,
    )
    came = swap(cross, n_item // 2)
    came, mine = lax.optimization_barrier((came, user_vectors))
    users |= {mask: swap(mine, mask) for mask in steps}
    (pair,) = call(pair_kernel, [((devices // 2, 2, (1 + near) * slots), i32)], stay, came, free=True)
    halves_of = [[k for k in range(devices) if bool(k & (n_item // 2)) == side] for side in (False, True)]
    asked = lax.all_to_all(
        pair, ("batch", "item"), split_axis=0, concat_axis=0, axis_index_groups=halves_of, tiled=True
    ).reshape(devices, (1 + near) * slots)
    asked, mine, *values = lax.optimization_barrier((asked, mine, *[users[mask] for mask in far]))
    users |= dict(zip(far, values)) | {0: mine}

    def fetch(parts):
        return call(
            functools.partial(fetch_kernel, parts, near, n_batch),
            [((size, width), bf16)] * len(parts),
            asked,
            item_table,
            flops=2 * size * len(parts) * rows * width,
        )

    fetched = {}
    for parts in [[near - 1], list(range(1, near - 1)), [0]]:
        asked, *values = lax.optimization_barrier((asked, *fetch(parts)))
        if 1 in parts:
            _, across = lax.optimization_barrier((values, [users[mask] for mask in steps]))
            users |= dict(zip(steps, across))
        for part, value in zip(parts, values):
            fetched[part] = swap(value, part) if part else value
    for level in range(1, levels):
        if near * level not in users:
            top = 1 << log2(level)
            users[near * level] = swap(users[near * (level - top)], near * top)
        for mask in far:
            users[mask + near * level] = swap(users[near * level], mask)
    fetched = [fetched[part] for part in range(near)]

    for mask in [0, *far]:
        users[mask + n_item] = swap(users[mask], n_item)

    def group(level):
        return [users[near * level + batch * n_item] for batch in range(n_batch)]

    group_outs = [((n_batch * n, width), bf16), ((total // levels, width), bf16)]
    place, low_hot, block, *first = call(
        functools.partial(prepare_kernel, near, n_batch),
        [((total, 1), i32)] + [((BLOCK, total), bf16)] * 2 + group_outs,
        asked,
        *group(0),
        free=True,
    )
    late = {mask: users[mask] for mask in users if mask & (n_item - near)}
    place, late = lax.optimization_barrier((place, late))
    users |= late | {mask + n_item: swap(late[mask], n_item) for mask in late}
    units, owns = zip(
        first,
        *[
            call(functools.partial(users_kernel, level, near), group_outs, place, *group(level), free=True)
            for level in range(1, levels)
        ],
    )
    hidden = call(
        functools.partial(hidden_kernel, levels),
        [((total, width), f32), ((total, 1), f32), ((total, width), bf16)],
        tower_weight,
        *fetched,
        flops=1 << 34,
    )
    dhidden = call(
        functools.partial(main_kernel, levels),
        [((size, width), bf16)] * near,
        *hidden,
        *units,
        *owns,
        flops=1 << 31,
        mib=40,
    )
    incoming = [swap(dhidden[part], part) for part in range(1, near)]
    (drow,) = call(row_kernel, [((total, width), bf16)], tower_weight, dhidden[0], *incoming, free=True)
    terms, drow = reduce_scatter(fetched, dhidden, drow)
    table_grad = pl.pallas_call(
        functools.partial(table_kernel, sizes),
        out_specs=pl.BlockSpec(memory_space=pl.ANY),
        out_shape=jax.ShapeDtypeStruct((rows, width), bf16),
        scratch_shapes=[pltpu.VMEM((rows, width), bf16), pltpu.SemaphoreType.DMA((len(sizes),))],
        compiler_params=params(16),
        cost_estimate=cost(2 * total * rows * width, 2 * rows * width),
    )(low_hot, block, drow)
    table_grad, *terms = lax.optimization_barrier((table_grad, *terms))
    (weight_grad,) = call(last_kernel, [((width // devices, width), f32)], *terms)
    return (table_grad, weight_grad)


def solution(mesh):
    return jax.shard_map(
        local,
        mesh=mesh,
        in_specs=(
            P(("batch", "item"), None),
            P(("batch", "item"), None),
            P(),
            P(("batch", "item"), None),
            P(("batch", "item")),
        ),
        out_specs=(P(("batch", "item"), None), P(("batch", "item"), None)),
        check_vma=False,
    )
```

```python
import functools

import jax
import jax.numpy as jnp
from jax import lax
from jax.experimental import pallas as pl
from jax.experimental.pallas import tpu as pltpu
from jax.sharding import PartitionSpec as P

epsilon = 1e-06
score_scale = 60.0
cauchy_scale = 4.0
f32 = jnp.float32
bf16 = jnp.bfloat16
i32 = jnp.int32
BLOCK = 256


def iota(shape, dim):
    return lax.broadcasted_iota(i32, shape, dim)


def hot(mask):
    return jnp.where(mask, 1.0, 0.0).astype(bf16)


def dot(a, b, a_dim=1, b_dim=0):
    return lax.dot_general(a, b, (((a_dim,), (b_dim,)), ((), ())), preferred_element_type=f32)


def halves(value):
    return (value >> 8).astype(f32), (value & 255).astype(f32)


def position():
    return lax.axis_index("batch") * lax.axis_size("item") + lax.axis_index("item")


def log2(value):
    return value.bit_length() - 1


def request_kernel(near, named_ref, request_ref):
    devices, lanes = request_ref.shape
    slots = lanes // (1 + near)
    n = named_ref.shape[1]
    owner, row = named_ref[0:1], named_ref[1:2]
    device = iota((devices, n), 0)
    named = owner == device
    count = dot(hot(named), hot(iota((n, n), 0) <= iota((n, n), 1)))
    rank = jnp.sum(jnp.where(named, count, 0.0), axis=0, keepdims=True).astype(i32) - 1
    in_slot = hot(rank == iota((slots, n), 0))
    which = iota((1, n), 1)
    for k, (value, mask) in enumerate([(row, 0)] + [(which, mask) for mask in range(near)]):
        high, low = halves(value + 1)
        here = (owner ^ mask) == device
        high = dot(jnp.where(here, high, 0.0).astype(bf16), in_slot, 1, 1)
        low = dot(jnp.where(here, low, 0.0).astype(bf16), in_slot, 1, 1)
        request_ref[:, k * slots : (k + 1) * slots] = (high * 256.0 + low).astype(i32) - 1


def asker_of(spot, part, near, n_batch, slots):
    batch = (spot >> log2(slots)) & (n_batch - 1)
    level = spot >> log2(slots * n_batch)
    return position() ^ (batch * lax.axis_size("item") + level * near + part)


def slot_column(asked, part, near, n_batch):
    devices, slots = asked.shape
    total = devices * slots // near
    asker = asker_of(iota((total, devices), 0), part, near, n_batch, slots)
    pick = hot(asker == iota((total, devices), 1))
    high, low = halves(asked)
    value = dot(pick, high.astype(bf16)) * 256.0 + dot(pick, low.astype(bf16))
    mine = (iota((total, slots), 0) & (slots - 1)) == iota((total, slots), 1)
    return jnp.sum(jnp.where(mine, value, 0.0), axis=1, keepdims=True)


def slot_line(asked, near, n_batch):
    devices, slots = asked.shape
    total = devices * slots
    pick = hot((iota((slots, total), 1) & (slots - 1)) == iota((slots, total), 0))
    high, low = halves(asked)
    value = dot(high.astype(bf16), pick) * 256.0 + dot(low.astype(bf16), pick)
    spot = iota((devices, total), 1)
    asker = asker_of(spot & (total // near - 1), spot >> log2(total // near), near, n_batch, slots)
    return jnp.sum(jnp.where(asker == iota((devices, total), 0), value, 0.0), axis=0, keepdims=True)


def parts_of(value):
    return value >> 8, value & 255


def fetch_kernel(parts, near, n_batch, asked_ref, table_ref, *found):
    slots = asked_ref.shape[1] // (1 + near)
    asked = asked_ref[:, :slots]
    column = jnp.concatenate([slot_column(asked, part, near, n_batch) for part in parts], axis=0)
    block, low = parts_of(column.astype(i32))
    total = block.shape[0]
    low_hot = hot(low == iota((total, BLOCK), 1))
    block = jnp.broadcast_to(block.astype(f32), (total, BLOCK)).astype(bf16)
    picks = [
        jnp.where(block == jnp.bfloat16(k), low_hot, jnp.bfloat16(0)) for k in range(table_ref.shape[0] // BLOCK)
    ]
    rows = dot(jnp.concatenate(picks, axis=1), table_ref[...]).astype(bf16)
    size = total // len(found)
    for k, ref in enumerate(found):
        ref[...] = rows[k * size : (k + 1) * size]


def prepare_kernel(near, n_batch, asked_ref, *refs):
    *users, place_ref, low_hot_ref, block_ref, unit_ref, own_ref = refs
    n = users[0].shape[0]
    slots = asked_ref.shape[1] // (1 + near)
    size = place_ref.shape[0] // near
    batch = (iota((size, 1), 0) >> log2(slots)) & (n_batch - 1)
    for part in range(near):
        asked = asked_ref[:, (1 + part) * slots : (2 + part) * slots]
        which = slot_column(asked, 0, near, n_batch).astype(i32)
        place_ref[pl.ds(part * size, size)] = jnp.where(which < 0, -1, batch * n + which)
    block, low = parts_of(slot_line(asked_ref[:, :slots], near, n_batch).astype(i32))
    low_hot_ref[...] = hot(low == iota(low_hot_ref.shape, 0))
    block_ref[...] = jnp.broadcast_to(block.astype(f32), block_ref.shape).astype(bf16)
    users_kernel(0, near, place_ref, *users, unit_ref, own_ref)


def users_kernel(level, near, place_ref, *refs):
    *users, unit_ref, own_ref = refs
    n, width = users[0].shape
    for k, ref in enumerate(users):
        value = ref[...].astype(f32)
        mean = jnp.mean(value * value, axis=1, keepdims=True)
        unit_ref[pl.ds(k * n, n)] = (value * lax.rsqrt(mean + epsilon) * (1.0 / width**0.5)).astype(bf16)
    step = place_ref.shape[0] // near
    size = own_ref.shape[0] // near
    place = jnp.concatenate([place_ref[pl.ds(k * step + level * size, size)] for k in range(near)], axis=0)
    own_ref[...] = dot(hot(place == iota((place.shape[0], unit_ref.shape[0]), 1)), unit_ref[...]).astype(bf16)


def hidden_kernel(levels, weight_ref, *refs):
    *fetched, hidden_ref, rscale_ref, item_ref = refs
    width = weight_ref.shape[0]
    size = fetched[0].shape[0] // levels
    for level in range(levels):
        embed = jnp.concatenate([ref[pl.ds(level * size, size)] for ref in fetched], axis=0)
        here = pl.ds(level * embed.shape[0], embed.shape[0])
        hidden = dot(embed, weight_ref[...])
        rscale = lax.rsqrt(jnp.mean(hidden * hidden, axis=1, keepdims=True) + epsilon)
        hidden_ref[here] = hidden
        rscale_ref[here] = rscale
        item_ref[here] = (hidden * (rscale * (1.0 / width**0.5))).astype(bf16)


def main_kernel(levels, hidden_ref, rscale_ref, item_ref, *refs):
    units, owns, outs = refs[:levels], refs[levels : 2 * levels], refs[2 * levels :]
    total, width = hidden_ref.shape
    size = outs[0].shape[0] // levels
    root = 1.0 / width**0.5
    for level in range(levels):
        here = pl.ds(level * (total // levels), total // levels)
        hidden, rscale, item_vec = hidden_ref[here], rscale_ref[here], item_ref[here]
        unit = units[level][...]
        expo = jnp.exp(dot(item_vec, unit, 1, 1) * score_scale)
        sums = jnp.sum(expo, axis=1, keepdims=True)
        mixed = dot(expo.astype(bf16), unit)
        own = owns[level][...].astype(f32)
        positive = jnp.sum(item_vec.astype(f32) * own, axis=1, keepdims=True) * score_scale
        xent = jnp.log(sums) - positive
        cweight = 1.0 / (1.0 + xent * (1.0 / cauchy_scale))
        dvec = (cweight * score_scale) * (mixed * (1.0 / sums) - own)
        inner = jnp.sum(hidden * dvec, axis=1, keepdims=True)
        dhidden = (rscale * root * (dvec - hidden * (rscale * rscale * inner * (1.0 / width)))).astype(bf16)
        for spot, ref in enumerate(outs):
            part = -spot % len(outs)
            ref[pl.ds(level * size, size)] = dhidden[part * size : (part + 1) * size]


def coordinate(bits):
    return sum(((lax.axis_index(axis) >> level) & 1) << k for k, (axis, level) in enumerate(reversed(bits)))


def cut(blocks, bits, refs):
    size = refs[0].shape[0]
    for step, ref in enumerate(refs):
        ref[...] = blocks[pl.ds((coordinate(bits) ^ step) * size, size)].astype(ref.dtype)


def share_kernel(order, bits, count, *refs):
    values, (*refs, blocks) = refs[:count], refs[count:]
    embed, dhidden = (jnp.concatenate([ref[...] for ref in half], axis=0) for half in (values[: count // 2], values[count // 2 :]))
    share = dot(embed, dhidden, 0, 0)
    size = blocks.shape[1]
    for spot, block in enumerate(order):
        blocks[spot] = share[block * size : (block + 1) * size]
    cut(blocks, bits, refs)


def stage_kernel(bits, count, *refs):
    came, (*refs, blocks) = refs[:count], refs[count:]
    blocks[...] = sum(ref[...].astype(f32) for ref in came)
    cut(blocks, bits, refs)


def last_kernel(*refs):
    *came, total_ref = refs
    total_ref[...] = sum(ref[...].astype(f32) for ref in came)[0]


def row_kernel(weight_ref, *refs):
    *incoming, drow_ref = refs
    drow_ref[...] = dot(jnp.concatenate([ref[...] for ref in incoming], axis=0), weight_ref[...], 1, 1).astype(bf16)


def table_kernel(sizes, low_hot_ref, block_ref, drow_ref, table_grad_hbm, ready, sems):
    copies, start = [], 0
    for g, size in enumerate(sizes):
        here = pl.ds(start, size)
        picks = [
            jnp.where(block_ref[...] == jnp.bfloat16(k), low_hot_ref[...], jnp.bfloat16(0))
            for k in range(start // BLOCK, (start + size) // BLOCK)
        ]
        ready[here] = dot(jnp.concatenate(picks, axis=0), drow_ref[...]).astype(bf16)
        copy = pltpu.make_async_copy(ready.at[here], table_grad_hbm.at[here], sems.at[g])
        copy.start()
        copies.append(copy)
        start += size
    for copy in copies:
        copy.wait()


def params(mib):
    return pltpu.CompilerParams(vmem_limit_bytes=mib * 1024 * 1024)


def cost(flops, bytes_accessed=1 << 20):
    return pl.CostEstimate(flops=flops, bytes_accessed=bytes_accessed, transcendentals=0)


def call(kernel, outs, *args, flops=0, scratch=(), mib=16, free=False):
    return pl.pallas_call(
        kernel,
        out_shape=[jax.ShapeDtypeStruct(shape, dtype) for shape, dtype in outs],
        scratch_shapes=scratch,
        compiler_params=params(mib),
        cost_estimate=cost(flops, 0 if free else 1 << 20),
    )(*args)


def swap(value, mask):
    devices = lax.axis_size("batch") * lax.axis_size("item")
    return lax.ppermute(value, ("batch", "item"), [(k, k ^ mask) for k in range(devices)])


def bits_of(axis):
    return [(axis, level) for level in range(log2(lax.axis_size(axis)))]


def mask_of(bits):
    return sum((lax.axis_size("item") if axis == "batch" else 1) << level for axis, level in bits)


def reduce_scatter(fetched, dhidden, drow):
    width = dhidden[0].shape[1]
    n_item, devices = lax.axis_size("item"), lax.axis_size("batch") * lax.axis_size("item")
    part = width // devices
    close = log2(len(dhidden))
    batch_bits, item_bits = bits_of("batch"), bits_of("item")
    stages = [batch_bits[:1], batch_bits[1:], item_bits[:close], item_bits[close:]]
    bits = sum(stages, [])
    order = []
    for spot in range(devices):
        at = {"batch": 0, "item": 0}
        for k, (axis, level) in enumerate(bits):
            at[axis] |= (spot >> (len(bits) - 1 - k) & 1) << level
        order.append(at["batch"] * n_item + at["item"])
    left, values = devices, [*fetched, *dhidden]
    for k, stage in enumerate(stages):
        whole, left = left, left >> len(stage)
        masks = [
            mask_of([bit for j, bit in enumerate(reversed(stage)) if step >> j & 1]) for step in range(1, 1 << len(stage))
        ]
        sent = f32 if k == len(stages) - 1 else bf16
        count = len(values)
        kernel = functools.partial(stage_kernel, stage, count) if k else functools.partial(share_kernel, order, stage, count)
        kept, *sends = call(
            kernel,
            [((left, part, width), f32)] + [((left, part, width), sent)] * len(masks),
            *values,
            scratch=[pltpu.VMEM((whole, part, width), f32)],
            free=True,
        )
        values = [kept] + [swap(value, mask) for mask, value in zip(masks, sends)]
        if k == 2:
            values, drow = lax.optimization_barrier((values, drow))
    return values, drow


def local(user_vectors, item_table, tower_weight, item_owner, item_row):
    n, width = user_vectors.shape
    rows = item_table.shape[0]
    n_batch, n_item = lax.axis_size("batch"), lax.axis_size("item")
    devices = n_batch * n_item
    near = min(4, n_item)
    levels = n_item // near
    slots = 2 * n // devices
    total = devices * slots
    size = total // near
    sizes = [rows // 8] + [rows // 4] * 3 + [rows // 8]

    far = [batch * n_item for batch in range(2, n_batch, 2)]
    users = {0: user_vectors}
    for mask in [near << k for k in range(log2(levels))] + far:
        users[mask] = swap(user_vectors, mask)

    (request,) = call(
        functools.partial(request_kernel, near),
        [((devices, (1 + near) * slots), i32)],
        jnp.stack([item_owner.reshape(n), item_row]),
        flops=1 << 34,
    )
    asked = lax.all_to_all(request, ("batch", "item"), split_axis=0, concat_axis=0, tiled=True)
    early = list(users)
    asked, *values = lax.optimization_barrier((asked, *users.values()))
    users = dict(zip(early, values))

    for level in range(1, levels):
        if near * level not in users:
            top = 1 << log2(level)
            users[near * level] = swap(users[near * (level - top)], near * top)
        for mask in far:
            users[mask + near * level] = swap(users[near * level], mask)

    def fetch(parts):
        return call(
            functools.partial(fetch_kernel, parts, near, n_batch),
            [((size, width), bf16)] * len(parts),
            asked,
            item_table,
            flops=2 * size * len(parts) * rows * width,
        )

    fetched = {}
    for parts in [list(reversed(range(1, near))), [0]]:
        asked, *values = lax.optimization_barrier((asked, *fetch(parts)))
        for part, value in zip(parts, values):
            fetched[part] = swap(value, part) if part else value
    fetched = [fetched[part] for part in range(near)]

    for mask in [0, *far]:
        users[mask + n_item] = swap(users[mask], n_item)

    def group(level):
        return [users[near * level + batch * n_item] for batch in range(n_batch)]

    group_outs = [((n_batch * n, width), bf16), ((total // levels, width), bf16)]
    place, low_hot, block, *first = call(
        functools.partial(prepare_kernel, near, n_batch),
        [((total, 1), i32)] + [((BLOCK, total), bf16)] * 2 + group_outs,
        asked,
        *group(0),
        free=True,
    )
    late = {mask: users[mask] for mask in users if mask & (n_item - near)}
    place, late = lax.optimization_barrier((place, late))
    users |= late | {mask + n_item: swap(late[mask], n_item) for mask in late}
    units, owns = zip(
        first,
        *[
            call(functools.partial(users_kernel, level, near), group_outs, place, *group(level), free=True)
            for level in range(1, levels)
        ],
    )
    hidden = call(
        functools.partial(hidden_kernel, levels),
        [((total, width), f32), ((total, 1), f32), ((total, width), bf16)],
        tower_weight,
        *fetched,
        flops=1 << 34,
    )
    dhidden = call(
        functools.partial(main_kernel, levels),
        [((size, width), bf16)] * near,
        *hidden,
        *units,
        *owns,
        flops=1 << 31,
        mib=40,
    )
    dhidden = [dhidden[-part % near] for part in range(near)]
    incoming = [swap(dhidden[part], part) for part in range(1, near)]
    (drow,) = call(row_kernel, [((total, width), bf16)], tower_weight, dhidden[0], *incoming, free=True)
    terms, drow = reduce_scatter(fetched, dhidden, drow)
    table_grad = pl.pallas_call(
        functools.partial(table_kernel, sizes),
        out_specs=pl.BlockSpec(memory_space=pl.ANY),
        out_shape=jax.ShapeDtypeStruct((rows, width), bf16),
        scratch_shapes=[pltpu.VMEM((rows, width), bf16), pltpu.SemaphoreType.DMA((len(sizes),))],
        compiler_params=params(16),
        cost_estimate=cost(2 * total * rows * width, 2 * rows * width),
    )(low_hot, block, drow)
    table_grad, *terms = lax.optimization_barrier((table_grad, *terms))
    (weight_grad,) = call(last_kernel, [((width // devices, width), f32)], *terms)
    return (table_grad, weight_grad)


def solution(mesh):
    return jax.shard_map(
        local,
        mesh=mesh,
        in_specs=(
            P(("batch", "item"), None),
            P(("batch", "item"), None),
            P(),
            P(("batch", "item"), None),
            P(("batch", "item")),
        ),
        out_specs=(P(("batch", "item"), None), P(("batch", "item"), None)),
        check_vma=False,
    )
```

```python
import functools

import jax
import jax.numpy as jnp
from jax import lax
from jax.experimental import pallas as pl
from jax.experimental.pallas import tpu as pltpu
from jax.sharding import PartitionSpec as P

epsilon = 1e-06
score_scale = 60.0
cauchy_scale = 4.0
f32 = jnp.float32
bf16 = jnp.bfloat16
i32 = jnp.int32
BLOCK = 256


def iota(shape, dim):
    return lax.broadcasted_iota(i32, shape, dim)


def hot(mask):
    return jnp.where(mask, 1.0, 0.0).astype(bf16)


def dot(a, b, a_dim=1, b_dim=0):
    return lax.dot_general(a, b, (((a_dim,), (b_dim,)), ((), ())), preferred_element_type=f32)


def halves(value):
    return (value >> 8).astype(f32), (value & 255).astype(f32)


def position():
    return lax.axis_index("batch") * lax.axis_size("item") + lax.axis_index("item")


def log2(value):
    return value.bit_length() - 1


def request_kernel(near, named_ref, request_ref):
    devices, lanes = request_ref.shape
    slots = lanes // (1 + near)
    n = named_ref.shape[1]
    owner, row = named_ref[0:1], named_ref[1:2]
    device = iota((devices, n), 0)
    named = owner == device
    count = dot(hot(named), hot(iota((n, n), 0) <= iota((n, n), 1)))
    rank = jnp.sum(jnp.where(named, count, 0.0), axis=0, keepdims=True).astype(i32) - 1
    in_slot = hot(rank == iota((slots, n), 0))
    which = iota((1, n), 1)
    for k, (value, mask) in enumerate([(row, 0)] + [(which, mask) for mask in range(near)]):
        high, low = halves(value + 1)
        here = (owner ^ mask) == device
        high = dot(jnp.where(here, high, 0.0).astype(bf16), in_slot, 1, 1)
        low = dot(jnp.where(here, low, 0.0).astype(bf16), in_slot, 1, 1)
        request_ref[:, k * slots : (k + 1) * slots] = (high * 256.0 + low).astype(i32) - 1


def asker_of(spot, part, near, n_batch, slots):
    batch = (spot >> log2(slots)) & (n_batch - 1)
    level = spot >> log2(slots * n_batch)
    return position() ^ (batch * lax.axis_size("item") + level * near + part)


def slot_column(asked, part, near, n_batch):
    devices, slots = asked.shape
    total = devices * slots // near
    asker = asker_of(iota((total, devices), 0), part, near, n_batch, slots)
    pick = hot(asker == iota((total, devices), 1))
    high, low = halves(asked)
    value = dot(pick, high.astype(bf16)) * 256.0 + dot(pick, low.astype(bf16))
    mine = (iota((total, slots), 0) & (slots - 1)) == iota((total, slots), 1)
    return jnp.sum(jnp.where(mine, value, 0.0), axis=1, keepdims=True)


def slot_line(asked, near, n_batch):
    devices, slots = asked.shape
    total = devices * slots
    pick = hot((iota((slots, total), 1) & (slots - 1)) == iota((slots, total), 0))
    high, low = halves(asked)
    value = dot(high.astype(bf16), pick) * 256.0 + dot(low.astype(bf16), pick)
    spot = iota((devices, total), 1)
    asker = asker_of(spot & (total // near - 1), spot >> log2(total // near), near, n_batch, slots)
    return jnp.sum(jnp.where(asker == iota((devices, total), 0), value, 0.0), axis=0, keepdims=True)


def parts_of(value):
    return value >> 8, value & 255


def fetch_kernel(parts, near, n_batch, asked_ref, table_ref, *found):
    slots = asked_ref.shape[1] // (1 + near)
    asked = asked_ref[:, :slots]
    column = jnp.concatenate([slot_column(asked, part, near, n_batch) for part in parts], axis=0)
    block, low = parts_of(column.astype(i32))
    total = block.shape[0]
    low_hot = hot(low == iota((total, BLOCK), 1))
    block = jnp.broadcast_to(block.astype(f32), (total, BLOCK)).astype(bf16)
    picks = [
        jnp.where(block == jnp.bfloat16(k), low_hot, jnp.bfloat16(0)) for k in range(table_ref.shape[0] // BLOCK)
    ]
    rows = dot(jnp.concatenate(picks, axis=1), table_ref[...]).astype(bf16)
    size = total // len(found)
    for k, ref in enumerate(found):
        ref[...] = rows[k * size : (k + 1) * size]


def prepare_kernel(near, n_batch, asked_ref, *refs):
    *users, place_ref, low_hot_ref, block_ref, unit_ref, own_ref = refs
    n = users[0].shape[0]
    slots = asked_ref.shape[1] // (1 + near)
    size = place_ref.shape[0] // near
    batch = (iota((size, 1), 0) >> log2(slots)) & (n_batch - 1)
    for part in range(near):
        asked = asked_ref[:, (1 + part) * slots : (2 + part) * slots]
        which = slot_column(asked, 0, near, n_batch).astype(i32)
        place_ref[pl.ds(part * size, size)] = jnp.where(which < 0, -1, batch * n + which)
    block, low = parts_of(slot_line(asked_ref[:, :slots], near, n_batch).astype(i32))
    low_hot_ref[...] = hot(low == iota(low_hot_ref.shape, 0))
    block_ref[...] = jnp.broadcast_to(block.astype(f32), block_ref.shape).astype(bf16)
    users_kernel(0, near, place_ref, *users, unit_ref, own_ref)


def users_kernel(level, near, place_ref, *refs):
    *users, unit_ref, own_ref = refs
    n, width = users[0].shape
    for k, ref in enumerate(users):
        value = ref[...].astype(f32)
        mean = jnp.mean(value * value, axis=1, keepdims=True)
        unit_ref[pl.ds(k * n, n)] = (value * lax.rsqrt(mean + epsilon) * (1.0 / width**0.5)).astype(bf16)
    step = place_ref.shape[0] // near
    size = own_ref.shape[0] // near
    place = jnp.concatenate([place_ref[pl.ds(k * step + level * size, size)] for k in range(near)], axis=0)
    own_ref[...] = dot(hot(place == iota((place.shape[0], unit_ref.shape[0]), 1)), unit_ref[...]).astype(bf16)


def hidden_kernel(levels, weight_ref, *refs):
    *fetched, hidden_ref, rscale_ref, item_ref = refs
    width = weight_ref.shape[0]
    size = fetched[0].shape[0] // levels
    for level in range(levels):
        embed = jnp.concatenate([ref[pl.ds(level * size, size)] for ref in fetched], axis=0)
        here = pl.ds(level * embed.shape[0], embed.shape[0])
        hidden = dot(embed, weight_ref[...])
        rscale = lax.rsqrt(jnp.mean(hidden * hidden, axis=1, keepdims=True) + epsilon)
        hidden_ref[here] = hidden
        rscale_ref[here] = rscale
        item_ref[here] = (hidden * (rscale * (1.0 / width**0.5))).astype(bf16)


def main_kernel(levels, hidden_ref, rscale_ref, item_ref, *refs):
    units, owns, outs = refs[:levels], refs[levels : 2 * levels], refs[2 * levels :]
    total, width = hidden_ref.shape
    size = outs[0].shape[0] // levels
    root = 1.0 / width**0.5
    for level in range(levels):
        here = pl.ds(level * (total // levels), total // levels)
        hidden, rscale, item_vec = hidden_ref[here], rscale_ref[here], item_ref[here]
        unit = units[level][...]
        expo = jnp.exp(dot(item_vec, unit, 1, 1) * score_scale)
        sums = jnp.sum(expo, axis=1, keepdims=True)
        mixed = dot(expo.astype(bf16), unit)
        own = owns[level][...].astype(f32)
        positive = jnp.sum(item_vec.astype(f32) * own, axis=1, keepdims=True) * score_scale
        xent = jnp.log(sums) - positive
        cweight = 1.0 / (1.0 + xent * (1.0 / cauchy_scale))
        dvec = (cweight * score_scale) * (mixed * (1.0 / sums) - own)
        inner = jnp.sum(hidden * dvec, axis=1, keepdims=True)
        dhidden = (rscale * root * (dvec - hidden * (rscale * rscale * inner * (1.0 / width)))).astype(bf16)
        for part, ref in enumerate(outs):
            ref[pl.ds(level * size, size)] = dhidden[part * size : (part + 1) * size]


def coordinate(bits):
    return sum(((lax.axis_index(axis) >> level) & 1) << k for k, (axis, level) in enumerate(reversed(bits)))


def steps_of(bits):
    return sorted(range(1 << len(bits)), key=lambda step: -step.bit_count() if step else -len(bits) - 1)


def cut(blocks, bits, refs):
    size = refs[0].shape[0]
    for step, ref in zip(steps_of(bits), refs):
        ref[...] = blocks[pl.ds((coordinate(bits) ^ step) * size, size)].astype(ref.dtype)


def share_kernel(order, bits, count, *refs):
    values, (*refs, blocks) = refs[:count], refs[count:]
    embed, dhidden = (jnp.concatenate([ref[...] for ref in half], axis=0) for half in (values[: count // 2], values[count // 2 :]))
    share = dot(embed, dhidden, 0, 0)
    size = blocks.shape[1]
    for spot, block in enumerate(order):
        blocks[spot] = share[block * size : (block + 1) * size]
    cut(blocks, bits, refs)


def stage_kernel(bits, count, *refs):
    came, (*refs, blocks) = refs[:count], refs[count:]
    blocks[...] = sum(ref[...].astype(f32) for ref in came)
    cut(blocks, bits, refs)


def last_kernel(*refs):
    *came, total_ref = refs
    total_ref[...] = sum(ref[...].astype(f32) for ref in came)[0]


def row_kernel(weight_ref, *refs):
    *incoming, drow_ref = refs
    dhidden = jnp.concatenate([ref[...] for ref in reversed(incoming)], axis=0)
    drow_ref[...] = dot(dhidden, weight_ref[...], 1, 1).astype(bf16)


def table_kernel(sizes, low_hot_ref, block_ref, drow_ref, table_grad_hbm, ready, sems):
    copies, start = [], 0
    for g, size in enumerate(sizes):
        here = pl.ds(start, size)
        picks = [
            jnp.where(block_ref[...] == jnp.bfloat16(k), low_hot_ref[...], jnp.bfloat16(0))
            for k in range(start // BLOCK, (start + size) // BLOCK)
        ]
        ready[here] = dot(jnp.concatenate(picks, axis=0), drow_ref[...]).astype(bf16)
        copy = pltpu.make_async_copy(ready.at[here], table_grad_hbm.at[here], sems.at[g])
        copy.start()
        copies.append(copy)
        start += size
    for copy in copies:
        copy.wait()


def params(mib):
    return pltpu.CompilerParams(vmem_limit_bytes=mib * 1024 * 1024)


def cost(flops, bytes_accessed=1 << 20):
    return pl.CostEstimate(flops=flops, bytes_accessed=bytes_accessed, transcendentals=0)


def call(kernel, outs, *args, flops=0, scratch=(), mib=16, free=False):
    return pl.pallas_call(
        kernel,
        out_shape=[jax.ShapeDtypeStruct(shape, dtype) for shape, dtype in outs],
        scratch_shapes=scratch,
        compiler_params=params(mib),
        cost_estimate=cost(flops, 0 if free else 1 << 20),
    )(*args)


def swap(value, mask):
    devices = lax.axis_size("batch") * lax.axis_size("item")
    return lax.ppermute(value, ("batch", "item"), [(k, k ^ mask) for k in range(devices)])


def bits_of(axis):
    return [(axis, level) for level in range(log2(lax.axis_size(axis)))]


def mask_of(bits):
    return sum((lax.axis_size("item") if axis == "batch" else 1) << level for axis, level in bits)


def reduce_scatter(fetched, dhidden, drow):
    width = dhidden[0].shape[1]
    n_item, devices = lax.axis_size("item"), lax.axis_size("batch") * lax.axis_size("item")
    part = width // devices
    close = log2(len(dhidden))
    batch_bits, item_bits = bits_of("batch"), bits_of("item")
    stages = [batch_bits[:1], batch_bits[1:], item_bits[:close], item_bits[close:]]
    bits = sum(stages, [])
    order = []
    for spot in range(devices):
        at = {"batch": 0, "item": 0}
        for k, (axis, level) in enumerate(bits):
            at[axis] |= (spot >> (len(bits) - 1 - k) & 1) << level
        order.append(at["batch"] * n_item + at["item"])
    left, values = devices, [*fetched, *dhidden]
    for k, stage in enumerate(stages):
        whole, left = left, left >> len(stage)
        masks = [
            mask_of([bit for j, bit in enumerate(reversed(stage)) if step >> j & 1]) for step in steps_of(stage)[1:]
        ]
        sent = f32 if k == len(stages) - 1 else bf16
        count = len(values)
        kernel = functools.partial(stage_kernel, stage, count) if k else functools.partial(share_kernel, order, stage, count)
        kept, *sends = call(
            kernel,
            [((left, part, width), f32)] + [((left, part, width), sent)] * len(masks),
            *values,
            scratch=[pltpu.VMEM((whole, part, width), f32)],
            free=True,
        )
        values = [kept] + [swap(value, mask) for mask, value in zip(masks, sends)]
        if k == 2:
            values, drow = lax.optimization_barrier((values, drow))
    return values, drow


def local(user_vectors, item_table, tower_weight, item_owner, item_row):
    n, width = user_vectors.shape
    rows = item_table.shape[0]
    n_batch, n_item = lax.axis_size("batch"), lax.axis_size("item")
    devices = n_batch * n_item
    near = min(4, n_item)
    levels = n_item // near
    slots = 2 * n // devices
    total = devices * slots
    size = total // near
    sizes = [rows // 8] + [rows // 4] * 3 + [rows // 8]

    far = [batch * n_item for batch in range(2, n_batch, 2)]
    users = {0: user_vectors}
    for mask in [near << k for k in range(log2(levels))] + far:
        users[mask] = swap(user_vectors, mask)

    (request,) = call(
        functools.partial(request_kernel, near),
        [((devices, (1 + near) * slots), i32)],
        jnp.stack([item_owner.reshape(n), item_row]),
        flops=1 << 34,
    )
    asked = lax.all_to_all(request, ("batch", "item"), split_axis=0, concat_axis=0, tiled=True)
    early = list(users)
    asked, *values = lax.optimization_barrier((asked, *users.values()))
    users = dict(zip(early, values))

    for level in range(1, levels):
        if near * level not in users:
            top = 1 << log2(level)
            users[near * level] = swap(users[near * (level - top)], near * top)
        for mask in far:
            users[mask + near * level] = swap(users[near * level], mask)

    def fetch(parts):
        return call(
            functools.partial(fetch_kernel, parts, near, n_batch),
            [((size, width), bf16)] * len(parts),
            asked,
            item_table,
            flops=2 * size * len(parts) * rows * width,
        )

    fetched = {}
    for parts in [[near - 1], list(range(1, near - 1)), [0]]:
        asked, *values = lax.optimization_barrier((asked, *fetch(parts)))
        for part, value in zip(parts, values):
            fetched[part] = swap(value, part) if part else value
    fetched = [fetched[part] for part in range(near)]

    for mask in [0, *far]:
        users[mask + n_item] = swap(users[mask], n_item)

    def group(level):
        return [users[near * level + batch * n_item] for batch in range(n_batch)]

    group_outs = [((n_batch * n, width), bf16), ((total // levels, width), bf16)]
    place, low_hot, block, *first = call(
        functools.partial(prepare_kernel, near, n_batch),
        [((total, 1), i32)] + [((BLOCK, total), bf16)] * 2 + group_outs,
        asked,
        *group(0),
        free=True,
    )
    late = {mask: users[mask] for mask in users if mask & (n_item - near)}
    place, late = lax.optimization_barrier((place, late))
    users |= late | {mask + n_item: swap(late[mask], n_item) for mask in late}
    units, owns = zip(
        first,
        *[
            call(functools.partial(users_kernel, level, near), group_outs, place, *group(level), free=True)
            for level in range(1, levels)
        ],
    )
    hidden = call(
        functools.partial(hidden_kernel, levels),
        [((total, width), f32), ((total, 1), f32), ((total, width), bf16)],
        tower_weight,
        *fetched,
        flops=1 << 34,
    )
    dhidden = call(
        functools.partial(main_kernel, levels),
        [((size, width), bf16)] * near,
        *hidden,
        *units,
        *owns,
        flops=1 << 31,
        mib=40,
    )
    incoming = [swap(dhidden[part], part) for part in range(1, near)]
    (drow,) = call(row_kernel, [((total, width), bf16)], tower_weight, *reversed(incoming), dhidden[0], free=True)
    order = [-part % near for part in range(near)]
    terms, drow = reduce_scatter([fetched[part] for part in order], [dhidden[part] for part in order], drow)
    table_grad = pl.pallas_call(
        functools.partial(table_kernel, sizes),
        out_specs=pl.BlockSpec(memory_space=pl.ANY),
        out_shape=jax.ShapeDtypeStruct((rows, width), bf16),
        scratch_shapes=[pltpu.VMEM((rows, width), bf16), pltpu.SemaphoreType.DMA((len(sizes),))],
        compiler_params=params(16),
        cost_estimate=cost(2 * total * rows * width, 2 * rows * width),
    )(low_hot, block, drow)
    table_grad, *terms = lax.optimization_barrier((table_grad, *terms))
    (weight_grad,) = call(last_kernel, [((width // devices, width), f32)], *terms)
    return (table_grad, weight_grad)


def solution(mesh):
    return jax.shard_map(
        local,
        mesh=mesh,
        in_specs=(
            P(("batch", "item"), None),
            P(("batch", "item"), None),
            P(),
            P(("batch", "item"), None),
            P(("batch", "item")),
        ),
        out_specs=(P(("batch", "item"), None), P(("batch", "item"), None)),
        check_vma=False,
    )
```

```python
import functools

import jax
import jax.numpy as jnp
from jax import lax
from jax.experimental import pallas as pl
from jax.experimental.pallas import tpu as pltpu
from jax.sharding import PartitionSpec as P

epsilon = 1e-06
score_scale = 60.0
cauchy_scale = 4.0
f32 = jnp.float32
bf16 = jnp.bfloat16
i32 = jnp.int32
BLOCK = 256


def iota(shape, dim):
    return lax.broadcasted_iota(i32, shape, dim)


def hot(mask):
    return jnp.where(mask, 1.0, 0.0).astype(bf16)


def dot(a, b, a_dim=1, b_dim=0):
    return lax.dot_general(a, b, (((a_dim,), (b_dim,)), ((), ())), preferred_element_type=f32)


def halves(value):
    return (value >> 8).astype(f32), (value & 255).astype(f32)


def position():
    return lax.axis_index("batch") * lax.axis_size("item") + lax.axis_index("item")


def log2(value):
    return value.bit_length() - 1


def request_kernel(near, named_ref, request_ref):
    devices, lanes = request_ref.shape
    slots = lanes // (1 + near)
    n = named_ref.shape[1]
    owner, row = named_ref[0:1], named_ref[1:2]
    device = iota((devices, n), 0)
    named = owner == device
    count = dot(hot(named), hot(iota((n, n), 0) <= iota((n, n), 1)))
    rank = jnp.sum(jnp.where(named, count, 0.0), axis=0, keepdims=True).astype(i32) - 1
    in_slot = hot(rank == iota((slots, n), 0))
    which = iota((1, n), 1)
    for k, (value, mask) in enumerate([(row, 0)] + [(which, mask) for mask in range(near)]):
        high, low = halves(value + 1)
        here = (owner ^ mask) == device
        high = dot(jnp.where(here, high, 0.0).astype(bf16), in_slot, 1, 1)
        low = dot(jnp.where(here, low, 0.0).astype(bf16), in_slot, 1, 1)
        request_ref[:, k * slots : (k + 1) * slots] = (high * 256.0 + low).astype(i32) - 1


def asker_of(spot, part, near, n_batch, slots):
    batch = (spot >> log2(slots)) & (n_batch - 1)
    level = spot >> log2(slots * n_batch)
    return position() ^ (batch * lax.axis_size("item") + level * near + part)


def slot_column(asked, part, near, n_batch):
    devices, slots = asked.shape
    total = devices * slots // near
    asker = asker_of(iota((total, devices), 0), part, near, n_batch, slots)
    pick = hot(asker == iota((total, devices), 1))
    high, low = halves(asked)
    value = dot(pick, high.astype(bf16)) * 256.0 + dot(pick, low.astype(bf16))
    mine = (iota((total, slots), 0) & (slots - 1)) == iota((total, slots), 1)
    return jnp.sum(jnp.where(mine, value, 0.0), axis=1, keepdims=True)


def slot_line(asked, near, n_batch):
    devices, slots = asked.shape
    total = devices * slots
    pick = hot((iota((slots, total), 1) & (slots - 1)) == iota((slots, total), 0))
    high, low = halves(asked)
    value = dot(high.astype(bf16), pick) * 256.0 + dot(low.astype(bf16), pick)
    spot = iota((devices, total), 1)
    asker = asker_of(spot & (total // near - 1), spot >> log2(total // near), near, n_batch, slots)
    return jnp.sum(jnp.where(asker == iota((devices, total), 0), value, 0.0), axis=0, keepdims=True)


def parts_of(value):
    return value >> 8, value & 255


def fetch_kernel(parts, near, n_batch, asked_ref, table_ref, *found):
    slots = asked_ref.shape[1] // (1 + near)
    asked = asked_ref[:, :slots]
    column = jnp.concatenate([slot_column(asked, part, near, n_batch) for part in parts], axis=0)
    block, low = parts_of(column.astype(i32))
    total = block.shape[0]
    low_hot = hot(low == iota((total, BLOCK), 1))
    block = jnp.broadcast_to(block.astype(f32), (total, BLOCK)).astype(bf16)
    picks = [
        jnp.where(block == jnp.bfloat16(k), low_hot, jnp.bfloat16(0)) for k in range(table_ref.shape[0] // BLOCK)
    ]
    rows = dot(jnp.concatenate(picks, axis=1), table_ref[...]).astype(bf16)
    size = total // len(found)
    for k, ref in enumerate(found):
        ref[...] = rows[k * size : (k + 1) * size]


def prepare_kernel(near, n_batch, asked_ref, *refs):
    *users, place_ref, low_hot_ref, block_ref, unit_ref, own_ref = refs
    n = users[0].shape[0]
    slots = asked_ref.shape[1] // (1 + near)
    size = place_ref.shape[0] // near
    batch = (iota((size, 1), 0) >> log2(slots)) & (n_batch - 1)
    for part in range(near):
        asked = asked_ref[:, (1 + part) * slots : (2 + part) * slots]
        which = slot_column(asked, 0, near, n_batch).astype(i32)
        place_ref[pl.ds(part * size, size)] = jnp.where(which < 0, -1, batch * n + which)
    block, low = parts_of(slot_line(asked_ref[:, :slots], near, n_batch).astype(i32))
    low_hot_ref[...] = hot(low == iota(low_hot_ref.shape, 0))
    block_ref[...] = jnp.broadcast_to(block.astype(f32), block_ref.shape).astype(bf16)
    users_kernel(0, near, place_ref, *users, unit_ref, own_ref)


def users_kernel(level, near, place_ref, *refs):
    *users, unit_ref, own_ref = refs
    n, width = users[0].shape
    for k, ref in enumerate(users):
        value = ref[...].astype(f32)
        mean = jnp.mean(value * value, axis=1, keepdims=True)
        unit_ref[pl.ds(k * n, n)] = (value * lax.rsqrt(mean + epsilon) * (1.0 / width**0.5)).astype(bf16)
    step = place_ref.shape[0] // near
    size = own_ref.shape[0] // near
    place = jnp.concatenate([place_ref[pl.ds(k * step + level * size, size)] for k in range(near)], axis=0)
    own_ref[...] = dot(hot(place == iota((place.shape[0], unit_ref.shape[0]), 1)), unit_ref[...]).astype(bf16)


def hidden_kernel(levels, weight_ref, *refs):
    *fetched, hidden_ref, rscale_ref, item_ref = refs
    width = weight_ref.shape[0]
    size = fetched[0].shape[0] // levels
    for level in range(levels):
        embed = jnp.concatenate([ref[pl.ds(level * size, size)] for ref in fetched], axis=0)
        here = pl.ds(level * embed.shape[0], embed.shape[0])
        hidden = dot(embed, weight_ref[...])
        rscale = lax.rsqrt(jnp.mean(hidden * hidden, axis=1, keepdims=True) + epsilon)
        hidden_ref[here] = hidden
        rscale_ref[here] = rscale
        item_ref[here] = (hidden * (rscale * (1.0 / width**0.5))).astype(bf16)


def main_kernel(levels, hidden_ref, rscale_ref, item_ref, *refs):
    units, owns, outs = refs[:levels], refs[levels : 2 * levels], refs[2 * levels :]
    total, width = hidden_ref.shape
    size = outs[0].shape[0] // levels
    root = 1.0 / width**0.5
    for level in range(levels):
        here = pl.ds(level * (total // levels), total // levels)
        hidden, rscale, item_vec = hidden_ref[here], rscale_ref[here], item_ref[here]
        unit = units[level][...]
        expo = jnp.exp(dot(item_vec, unit, 1, 1) * score_scale)
        sums = jnp.sum(expo, axis=1, keepdims=True)
        mixed = dot(expo.astype(bf16), unit)
        own = owns[level][...].astype(f32)
        positive = jnp.sum(item_vec.astype(f32) * own, axis=1, keepdims=True) * score_scale
        xent = jnp.log(sums) - positive
        cweight = 1.0 / (1.0 + xent * (1.0 / cauchy_scale))
        dvec = (cweight * score_scale) * (mixed * (1.0 / sums) - own)
        inner = jnp.sum(hidden * dvec, axis=1, keepdims=True)
        dhidden = (rscale * root * (dvec - hidden * (rscale * rscale * inner * (1.0 / width)))).astype(bf16)
        for part, ref in enumerate(outs):
            ref[pl.ds(level * size, size)] = dhidden[part * size : (part + 1) * size]


def coordinate(bits):
    return sum(((lax.axis_index(axis) >> level) & 1) << k for k, (axis, level) in enumerate(reversed(bits)))


def steps_of(bits):
    return sorted(range(1 << len(bits)), key=lambda step: -step.bit_count() if step else -len(bits) - 1)


def cut(blocks, bits, refs):
    size = refs[0].shape[0]
    for step, ref in zip(steps_of(bits), refs):
        ref[...] = blocks[pl.ds((coordinate(bits) ^ step) * size, size)].astype(ref.dtype)


def share_kernel(order, bits, count, *refs):
    values, (*refs, blocks) = refs[:count], refs[count:]
    embed, dhidden = (jnp.concatenate([ref[...] for ref in half], axis=0) for half in (values[: count // 2], values[count // 2 :]))
    share = dot(embed, dhidden, 0, 0)
    size = blocks.shape[1]
    for spot, block in enumerate(order):
        blocks[spot] = share[block * size : (block + 1) * size]
    cut(blocks, bits, refs)


def stage_kernel(bits, count, *refs):
    came, (*refs, blocks) = refs[:count], refs[count:]
    blocks[...] = sum(ref[...].astype(f32) for ref in came)
    cut(blocks, bits, refs)


def last_kernel(*refs):
    *came, total_ref = refs
    total_ref[...] = sum(ref[...].astype(f32) for ref in came)[0]


def row_kernel(weight_ref, *refs):
    *incoming, drow_ref = refs
    dhidden = jnp.concatenate([ref[...] for ref in reversed(incoming)], axis=0)
    drow_ref[...] = dot(dhidden, weight_ref[...], 1, 1).astype(bf16)


def table_kernel(first, sizes, low_hot_ref, block_ref, drow_ref, *refs):
    *_, table_grad_hbm, ready, sems = refs
    copies, start = [], first
    for g, size in enumerate(sizes):
        here = pl.ds(start - first, size)
        picks = [
            jnp.where(block_ref[...] == jnp.bfloat16(k), low_hot_ref[...], jnp.bfloat16(0))
            for k in range(start // BLOCK, (start + size) // BLOCK)
        ]
        ready[here] = dot(jnp.concatenate(picks, axis=0), drow_ref[...]).astype(bf16)
        copy = pltpu.make_async_copy(ready.at[here], table_grad_hbm.at[pl.ds(start, size)], sems.at[g])
        copy.start()
        copies.append(copy)
        start += size
    for copy in copies:
        copy.wait()


def params(mib):
    return pltpu.CompilerParams(vmem_limit_bytes=mib * 1024 * 1024)


def cost(flops, bytes_accessed=1 << 20):
    return pl.CostEstimate(flops=flops, bytes_accessed=bytes_accessed, transcendentals=0)


def call(kernel, outs, *args, flops=0, scratch=(), mib=16, free=False):
    return pl.pallas_call(
        kernel,
        out_shape=[jax.ShapeDtypeStruct(shape, dtype) for shape, dtype in outs],
        scratch_shapes=scratch,
        compiler_params=params(mib),
        cost_estimate=cost(flops, 0 if free else 1 << 20),
    )(*args)


def swap(value, mask):
    devices = lax.axis_size("batch") * lax.axis_size("item")
    return lax.ppermute(value, ("batch", "item"), [(k, k ^ mask) for k in range(devices)])


def bits_of(axis):
    return [(axis, level) for level in range(log2(lax.axis_size(axis)))]


def mask_of(bits):
    return sum((lax.axis_size("item") if axis == "batch" else 1) << level for axis, level in bits)


def table_call(rows, first, sizes, masks, drow, *before, flops=0):
    total, width = drow.shape
    return pl.pallas_call(
        functools.partial(table_kernel, first, sizes),
        in_specs=[pl.BlockSpec(memory_space=pltpu.VMEM)] * 3 + [pl.BlockSpec(memory_space=pl.ANY)] * len(before),
        out_specs=pl.BlockSpec(memory_space=pl.ANY),
        out_shape=jax.ShapeDtypeStruct((rows, width), bf16),
        scratch_shapes=[pltpu.VMEM((sum(sizes), width), bf16), pltpu.SemaphoreType.DMA((len(sizes),))],
        input_output_aliases={3: 0} if before else {},
        compiler_params=params(16),
        cost_estimate=cost(flops, 2 * sum(sizes) * width if flops else 0),
    )(*masks, drow, *before)


def reduce_scatter(fetched, dhidden, drow):
    width = dhidden[0].shape[1]
    n_item, devices = lax.axis_size("item"), lax.axis_size("batch") * lax.axis_size("item")
    part = width // devices
    close = log2(len(dhidden))
    batch_bits, item_bits = bits_of("batch"), bits_of("item")
    stages = [batch_bits[:1], batch_bits[1:], item_bits[:close], item_bits[close:]]
    bits = sum(stages, [])
    order = []
    for spot in range(devices):
        at = {"batch": 0, "item": 0}
        for k, (axis, level) in enumerate(bits):
            at[axis] |= (spot >> (len(bits) - 1 - k) & 1) << level
        order.append(at["batch"] * n_item + at["item"])
    left, values = devices, [*fetched, *dhidden]
    for k, stage in enumerate(stages):
        whole, left = left, left >> len(stage)
        masks = [
            mask_of([bit for j, bit in enumerate(reversed(stage)) if step >> j & 1]) for step in steps_of(stage)[1:]
        ]
        sent = f32 if k == len(stages) - 1 else bf16
        count = len(values)
        kernel = functools.partial(stage_kernel, stage, count) if k else functools.partial(share_kernel, order, stage, count)
        kept, *sends = call(
            kernel,
            [((left, part, width), f32)] + [((left, part, width), sent)] * len(masks),
            *values,
            scratch=[pltpu.VMEM((whole, part, width), f32)],
            free=True,
        )
        values = [kept] + [swap(value, mask) for mask, value in zip(masks, sends)]
        if k == 2:
            values, drow = lax.optimization_barrier((values, drow))
    return values, drow


def local(user_vectors, item_table, tower_weight, item_owner, item_row):
    n, width = user_vectors.shape
    rows = item_table.shape[0]
    n_batch, n_item = lax.axis_size("batch"), lax.axis_size("item")
    devices = n_batch * n_item
    near = min(4, n_item)
    levels = n_item // near
    slots = 2 * n // devices
    total = devices * slots
    size = total // near
    sizes = [rows // 8] * 3 + [rows // 4] * 2 + [rows // 8]

    far = [batch * n_item for batch in range(2, n_batch, 2)]
    users = {0: user_vectors}
    for mask in [near << k for k in range(log2(levels))] + far:
        users[mask] = swap(user_vectors, mask)

    (request,) = call(
        functools.partial(request_kernel, near),
        [((devices, (1 + near) * slots), i32)],
        jnp.stack([item_owner.reshape(n), item_row]),
        flops=1 << 34,
    )
    asked = lax.all_to_all(request, ("batch", "item"), split_axis=0, concat_axis=0, tiled=True)
    early = list(users)
    asked, *values = lax.optimization_barrier((asked, *users.values()))
    users = dict(zip(early, values))

    for level in range(1, levels):
        if near * level not in users:
            top = 1 << log2(level)
            users[near * level] = swap(users[near * (level - top)], near * top)
        for mask in far:
            users[mask + near * level] = swap(users[near * level], mask)

    def fetch(parts):
        return call(
            functools.partial(fetch_kernel, parts, near, n_batch),
            [((size, width), bf16)] * len(parts),
            asked,
            item_table,
            flops=2 * size * len(parts) * rows * width,
        )

    fetched = {}
    for parts in [[near - 1], list(range(1, near - 1)), [0]]:
        asked, *values = lax.optimization_barrier((asked, *fetch(parts)))
        for part, value in zip(parts, values):
            fetched[part] = swap(value, part) if part else value
    fetched = [fetched[part] for part in range(near)]

    for mask in [0, *far]:
        users[mask + n_item] = swap(users[mask], n_item)

    def group(level):
        return [users[near * level + batch * n_item] for batch in range(n_batch)]

    group_outs = [((n_batch * n, width), bf16), ((total // levels, width), bf16)]
    place, low_hot, block, *first = call(
        functools.partial(prepare_kernel, near, n_batch),
        [((total, 1), i32)] + [((BLOCK, total), bf16)] * 2 + group_outs,
        asked,
        *group(0),
        free=True,
    )
    late = {mask: users[mask] for mask in users if mask & (n_item - near)}
    place, late = lax.optimization_barrier((place, late))
    users |= late | {mask + n_item: swap(late[mask], n_item) for mask in late}
    units, owns = zip(
        first,
        *[
            call(functools.partial(users_kernel, level, near), group_outs, place, *group(level), free=True)
            for level in range(1, levels)
        ],
    )
    hidden = call(
        functools.partial(hidden_kernel, levels),
        [((total, width), f32), ((total, 1), f32), ((total, width), bf16)],
        tower_weight,
        *fetched,
        flops=1 << 34,
    )
    dhidden = call(
        functools.partial(main_kernel, levels),
        [((size, width), bf16)] * near,
        *hidden,
        *units,
        *owns,
        flops=1 << 31,
        mib=40,
    )
    incoming = [swap(dhidden[part], part) for part in range(1, near)]
    (drow,) = call(row_kernel, [((total, width), bf16)], tower_weight, *reversed(incoming), dhidden[0], free=True)
    order = [-part % near for part in range(near)]
    table_grad = table_call(rows, 0, sizes[:2], (low_hot, block), drow)
    terms, (drow, table_grad) = reduce_scatter(
        [fetched[part] for part in order], [dhidden[part] for part in order], (drow, table_grad)
    )
    flops = 2 * total * rows * width
    table_grad = table_call(rows, sum(sizes[:2]), sizes[2:], (low_hot, block), drow, table_grad, flops=flops)
    table_grad, *terms = lax.optimization_barrier((table_grad, *terms))
    (weight_grad,) = call(last_kernel, [((width // devices, width), f32)], *terms)
    return (table_grad, weight_grad)


def solution(mesh):
    return jax.shard_map(
        local,
        mesh=mesh,
        in_specs=(
            P(("batch", "item"), None),
            P(("batch", "item"), None),
            P(),
            P(("batch", "item"), None),
            P(("batch", "item")),
        ),
        out_specs=(P(("batch", "item"), None), P(("batch", "item"), None)),
        check_vma=False,
    )
```

```python
import functools

import jax
import jax.numpy as jnp
from jax import lax
from jax.experimental import pallas as pl
from jax.experimental.pallas import tpu as pltpu
from jax.sharding import PartitionSpec as P

epsilon = 1e-06
score_scale = 60.0
cauchy_scale = 4.0
f32 = jnp.float32
bf16 = jnp.bfloat16
i32 = jnp.int32
BLOCK = 256


def iota(shape, dim):
    return lax.broadcasted_iota(i32, shape, dim)


def hot(mask):
    return jnp.where(mask, 1.0, 0.0).astype(bf16)


def dot(a, b, a_dim=1, b_dim=0):
    return lax.dot_general(a, b, (((a_dim,), (b_dim,)), ((), ())), preferred_element_type=f32)


def halves(value):
    return (value >> 8).astype(f32), (value & 255).astype(f32)


def position():
    return lax.axis_index("batch") * lax.axis_size("item") + lax.axis_index("item")


def log2(value):
    return value.bit_length() - 1


def request_kernel(near, named_ref, request_ref):
    devices, lanes = request_ref.shape
    slots = lanes // (1 + near)
    n = named_ref.shape[1]
    owner, row = named_ref[0:1], named_ref[1:2]
    device = iota((devices, n), 0)
    named = owner == device
    count = dot(hot(named), hot(iota((n, n), 0) <= iota((n, n), 1)))
    rank = jnp.sum(jnp.where(named, count, 0.0), axis=0, keepdims=True).astype(i32) - 1
    in_slot = hot(rank == iota((slots, n), 0))
    which = iota((1, n), 1)
    for k, (value, mask) in enumerate([(row, 0)] + [(which, mask) for mask in range(near)]):
        high, low = halves(value + 1)
        here = (owner ^ mask) == device
        high = dot(jnp.where(here, high, 0.0).astype(bf16), in_slot, 1, 1)
        low = dot(jnp.where(here, low, 0.0).astype(bf16), in_slot, 1, 1)
        request_ref[:, k * slots : (k + 1) * slots] = (high * 256.0 + low).astype(i32) - 1


def asker_of(spot, part, near, n_batch, slots):
    batch = (spot >> log2(slots)) & (n_batch - 1)
    level = spot >> log2(slots * n_batch)
    return position() ^ (batch * lax.axis_size("item") + level * near + part)


def slot_column(asked, part, near, n_batch):
    devices, slots = asked.shape
    total = devices * slots // near
    asker = asker_of(iota((total, devices), 0), part, near, n_batch, slots)
    pick = hot(asker == iota((total, devices), 1))
    high, low = halves(asked)
    value = dot(pick, high.astype(bf16)) * 256.0 + dot(pick, low.astype(bf16))
    mine = (iota((total, slots), 0) & (slots - 1)) == iota((total, slots), 1)
    return jnp.sum(jnp.where(mine, value, 0.0), axis=1, keepdims=True)


def slot_line(asked, near, n_batch):
    devices, slots = asked.shape
    total = devices * slots
    pick = hot((iota((slots, total), 1) & (slots - 1)) == iota((slots, total), 0))
    high, low = halves(asked)
    value = dot(high.astype(bf16), pick) * 256.0 + dot(low.astype(bf16), pick)
    spot = iota((devices, total), 1)
    asker = asker_of(spot & (total // near - 1), spot >> log2(total // near), near, n_batch, slots)
    return jnp.sum(jnp.where(asker == iota((devices, total), 0), value, 0.0), axis=0, keepdims=True)


def parts_of(value):
    return value >> 8, value & 255


def fetch_kernel(parts, near, n_batch, asked_ref, table_ref, *found):
    slots = asked_ref.shape[1] // (1 + near)
    asked = asked_ref[:, :slots]
    column = jnp.concatenate([slot_column(asked, part, near, n_batch) for part in parts], axis=0)
    block, low = parts_of(column.astype(i32))
    total = block.shape[0]
    low_hot = hot(low == iota((total, BLOCK), 1))
    block = jnp.broadcast_to(block.astype(f32), (total, BLOCK)).astype(bf16)
    picks = [
        jnp.where(block == jnp.bfloat16(k), low_hot, jnp.bfloat16(0)) for k in range(table_ref.shape[0] // BLOCK)
    ]
    rows = dot(jnp.concatenate(picks, axis=1), table_ref[...]).astype(bf16)
    size = total // len(found)
    for k, ref in enumerate(found):
        ref[...] = rows[k * size : (k + 1) * size]


def prepare_kernel(near, n_batch, asked_ref, *refs):
    *users, place_ref, low_hot_ref, block_ref, unit_ref, own_ref = refs
    n = users[0].shape[0]
    slots = asked_ref.shape[1] // (1 + near)
    size = place_ref.shape[0] // near
    batch = (iota((size, 1), 0) >> log2(slots)) & (n_batch - 1)
    for part in range(near):
        asked = asked_ref[:, (1 + part) * slots : (2 + part) * slots]
        which = slot_column(asked, 0, near, n_batch).astype(i32)
        place_ref[pl.ds(part * size, size)] = jnp.where(which < 0, -1, batch * n + which)
    block, low = parts_of(slot_line(asked_ref[:, :slots], near, n_batch).astype(i32))
    low_hot_ref[...] = hot(low == iota(low_hot_ref.shape, 0))
    block_ref[...] = jnp.broadcast_to(block.astype(f32), block_ref.shape).astype(bf16)
    users_kernel(0, near, place_ref, *users, unit_ref, own_ref)


def users_kernel(level, near, place_ref, *refs):
    *users, unit_ref, own_ref = refs
    n, width = users[0].shape
    for k, ref in enumerate(users):
        value = ref[...].astype(f32)
        mean = jnp.mean(value * value, axis=1, keepdims=True)
        unit_ref[pl.ds(k * n, n)] = (value * lax.rsqrt(mean + epsilon) * (1.0 / width**0.5)).astype(bf16)
    step = place_ref.shape[0] // near
    size = own_ref.shape[0] // near
    place = jnp.concatenate([place_ref[pl.ds(k * step + level * size, size)] for k in range(near)], axis=0)
    own_ref[...] = dot(hot(place == iota((place.shape[0], unit_ref.shape[0]), 1)), unit_ref[...]).astype(bf16)


def hidden_kernel(levels, weight_ref, *refs):
    *fetched, hidden_ref, rscale_ref, item_ref = refs
    width = weight_ref.shape[0]
    size = fetched[0].shape[0] // levels
    for level in range(levels):
        embed = jnp.concatenate([ref[pl.ds(level * size, size)] for ref in fetched], axis=0)
        here = pl.ds(level * embed.shape[0], embed.shape[0])
        hidden = dot(embed, weight_ref[...])
        rscale = lax.rsqrt(jnp.mean(hidden * hidden, axis=1, keepdims=True) + epsilon)
        hidden_ref[here] = hidden
        rscale_ref[here] = rscale
        item_ref[here] = (hidden * (rscale * (1.0 / width**0.5))).astype(bf16)


def main_kernel(levels, near, place_ref, hidden_ref, rscale_ref, item_ref, *refs):
    later = levels - 1
    units, owns = refs[0:1] + refs[len(refs) - 2 * later : len(refs) - later], refs[1:2] + refs[len(refs) - later :]
    users, outs = refs[2 : len(refs) - 2 * later - near], refs[len(refs) - 2 * later - near : len(refs) - 2 * later]
    for level in range(1, levels):
        few = len(users) // later
        users_kernel(level, near, place_ref, *users[(level - 1) * few : level * few], units[level], owns[level])
    total, width = hidden_ref.shape
    size = outs[0].shape[0] // levels
    root = 1.0 / width**0.5
    for level in range(levels):
        here = pl.ds(level * (total // levels), total // levels)
        hidden, rscale, item_vec = hidden_ref[here], rscale_ref[here], item_ref[here]
        unit = units[level][...]
        expo = jnp.exp(dot(item_vec, unit, 1, 1) * score_scale)
        sums = jnp.sum(expo, axis=1, keepdims=True)
        mixed = dot(expo.astype(bf16), unit)
        own = owns[level][...].astype(f32)
        positive = jnp.sum(item_vec.astype(f32) * own, axis=1, keepdims=True) * score_scale
        xent = jnp.log(sums) - positive
        cweight = 1.0 / (1.0 + xent * (1.0 / cauchy_scale))
        dvec = (cweight * score_scale) * (mixed * (1.0 / sums) - own)
        inner = jnp.sum(hidden * dvec, axis=1, keepdims=True)
        dhidden = (rscale * root * (dvec - hidden * (rscale * rscale * inner * (1.0 / width)))).astype(bf16)
        for part, ref in enumerate(outs):
            ref[pl.ds(level * size, size)] = dhidden[part * size : (part + 1) * size]


def coordinate(bits):
    return sum(((lax.axis_index(axis) >> level) & 1) << k for k, (axis, level) in enumerate(reversed(bits)))


def steps_of(bits):
    return sorted(range(1 << len(bits)), key=lambda step: -step.bit_count() if step else -len(bits) - 1)


def cut(blocks, bits, refs):
    size = refs[0].shape[0]
    for step, ref in zip(steps_of(bits), refs):
        ref[...] = blocks[pl.ds((coordinate(bits) ^ step) * size, size)].astype(ref.dtype)


def share_kernel(order, bits, count, *refs):
    values, (*refs, blocks) = refs[:count], refs[count:]
    embed, dhidden = (jnp.concatenate([ref[...] for ref in half], axis=0) for half in (values[: count // 2], values[count // 2 :]))
    share = dot(embed, dhidden, 0, 0)
    size = blocks.shape[1]
    for spot, block in enumerate(order):
        blocks[spot] = share[block * size : (block + 1) * size]
    cut(blocks, bits, refs)


def stage_kernel(bits, count, *refs):
    came, (*refs, blocks) = refs[:count], refs[count:]
    blocks[...] = sum(ref[...].astype(f32) for ref in came)
    cut(blocks, bits, refs)


def last_kernel(*refs):
    *came, total_ref = refs
    total_ref[...] = sum(ref[...].astype(f32) for ref in came)[0]


def row_kernel(weight_ref, *refs):
    *incoming, drow_ref = refs
    dhidden = jnp.concatenate([ref[...] for ref in reversed(incoming)], axis=0)
    drow_ref[...] = dot(dhidden, weight_ref[...], 1, 1).astype(bf16)


def table_kernel(sizes, low_hot_ref, block_ref, drow_ref, table_grad_hbm, ready, sems):
    copies, start = [], 0
    for g, size in enumerate(sizes):
        here = pl.ds(start, size)
        picks = [
            jnp.where(block_ref[...] == jnp.bfloat16(k), low_hot_ref[...], jnp.bfloat16(0))
            for k in range(start // BLOCK, (start + size) // BLOCK)
        ]
        ready[here] = dot(jnp.concatenate(picks, axis=0), drow_ref[...]).astype(bf16)
        copy = pltpu.make_async_copy(ready.at[here], table_grad_hbm.at[here], sems.at[g])
        copy.start()
        copies.append(copy)
        start += size
    for copy in copies:
        copy.wait()


def params(mib):
    return pltpu.CompilerParams(vmem_limit_bytes=mib * 1024 * 1024)


def cost(flops, bytes_accessed=1 << 20):
    return pl.CostEstimate(flops=flops, bytes_accessed=bytes_accessed, transcendentals=0)


def call(kernel, outs, *args, flops=0, scratch=(), mib=16, free=False):
    return pl.pallas_call(
        kernel,
        out_shape=[jax.ShapeDtypeStruct(shape, dtype) for shape, dtype in outs],
        scratch_shapes=scratch,
        compiler_params=params(mib),
        cost_estimate=cost(flops, 0 if free else 1 << 20),
    )(*args)


def swap(value, mask):
    devices = lax.axis_size("batch") * lax.axis_size("item")
    return lax.ppermute(value, ("batch", "item"), [(k, k ^ mask) for k in range(devices)])


def bits_of(axis):
    return [(axis, level) for level in range(log2(lax.axis_size(axis)))]


def mask_of(bits):
    return sum((lax.axis_size("item") if axis == "batch" else 1) << level for axis, level in bits)


def reduce_scatter(fetched, dhidden, drow):
    width = dhidden[0].shape[1]
    n_item, devices = lax.axis_size("item"), lax.axis_size("batch") * lax.axis_size("item")
    part = width // devices
    close = log2(len(dhidden))
    batch_bits, item_bits = bits_of("batch"), bits_of("item")
    stages = [batch_bits[:1], batch_bits[1:], item_bits[:close], item_bits[close:]]
    bits = sum(stages, [])
    order = []
    for spot in range(devices):
        at = {"batch": 0, "item": 0}
        for k, (axis, level) in enumerate(bits):
            at[axis] |= (spot >> (len(bits) - 1 - k) & 1) << level
        order.append(at["batch"] * n_item + at["item"])
    left, values = devices, [*fetched, *dhidden]
    for k, stage in enumerate(stages):
        whole, left = left, left >> len(stage)
        masks = [
            mask_of([bit for j, bit in enumerate(reversed(stage)) if step >> j & 1]) for step in steps_of(stage)[1:]
        ]
        sent = f32 if k == len(stages) - 1 else bf16
        count = len(values)
        kernel = functools.partial(stage_kernel, stage, count) if k else functools.partial(share_kernel, order, stage, count)
        kept, *sends = call(
            kernel,
            [((left, part, width), f32)] + [((left, part, width), sent)] * len(masks),
            *values,
            scratch=[pltpu.VMEM((whole, part, width), f32)],
            free=True,
        )
        values = [kept] + [swap(value, mask) for mask, value in zip(masks, sends)]
        if k == 2:
            values, drow = lax.optimization_barrier((values, drow))
    return values, drow


def local(user_vectors, item_table, tower_weight, item_owner, item_row):
    n, width = user_vectors.shape
    rows = item_table.shape[0]
    n_batch, n_item = lax.axis_size("batch"), lax.axis_size("item")
    devices = n_batch * n_item
    near = min(4, n_item)
    levels = n_item // near
    slots = 2 * n // devices
    total = devices * slots
    size = total // near
    sizes = [rows // 8] + [rows // 4] * 3 + [rows // 8]

    far = [batch * n_item for batch in range(2, n_batch, 2)]
    users = {0: user_vectors}
    for mask in [near << k for k in range(log2(levels))] + far:
        users[mask] = swap(user_vectors, mask)

    (request,) = call(
        functools.partial(request_kernel, near),
        [((devices, (1 + near) * slots), i32)],
        jnp.stack([item_owner.reshape(n), item_row]),
        flops=1 << 34,
    )
    asked = lax.all_to_all(request, ("batch", "item"), split_axis=0, concat_axis=0, tiled=True)
    early = list(users)
    asked, *values = lax.optimization_barrier((asked, *users.values()))
    users = dict(zip(early, values))

    for level in range(1, levels):
        if near * level not in users:
            top = 1 << log2(level)
            users[near * level] = swap(users[near * (level - top)], near * top)
        for mask in far:
            users[mask + near * level] = swap(users[near * level], mask)

    def fetch(parts):
        return call(
            functools.partial(fetch_kernel, parts, near, n_batch),
            [((size, width), bf16)] * len(parts),
            asked,
            item_table,
            flops=2 * size * len(parts) * rows * width,
        )

    fetched = {}
    for parts in [[near - 1], list(range(1, near - 1)), [0]]:
        asked, *values = lax.optimization_barrier((asked, *fetch(parts)))
        for part, value in zip(parts, values):
            fetched[part] = swap(value, part) if part else value
    fetched = [fetched[part] for part in range(near)]

    for mask in [0, *far]:
        users[mask + n_item] = swap(users[mask], n_item)

    def group(level):
        return [users[near * level + batch * n_item] for batch in range(n_batch)]

    group_outs = [((n_batch * n, width), bf16), ((total // levels, width), bf16)]
    place, low_hot, block, *first = call(
        functools.partial(prepare_kernel, near, n_batch),
        [((total, 1), i32)] + [((BLOCK, total), bf16)] * 2 + group_outs,
        asked,
        *group(0),
        free=True,
    )
    late = {mask: users[mask] for mask in users if mask & (n_item - near)}
    place, late = lax.optimization_barrier((place, late))
    users |= late | {mask + n_item: swap(late[mask], n_item) for mask in late}
    hidden = call(
        functools.partial(hidden_kernel, levels),
        [((total, width), f32), ((total, 1), f32), ((total, width), bf16)],
        tower_weight,
        *fetched,
        flops=1 << 34,
    )
    dhidden = call(
        functools.partial(main_kernel, levels, near),
        [((size, width), bf16)] * near,
        place,
        *hidden,
        *first,
        *[value for level in range(1, levels) for value in group(level)],
        flops=1 << 31,
        mib=40,
        scratch=[pltpu.VMEM(shape, kind) for shape, kind in group_outs[:1] * (levels - 1) + group_outs[1:] * (levels - 1)],
    )
    incoming = [swap(dhidden[part], part) for part in range(1, near)]
    (drow,) = call(row_kernel, [((total, width), bf16)], tower_weight, *reversed(incoming), dhidden[0], free=True)
    order = [-part % near for part in range(near)]
    terms, drow = reduce_scatter([fetched[part] for part in order], [dhidden[part] for part in order], drow)
    table_grad = pl.pallas_call(
        functools.partial(table_kernel, sizes),
        out_specs=pl.BlockSpec(memory_space=pl.ANY),
        out_shape=jax.ShapeDtypeStruct((rows, width), bf16),
        scratch_shapes=[pltpu.VMEM((rows, width), bf16), pltpu.SemaphoreType.DMA((len(sizes),))],
        compiler_params=params(16),
        cost_estimate=cost(2 * total * rows * width, 2 * rows * width),
    )(low_hot, block, drow)
    table_grad, *terms = lax.optimization_barrier((table_grad, *terms))
    (weight_grad,) = call(last_kernel, [((width // devices, width), f32)], *terms)
    return (table_grad, weight_grad)


def solution(mesh):
    return jax.shard_map(
        local,
        mesh=mesh,
        in_specs=(
            P(("batch", "item"), None),
            P(("batch", "item"), None),
            P(),
            P(("batch", "item"), None),
            P(("batch", "item")),
        ),
        out_specs=(P(("batch", "item"), None), P(("batch", "item"), None)),
        check_vma=False,
    )
```

```python
import functools

import jax
import jax.numpy as jnp
from jax import lax
from jax.experimental import pallas as pl
from jax.experimental.pallas import tpu as pltpu
from jax.sharding import PartitionSpec as P

epsilon = 1e-06
score_scale = 60.0
cauchy_scale = 4.0
f32 = jnp.float32
bf16 = jnp.bfloat16
i32 = jnp.int32
BLOCK = 256


def iota(shape, dim):
    return lax.broadcasted_iota(i32, shape, dim)


def hot(mask):
    return jnp.where(mask, 1.0, 0.0).astype(bf16)


def dot(a, b, a_dim=1, b_dim=0):
    return lax.dot_general(a, b, (((a_dim,), (b_dim,)), ((), ())), preferred_element_type=f32)


def halves(value):
    return (value >> 8).astype(f32), (value & 255).astype(f32)


def position():
    return lax.axis_index("batch") * lax.axis_size("item") + lax.axis_index("item")


def log2(value):
    return value.bit_length() - 1


def request_kernel(near, named_ref, request_ref):
    devices, lanes = request_ref.shape
    slots = lanes // (1 + near)
    n = named_ref.shape[1]
    owner, row = named_ref[0:1], named_ref[1:2]
    device = iota((devices, n), 0)
    named = owner == device
    count = dot(hot(named), hot(iota((n, n), 0) <= iota((n, n), 1)))
    rank = jnp.sum(jnp.where(named, count, 0.0), axis=0, keepdims=True).astype(i32) - 1
    in_slot = hot(rank == iota((slots, n), 0))
    which = iota((1, n), 1)
    for k, (value, mask) in enumerate([(row, 0)] + [(which, mask) for mask in range(near)]):
        high, low = halves(value + 1)
        here = (owner ^ mask) == device
        high = dot(jnp.where(here, high, 0.0).astype(bf16), in_slot, 1, 1)
        low = dot(jnp.where(here, low, 0.0).astype(bf16), in_slot, 1, 1)
        request_ref[:, k * slots : (k + 1) * slots] = (high * 256.0 + low).astype(i32) - 1


def asker_of(spot, part, near, n_batch, slots):
    batch = (spot >> log2(slots)) & (n_batch - 1)
    level = spot >> log2(slots * n_batch)
    return position() ^ (batch * lax.axis_size("item") + level * near + part)


def slot_column(asked, part, near, n_batch):
    devices, slots = asked.shape
    total = devices * slots // near
    asker = asker_of(iota((total, devices), 0), part, near, n_batch, slots)
    pick = hot(asker == iota((total, devices), 1))
    high, low = halves(asked)
    value = dot(pick, high.astype(bf16)) * 256.0 + dot(pick, low.astype(bf16))
    mine = (iota((total, slots), 0) & (slots - 1)) == iota((total, slots), 1)
    return jnp.sum(jnp.where(mine, value, 0.0), axis=1, keepdims=True)


def slot_line(asked, near, n_batch):
    devices, slots = asked.shape
    total = devices * slots
    pick = hot((iota((slots, total), 1) & (slots - 1)) == iota((slots, total), 0))
    high, low = halves(asked)
    value = dot(high.astype(bf16), pick) * 256.0 + dot(low.astype(bf16), pick)
    spot = iota((devices, total), 1)
    asker = asker_of(spot & (total // near - 1), spot >> log2(total // near), near, n_batch, slots)
    return jnp.sum(jnp.where(asker == iota((devices, total), 0), value, 0.0), axis=0, keepdims=True)


def parts_of(value):
    return value >> 8, value & 255


def fetch_kernel(parts, near, n_batch, asked_ref, table_ref, *found):
    slots = asked_ref.shape[1] // (1 + near)
    asked = asked_ref[:, :slots]
    column = jnp.concatenate([slot_column(asked, part, near, n_batch) for part in parts], axis=0)
    block, low = parts_of(column.astype(i32))
    total = block.shape[0]
    low_hot = hot(low == iota((total, BLOCK), 1))
    block = jnp.broadcast_to(block.astype(f32), (total, BLOCK)).astype(bf16)
    picks = [
        jnp.where(block == jnp.bfloat16(k), low_hot, jnp.bfloat16(0)) for k in range(table_ref.shape[0] // BLOCK)
    ]
    rows = dot(jnp.concatenate(picks, axis=1), table_ref[...]).astype(bf16)
    size = total // len(found)
    for k, ref in enumerate(found):
        ref[...] = rows[k * size : (k + 1) * size]


def prepare_kernel(near, n_batch, asked_ref, *refs):
    *users, place_ref, low_hot_ref, block_ref, unit_ref, own_ref = refs
    n = users[0].shape[0]
    slots = asked_ref.shape[1] // (1 + near)
    size = place_ref.shape[0] // near
    batch = (iota((size, 1), 0) >> log2(slots)) & (n_batch - 1)
    for part in range(near):
        asked = asked_ref[:, (1 + part) * slots : (2 + part) * slots]
        which = slot_column(asked, 0, near, n_batch).astype(i32)
        place_ref[pl.ds(part * size, size)] = jnp.where(which < 0, -1, batch * n + which)
    block, low = parts_of(slot_line(asked_ref[:, :slots], near, n_batch).astype(i32))
    low_hot_ref[...] = hot(low == iota(low_hot_ref.shape, 0))
    block_ref[...] = jnp.broadcast_to(block.astype(f32), block_ref.shape).astype(bf16)
    users_kernel(0, near, place_ref, *users, unit_ref, own_ref)


def users_kernel(level, near, place_ref, *refs):
    *users, unit_ref, own_ref = refs
    n, width = users[0].shape
    for k, ref in enumerate(users):
        value = ref[...].astype(f32)
        mean = jnp.mean(value * value, axis=1, keepdims=True)
        unit_ref[pl.ds(k * n, n)] = (value * lax.rsqrt(mean + epsilon) * (1.0 / width**0.5)).astype(bf16)
    step = place_ref.shape[0] // near
    size = own_ref.shape[0] // near
    place = jnp.concatenate([place_ref[pl.ds(k * step + level * size, size)] for k in range(near)], axis=0)
    own_ref[...] = dot(hot(place == iota((place.shape[0], unit_ref.shape[0]), 1)), unit_ref[...]).astype(bf16)


def hidden_kernel(levels, weight_ref, *refs):
    *fetched, hidden_ref, rscale_ref, item_ref = refs
    width = weight_ref.shape[0]
    size = fetched[0].shape[0] // levels
    for level in range(levels):
        embed = jnp.concatenate([ref[pl.ds(level * size, size)] for ref in fetched], axis=0)
        here = pl.ds(level * embed.shape[0], embed.shape[0])
        hidden = dot(embed, weight_ref[...])
        rscale = lax.rsqrt(jnp.mean(hidden * hidden, axis=1, keepdims=True) + epsilon)
        hidden_ref[here] = hidden
        rscale_ref[here] = rscale
        item_ref[here] = (hidden * (rscale * (1.0 / width**0.5))).astype(bf16)


def main_kernel(levels, near, order, bits, place_ref, hidden_ref, rscale_ref, item_ref, *refs):
    fetched, *refs = refs[:near], *refs[near:-1], refs[-1]
    *refs, blocks = refs
    scratch = 2 * (levels - 1)
    shares, refs = refs[len(refs) - scratch - 2 : len(refs) - scratch], refs[: len(refs) - scratch - 2] + refs[len(refs) - scratch :]
    later = levels - 1
    units, owns = [refs[0], *refs[len(refs) - 2 * later : len(refs) - later]], [refs[1], *refs[len(refs) - later :]]
    users, outs = refs[2 : len(refs) - 2 * later - near], refs[len(refs) - 2 * later - near : len(refs) - 2 * later]
    for level in range(1, levels):
        few = len(users) // later
        users_kernel(level, near, place_ref, *users[(level - 1) * few : level * few], units[level], owns[level])
    total, width = hidden_ref.shape
    size = outs[0].shape[0] // levels
    root = 1.0 / width**0.5
    for level in range(levels):
        here = pl.ds(level * (total // levels), total // levels)
        hidden, rscale, item_vec = hidden_ref[here], rscale_ref[here], item_ref[here]
        unit = units[level][...]
        expo = jnp.exp(dot(item_vec, unit, 1, 1) * score_scale)
        sums = jnp.sum(expo, axis=1, keepdims=True)
        mixed = dot(expo.astype(bf16), unit)
        own = owns[level][...].astype(f32)
        positive = jnp.sum(item_vec.astype(f32) * own, axis=1, keepdims=True) * score_scale
        xent = jnp.log(sums) - positive
        cweight = 1.0 / (1.0 + xent * (1.0 / cauchy_scale))
        dvec = (cweight * score_scale) * (mixed * (1.0 / sums) - own)
        inner = jnp.sum(hidden * dvec, axis=1, keepdims=True)
        dhidden = (rscale * root * (dvec - hidden * (rscale * rscale * inner * (1.0 / width)))).astype(bf16)
        for part, ref in enumerate(outs):
            ref[pl.ds(level * size, size)] = dhidden[part * size : (part + 1) * size]
    share_kernel(order, bits, 2 * near, *fetched, *outs, *shares, blocks)


def coordinate(bits):
    return sum(((lax.axis_index(axis) >> level) & 1) << k for k, (axis, level) in enumerate(reversed(bits)))


def steps_of(bits):
    return sorted(range(1 << len(bits)), key=lambda step: -step.bit_count() if step else -len(bits) - 1)


def cut(blocks, bits, refs):
    size = refs[0].shape[0]
    for step, ref in zip(steps_of(bits), refs):
        ref[...] = blocks[pl.ds((coordinate(bits) ^ step) * size, size)].astype(ref.dtype)


def share_kernel(order, bits, count, *refs):
    values, (*refs, blocks) = refs[:count], refs[count:]
    embed, dhidden = (jnp.concatenate([ref[...] for ref in half], axis=0) for half in (values[: count // 2], values[count // 2 :]))
    share = dot(embed, dhidden, 0, 0)
    size = blocks.shape[1]
    for spot, block in enumerate(order):
        blocks[spot] = share[block * size : (block + 1) * size]
    cut(blocks, bits, refs)


def stage_kernel(bits, count, *refs):
    came, (*refs, blocks) = refs[:count], refs[count:]
    blocks[...] = sum(ref[...].astype(f32) for ref in came)
    cut(blocks, bits, refs)


def last_kernel(*refs):
    *came, total_ref = refs
    total_ref[...] = sum(ref[...].astype(f32) for ref in came)[0]


def row_kernel(weight_ref, *refs):
    *incoming, drow_ref = refs
    dhidden = jnp.concatenate([ref[...] for ref in reversed(incoming)], axis=0)
    drow_ref[...] = dot(dhidden, weight_ref[...], 1, 1).astype(bf16)


def table_kernel(sizes, low_hot_ref, block_ref, drow_ref, table_grad_hbm, ready, sems):
    copies, start = [], 0
    for g, size in enumerate(sizes):
        here = pl.ds(start, size)
        picks = [
            jnp.where(block_ref[...] == jnp.bfloat16(k), low_hot_ref[...], jnp.bfloat16(0))
            for k in range(start // BLOCK, (start + size) // BLOCK)
        ]
        ready[here] = dot(jnp.concatenate(picks, axis=0), drow_ref[...]).astype(bf16)
        copy = pltpu.make_async_copy(ready.at[here], table_grad_hbm.at[here], sems.at[g])
        copy.start()
        copies.append(copy)
        start += size
    for copy in copies:
        copy.wait()


def params(mib):
    return pltpu.CompilerParams(vmem_limit_bytes=mib * 1024 * 1024)


def cost(flops, bytes_accessed=1 << 20):
    return pl.CostEstimate(flops=flops, bytes_accessed=bytes_accessed, transcendentals=0)


def call(kernel, outs, *args, flops=0, scratch=(), mib=16, free=False):
    return pl.pallas_call(
        kernel,
        out_shape=[jax.ShapeDtypeStruct(shape, dtype) for shape, dtype in outs],
        scratch_shapes=scratch,
        compiler_params=params(mib),
        cost_estimate=cost(flops, 0 if free else 1 << 20),
    )(*args)


def swap(value, mask):
    devices = lax.axis_size("batch") * lax.axis_size("item")
    return lax.ppermute(value, ("batch", "item"), [(k, k ^ mask) for k in range(devices)])


def bits_of(axis):
    return [(axis, level) for level in range(log2(lax.axis_size(axis)))]


def mask_of(bits):
    return sum((lax.axis_size("item") if axis == "batch" else 1) << level for axis, level in bits)


def stages_of(near):
    n_item, devices = lax.axis_size("item"), lax.axis_size("batch") * lax.axis_size("item")
    close = log2(near)
    batch_bits, item_bits = bits_of("batch"), bits_of("item")
    stages = [batch_bits[:1], batch_bits[1:], item_bits[:close], item_bits[close:]]
    bits = sum(stages, [])
    order = []
    for spot in range(devices):
        at = {"batch": 0, "item": 0}
        for k, (axis, level) in enumerate(bits):
            at[axis] |= (spot >> (len(bits) - 1 - k) & 1) << level
        order.append(at["batch"] * n_item + at["item"])
    return stages, order


def reduce_scatter(stages, first, width, drow):
    devices = lax.axis_size("batch") * lax.axis_size("item")
    left, part, values = devices, width // devices, None
    for k, stage in enumerate(stages):
        whole, left = left, left >> len(stage)
        masks = [
            mask_of([bit for j, bit in enumerate(reversed(stage)) if step >> j & 1]) for step in steps_of(stage)[1:]
        ]
        sent = f32 if k == len(stages) - 1 else bf16
        kept, *sends = first if k == 0 else call(
            functools.partial(stage_kernel, stage, len(values)),
            [((left, part, width), f32)] + [((left, part, width), sent)] * len(masks),
            *values,
            scratch=[pltpu.VMEM((whole, part, width), f32)],
            free=True,
        )
        values = [kept] + [swap(value, mask) for mask, value in zip(masks, sends)]
        if k == 2:
            values, drow = lax.optimization_barrier((values, drow))
    return values, drow


def local(user_vectors, item_table, tower_weight, item_owner, item_row):
    n, width = user_vectors.shape
    rows = item_table.shape[0]
    n_batch, n_item = lax.axis_size("batch"), lax.axis_size("item")
    devices = n_batch * n_item
    near = min(4, n_item)
    levels = n_item // near
    slots = 2 * n // devices
    total = devices * slots
    size = total // near
    sizes = [rows // 8] + [rows // 4] * 3 + [rows // 8]

    far = [batch * n_item for batch in range(2, n_batch, 2)]
    users = {0: user_vectors}
    for mask in [near << k for k in range(log2(levels))] + far:
        users[mask] = swap(user_vectors, mask)

    (request,) = call(
        functools.partial(request_kernel, near),
        [((devices, (1 + near) * slots), i32)],
        jnp.stack([item_owner.reshape(n), item_row]),
        flops=1 << 34,
    )
    asked = lax.all_to_all(request, ("batch", "item"), split_axis=0, concat_axis=0, tiled=True)
    early = list(users)
    asked, *values = lax.optimization_barrier((asked, *users.values()))
    users = dict(zip(early, values))

    for level in range(1, levels):
        if near * level not in users:
            top = 1 << log2(level)
            users[near * level] = swap(users[near * (level - top)], near * top)
        for mask in far:
            users[mask + near * level] = swap(users[near * level], mask)

    def fetch(parts):
        return call(
            functools.partial(fetch_kernel, parts, near, n_batch),
            [((size, width), bf16)] * len(parts),
            asked,
            item_table,
            flops=2 * size * len(parts) * rows * width,
        )

    fetched = {}
    for parts in [[near - 1], list(range(1, near - 1)), [0]]:
        asked, *values = lax.optimization_barrier((asked, *fetch(parts)))
        for part, value in zip(parts, values):
            fetched[part] = swap(value, part) if part else value
    fetched = [fetched[part] for part in range(near)]

    for mask in [0, *far]:
        users[mask + n_item] = swap(users[mask], n_item)

    def group(level):
        return [users[near * level + batch * n_item] for batch in range(n_batch)]

    group_outs = [((n_batch * n, width), bf16), ((total // levels, width), bf16)]
    place, low_hot, block, *first = call(
        functools.partial(prepare_kernel, near, n_batch),
        [((total, 1), i32)] + [((BLOCK, total), bf16)] * 2 + group_outs,
        asked,
        *group(0),
        free=True,
    )
    late = {mask: users[mask] for mask in users if mask & (n_item - near)}
    place, late = lax.optimization_barrier((place, late))
    users |= late | {mask + n_item: swap(late[mask], n_item) for mask in late}
    hidden = call(
        functools.partial(hidden_kernel, levels),
        [((total, width), f32), ((total, 1), f32), ((total, width), bf16)],
        tower_weight,
        *fetched,
        flops=1 << 34,
    )
    stages, order = stages_of(near)
    half, part = devices // 2, width // devices
    *dhidden, kept, sent = call(
        functools.partial(main_kernel, levels, near, order, stages[0]),
        [((size, width), bf16)] * near + [((half, part, width), f32), ((half, part, width), bf16)],
        place,
        *hidden,
        *fetched,
        *first,
        *[value for level in range(1, levels) for value in group(level)],
        flops=1 << 31,
        mib=40,
        scratch=[pltpu.VMEM(shape, kind) for shape, kind in group_outs[:1] * (levels - 1) + group_outs[1:] * (levels - 1)]
        + [pltpu.VMEM((devices, part, width), f32)],
    )
    incoming = [swap(dhidden[part], part) for part in range(1, near)]
    (drow,) = call(row_kernel, [((total, width), bf16)], tower_weight, *reversed(incoming), dhidden[0], free=True)
    terms, drow = reduce_scatter(stages, (kept, sent), width, drow)
    table_grad = pl.pallas_call(
        functools.partial(table_kernel, sizes),
        out_specs=pl.BlockSpec(memory_space=pl.ANY),
        out_shape=jax.ShapeDtypeStruct((rows, width), bf16),
        scratch_shapes=[pltpu.VMEM((rows, width), bf16), pltpu.SemaphoreType.DMA((len(sizes),))],
        compiler_params=params(16),
        cost_estimate=cost(2 * total * rows * width, 2 * rows * width),
    )(low_hot, block, drow)
    table_grad, *terms = lax.optimization_barrier((table_grad, *terms))
    (weight_grad,) = call(last_kernel, [((width // devices, width), f32)], *terms)
    return (table_grad, weight_grad)


def solution(mesh):
    return jax.shard_map(
        local,
        mesh=mesh,
        in_specs=(
            P(("batch", "item"), None),
            P(("batch", "item"), None),
            P(),
            P(("batch", "item"), None),
            P(("batch", "item")),
        ),
        out_specs=(P(("batch", "item"), None), P(("batch", "item"), None)),
        check_vma=False,
    )
```

```python
import functools

import jax
import jax.numpy as jnp
from jax import lax
from jax.experimental import pallas as pl
from jax.experimental.pallas import tpu as pltpu
from jax.sharding import PartitionSpec as P

epsilon = 1e-06
score_scale = 60.0
cauchy_scale = 4.0
f32 = jnp.float32
bf16 = jnp.bfloat16
i32 = jnp.int32
BLOCK = 256


def iota(shape, dim):
    return lax.broadcasted_iota(i32, shape, dim)


def hot(mask):
    return jnp.where(mask, 1.0, 0.0).astype(bf16)


def dot(a, b, a_dim=1, b_dim=0):
    return lax.dot_general(a, b, (((a_dim,), (b_dim,)), ((), ())), preferred_element_type=f32)


def halves(value):
    return (value >> 8).astype(f32), (value & 255).astype(f32)


def position():
    return lax.axis_index("batch") * lax.axis_size("item") + lax.axis_index("item")


def log2(value):
    return value.bit_length() - 1


def request_kernel(near, named_ref, request_ref):
    devices, lanes = request_ref.shape
    slots = lanes // (1 + near)
    n = named_ref.shape[1]
    owner, row = named_ref[0:1], named_ref[1:2]
    device = iota((devices, n), 0)
    named = owner == device
    count = dot(hot(named), hot(iota((n, n), 0) <= iota((n, n), 1)))
    rank = jnp.sum(jnp.where(named, count, 0.0), axis=0, keepdims=True).astype(i32) - 1
    in_slot = hot(rank == iota((slots, n), 0))
    which = iota((1, n), 1)
    for k, (value, mask) in enumerate([(row, 0)] + [(which, mask) for mask in range(near)]):
        high, low = halves(value + 1)
        here = (owner ^ mask) == device
        high = dot(jnp.where(here, high, 0.0).astype(bf16), in_slot, 1, 1)
        low = dot(jnp.where(here, low, 0.0).astype(bf16), in_slot, 1, 1)
        request_ref[:, k * slots : (k + 1) * slots] = (high * 256.0 + low).astype(i32) - 1


def asker_of(spot, part, near, n_batch, slots):
    batch = (spot >> log2(slots)) & (n_batch - 1)
    level = spot >> log2(slots * n_batch)
    return position() ^ (batch * lax.axis_size("item") + level * near + part)


def slot_column(asked, part, near, n_batch):
    devices, slots = asked.shape
    total = devices * slots // near
    asker = asker_of(iota((total, devices), 0), part, near, n_batch, slots)
    pick = hot(asker == iota((total, devices), 1))
    high, low = halves(asked)
    value = dot(pick, high.astype(bf16)) * 256.0 + dot(pick, low.astype(bf16))
    mine = (iota((total, slots), 0) & (slots - 1)) == iota((total, slots), 1)
    return jnp.sum(jnp.where(mine, value, 0.0), axis=1, keepdims=True)


def slot_line(asked, near, n_batch):
    devices, slots = asked.shape
    total = devices * slots
    pick = hot((iota((slots, total), 1) & (slots - 1)) == iota((slots, total), 0))
    high, low = halves(asked)
    value = dot(high.astype(bf16), pick) * 256.0 + dot(low.astype(bf16), pick)
    spot = iota((devices, total), 1)
    asker = asker_of(spot & (total // near - 1), spot >> log2(total // near), near, n_batch, slots)
    return jnp.sum(jnp.where(asker == iota((devices, total), 0), value, 0.0), axis=0, keepdims=True)


def parts_of(value):
    return value >> 8, value & 255


def fetch_kernel(parts, near, n_batch, asked_ref, table_ref, *found):
    slots = asked_ref.shape[1] // (1 + near)
    asked = asked_ref[:, :slots]
    column = jnp.concatenate([slot_column(asked, part, near, n_batch) for part in parts], axis=0)
    block, low = parts_of(column.astype(i32))
    total = block.shape[0]
    low_hot = hot(low == iota((total, BLOCK), 1))
    block = jnp.broadcast_to(block.astype(f32), (total, BLOCK)).astype(bf16)
    picks = [
        jnp.where(block == jnp.bfloat16(k), low_hot, jnp.bfloat16(0)) for k in range(table_ref.shape[0] // BLOCK)
    ]
    rows = dot(jnp.concatenate(picks, axis=1), table_ref[...]).astype(bf16)
    size = total // len(found)
    for k, ref in enumerate(found):
        ref[...] = rows[k * size : (k + 1) * size]


def prepare_kernel(near, n_batch, asked_ref, *refs):
    *users, place_ref, low_hot_ref, block_ref, unit_ref, own_ref = refs
    n = users[0].shape[0]
    slots = asked_ref.shape[1] // (1 + near)
    size = place_ref.shape[0] // near
    batch = (iota((size, 1), 0) >> log2(slots)) & (n_batch - 1)
    for part in range(near):
        asked = asked_ref[:, (1 + part) * slots : (2 + part) * slots]
        which = slot_column(asked, 0, near, n_batch).astype(i32)
        place_ref[pl.ds(part * size, size)] = jnp.where(which < 0, -1, batch * n + which)
    block, low = parts_of(slot_line(asked_ref[:, :slots], near, n_batch).astype(i32))
    low_hot_ref[...] = hot(low == iota(low_hot_ref.shape, 0))
    block_ref[...] = jnp.broadcast_to(block.astype(f32), block_ref.shape).astype(bf16)
    users_kernel(0, near, place_ref, *users, unit_ref, own_ref)


def users_kernel(level, near, place_ref, *refs):
    *users, unit_ref, own_ref = refs
    n, width = users[0].shape
    for k, ref in enumerate(users):
        value = ref[...].astype(f32)
        mean = jnp.mean(value * value, axis=1, keepdims=True)
        unit_ref[pl.ds(k * n, n)] = (value * lax.rsqrt(mean + epsilon) * (1.0 / width**0.5)).astype(bf16)
    step = place_ref.shape[0] // near
    size = own_ref.shape[0] // near
    place = jnp.concatenate([place_ref[pl.ds(k * step + level * size, size)] for k in range(near)], axis=0)
    own_ref[...] = dot(hot(place == iota((place.shape[0], unit_ref.shape[0]), 1)), unit_ref[...]).astype(bf16)


def hidden_kernel(levels, weight_ref, *refs):
    *fetched, hidden_ref, rscale_ref, item_ref = refs
    width = weight_ref.shape[0]
    size = fetched[0].shape[0] // levels
    for level in range(levels):
        embed = jnp.concatenate([ref[pl.ds(level * size, size)] for ref in fetched], axis=0)
        here = pl.ds(level * embed.shape[0], embed.shape[0])
        hidden = dot(embed, weight_ref[...])
        rscale = lax.rsqrt(jnp.mean(hidden * hidden, axis=1, keepdims=True) + epsilon)
        hidden_ref[here] = hidden
        rscale_ref[here] = rscale
        item_ref[here] = (hidden * (rscale * (1.0 / width**0.5))).astype(bf16)


def main_kernel(levels, near, place_ref, hidden_ref, rscale_ref, item_ref, *refs):
    later = levels - 1
    units, owns = refs[0:1] + refs[len(refs) - 2 * later : len(refs) - later], refs[1:2] + refs[len(refs) - later :]
    users, outs = refs[2 : len(refs) - 2 * later - near], refs[len(refs) - 2 * later - near : len(refs) - 2 * later]
    for level in range(1, levels):
        few = len(users) // later
        users_kernel(level, near, place_ref, *users[(level - 1) * few : level * few], units[level], owns[level])
    total, width = hidden_ref.shape
    size = outs[0].shape[0] // levels
    root = 1.0 / width**0.5
    for level in range(levels):
        here = pl.ds(level * (total // levels), total // levels)
        hidden, rscale, item_vec = hidden_ref[here], rscale_ref[here], item_ref[here]
        unit = units[level][...]
        expo = jnp.exp(dot(item_vec, unit, 1, 1) * score_scale)
        sums = jnp.sum(expo, axis=1, keepdims=True)
        mixed = dot(expo.astype(bf16), unit)
        own = owns[level][...].astype(f32)
        positive = jnp.sum(item_vec.astype(f32) * own, axis=1, keepdims=True) * score_scale
        xent = jnp.log(sums) - positive
        cweight = 1.0 / (1.0 + xent * (1.0 / cauchy_scale))
        dvec = (cweight * score_scale) * (mixed * (1.0 / sums) - own)
        inner = jnp.sum(hidden * dvec, axis=1, keepdims=True)
        dhidden = (rscale * root * (dvec - hidden * (rscale * rscale * inner * (1.0 / width)))).astype(bf16)
        for part, ref in enumerate(outs):
            ref[pl.ds(level * size, size)] = dhidden[part * size : (part + 1) * size]


def coordinate(bits):
    return sum(((lax.axis_index(axis) >> level) & 1) << k for k, (axis, level) in enumerate(reversed(bits)))


def steps_of(bits):
    return sorted(range(1 << len(bits)), key=lambda step: -step.bit_count() if step else -len(bits) - 1)


def cut(blocks, bits, refs):
    size = refs[0].shape[0]
    for step, ref in zip(steps_of(bits), refs):
        ref[...] = blocks[pl.ds((coordinate(bits) ^ step) * size, size)].astype(ref.dtype)


def share_kernel(order, bits, count, *refs):
    values, (*refs, blocks) = refs[:count], refs[count:]
    embed, dhidden = (jnp.concatenate([ref[...] for ref in half], axis=0) for half in (values[: count // 2], values[count // 2 :]))
    share = dot(embed, dhidden, 0, 0)
    size = blocks.shape[1]
    for spot, block in enumerate(order):
        blocks[spot] = share[block * size : (block + 1) * size]
    cut(blocks, bits, refs)


def stage_kernel(bits, count, *refs):
    came, (*refs, blocks) = refs[:count], refs[count:]
    blocks[...] = sum(ref[...].astype(f32) for ref in came)
    cut(blocks, bits, refs)


def last_kernel(*refs):
    *came, total_ref = refs
    total_ref[...] = sum(ref[...].astype(f32) for ref in came)[0]


def row_kernel(weight_ref, *refs):
    *incoming, drow_ref = refs
    dhidden = jnp.concatenate([ref[...] for ref in reversed(incoming)], axis=0)
    drow_ref[...] = dot(dhidden, weight_ref[...], 1, 1).astype(bf16)


def table_kernel(sizes, low_hot_ref, block_ref, drow_ref, table_grad_hbm, ready, sems):
    copies, start = [], 0
    for g, size in enumerate(sizes):
        here = pl.ds(start, size)
        picks = [
            jnp.where(block_ref[...] == jnp.bfloat16(k), low_hot_ref[...], jnp.bfloat16(0))
            for k in range(start // BLOCK, (start + size) // BLOCK)
        ]
        ready[here] = dot(jnp.concatenate(picks, axis=0), drow_ref[...]).astype(bf16)
        copy = pltpu.make_async_copy(ready.at[here], table_grad_hbm.at[here], sems.at[g])
        copy.start()
        copies.append(copy)
        start += size
    for copy in copies:
        copy.wait()


def params(mib):
    return pltpu.CompilerParams(vmem_limit_bytes=mib * 1024 * 1024)


def cost(flops, bytes_accessed=1 << 20):
    return pl.CostEstimate(flops=flops, bytes_accessed=bytes_accessed, transcendentals=0)


def call(kernel, outs, *args, flops=0, scratch=(), mib=16, free=False):
    return pl.pallas_call(
        kernel,
        out_shape=[jax.ShapeDtypeStruct(shape, dtype) for shape, dtype in outs],
        scratch_shapes=scratch,
        compiler_params=params(mib),
        cost_estimate=cost(flops, 0 if free else 1 << 20),
    )(*args)


def swap(value, mask):
    devices = lax.axis_size("batch") * lax.axis_size("item")
    return lax.ppermute(value, ("batch", "item"), [(k, k ^ mask) for k in range(devices)])


def bits_of(axis):
    return [(axis, level) for level in range(log2(lax.axis_size(axis)))]


def mask_of(bits):
    return sum((lax.axis_size("item") if axis == "batch" else 1) << level for axis, level in bits)


def reduce_scatter(fetched, dhidden, drow):
    width = dhidden[0].shape[1]
    n_item, devices = lax.axis_size("item"), lax.axis_size("batch") * lax.axis_size("item")
    part = width // devices
    close = log2(len(dhidden))
    batch_bits, item_bits = bits_of("batch"), bits_of("item")
    stages = [batch_bits[:1], batch_bits[1:], item_bits[:close], item_bits[close:]]
    bits = sum(stages, [])
    order = []
    for spot in range(devices):
        at = {"batch": 0, "item": 0}
        for k, (axis, level) in enumerate(bits):
            at[axis] |= (spot >> (len(bits) - 1 - k) & 1) << level
        order.append(at["batch"] * n_item + at["item"])
    left, values = devices, [*fetched, *dhidden]
    for k, stage in enumerate(stages):
        whole, left = left, left >> len(stage)
        masks = [
            mask_of([bit for j, bit in enumerate(reversed(stage)) if step >> j & 1]) for step in steps_of(stage)[1:]
        ]
        sent = f32 if k == len(stages) - 1 else bf16
        count = len(values)
        kernel = functools.partial(stage_kernel, stage, count) if k else functools.partial(share_kernel, order, stage, count)
        kept, *sends = call(
            kernel,
            [((left, part, width), f32)] + [((left, part, width), sent)] * len(masks),
            *values,
            scratch=[pltpu.VMEM((whole, part, width), f32)],
            free=True,
        )
        values = [kept] + [swap(value, mask) for mask, value in zip(masks, sends)]
        if k == 2:
            values, drow = lax.optimization_barrier((values, drow))
    return values, drow


def local(user_vectors, item_table, tower_weight, item_owner, item_row):
    n, width = user_vectors.shape
    rows = item_table.shape[0]
    n_batch, n_item = lax.axis_size("batch"), lax.axis_size("item")
    devices = n_batch * n_item
    near = min(4, n_item)
    levels = n_item // near
    slots = 2 * n // devices
    total = devices * slots
    size = total // near
    sizes = [rows // 16 * k for k in (1, 2, 4, 4, 3, 2)]

    far = [batch * n_item for batch in range(2, n_batch, 2)]
    users = {0: user_vectors}
    for mask in [near << k for k in range(log2(levels))] + far:
        users[mask] = swap(user_vectors, mask)

    (request,) = call(
        functools.partial(request_kernel, near),
        [((devices, (1 + near) * slots), i32)],
        jnp.stack([item_owner.reshape(n), item_row]),
        flops=1 << 34,
    )
    asked = lax.all_to_all(request, ("batch", "item"), split_axis=0, concat_axis=0, tiled=True)
    early = list(users)
    asked, *values = lax.optimization_barrier((asked, *users.values()))
    users = dict(zip(early, values))

    for level in range(1, levels):
        if near * level not in users:
            top = 1 << log2(level)
            users[near * level] = swap(users[near * (level - top)], near * top)
        for mask in far:
            users[mask + near * level] = swap(users[near * level], mask)

    def fetch(parts):
        return call(
            functools.partial(fetch_kernel, parts, near, n_batch),
            [((size, width), bf16)] * len(parts),
            asked,
            item_table,
            flops=2 * size * len(parts) * rows * width,
        )

    fetched = {}
    for parts in [[near - 1], list(range(1, near - 1)), [0]]:
        asked, *values = lax.optimization_barrier((asked, *fetch(parts)))
        for part, value in zip(parts, values):
            fetched[part] = swap(value, part) if part else value
    fetched = [fetched[part] for part in range(near)]

    for mask in [0, *far]:
        users[mask + n_item] = swap(users[mask], n_item)

    def group(level):
        return [users[near * level + batch * n_item] for batch in range(n_batch)]

    group_outs = [((n_batch * n, width), bf16), ((total // levels, width), bf16)]
    place, low_hot, block, *first = call(
        functools.partial(prepare_kernel, near, n_batch),
        [((total, 1), i32)] + [((BLOCK, total), bf16)] * 2 + group_outs,
        asked,
        *group(0),
        free=True,
    )
    late = {mask: users[mask] for mask in users if mask & (n_item - near)}
    place, late = lax.optimization_barrier((place, late))
    users |= late | {mask + n_item: swap(late[mask], n_item) for mask in late}
    hidden = call(
        functools.partial(hidden_kernel, levels),
        [((total, width), f32), ((total, 1), f32), ((total, width), bf16)],
        tower_weight,
        *fetched,
        flops=1 << 34,
    )
    dhidden = call(
        functools.partial(main_kernel, levels, near),
        [((size, width), bf16)] * near,
        place,
        *hidden,
        *first,
        *[value for level in range(1, levels) for value in group(level)],
        flops=1 << 31,
        mib=40,
        scratch=[pltpu.VMEM(shape, kind) for shape, kind in group_outs[:1] * (levels - 1) + group_outs[1:] * (levels - 1)],
    )
    incoming = [swap(dhidden[part], part) for part in range(1, near)]
    (drow,) = call(row_kernel, [((total, width), bf16)], tower_weight, *reversed(incoming), dhidden[0], free=True)
    order = [-part % near for part in range(near)]
    terms, drow = reduce_scatter([fetched[part] for part in order], [dhidden[part] for part in order], drow)
    table_grad = pl.pallas_call(
        functools.partial(table_kernel, sizes),
        out_specs=pl.BlockSpec(memory_space=pl.ANY),
        out_shape=jax.ShapeDtypeStruct((rows, width), bf16),
        scratch_shapes=[pltpu.VMEM((rows, width), bf16), pltpu.SemaphoreType.DMA((len(sizes),))],
        compiler_params=params(16),
        cost_estimate=cost(2 * total * rows * width, 2 * rows * width),
    )(low_hot, block, drow)
    table_grad, *terms = lax.optimization_barrier((table_grad, *terms))
    (weight_grad,) = call(last_kernel, [((width // devices, width), f32)], *terms)
    return (table_grad, weight_grad)


def solution(mesh):
    return jax.shard_map(
        local,
        mesh=mesh,
        in_specs=(
            P(("batch", "item"), None),
            P(("batch", "item"), None),
            P(),
            P(("batch", "item"), None),
            P(("batch", "item")),
        ),
        out_specs=(P(("batch", "item"), None), P(("batch", "item"), None)),
        check_vma=False,
    )
```

```python
import functools

import jax
import jax.numpy as jnp
from jax import lax
from jax.experimental import pallas as pl
from jax.experimental.pallas import tpu as pltpu
from jax.sharding import PartitionSpec as P

epsilon = 1e-06
score_scale = 60.0
cauchy_scale = 4.0
f32 = jnp.float32
bf16 = jnp.bfloat16
i32 = jnp.int32
BLOCK = 256


def iota(shape, dim):
    return lax.broadcasted_iota(i32, shape, dim)


def hot(mask):
    return jnp.where(mask, 1.0, 0.0).astype(bf16)


def dot(a, b, a_dim=1, b_dim=0):
    return lax.dot_general(a, b, (((a_dim,), (b_dim,)), ((), ())), preferred_element_type=f32)


def halves(value):
    return (value >> 8).astype(f32), (value & 255).astype(f32)


def position():
    return lax.axis_index("batch") * lax.axis_size("item") + lax.axis_index("item")


def log2(value):
    return value.bit_length() - 1


def request_kernel(near, named_ref, request_ref):
    devices, lanes = request_ref.shape
    slots = lanes // (1 + near)
    n = named_ref.shape[1]
    owner, row = named_ref[0:1], named_ref[1:2]
    device = iota((devices, n), 0)
    named = owner == device
    count = dot(hot(named), hot(iota((n, n), 0) <= iota((n, n), 1)))
    rank = jnp.sum(jnp.where(named, count, 0.0), axis=0, keepdims=True).astype(i32) - 1
    in_slot = hot(rank == iota((slots, n), 0))
    which = iota((1, n), 1)
    for k, (value, mask) in enumerate([(row, 0)] + [(which, mask) for mask in range(near)]):
        high, low = halves(value + 1)
        here = (owner ^ mask) == device
        high = dot(jnp.where(here, high, 0.0).astype(bf16), in_slot, 1, 1)
        low = dot(jnp.where(here, low, 0.0).astype(bf16), in_slot, 1, 1)
        request_ref[:, k * slots : (k + 1) * slots] = (high * 256.0 + low).astype(i32) - 1


def asker_of(spot, part, near, n_batch, slots):
    batch = (spot >> log2(slots)) & (n_batch - 1)
    level = spot >> log2(slots * n_batch)
    return position() ^ (batch * lax.axis_size("item") + level * near + part)


def slot_column(asked, part, near, n_batch):
    devices, slots = asked.shape
    total = devices * slots // near
    asker = asker_of(iota((total, devices), 0), part, near, n_batch, slots)
    pick = hot(asker == iota((total, devices), 1))
    high, low = halves(asked)
    value = dot(pick, high.astype(bf16)) * 256.0 + dot(pick, low.astype(bf16))
    mine = (iota((total, slots), 0) & (slots - 1)) == iota((total, slots), 1)
    return jnp.sum(jnp.where(mine, value, 0.0), axis=1, keepdims=True)


def slot_line(asked, near, n_batch):
    devices, slots = asked.shape
    total = devices * slots
    pick = hot((iota((slots, total), 1) & (slots - 1)) == iota((slots, total), 0))
    high, low = halves(asked)
    value = dot(high.astype(bf16), pick) * 256.0 + dot(low.astype(bf16), pick)
    spot = iota((devices, total), 1)
    asker = asker_of(spot & (total // near - 1), spot >> log2(total // near), near, n_batch, slots)
    return jnp.sum(jnp.where(asker == iota((devices, total), 0), value, 0.0), axis=0, keepdims=True)


def parts_of(value):
    return value >> 8, value & 255


def fetch_kernel(parts, near, n_batch, asked_ref, table_ref, *found):
    slots = asked_ref.shape[1] // (1 + near)
    asked = asked_ref[:, :slots]
    column = jnp.concatenate([slot_column(asked, part, near, n_batch) for part in parts], axis=0)
    block, low = parts_of(column.astype(i32))
    total = block.shape[0]
    low_hot = hot(low == iota((total, BLOCK), 1))
    block = jnp.broadcast_to(block.astype(f32), (total, BLOCK)).astype(bf16)
    picks = [
        jnp.where(block == jnp.bfloat16(k), low_hot, jnp.bfloat16(0)) for k in range(table_ref.shape[0] // BLOCK)
    ]
    rows = dot(jnp.concatenate(picks, axis=1), table_ref[...]).astype(bf16)
    size = total // len(found)
    for k, ref in enumerate(found):
        ref[...] = rows[k * size : (k + 1) * size]


def prepare_kernel(near, n_batch, asked_ref, *refs):
    *users, place_ref, low_hot_ref, block_ref, unit_ref, own_ref = refs
    n = users[0].shape[0]
    slots = asked_ref.shape[1] // (1 + near)
    size = place_ref.shape[0] // near
    batch = (iota((size, 1), 0) >> log2(slots)) & (n_batch - 1)
    for part in range(near):
        asked = asked_ref[:, (1 + part) * slots : (2 + part) * slots]
        which = slot_column(asked, 0, near, n_batch).astype(i32)
        place_ref[pl.ds(part * size, size)] = jnp.where(which < 0, -1, batch * n + which)
    block, low = parts_of(slot_line(asked_ref[:, :slots], near, n_batch).astype(i32))
    low_hot_ref[...] = hot(low == iota(low_hot_ref.shape, 0))
    block_ref[...] = jnp.broadcast_to(block.astype(f32), block_ref.shape).astype(bf16)
    users_kernel(0, near, place_ref, *users, unit_ref, own_ref)


def users_kernel(level, near, place_ref, *refs):
    *users, unit_ref, own_ref = refs
    n, width = users[0].shape
    for k, ref in enumerate(users):
        value = ref[...].astype(f32)
        mean = jnp.mean(value * value, axis=1, keepdims=True)
        unit_ref[pl.ds(k * n, n)] = (value * lax.rsqrt(mean + epsilon) * (1.0 / width**0.5)).astype(bf16)
    step = place_ref.shape[0] // near
    size = own_ref.shape[0] // near
    place = jnp.concatenate([place_ref[pl.ds(k * step + level * size, size)] for k in range(near)], axis=0)
    own_ref[...] = dot(hot(place == iota((place.shape[0], unit_ref.shape[0]), 1)), unit_ref[...]).astype(bf16)


def hidden_kernel(levels, weight_ref, *refs):
    *fetched, hidden_ref, rscale_ref, item_ref = refs
    width = weight_ref.shape[0]
    size = fetched[0].shape[0] // levels
    for level in range(levels):
        embed = jnp.concatenate([ref[pl.ds(level * size, size)] for ref in fetched], axis=0)
        here = pl.ds(level * embed.shape[0], embed.shape[0])
        hidden = dot(embed, weight_ref[...])
        rscale = lax.rsqrt(jnp.mean(hidden * hidden, axis=1, keepdims=True) + epsilon)
        hidden_ref[here] = hidden
        rscale_ref[here] = rscale
        item_ref[here] = (hidden * (rscale * (1.0 / width**0.5))).astype(bf16)


def main_kernel(levels, near, place_ref, hidden_ref, rscale_ref, item_ref, *refs):
    later = levels - 1
    units, owns = refs[0:1] + refs[len(refs) - 2 * later : len(refs) - later], refs[1:2] + refs[len(refs) - later :]
    users, outs = refs[2 : len(refs) - 2 * later - near], refs[len(refs) - 2 * later - near : len(refs) - 2 * later]
    for level in range(1, levels):
        few = len(users) // later
        users_kernel(level, near, place_ref, *users[(level - 1) * few : level * few], units[level], owns[level])
    total, width = hidden_ref.shape
    size = outs[0].shape[0] // levels
    root = 1.0 / width**0.5
    for level in range(levels):
        here = pl.ds(level * (total // levels), total // levels)
        hidden, rscale, item_vec = hidden_ref[here], rscale_ref[here], item_ref[here]
        unit = units[level][...]
        expo = jnp.exp(dot(item_vec, unit, 1, 1) * score_scale)
        sums = jnp.sum(expo, axis=1, keepdims=True)
        mixed = dot(expo.astype(bf16), unit)
        own = owns[level][...].astype(f32)
        positive = jnp.sum(item_vec.astype(f32) * own, axis=1, keepdims=True) * score_scale
        xent = jnp.log(sums) - positive
        cweight = 1.0 / (1.0 + xent * (1.0 / cauchy_scale))
        dvec = (cweight * score_scale) * (mixed * (1.0 / sums) - own)
        inner = jnp.sum(hidden * dvec, axis=1, keepdims=True)
        dhidden = (rscale * root * (dvec - hidden * (rscale * rscale * inner * (1.0 / width)))).astype(bf16)
        for part, ref in enumerate(outs):
            ref[pl.ds(level * size, size)] = dhidden[part * size : (part + 1) * size]


def coordinate(bits):
    return sum(((lax.axis_index(axis) >> level) & 1) << k for k, (axis, level) in enumerate(reversed(bits)))


def steps_of(bits):
    return sorted(range(1 << len(bits)), key=lambda step: -step.bit_count() if step else -len(bits) - 1)


def cut(blocks, bits, refs):
    size = refs[0].shape[0]
    for step, ref in zip(steps_of(bits), refs):
        ref[...] = blocks[pl.ds((coordinate(bits) ^ step) * size, size)].astype(ref.dtype)


def share_kernel(order, bits, count, *refs):
    values, (*refs, blocks) = refs[:count], refs[count:]
    embed, dhidden = (jnp.concatenate([ref[...] for ref in half], axis=0) for half in (values[: count // 2], values[count // 2 :]))
    share = dot(embed, dhidden, 0, 0)
    size = blocks.shape[1]
    for spot, block in enumerate(order):
        blocks[spot] = share[block * size : (block + 1) * size]
    cut(blocks, bits, refs)


def stage_kernel(bits, count, *refs):
    came, (*refs, blocks) = refs[:count], refs[count:]
    blocks[...] = sum(ref[...].astype(f32) for ref in came)
    cut(blocks, bits, refs)


def last_kernel(*refs):
    *came, total_ref = refs
    total_ref[...] = sum(ref[...].astype(f32) for ref in came)[0]


def row_kernel(weight_ref, *refs):
    *incoming, drow_ref = refs
    dhidden = jnp.concatenate([ref[...] for ref in reversed(incoming)], axis=0)
    drow_ref[...] = dot(dhidden, weight_ref[...], 1, 1).astype(bf16)


def table_kernel(sizes, low_hot_ref, block_ref, drow_ref, table_grad_hbm, ready, sems):
    copies, start = [], 0
    for g, size in enumerate(sizes):
        here = pl.ds(start, size)
        picks = [
            jnp.where(block_ref[...] == jnp.bfloat16(k), low_hot_ref[...], jnp.bfloat16(0))
            for k in range(start // BLOCK, (start + size) // BLOCK)
        ]
        ready[here] = dot(jnp.concatenate(picks, axis=0), drow_ref[...]).astype(bf16)
        copy = pltpu.make_async_copy(ready.at[here], table_grad_hbm.at[here], sems.at[g])
        copy.start()
        copies.append(copy)
        start += size
    for copy in copies:
        copy.wait()


def params(mib):
    return pltpu.CompilerParams(vmem_limit_bytes=mib * 1024 * 1024)


def cost(flops, bytes_accessed=1 << 20):
    return pl.CostEstimate(flops=flops, bytes_accessed=bytes_accessed, transcendentals=0)


def call(kernel, outs, *args, flops=0, scratch=(), mib=16, free=False):
    return pl.pallas_call(
        kernel,
        out_shape=[jax.ShapeDtypeStruct(shape, dtype) for shape, dtype in outs],
        scratch_shapes=scratch,
        compiler_params=params(mib),
        cost_estimate=cost(flops, 0 if free else 1 << 20),
    )(*args)


def swap(value, mask):
    devices = lax.axis_size("batch") * lax.axis_size("item")
    return lax.ppermute(value, ("batch", "item"), [(k, k ^ mask) for k in range(devices)])


def bits_of(axis):
    return [(axis, level) for level in range(log2(lax.axis_size(axis)))]


def mask_of(bits):
    return sum((lax.axis_size("item") if axis == "batch" else 1) << level for axis, level in bits)


def reduce_scatter(fetched, dhidden, drow):
    width = dhidden[0].shape[1]
    n_item, devices = lax.axis_size("item"), lax.axis_size("batch") * lax.axis_size("item")
    part = width // devices
    close = log2(len(dhidden))
    batch_bits, item_bits = bits_of("batch"), bits_of("item")
    stages = [batch_bits[:1], batch_bits[1:], item_bits[:close], item_bits[close:]]
    bits = sum(stages, [])
    order = []
    for spot in range(devices):
        at = {"batch": 0, "item": 0}
        for k, (axis, level) in enumerate(bits):
            at[axis] |= (spot >> (len(bits) - 1 - k) & 1) << level
        order.append(at["batch"] * n_item + at["item"])
    left, values = devices, [*fetched, *dhidden]
    for k, stage in enumerate(stages):
        whole, left = left, left >> len(stage)
        masks = [
            mask_of([bit for j, bit in enumerate(reversed(stage)) if step >> j & 1]) for step in steps_of(stage)[1:]
        ]
        sent = bf16
        count = len(values)
        kernel = functools.partial(stage_kernel, stage, count) if k else functools.partial(share_kernel, order, stage, count)
        kept, *sends = call(
            kernel,
            [((left, part, width), f32)] + [((left, part, width), sent)] * len(masks),
            *values,
            scratch=[pltpu.VMEM((whole, part, width), f32)],
            free=True,
        )
        values = [kept] + [swap(value, mask) for mask, value in zip(masks, sends)]
        if k == 2:
            values, drow = lax.optimization_barrier((values, drow))
    return values, drow


def local(user_vectors, item_table, tower_weight, item_owner, item_row):
    n, width = user_vectors.shape
    rows = item_table.shape[0]
    n_batch, n_item = lax.axis_size("batch"), lax.axis_size("item")
    devices = n_batch * n_item
    near = min(4, n_item)
    levels = n_item // near
    slots = 2 * n // devices
    total = devices * slots
    size = total // near
    sizes = [rows // 16 * k for k in (1, 2, 4, 4, 3, 2)]

    far = [batch * n_item for batch in range(2, n_batch, 2)]
    users = {0: user_vectors}
    for mask in [near << k for k in range(log2(levels))] + far:
        users[mask] = swap(user_vectors, mask)

    (request,) = call(
        functools.partial(request_kernel, near),
        [((devices, (1 + near) * slots), i32)],
        jnp.stack([item_owner.reshape(n), item_row]),
        flops=1 << 34,
    )
    asked = lax.all_to_all(request, ("batch", "item"), split_axis=0, concat_axis=0, tiled=True)
    early = list(users)
    asked, *values = lax.optimization_barrier((asked, *users.values()))
    users = dict(zip(early, values))

    for level in range(1, levels):
        if near * level not in users:
            top = 1 << log2(level)
            users[near * level] = swap(users[near * (level - top)], near * top)
        for mask in far:
            users[mask + near * level] = swap(users[near * level], mask)

    def fetch(parts):
        return call(
            functools.partial(fetch_kernel, parts, near, n_batch),
            [((size, width), bf16)] * len(parts),
            asked,
            item_table,
            flops=2 * size * len(parts) * rows * width,
        )

    fetched = {}
    for parts in [[near - 1], list(range(1, near - 1)), [0]]:
        asked, *values = lax.optimization_barrier((asked, *fetch(parts)))
        for part, value in zip(parts, values):
            fetched[part] = swap(value, part) if part else value
    fetched = [fetched[part] for part in range(near)]

    for mask in [0, *far]:
        users[mask + n_item] = swap(users[mask], n_item)

    def group(level):
        return [users[near * level + batch * n_item] for batch in range(n_batch)]

    group_outs = [((n_batch * n, width), bf16), ((total // levels, width), bf16)]
    place, low_hot, block, *first = call(
        functools.partial(prepare_kernel, near, n_batch),
        [((total, 1), i32)] + [((BLOCK, total), bf16)] * 2 + group_outs,
        asked,
        *group(0),
        free=True,
    )
    late = {mask: users[mask] for mask in users if mask & (n_item - near)}
    place, late = lax.optimization_barrier((place, late))
    users |= late | {mask + n_item: swap(late[mask], n_item) for mask in late}
    hidden = call(
        functools.partial(hidden_kernel, levels),
        [((total, width), f32), ((total, 1), f32), ((total, width), bf16)],
        tower_weight,
        *fetched,
        flops=1 << 34,
    )
    dhidden = call(
        functools.partial(main_kernel, levels, near),
        [((size, width), bf16)] * near,
        place,
        *hidden,
        *first,
        *[value for level in range(1, levels) for value in group(level)],
        flops=1 << 31,
        mib=40,
        scratch=[pltpu.VMEM(shape, kind) for shape, kind in group_outs[:1] * (levels - 1) + group_outs[1:] * (levels - 1)],
    )
    incoming = [swap(dhidden[part], part) for part in range(1, near)]
    (drow,) = call(row_kernel, [((total, width), bf16)], tower_weight, *reversed(incoming), dhidden[0], free=True)
    order = [-part % near for part in range(near)]
    terms, drow = reduce_scatter([fetched[part] for part in order], [dhidden[part] for part in order], drow)
    table_grad = pl.pallas_call(
        functools.partial(table_kernel, sizes),
        out_specs=pl.BlockSpec(memory_space=pl.ANY),
        out_shape=jax.ShapeDtypeStruct((rows, width), bf16),
        scratch_shapes=[pltpu.VMEM((rows, width), bf16), pltpu.SemaphoreType.DMA((len(sizes),))],
        compiler_params=params(16),
        cost_estimate=cost(2 * total * rows * width, 2 * rows * width),
    )(low_hot, block, drow)
    table_grad, *terms = lax.optimization_barrier((table_grad, *terms))
    (weight_grad,) = call(last_kernel, [((width // devices, width), f32)], *terms)
    return (table_grad, weight_grad)


def solution(mesh):
    return jax.shard_map(
        local,
        mesh=mesh,
        in_specs=(
            P(("batch", "item"), None),
            P(("batch", "item"), None),
            P(),
            P(("batch", "item"), None),
            P(("batch", "item")),
        ),
        out_specs=(P(("batch", "item"), None), P(("batch", "item"), None)),
        check_vma=False,
    )
```
